128 devices in a mesh: ha: 16 (over z, y_lo, core), wa: 8 (over x, y_hi).
Axes of the slice: x: 4, y: 4 (y_hi: 2, y_lo: 2; y = y_hi * 2 + y_lo), z: 4, core: 2. Of those that a mesh axis runs over, the one named last changes fastest.
Arguments:
- frames: bfloat16 [64, 256, 2048], P(None, 'ha', 'wa'), may hold values from -6 to 6
- w_in: bfloat16 [128, 64], replicated, may hold values from -0.75 to 0.75
- grid_mix: bfloat16 [256, 256], replicated, may hold values from -0.375 to 0.375
- block_mix: bfloat16 [256, 256], replicated, may hold values from -0.375 to 0.375
- w_out: bfloat16 [64, 64], replicated, may hold values from -0.75 to 0.75
- conv_w: bfloat16 [3, 3, 64, 64], replicated, may hold values from -0.25 to 0.25
- cotangent: bfloat16 [64, 256, 2048], P(None, 'ha', 'wa'), may hold values from -6 to 6
Outputs:
- restored: bfloat16 [64, 256, 2048], P(None, 'ha', 'wa')
- grad_frames: bfloat16 [64, 256, 2048], P(None, 'ha', 'wa')
- grad_w_in: float32 [128, 64], replicated
- grad_grid: float32 [256, 256], replicated
- grad_block: float32 [256, 256], replicated
- grad_w_out: float32 [64, 64], replicated
- grad_conv: float32 [3, 3, 64, 64], replicated
The draws below stay inside these ranges and needn't reach their ends.
All inputs are finite; a program needn't handle non-finite values.
Results may differ from the reference program's by a relative error of at most 0.0079.
Values may be sent and summed in bfloat16 or wider, within the bound.
A program may use at most 64 MiB of HBM per device.

```python
from functools import partial
import jax
import jax.numpy as jnp
from jax import lax

C = 64
GRID = 16
BLOCK = 16
H = 256
W = 2048


def steps_of(own_key, extent, cuts, least, largest):
    def one(position, parts):
        steps = jax.random.uniform(jax.random.fold_in(jax.random.fold_in(own_key, 6), position), (parts,), jnp.float32, least / len(cuts), largest / len(cuts))
        return jnp.repeat(jnp.exp(steps), extent[position] // parts).reshape((-1,) + (1,) * (len(extent) - position - 1))

    loudness = one(*cuts[0])
    for cut in cuts[1:]:
        loudness = loudness * one(*cut)
    return loudness


def centred(own_key, dims, deviation, most, shards=(), held_as=jnp.bfloat16):
    values = deviation * jax.random.normal(own_key, dims, jnp.float32)
    if shards:
        values = values * steps_of(own_key, dims, shards, -0.22, 0.18)
    return jnp.clip(values, -most, most).astype(held_as)


def setup_inputs(seed: int = 0) -> dict:
    streams_of = jax.random.split(jax.random.key(seed), 8)
    return {
        "frames": centred(streams_of[0], (C, H, W), 1.0, 6.0, ((1, 16), (2, 8))),
        "w_in": centred(streams_of[1], (2 * C, C), C ** -0.5, 0.75),
        "grid_mix": centred(streams_of[2], (GRID * GRID, GRID * GRID), (GRID * GRID) ** -0.5, 0.375),
        "block_mix": centred(streams_of[3], (BLOCK * BLOCK, BLOCK * BLOCK), (BLOCK * BLOCK) ** -0.5, 0.375),
        "w_out": centred(streams_of[4], (C, C), C ** -0.5, 0.75),
        "conv_w": centred(streams_of[5], (3, 3, C, C), (9 * C) ** -0.5, 0.25),
        "cotangent": centred(streams_of[6], (C, H, W), 1.0, 6.0, ((1, 16), (2, 8))),
    }


EPS = 1e-06

def grid_cells(field):
    depth, height, breadth = field.shape
    shaped = field.reshape(depth, GRID, height // GRID, GRID, breadth // GRID)
    return shaped.transpose(1, 3, 0, 2, 4).reshape(GRID * GRID, depth * (height // GRID) * (breadth // GRID))

def grid_field(table, depth, height, breadth):
    shaped = table.reshape(GRID, GRID, depth, height // GRID, breadth // GRID)
    return shaped.transpose(2, 0, 3, 1, 4).reshape(depth, height * breadth)

def block_cells(field):
    depth, height, breadth = field.shape
    shaped = field.reshape(depth, height // BLOCK, BLOCK, breadth // BLOCK, BLOCK)
    return shaped.transpose(2, 4, 0, 1, 3).reshape(BLOCK * BLOCK, depth * (height // BLOCK) * (breadth // BLOCK))

def block_field(table, depth, height, breadth):
    shaped = table.reshape(BLOCK, BLOCK, depth, height // BLOCK, breadth // BLOCK)
    return shaped.transpose(2, 3, 0, 4, 1).reshape(depth, height * breadth)

def contract(left, right):
    return lax.dot_general(left, right, (((1,), (1,)), ((), ())), preferred_element_type=jnp.float32)

def conv_apply(padded, kernel, height, breadth):
    total = jnp.zeros((kernel.shape[2], height * breadth), jnp.float32)
    for row_tap in range(3):
        for col_tap in range(3):
            window = padded[:, row_tap:row_tap + height, col_tap:col_tap + breadth].reshape(padded.shape[0], height * breadth)
            total = total + jnp.dot(kernel[row_tap, col_tap], window, preferred_element_type=jnp.float32)
    return total

def conv_back(padded, kernel, height, breadth):
    total = jnp.zeros((kernel.shape[3], height * breadth), jnp.float32)
    for row_tap in range(3):
        for col_tap in range(3):
            window = padded[:, 2 - row_tap:2 - row_tap + height, 2 - col_tap:2 - col_tap + breadth].reshape(padded.shape[0], height * breadth)
            total = total + jnp.dot(kernel[row_tap, col_tap].T, window, preferred_element_type=jnp.float32)
    return total

def conv_grad(upstream, padded, height, breadth):
    taps = []
    for row_tap in range(3):
        for col_tap in range(3):
            window = padded[:, row_tap:row_tap + height, col_tap:col_tap + breadth].reshape(padded.shape[0], height * breadth)
            taps.append(contract(upstream, window))
    return jnp.stack(taps).reshape(3, 3, upstream.shape[0], padded.shape[0])

def reference(frames, w_in, grid_mix, block_mix, w_out, conv_w, cotangent):
    channels, height, breadth = frames.shape
    half_chan = channels // 2
    pixels = height * breadth
    scale = float(height * breadth) ** (-0.5)
    source = frames.astype(jnp.float32).reshape(channels, pixels)
    centre = lax.optimization_barrier(jnp.mean(source, axis=0, keepdims=True))
    offset = source - centre
    inv_std = lax.rsqrt(lax.optimization_barrier(jnp.mean(offset * offset, axis=0, keepdims=True)) + EPS)
    unit = offset * inv_std
    normed = unit.astype(jnp.bfloat16)
    before = jnp.dot(w_in, normed, preferred_element_type=jnp.float32)
    hidden = jax.nn.gelu(before, approximate=True).astype(jnp.bfloat16)
    grid_gate = hidden[:half_chan].astype(jnp.float32)
    grid_value = hidden[half_chan:channels]
    block_gate = hidden[channels:channels + half_chan].astype(jnp.float32)
    block_value = hidden[channels + half_chan:]
    grid_table = grid_cells(grid_value.reshape(half_chan, height, breadth))
    grid_mixed = grid_field(jnp.dot(grid_mix, grid_table, preferred_element_type=jnp.float32).astype(jnp.bfloat16), half_chan, height, breadth).astype(jnp.float32)
    block_table = block_cells(block_value.reshape(half_chan, height, breadth))
    block_mixed = block_field(jnp.dot(block_mix, block_table, preferred_element_type=jnp.float32), half_chan, height, breadth)
    gated = jnp.concatenate([grid_gate * (grid_mixed + 1.0), block_gate * (block_mixed + 1.0)], axis=0).astype(jnp.bfloat16)
    joined = (source + jnp.dot(w_out, gated, preferred_element_type=jnp.float32)).astype(jnp.bfloat16)
    padded = jnp.pad(joined.reshape(channels, height, breadth), ((0, 0), (1, 1), (1, 1)))
    restored = (joined.astype(jnp.float32) + conv_apply(padded, conv_w, height, breadth)).astype(jnp.bfloat16)
    upstream = cotangent.reshape(channels, pixels)
    grad_conv = conv_grad(upstream, padded, height, breadth) * scale
    up_padded = jnp.pad(cotangent, ((0, 0), (1, 1), (1, 1)))
    grad_joined = (upstream.astype(jnp.float32) + conv_back(up_padded, conv_w, height, breadth)).astype(jnp.bfloat16)
    grad_w_out = contract(grad_joined, gated) * scale
    grad_gated = jnp.dot(w_out.T, grad_joined, preferred_element_type=jnp.float32)
    grad_grid_gate = grad_gated[:half_chan] * (grid_mixed + 1.0)
    grad_grid_mixed = (grad_gated[:half_chan] * grid_gate).astype(jnp.bfloat16)
    grad_block_gate = grad_gated[half_chan:] * (block_mixed + 1.0)
    grad_block_mixed = (grad_gated[half_chan:] * block_gate).astype(jnp.bfloat16)
    grid_back = grid_cells(grad_grid_mixed.reshape(half_chan, height, breadth))
    grad_grid = contract(grid_back, grid_table) * scale
    grad_grid_value = grid_field(jnp.dot(grid_mix.T, grid_back, preferred_element_type=jnp.float32).astype(jnp.bfloat16), half_chan, height, breadth).astype(jnp.float32)
    block_back = block_cells(grad_block_mixed.reshape(half_chan, height, breadth))
    grad_block = contract(block_back, block_table) * scale
    grad_block_value = block_field(jnp.dot(block_mix.T, block_back, preferred_element_type=jnp.float32), half_chan, height, breadth)
    grad_hidden = jnp.concatenate([grad_grid_gate, grad_grid_value, grad_block_gate, grad_block_value], axis=0)
    grad_before = jax.vjp(partial(jax.nn.gelu, approximate=True), before)[1](grad_hidden)[0].astype(jnp.bfloat16)
    grad_w_in = contract(grad_before, normed) * scale
    grad_normed = jnp.dot(w_in.T, grad_before, preferred_element_type=jnp.float32)
    mean_grad = lax.optimization_barrier(jnp.mean(grad_normed, axis=0, keepdims=True))
    mean_proj = lax.optimization_barrier(jnp.mean(grad_normed * unit, axis=0, keepdims=True))
    grad_source = inv_std * (grad_normed - mean_grad - unit * mean_proj)
    grad_frames = (grad_joined.astype(jnp.float32) + grad_source).astype(jnp.bfloat16)
    return (restored.reshape(channels, height, breadth), grad_frames.reshape(channels, height, breadth), grad_w_in, grad_grid, grad_block, grad_w_out, grad_conv)
```

```python
import jax
import jax.numpy as jnp
from jax import lax
from jax.experimental import pallas as pl
from jax.experimental.pallas import tpu as pltpu
from jax.sharding import PartitionSpec as P

BF = jnp.bfloat16
F32 = jnp.float32
EPS = 1e-06
MESH = pl.DeviceIdType.MESH

CH = 64
HC = 32
ROWS = 16
COLS = 256
LANES = 128
NA = 16
NW = 8

(G_ROW0, G_PACK0, G_ROW1, G_PACK1, G_VA, G_GA, G_B, G_B2, G_A2, G_E1, G_E2, G_E3, G_E4, G_T1, G_T2, G_T3) = range(16)
GROUPS = 16


def dot(a, b):
    return lax.dot_general(a, b, (((1,), (0,)), ((), ())), preferred_element_type=F32)


def dot_nt(a, b):
    return lax.dot_general(a, b, (((1,), (1,)), ((), ())), preferred_element_type=F32)


def dot_tn(a, b):
    return lax.dot_general(a, b, (((0,), (0,)), ((), ())), preferred_element_type=F32)


def swap_granules(load, store, depth):
    lane = lax.broadcasted_iota(jnp.int32, (depth, LANES), 1)
    for row_half in range(2):
        for col_half in range(2):
            held = [load(row_half * 8 + k, col_half) for k in range(8)]
            for s in range(3):
                width = 16 << s
                low = (lane & width) == 0
                for k in range(8):
                    if not k & (1 << s):
                        a, b = held[k], held[k | (1 << s)]
                        held[k] = jnp.where(low, a, pltpu.roll(b, width, 1))
                        held[k | (1 << s)] = jnp.where(low, pltpu.roll(a, LANES - width, 1), b)
            for k in range(8):
                store(col_half * 8 + k, row_half, held[k])


def half(t):
    return slice(t * LANES, (t + 1) * LANES)


def kernel(
    frames, w_in, grid_mix, block_mix, w_out, conv_w, cot,
    rest_out, gframe_out, early_out, tail_out,
    turn, xb, nb, unit, inv, dgelu, gates, bval, u3, v3, gj, gg, bback, xt, bt, bm, gbv,
    sa, ra, x32, sb, rb, sb2, rb2, sa2, ra2, gated, gbef, jp,
    row_in, pack_out, pack_in, edge_l, edge_r,
    se, re1, e1, re2, e2, re3, e4, re4, st, rt1, t1, rt2, t2, rt3,
    ssem, rsem,
):
    ia = lax.axis_index("ha")
    iw = lax.axis_index("wa")
    up, down = lax.rem(ia + NA - 1, NA), lax.rem(ia + 1, NA)
    left, right = lax.rem(iw + NW - 1, NW), lax.rem(iw + 1, NW)
    lane = lax.broadcasted_iota(jnp.int32, (CH, LANES), 1)

    def push(src, dst, g, where):
        pltpu.make_async_remote_copy(
            src_ref=src, dst_ref=dst, send_sem=ssem.at[g], recv_sem=rsem.at[g], device_id=where, device_id_type=MESH
        ).start()

    def over_w(src_of, dst, g):
        for k in range(1, NW):
            peer = lax.rem(iw + k, NW)
            push(src_of(peer), dst, g, (ia, peer))

    def over_a(src_of, dst, g):
        for k in range(1, NA):
            peer = lax.rem(ia + k, NA)
            push(src_of(peer), dst, g, (peer, iw))

    def arrived(ref, g):
        pltpu.make_async_copy(ref, ref, rsem.at[g]).wait()

    def gone(ref, g):
        pltpu.make_async_copy(ref, ref, ssem.at[g]).wait()

    barrier = pltpu.get_barrier_semaphore()
    peers = [(ia, lax.rem(iw + k, NW)) for k in range(1, NW)]
    peers += [(lax.rem(ia + k, NA), iw) for k in range(1, NA)]
    peers += [(a, b) for a in (up, down) for b in (left, right)]
    for peer in peers:
        pl.semaphore_signal(barrier, inc=1, device_id=peer, device_id_type=MESH)

    def turn_in(src):
        for t in range(2):
            turn[t] = src[:, :, half(t)].astype(F32).reshape(CH * ROWS, LANES)

    def turned(r, t):
        return turn[t, pl.ds(r, CH, stride=ROWS), :]

    def edges(pack, t0, t1, r):
        pack = jnp.where(lane == r, pltpu.roll(t0, r, 1), pack)
        return jnp.where(lane == ROWS + r, pltpu.roll(t1, r + 17, 1), pack)

    def send_halo(field, pack, which, g_row, g_pack):
        pack_out[which] = pack.astype(BF)
        push(field.at[1, CH : 2 * CH], row_in.at[which, 1], g_row, (up, iw))
        push(field.at[ROWS, CH : 2 * CH], row_in.at[which, 0], g_row, (down, iw))
        for slot, where in enumerate(
            [(ia, right), (ia, left), (down, right), (down, left), (up, right), (up, left)]
        ):
            push(pack_out.at[which], pack_in.at[which, slot], g_pack, where)

    def take_halo(field, which, g_row, g_pack):
        arrived(row_in.at[which], g_row)
        arrived(pack_in.at[which], g_pack)
        top = row_in[which, 0].astype(F32) * jnp.where(ia > 0, 1.0, 0.0)
        field[0, CH : 2 * CH] = top.astype(BF)
        bottom = row_in[which, 1].astype(F32) * jnp.where(ia < NA - 1, 1.0, 0.0)
        field[ROWS + 1, CH : 2 * CH] = bottom.astype(BF)
        first = jnp.where(ia > 0, 0, 1)
        last = jnp.where(ia < NA - 1, ROWS + 2, ROWS + 1)
        got = [pack_in[which, k].astype(F32) for k in range(6)]

        def assemble(middle, above, below, has):
            joined = jnp.where(lane == 0, above, jnp.where(lane == ROWS + 1, below, middle))
            return jnp.where((lane >= first) & (lane < jnp.where(has, last, 0)), joined, 0.0)

        edge_l[...] = assemble(
            pltpu.roll(got[0], 113, 1), pltpu.roll(got[2], 97, 1), pltpu.roll(got[4], 1, 1), iw > 0
        )
        edge_r[...] = assemble(
            pltpu.roll(got[1], 1, 1), pltpu.roll(got[3], 113, 1), pltpu.roll(got[5], 17, 1), iw < NW - 1
        )

        def shifts(p, carry):
            t0 = field[p, CH : 2 * CH, half(0)].astype(F32)
            t1 = field[p, CH : 2 * CH, half(1)].astype(F32)
            a0, a1 = pltpu.roll(t0, 1, 1), pltpu.roll(t1, 1, 1)
            b0, b1 = pltpu.roll(t0, LANES - 1, 1), pltpu.roll(t1, LANES - 1, 1)
            lh = pltpu.roll(edge_l[...], lax.rem(LANES - p, LANES), 1)
            rh = pltpu.roll(edge_r[...], LANES - 1 - p, 1)
            field[p, 0:CH, half(0)] = jnp.where(lane == 0, lh, a0).astype(BF)
            field[p, 0:CH, half(1)] = jnp.where(lane == 0, a0, a1).astype(BF)
            field[p, 2 * CH :, half(0)] = jnp.where(lane == LANES - 1, b1, b0).astype(BF)
            field[p, 2 * CH :, half(1)] = jnp.where(lane == LANES - 1, rh, b1).astype(BF)
            return carry

        lax.fori_loop(0, ROWS + 2, shifts, 0)

    turn_in(cot)

    def cot_row(r, pack):
        t0, t1 = turned(r, 0), turned(r, 1)
        u3[r + 1, CH : 2 * CH, half(0)] = t0.astype(BF)
        u3[r + 1, CH : 2 * CH, half(1)] = t1.astype(BF)
        return edges(pack, t0, t1, r)

    pack = lax.fori_loop(0, ROWS, cot_row, jnp.zeros((CH, LANES), F32))
    pl.semaphore_wait(barrier, len(peers))
    send_halo(u3, pack, 0, G_ROW0, G_PACK0)

    turn_in(frames)

    def first_row(r, carry):
        for t in range(2):
            x = turned(r, t)
            xb[r, :, half(t)] = x.astype(BF)
            off = x - jnp.mean(x, axis=0, keepdims=True)
            rstd = lax.rsqrt(jnp.mean(off * off, axis=0, keepdims=True) + EPS)
            u = off * rstd
            unit[r, :, half(t)] = u
            inv[r, :, half(t)] = jnp.broadcast_to(rstd, (8, LANES))
            nb[r, :, half(t)] = u.astype(BF)
        before = dot(w_in[...], nb[r])
        root = 0.7978845608028654
        square = before * before
        t = jnp.tanh(root * (before + 0.044715 * (before * square)))
        cdf = 0.5 * (1.0 + t)
        hidden = before * cdf
        dgelu[r] = cdf + before * ((0.5 * root) * (1.0 - t * t) * (1.0 + (3 * 0.044715) * square))
        hb = hidden.astype(BF)
        gates[r, 0:HC] = hb[0:HC]
        gates[r, HC:CH] = hb[CH : CH + HC]
        bval[r] = hb[CH + HC :]
        sa[0, r // 2, 0, lax.rem(r, 2)] = hb[HC:CH, half(0)]
        sa[0, r // 2, 1, lax.rem(r, 2)] = hb[HC:CH, half(1)]
        return carry

    lax.fori_loop(0, ROWS, first_row, 0)
    over_w(lambda peer: sa.at[0, peer], ra.at[0, iw], G_VA)
    ra[0, iw] = sa[0, iw]

    take_halo(u3, 0, G_ROW0, G_PACK0)
    back_w = jnp.concatenate(
        [conv_w[2 - a, 2 - b] for a in range(3) for b in range(3)], axis=0
    ).astype(F32).T.astype(BF)
    w_out_t = w_out[...].astype(F32).T.astype(BF)

    def back_row(r, carry):
        total = dot(back_w, u3[pl.ds(r, 3)].reshape(9 * CH, COLS))
        g = (total + u3[r + 1, CH : 2 * CH].astype(F32)).astype(BF)
        gj[r] = g
        up_gated = dot(w_out_t, g)
        gg[r] = up_gated
        mixed = (up_gated * gates[r].astype(F32)).astype(BF)
        sa[1, r // 2, 0, lax.rem(r, 2)] = mixed[0:HC, half(0)]
        sa[1, r // 2, 1, lax.rem(r, 2)] = mixed[0:HC, half(1)]
        bback[r] = mixed[HC:]
        return carry

    lax.fori_loop(0, ROWS, back_row, 0)
    over_w(lambda peer: sa.at[1, peer], ra.at[1, iw], G_GA)
    ra[1, iw] = sa[1, iw]

    def put(ref):
        def store(k, t, value):
            ref[k, :, half(t)] = value.astype(ref.dtype)

        return store

    swap_granules(lambda k, t: bval[k, :, half(t)].astype(F32), put(xt), HC)
    swap_granules(lambda k, t: bback[k, :, half(t)].astype(F32), put(bt), HC)
    values = xt[...].reshape(ROWS * HC, COLS)
    backs = bt[...].reshape(ROWS * HC, COLS)
    mixed = dot_nt(values, block_mix[...])
    swap_granules(lambda k, t: mixed[k * HC : (k + 1) * HC, half(t)], put(bm), HC)
    unmixed = dot(backs, block_mix[...])
    swap_granules(lambda k, t: unmixed[k * HC : (k + 1) * HC, half(t)], put(gbv), HC)
    part_block = dot_tn(backs, values).astype(BF)
    se[2 * COLS : 3 * COLS] = part_block[:, half(0)]
    se[3 * COLS :] = part_block[:, half(1)]

    arrived(ra.at[0, pl.ds(0, NW - 1)], G_VA)
    arrived(ra.at[1, pl.ds(0, NW - 1)], G_GA)

    def widen(j, carry):
        for a in range(2):
            for t in range(2):
                for r in range(2):
                    x32[pl.ds(((a * 2 + r) * 16 + j * 2 + t) * HC, HC), :] = ra[a, j, t, r].astype(F32)
        return carry

    lax.fori_loop(0, NW, widen, 0)

    def pick(q, carry):
        for a in range(2):
            for r in range(2):
                for c in range(4):
                    start = (a * 2 + r) * 16 * HC + q * 4 + c
                    sb[r * 8 + q, a, :, half(c)] = x32[pl.ds(start, 16, stride=HC), :].astype(BF)
        return carry

    lax.fori_loop(0, 8, pick, 0)
    over_a(lambda peer: sb.at[peer], rb.at[ia], G_B)
    rb[ia] = sb[ia]
    arrived(rb.at[pl.ds(0, NA - 1)], G_B)

    table = rb[:, 0].reshape(256, 512)
    back = rb[:, 1].reshape(256, 512)
    mix = grid_mix[...]
    sb2[:, 0] = dot(mix, table).astype(BF).reshape(NA, 16, 512)
    sb2[:, 1] = dot_tn(mix, back).astype(BF).reshape(NA, 16, 512)
    over_a(lambda peer: sb2.at[peer], rb2.at[ia], G_B2)
    rb2[ia] = sb2[ia]
    part_grid = dot_nt(back, table).astype(BF)
    se[0:COLS] = part_grid[:, half(0)]
    se[COLS : 2 * COLS] = part_grid[:, half(1)]
    over_w(lambda peer: se.at[pl.ds(pl.multiple_of(peer * 128, 128), 128)], re1.at[iw], G_E1)
    re1[iw] = se[pl.ds(pl.multiple_of(iw * 128, 128), 128)]

    arrived(rb2.at[pl.ds(0, NA - 1)], G_B2)

    def unpick(q, carry):
        for a in range(2):
            for r in range(2):
                for c in range(4):
                    start = ((a * 2 + r) * HC + q * 4 + c) * 16
                    x32[pl.ds(start, 16), :] = rb2[r * 8 + q, a, :, half(c)].astype(F32)
        return carry

    lax.fori_loop(0, 8, unpick, 0)

    def narrow(j, carry):
        for a in range(2):
            for t in range(2):
                for r in range(2):
                    start = (a * 2 + r) * HC * 16 + j * 2 + t
                    sa2[j, a, t, r] = x32[pl.ds(start, HC, stride=16), :].astype(BF)
        return carry

    lax.fori_loop(0, NW, narrow, 0)
    over_w(lambda peer: sa2.at[peer], ra2.at[iw], G_A2)
    ra2[iw] = sa2[iw]

    arrived(re1.at[pl.ds(0, NW - 1)], G_E1)
    total = re1[0].astype(F32)
    for k in range(1, NW):
        total = total + re1[k].astype(F32)
    e1[...] = total
    over_a(lambda peer: e1.at[pl.ds(pl.multiple_of(peer * 8, 8), 8)], re2.at[ia], G_E2)
    re2[ia] = e1[pl.ds(pl.multiple_of(ia * 8, 8), 8)]

    arrived(ra2.at[pl.ds(0, NW - 1)], G_A2)

    jp[0] = jnp.zeros((CH, COLS), BF)
    jp[1] = jnp.zeros((CH, COLS), BF)
    jp[ROWS + 2] = jnp.zeros((CH, COLS), BF)
    jp[ROWS + 3] = jnp.zeros((CH, COLS), BF)

    def returned(a, r):
        return [ra2[r // 2, a, t, lax.rem(r, 2)].astype(F32) for t in range(2)]

    def joined_row(r, pack):
        grid_mixed = returned(0, r)
        for t in range(2):
            gates_t = gates[r, :, half(t)].astype(F32)
            gated[r, 0:HC, half(t)] = (gates_t[0:HC] * (grid_mixed[t] + 1.0)).astype(BF)
            gated[r, HC:, half(t)] = (gates_t[HC:] * (bm[r, :, half(t)] + 1.0)).astype(BF)
        j = (xb[r].astype(F32) + dot(w_out[...], gated[r])).astype(BF)
        jp[r + 2] = j
        v3[r + 1, CH : 2 * CH] = j
        jf = j.astype(F32)
        return edges(pack, jf[:, half(0)], jf[:, half(1)], r)

    pack = lax.fori_loop(0, ROWS, joined_row, jnp.zeros((CH, LANES), F32))
    send_halo(v3, pack, 1, G_ROW1, G_PACK1)

    def before_row(r, carry):
        p_in, p_out = carry
        grid_mixed = returned(0, r)
        grid_back = returned(1, r)
        for t in range(2):
            g = gg[r, :, half(t)]
            d = dgelu[r, :, half(t)]
            gbef[r, 0:HC, half(t)] = (d[0:HC] * (g[0:HC] * (grid_mixed[t] + 1.0))).astype(BF)
            gbef[r, HC:CH, half(t)] = (d[HC:CH] * grid_back[t]).astype(BF)
            gbef[r, CH : CH + HC, half(t)] = (d[CH : CH + HC] * (g[HC:] * (bm[r, :, half(t)] + 1.0))).astype(BF)
            gbef[r, CH + HC :, half(t)] = (d[CH + HC :] * gbv[r, :, half(t)]).astype(BF)
        return p_in + dot_nt(gbef[r], nb[r]), p_out + dot_nt(gj[r], gated[r])

    p_in, p_out = lax.fori_loop(
        0, ROWS, before_row, (jnp.zeros((2 * CH, CH), F32), jnp.zeros((CH, CH), F32))
    )

    def conv_row(p, total):
        return total + dot_nt(u3[p], jp[pl.ds(p, 3)].reshape(3 * CH, COLS))

    p_conv = lax.fori_loop(0, ROWS + 2, conv_row, jnp.zeros((3 * CH, 3 * CH), F32))
    st[0 : 3 * CH] = p_conv[:, half(0)].astype(BF)
    st[3 * CH :] = jnp.concatenate(
        [p_conv[:, 2 * CH :], jnp.concatenate([p_in, p_out], axis=0)], axis=1
    ).astype(BF)
    over_w(lambda peer: st.at[pl.ds(pl.multiple_of(peer * 48, 16), 48)], rt1.at[iw], G_T1)
    rt1[iw] = st[pl.ds(pl.multiple_of(iw * 48, 16), 48)]

    arrived(re2.at[pl.ds(0, NA - 1)], G_E2)
    total = re2[0]
    for k in range(1, NA):
        total = total + re2[k]
    e2[...] = total
    over_a(lambda peer: e2, re3.at[ia], G_E3)
    re3[ia] = e2[...]

    w_in_t = w_in[...].astype(F32).T.astype(BF)

    def frame_row(r, carry):
        normed = dot(w_in_t, gbef[r])
        u = unit[r]
        mean_grad = jnp.mean(normed, axis=0, keepdims=True)
        mean_proj = jnp.mean(normed * u, axis=0, keepdims=True)
        source = inv[r, 0:1] * (normed - mean_grad - u * mean_proj)
        gframe_out[r] = (gj[r].astype(F32) + source).astype(BF)
        return carry

    lax.fori_loop(0, ROWS, frame_row, 0)

    arrived(rt1.at[pl.ds(0, NW - 1)], G_T1)
    total = rt1[0].astype(F32)
    for k in range(1, NW):
        total = total + rt1[k].astype(F32)
    t1[...] = total.astype(BF)
    over_a(lambda peer: t1, rt2.at[ia], G_T2)
    rt2[ia] = t1[...]

    arrived(re3.at[pl.ds(0, NA - 1)], G_E3)
    e4[...] = re3[...].reshape(128, LANES).astype(BF)
    over_w(lambda peer: e4, re4.at[iw], G_E4)
    re4[iw] = e4[...]

    take_halo(v3, 1, G_ROW1, G_PACK1)
    arrived(rt2.at[pl.ds(0, NA - 1)], G_T2)
    total = rt2[0].astype(F32)
    for k in range(1, NA):
        total = total + rt2[k].astype(F32)
    t2[...] = total.astype(BF)
    over_w(lambda peer: t2, rt3.at[iw], G_T3)
    rt3[iw] = t2[...]

    conv_k = jnp.concatenate(
        [conv_w[a, b].astype(F32).T for a in range(3) for b in range(3)], axis=0
    ).T.astype(BF)

    def out_row(r, carry):
        total = dot(conv_k, v3[pl.ds(r, 3)].reshape(9 * CH, COLS))
        rest_out[r] = (total + v3[r + 1, CH : 2 * CH].astype(F32)).astype(BF)
        return carry

    lax.fori_loop(0, ROWS, out_row, 0)

    arrived(re4.at[pl.ds(0, NW - 1)], G_E4)
    early_out[...] = re4[...]
    arrived(rt3.at[pl.ds(0, NW - 1)], G_T3)
    tail_out[...] = rt3[...]

    gone(row_in.at[0], G_ROW0)
    gone(pack_in.at[0], G_PACK0)
    gone(row_in.at[1], G_ROW1)
    gone(pack_in.at[1], G_PACK1)
    gone(sa.at[0, pl.ds(0, NW - 1)], G_VA)
    gone(sa.at[1, pl.ds(0, NW - 1)], G_GA)
    gone(sb.at[pl.ds(0, NA - 1)], G_B)
    gone(sb2.at[pl.ds(0, NA - 1)], G_B2)
    gone(sa2.at[pl.ds(0, NW - 1)], G_A2)
    gone(re1.at[pl.ds(0, NW - 1)], G_E1)
    gone(re2.at[pl.ds(0, NA - 1)], G_E2)
    gone(re3.at[pl.ds(0, NA - 1)], G_E3)
    gone(re4.at[pl.ds(0, NW - 1)], G_E4)
    gone(rt1.at[pl.ds(0, NW - 1)], G_T1)
    gone(rt2.at[pl.ds(0, NA - 1)], G_T2)
    gone(rt3.at[pl.ds(0, NW - 1)], G_T3)


def vm(*shape, dtype=BF):
    return pltpu.VMEM(shape, dtype)


SCRATCH = [
    vm(2, CH * ROWS, LANES, dtype=F32),
    vm(ROWS, CH, COLS),
    vm(ROWS, CH, COLS),
    vm(ROWS, CH, COLS, dtype=F32),
    vm(ROWS, 8, COLS, dtype=F32),
    vm(ROWS, 2 * CH, COLS, dtype=F32),
    vm(ROWS, CH, COLS),
    vm(ROWS, HC, COLS),
    vm(ROWS + 2, 3 * CH, COLS),
    vm(ROWS + 2, 3 * CH, COLS),
    vm(ROWS, CH, COLS),
    vm(ROWS, CH, COLS, dtype=F32),
    vm(ROWS, HC, COLS),
    vm(ROWS, HC, COLS),
    vm(ROWS, HC, COLS),
    vm(ROWS, HC, COLS, dtype=F32),
    vm(ROWS, HC, COLS, dtype=F32),
    vm(2, NW, 2, 2, HC, LANES),
    vm(2, NW, 2, 2, HC, LANES),
    vm(2 * 2 * 16 * HC, LANES, dtype=F32),
    vm(NA, 2, 16, 512),
    vm(NA, 2, 16, 512),
    vm(NA, 2, 16, 512),
    vm(NA, 2, 16, 512),
    vm(NW, 2, 2, 2, HC, LANES),
    vm(NW, 2, 2, 2, HC, LANES),
    vm(ROWS, CH, COLS),
    vm(ROWS, 2 * CH, COLS),
    vm(ROWS + 4, CH, COLS),
    vm(2, 2, CH, COLS),
    vm(2, CH, LANES),
    vm(2, 6, CH, LANES),
    vm(CH, LANES, dtype=F32),
    vm(CH, LANES, dtype=F32),
    vm(4 * COLS, LANES),
    vm(NW, 128, LANES),
    vm(128, LANES, dtype=F32),
    vm(NA, 8, LANES, dtype=F32),
    vm(8, LANES, dtype=F32),
    vm(NA, 8, LANES, dtype=F32),
    vm(128, LANES),
    vm(NW, 128, LANES),
    vm(6 * CH, LANES),
    vm(NW, 48, LANES),
    vm(48, LANES),
    vm(NA, 48, LANES),
    vm(48, LANES),
    vm(NW, 48, LANES),
    pltpu.SemaphoreType.DMA((GROUPS,)),
    pltpu.SemaphoreType.DMA((GROUPS,)),
]


def body(frames, w_in, grid_mix, block_mix, w_out, conv_w, cotangent):
    scale = float(ROWS * NA * COLS * NW) ** (-0.5)
    vmem = pl.BlockSpec(memory_space=pltpu.VMEM)
    rest, gframe, early, tail = pl.pallas_call(
        kernel,
        out_shape=(
            jax.ShapeDtypeStruct((ROWS, CH, COLS), BF),
            jax.ShapeDtypeStruct((ROWS, CH, COLS), BF),
            jax.ShapeDtypeStruct((NW, 128, LANES), BF),
            jax.ShapeDtypeStruct((NW, 48, LANES), BF),
        ),
        in_specs=[vmem] * 7,
        out_specs=(vmem,) * 4,
        scratch_shapes=SCRATCH,
        compiler_params=pltpu.CompilerParams(
            collective_id=0, has_side_effects=True, vmem_limit_bytes=56 * 1024 * 1024
        ),
    )(frames, w_in, grid_mix, block_mix, w_out, conv_w, cotangent)
    early = early.reshape(4, COLS, LANES).astype(F32) * scale
    tail = tail.reshape(2, 3 * CH, LANES).astype(F32) * scale
    grad_grid = jnp.concatenate([early[0], early[1]], axis=1)
    grad_block = jnp.concatenate([early[2], early[3]], axis=1)
    table = jnp.concatenate([tail[0], tail[1, :, :CH]], axis=1)
    grad_conv = table.reshape(3, CH, 3, CH)[::-1].transpose(2, 0, 1, 3)
    grad_w_in = tail[1, : 2 * CH, CH:]
    grad_w_out = tail[1, 2 * CH :, CH:]
    return (
        rest.transpose(1, 0, 2),
        gframe.transpose(1, 0, 2),
        grad_w_in,
        grad_grid,
        grad_block,
        grad_w_out,
        grad_conv,
    )


def solution(mesh):
    placed = (P(None, "ha", "wa"), P(), P(), P(), P(), P(), P(None, "ha", "wa"))
    return jax.shard_map(
        body,
        mesh=mesh,
        in_specs=placed,
        out_specs=(P(None, "ha", "wa"), P(None, "ha", "wa"), P(), P(), P(), P(), P()),
        check_vma=False,
    )
```

```python
import jax
import jax.numpy as jnp
from jax import lax
from jax.experimental import pallas as pl
from jax.experimental.pallas import tpu as pltpu
from jax.sharding import PartitionSpec as P

BF = jnp.bfloat16
F32 = jnp.float32
EPS = 1e-06
MESH = pl.DeviceIdType.MESH

CH = 64
HC = 32
ROWS = 16
COLS = 256
LANES = 128
NA = 16
NW = 8

(G_ROW0, G_PACK0, G_ROW1, G_PACK1, G_VA, G_VB, G_VC, G_VD, G_GA, G_GB, G_GC, G_GD) = range(12)
(G_E1, G_E2, G_E3, G_E4, G_T1, G_T2, G_T3) = range(12, 19)
GROUPS = 19


def dot(a, b):
    return lax.dot_general(a, b, (((1,), (0,)), ((), ())), preferred_element_type=F32)


def dot_nt(a, b):
    return lax.dot_general(a, b, (((1,), (1,)), ((), ())), preferred_element_type=F32)


def dot_tn(a, b):
    return lax.dot_general(a, b, (((0,), (0,)), ((), ())), preferred_element_type=F32)


def swap_granules(load, store, depth):
    lane = lax.broadcasted_iota(jnp.int32, (depth, LANES), 1)
    for row_half in range(2):
        for col_half in range(2):
            held = [load(row_half * 8 + k, col_half) for k in range(8)]
            for s in range(3):
                width = 16 << s
                low = (lane & width) == 0
                for k in range(8):
                    if not k & (1 << s):
                        a, b = held[k], held[k | (1 << s)]
                        held[k] = jnp.where(low, a, pltpu.roll(b, width, 1))
                        held[k | (1 << s)] = jnp.where(low, pltpu.roll(a, LANES - width, 1), b)
            for k in range(8):
                store(col_half * 8 + k, row_half, held[k])


def half(t):
    return slice(t * LANES, (t + 1) * LANES)


def loop(count, step, carry=0, unroll=1):
    return lax.fori_loop(0, count, step, carry, unroll=unroll)


def gelu_parts(x):
    root = 0.7978845608028654
    square = x * x
    t = jnp.tanh(root * (x + 0.044715 * (x * square)))
    cdf = 0.5 * (1.0 + t)
    return x * cdf, cdf + x * ((0.5 * root) * (1.0 - t * t) * (1.0 + (3 * 0.044715) * square))


def kernel(
    frames_hbm, w_in_t_hbm, grid_mix_hbm, block_mix_hbm, w_out_hbm, conv_w_hbm, cot_hbm,
    rest_out, gframe_out, early_out, tail_out,
    frames, w_in_t, grid_mix, block_mix, w_out, conv_w, cot, w_in,
    turn, xb, nb, unit, inv, dgelu, gates, bval, u3, v3, gj, gg, bback, xt, bt, bm, gbv,
    va, va_in, vx, vb, vb_in, vc, vc_in, vd, vd_in,
    ga, ga_in, gx, gb, gb_in, gc, gc_in, gd, gd_in,
    gated, gbef, jp, row_in, pack_out, pack_in, edge_l, edge_r,
    se, re1, e1, re2, e2, re3, e4, re4, st, rt1, t1, rt2, t2, rt3,
    ssem, rsem, isem,
):
    ia = lax.axis_index("ha")
    iw = lax.axis_index("wa")
    up, down = lax.rem(ia + NA - 1, NA), lax.rem(ia + 1, NA)
    left, right = lax.rem(iw + NW - 1, NW), lax.rem(iw + 1, NW)
    lane = lax.broadcasted_iota(jnp.int32, (CH, LANES), 1)

    loads = [
        pltpu.make_async_copy(src, dst, isem.at[k])
        for k, (src, dst) in enumerate(
            [
                (frames_hbm, frames),
                (w_in_t_hbm, w_in_t),
                (cot_hbm, cot),
                (conv_w_hbm, conv_w),
                (w_out_hbm, w_out),
                (block_mix_hbm, block_mix),
                (grid_mix_hbm, grid_mix),
            ]
        )
    ]
    for load in loads:
        load.start()

    def push(src, dst, g, where):
        pltpu.make_async_remote_copy(
            src_ref=src, dst_ref=dst, send_sem=ssem.at[g], recv_sem=rsem.at[g], device_id=where, device_id_type=MESH
        ).start()

    def over_w(src_of, dst, g):
        for k in range(1, NW):
            peer = lax.rem(iw + k, NW)
            push(src_of(peer), dst, g, (ia, peer))

    def over_a(src_of, dst, g):
        for k in range(1, NA):
            peer = lax.rem(ia + k, NA)
            push(src_of(peer), dst, g, (peer, iw))

    def arrived(ref, g):
        pltpu.make_async_copy(ref, ref, rsem.at[g]).wait()

    def gone(ref, g):
        pltpu.make_async_copy(ref, ref, ssem.at[g]).wait()

    def from_w(ref, g):
        arrived(ref.at[pl.ds(0, NW - 1)], g)

    def from_a(ref, g):
        arrived(ref.at[pl.ds(0, NA - 1)], g)

    barrier = pltpu.get_barrier_semaphore()
    peers = [(ia, lax.rem(iw + k, NW)) for k in range(1, NW)]
    peers += [(lax.rem(ia + k, NA), iw) for k in range(1, NA)]
    peers += [(a, b) for a in (up, down) for b in (left, right)]
    for peer in peers:
        pl.semaphore_signal(barrier, inc=1, device_id=peer, device_id_type=MESH)

    def turn_in(src):
        for t in range(2):
            turn[t] = src[:, :, half(t)].astype(F32).reshape(CH * ROWS, LANES)

    def turned(r, t):
        return turn[t, pl.ds(r, CH, stride=ROWS), :]

    def edges(pack, t0, t1, r):
        pack = jnp.where(lane == r, pltpu.roll(t0, r, 1), pack)
        return jnp.where(lane == ROWS + r, pltpu.roll(t1, r + 17, 1), pack)

    def send_halo(field, pack, which, g_row, g_pack):
        pack_out[which] = pack.astype(BF)
        push(field.at[1, CH : 2 * CH], row_in.at[which, 1], g_row, (up, iw))
        push(field.at[ROWS, CH : 2 * CH], row_in.at[which, 0], g_row, (down, iw))
        for slot, where in enumerate(
            [(ia, right), (ia, left), (down, right), (down, left), (up, right), (up, left)]
        ):
            push(pack_out.at[which], pack_in.at[which, slot], g_pack, where)

    def take_halo(field, which, g_row, g_pack):
        arrived(row_in.at[which], g_row)
        arrived(pack_in.at[which], g_pack)
        top = row_in[which, 0].astype(F32) * jnp.where(ia > 0, 1.0, 0.0)
        field[0, CH : 2 * CH] = top.astype(BF)
        bottom = row_in[which, 1].astype(F32) * jnp.where(ia < NA - 1, 1.0, 0.0)
        field[ROWS + 1, CH : 2 * CH] = bottom.astype(BF)
        first = jnp.where(ia > 0, 0, 1)
        last = jnp.where(ia < NA - 1, ROWS + 2, ROWS + 1)
        got = [pack_in[which, k].astype(F32) for k in range(6)]

        def assemble(middle, above, below, has):
            joined = jnp.where(lane == 0, above, jnp.where(lane == ROWS + 1, below, middle))
            return jnp.where((lane >= first) & (lane < jnp.where(has, last, 0)), joined, 0.0)

        edge_l[...] = assemble(
            pltpu.roll(got[0], 113, 1), pltpu.roll(got[2], 97, 1), pltpu.roll(got[4], 1, 1), iw > 0
        )
        edge_r[...] = assemble(
            pltpu.roll(got[1], 1, 1), pltpu.roll(got[3], 113, 1), pltpu.roll(got[5], 17, 1), iw < NW - 1
        )

        def shifts(p, carry):
            t0 = field[p, CH : 2 * CH, half(0)].astype(F32)
            t1 = field[p, CH : 2 * CH, half(1)].astype(F32)
            a0, a1 = pltpu.roll(t0, 1, 1), pltpu.roll(t1, 1, 1)
            b0, b1 = pltpu.roll(t0, LANES - 1, 1), pltpu.roll(t1, LANES - 1, 1)
            lh = pltpu.roll(edge_l[...], lax.rem(LANES - p, LANES), 1)
            rh = pltpu.roll(edge_r[...], LANES - 1 - p, 1)
            field[p, 0:CH, half(0)] = jnp.where(lane == 0, lh, a0).astype(BF)
            field[p, 0:CH, half(1)] = jnp.where(lane == 0, a0, a1).astype(BF)
            field[p, 2 * CH :, half(0)] = jnp.where(lane == LANES - 1, b1, b0).astype(BF)
            field[p, 2 * CH :, half(1)] = jnp.where(lane == LANES - 1, rh, b1).astype(BF)
            return carry

        loop(ROWS + 2, shifts, unroll=3)

    def step_a(a, a_in, g):
        over_w(lambda peer: a.at[peer], a_in.at[iw], g)
        a_in[iw] = a[iw]

    def step_b(a_in, x, b, b_in, g_a, g_b):
        from_w(a_in, g_a)

        def widen(j, carry):
            for t in range(2):
                for r in range(2):
                    x[pl.ds((r * 16 + j * 2 + t) * HC, HC), :] = a_in[j, t, r].astype(F32)
            return carry

        loop(NW, widen, unroll=4)

        def pick(q, carry):
            for r in range(2):
                for c in range(4):
                    b[r * 8 + q, :, half(c)] = x[pl.ds(r * 16 * HC + q * 4 + c, 16, stride=HC), :].astype(BF)
            return carry

        loop(8, pick, unroll=4)
        over_a(lambda peer: b.at[peer], b_in.at[ia], g_b)
        b_in[ia] = b[ia]

    def step_c(mixed, c, c_in, g):
        c[...] = mixed.astype(BF).reshape(NA, 16, 512)
        over_a(lambda peer: c.at[peer], c_in.at[ia], g)
        c_in[ia] = c[ia]

    def step_d(c_in, x, d, d_in, g_c, g_d):
        from_a(c_in, g_c)

        def unpick(q, carry):
            for r in range(2):
                for c in range(4):
                    x[pl.ds((r * HC + q * 4 + c) * 16, 16), :] = c_in[r * 8 + q, :, half(c)].astype(F32)
            return carry

        loop(8, unpick, unroll=4)

        def narrow(j, carry):
            for t in range(2):
                for r in range(2):
                    d[j, t, r] = x[pl.ds(r * HC * 16 + j * 2 + t, HC, stride=16), :].astype(BF)
            return carry

        loop(NW, narrow, unroll=4)
        over_w(lambda peer: d.at[peer], d_in.at[iw], g_d)
        d_in[iw] = d[iw]

    loads[0].wait()
    loads[1].wait()
    turn_in(frames)
    w_in[...] = w_in_t[...].astype(F32).T.astype(BF)

    def value_row(r, carry):
        for t in range(2):
            x = turned(r, t)
            xb[r, :, half(t)] = x.astype(BF)
            off = x - jnp.mean(x, axis=0, keepdims=True)
            rstd = lax.rsqrt(jnp.mean(off * off, axis=0, keepdims=True) + EPS)
            u = off * rstd
            unit[r, :, half(t)] = u
            inv[r, :, half(t)] = jnp.broadcast_to(rstd, (8, LANES))
            nb[r, :, half(t)] = u.astype(BF)
        value, slope = gelu_parts(dot(w_in[HC:CH], nb[r]))
        dgelu[r, HC:CH] = slope
        value = value.astype(BF)
        va[r // 2, 0, lax.rem(r, 2)] = value[:, half(0)]
        va[r // 2, 1, lax.rem(r, 2)] = value[:, half(1)]
        return carry

    loop(ROWS, value_row, unroll=4)
    pl.semaphore_wait(barrier, len(peers))
    step_a(va, va_in, G_VA)

    loads[2].wait()
    turn_in(cot)

    def cot_row(r, pack):
        t0, t1 = turned(r, 0), turned(r, 1)
        u3[r + 1, CH : 2 * CH, half(0)] = t0.astype(BF)
        u3[r + 1, CH : 2 * CH, half(1)] = t1.astype(BF)
        return edges(pack, t0, t1, r)

    pack = loop(ROWS, cot_row, jnp.zeros((CH, LANES), F32), unroll=4)
    send_halo(u3, pack, 0, G_ROW0, G_PACK0)

    def gate_row(r, carry):
        before = dot(w_in[...], nb[r])
        value, slope = gelu_parts(before[0:HC])
        gates[r, 0:HC] = value.astype(BF)
        dgelu[r, 0:HC] = slope
        value, slope = gelu_parts(before[CH:])
        dgelu[r, CH:] = slope
        value = value.astype(BF)
        gates[r, HC:CH] = value[0:HC]
        bval[r] = value[HC:]
        return carry

    loop(ROWS, gate_row, unroll=2)
    step_b(va_in, vx, vb, vb_in, G_VA, G_VB)

    take_halo(u3, 0, G_ROW0, G_PACK0)
    for load in loads[3:]:
        load.wait()
    back_w = jnp.concatenate(
        [conv_w[2 - a, 2 - b] for a in range(3) for b in range(3)], axis=0
    ).astype(F32).T.astype(BF)
    w_out_t = w_out[...].astype(F32).T.astype(BF)

    def back_row(r, carry):
        total = dot(back_w, u3[pl.ds(r, 3)].reshape(9 * CH, COLS))
        g = (total + u3[r + 1, CH : 2 * CH].astype(F32)).astype(BF)
        gj[r] = g
        up_gated = dot(w_out_t, g)
        gg[r] = up_gated
        mixed = (up_gated * gates[r].astype(F32)).astype(BF)
        ga[r // 2, 0, lax.rem(r, 2)] = mixed[0:HC, half(0)]
        ga[r // 2, 1, lax.rem(r, 2)] = mixed[0:HC, half(1)]
        bback[r] = mixed[HC:]
        return carry

    loop(ROWS, back_row, unroll=4)
    step_a(ga, ga_in, G_GA)

    mix = grid_mix[...]
    from_a(vb_in, G_VB)
    step_c(dot(mix, vb_in[...].reshape(256, 512)), vc, vc_in, G_VC)

    def put(ref):
        def store(k, t, value):
            ref[k, :, half(t)] = value.astype(ref.dtype)

        return store

    swap_granules(lambda k, t: bval[k, :, half(t)].astype(F32), put(xt), HC)
    values = xt[...].reshape(ROWS * HC, COLS)
    mixed = dot_nt(values, block_mix[...])
    swap_granules(lambda k, t: mixed[k * HC : (k + 1) * HC, half(t)], put(bm), HC)

    step_b(ga_in, gx, gb, gb_in, G_GA, G_GB)
    step_d(vc_in, vx, vd, vd_in, G_VC, G_VD)

    swap_granules(lambda k, t: bback[k, :, half(t)].astype(F32), put(bt), HC)
    backs = bt[...].reshape(ROWS * HC, COLS)
    unmixed = dot(backs, block_mix[...])
    swap_granules(lambda k, t: unmixed[k * HC : (k + 1) * HC, half(t)], put(gbv), HC)
    part_block = dot_tn(backs, values).astype(BF)
    se[2 * COLS : 3 * COLS] = part_block[:, half(0)]
    se[3 * COLS :] = part_block[:, half(1)]

    from_a(gb_in, G_GB)
    back = gb_in[...].reshape(256, 512)
    step_c(dot_tn(mix, back), gc, gc_in, G_GC)
    part_grid = dot_nt(back, vb_in[...].reshape(256, 512)).astype(BF)
    se[0:COLS] = part_grid[:, half(0)]
    se[COLS : 2 * COLS] = part_grid[:, half(1)]
    over_w(lambda peer: se.at[pl.ds(pl.multiple_of(peer * 128, 128), 128)], re1.at[iw], G_E1)
    re1[iw] = se[pl.ds(pl.multiple_of(iw * 128, 128), 128)]

    for k in (0, 1, ROWS + 2, ROWS + 3):
        jp[k] = jnp.zeros((CH, COLS), BF)
    from_w(vd_in, G_VD)

    def returned(ref, r):
        return [ref[r // 2, t, lax.rem(r, 2)].astype(F32) for t in range(2)]

    def joined_row(r, pack):
        grid_mixed = returned(vd_in, r)
        for t in range(2):
            gates_t = gates[r, :, half(t)].astype(F32)
            gated[r, 0:HC, half(t)] = (gates_t[0:HC] * (grid_mixed[t] + 1.0)).astype(BF)
            gated[r, HC:, half(t)] = (gates_t[HC:] * (bm[r, :, half(t)] + 1.0)).astype(BF)
        j = (xb[r].astype(F32) + dot(w_out[...], gated[r])).astype(BF)
        jp[r + 2] = j
        v3[r + 1, CH : 2 * CH] = j
        jf = j.astype(F32)
        return edges(pack, jf[:, half(0)], jf[:, half(1)], r)

    pack = loop(ROWS, joined_row, jnp.zeros((CH, LANES), F32), unroll=4)
    send_halo(v3, pack, 1, G_ROW1, G_PACK1)

    step_d(gc_in, gx, gd, gd_in, G_GC, G_GD)

    def conv_row(p, total):
        return total + dot_nt(u3[p], jp[pl.ds(p, 3)].reshape(3 * CH, COLS))

    p_conv = loop(ROWS + 2, conv_row, jnp.zeros((3 * CH, 3 * CH), F32), unroll=3)

    from_w(re1, G_E1)
    total = re1[0].astype(F32)
    for k in range(1, NW):
        total = total + re1[k].astype(F32)
    e1[...] = total
    over_a(lambda peer: e1.at[pl.ds(pl.multiple_of(peer * 8, 8), 8)], re2.at[ia], G_E2)
    re2[ia] = e1[pl.ds(pl.multiple_of(ia * 8, 8), 8)]

    from_w(gd_in, G_GD)

    def before_row(r, carry):
        p_in, p_out = carry
        grid_mixed = returned(vd_in, r)
        grid_back = returned(gd_in, r)
        for t in range(2):
            g = gg[r, :, half(t)]
            d = dgelu[r, :, half(t)]
            gbef[r, 0:HC, half(t)] = (d[0:HC] * (g[0:HC] * (grid_mixed[t] + 1.0))).astype(BF)
            gbef[r, HC:CH, half(t)] = (d[HC:CH] * grid_back[t]).astype(BF)
            gbef[r, CH : CH + HC, half(t)] = (d[CH : CH + HC] * (g[HC:] * (bm[r, :, half(t)] + 1.0))).astype(BF)
            gbef[r, CH + HC :, half(t)] = (d[CH + HC :] * gbv[r, :, half(t)]).astype(BF)
        return p_in + dot_nt(nb[r], gbef[r]), p_out + dot_nt(gj[r], gated[r])

    p_in, p_out = loop(
        ROWS, before_row, (jnp.zeros((CH, 2 * CH), F32), jnp.zeros((CH, CH), F32)), unroll=4
    )
    st[0 : 3 * CH] = p_conv[:, half(0)].astype(BF)
    st[3 * CH : 4 * CH] = p_in.astype(BF)
    third = p_conv[:, 2 * CH :]
    st[4 * CH :] = jnp.concatenate(
        [third[: 2 * CH], jnp.concatenate([third[2 * CH :], p_out], axis=0)], axis=1
    ).astype(BF)
    over_w(lambda peer: st.at[pl.ds(pl.multiple_of(peer * 48, 16), 48)], rt1.at[iw], G_T1)
    rt1[iw] = st[pl.ds(pl.multiple_of(iw * 48, 16), 48)]

    from_a(re2, G_E2)
    total = re2[0]
    for k in range(1, NA):
        total = total + re2[k]
    e2[...] = total
    over_a(lambda peer: e2, re3.at[ia], G_E3)
    re3[ia] = e2[...]

    def frame_row(r, carry):
        normed = dot(w_in_t[...], gbef[r])
        u = unit[r]
        mean_grad = jnp.mean(normed, axis=0, keepdims=True)
        mean_proj = jnp.mean(normed * u, axis=0, keepdims=True)
        source = gj[r].astype(F32) + inv[r, 0:1] * (normed - mean_grad - u * mean_proj)
        for t in range(2):
            gframe_out[t, pl.ds(r * CH, CH), :] = source[:, half(t)]
        return carry

    loop(ROWS, frame_row, unroll=4)

    from_w(rt1, G_T1)
    total = rt1[0].astype(F32)
    for k in range(1, NW):
        total = total + rt1[k].astype(F32)
    t1[...] = total.astype(BF)
    over_a(lambda peer: t1, rt2.at[ia], G_T2)
    rt2[ia] = t1[...]

    from_a(re3, G_E3)
    e4[...] = re3[...].reshape(128, LANES).astype(BF)
    over_w(lambda peer: e4, re4.at[iw], G_E4)
    re4[iw] = e4[...]

    take_halo(v3, 1, G_ROW1, G_PACK1)
    from_a(rt2, G_T2)
    total = rt2[0].astype(F32)
    for k in range(1, NA):
        total = total + rt2[k].astype(F32)
    t2[...] = total.astype(BF)
    over_w(lambda peer: t2, rt3.at[iw], G_T3)
    rt3[iw] = t2[...]

    conv_k = jnp.concatenate(
        [conv_w[a, b].astype(F32).T for a in range(3) for b in range(3)], axis=0
    ).T.astype(BF)

    def out_row(r, carry):
        total = dot(conv_k, v3[pl.ds(r, 3)].reshape(9 * CH, COLS))
        total = total + v3[r + 1, CH : 2 * CH].astype(F32)
        for t in range(2):
            rest_out[t, pl.ds(r * CH, CH), :] = total[:, half(t)]
        return carry

    loop(ROWS, out_row, unroll=4)

    from_w(re4, G_E4)
    early_out[...] = re4[...]
    from_w(rt3, G_T3)
    tail_out[...] = rt3[...]

    for which, g_row, g_pack in ((0, G_ROW0, G_PACK0), (1, G_ROW1, G_PACK1)):
        gone(row_in.at[which], g_row)
        gone(pack_in.at[which], g_pack)
    for ref, g in (
        (va_in, G_VA), (vd_in, G_VD), (ga_in, G_GA), (gd_in, G_GD),
        (re1, G_E1), (re4, G_E4), (rt1, G_T1), (rt3, G_T3),
    ):
        gone(ref.at[pl.ds(0, NW - 1)], g)
    for ref, g in (
        (vb_in, G_VB), (vc_in, G_VC), (gb_in, G_GB), (gc_in, G_GC), (re2, G_E2), (re3, G_E3), (rt2, G_T2),
    ):
        gone(ref.at[pl.ds(0, NA - 1)], g)


def finish(rest, gframe, early, tail, restored, grad_frames, grad_w_in_t, grad_grid, grad_block, grad_w_out, grad_conv):
    scale = float(ROWS * NA * COLS * NW) ** (-0.5)

    def channel(c, carry):
        for src, dst in ((rest, restored), (gframe, grad_frames)):
            for t in range(2):
                dst[c, :, half(t)] = src[t, pl.ds(c, ROWS, stride=CH), :].astype(BF)
        return carry

    loop(CH, channel, unroll=8)

    for k in range(2):
        grad_grid[:, half(k)] = early[k * COLS : (k + 1) * COLS].astype(F32) * scale
        grad_block[:, half(k)] = early[(2 + k) * COLS : (3 + k) * COLS].astype(F32) * scale
    grad_w_in_t[...] = tail[3 * CH : 4 * CH].astype(F32) * scale
    last = tail[4 * CH :].astype(F32) * scale
    grad_w_out[...] = last[CH:, CH:]
    for b in range(3):
        rows = slice((2 - b) * CH, (3 - b) * CH)
        pair = tail[rows].astype(F32) * scale
        grad_conv[0, b] = pair[:, :CH]
        grad_conv[1, b] = pair[:, CH:]
    grad_conv[2, 2] = last[:CH, :CH]
    grad_conv[2, 1] = last[CH:, :CH]
    grad_conv[2, 0] = last[:CH, CH:]


def vm(*shape, dtype=BF):
    return pltpu.VMEM(shape, dtype)


def exchange():
    message_w = vm(NW, 2, 2, HC, LANES)
    message_a = vm(NA, 16, 512)
    return [message_w, message_w, vm(2 * 16 * HC, LANES, dtype=F32)] + [message_a] * 4 + [message_w] * 2


SCRATCH = [
    vm(CH, ROWS, COLS),
    vm(CH, 2 * CH),
    vm(COLS, COLS),
    vm(COLS, COLS),
    vm(CH, CH),
    vm(3, 3, CH, CH),
    vm(CH, ROWS, COLS),
    vm(2 * CH, CH),
    vm(2, CH * ROWS, LANES, dtype=F32),
    vm(ROWS, CH, COLS),
    vm(ROWS, CH, COLS),
    vm(ROWS, CH, COLS, dtype=F32),
    vm(ROWS, 8, COLS, dtype=F32),
    vm(ROWS, 2 * CH, COLS, dtype=F32),
    vm(ROWS, CH, COLS),
    vm(ROWS, HC, COLS),
    vm(ROWS + 2, 3 * CH, COLS),
    vm(ROWS + 2, 3 * CH, COLS),
    vm(ROWS, CH, COLS),
    vm(ROWS, CH, COLS, dtype=F32),
    vm(ROWS, HC, COLS),
    vm(ROWS, HC, COLS),
    vm(ROWS, HC, COLS),
    vm(ROWS, HC, COLS, dtype=F32),
    vm(ROWS, HC, COLS, dtype=F32),
    *exchange(),
    *exchange(),
    vm(ROWS, CH, COLS),
    vm(ROWS, 2 * CH, COLS),
    vm(ROWS + 4, CH, COLS),
    vm(2, 2, CH, COLS),
    vm(2, CH, LANES),
    vm(2, 6, CH, LANES),
    vm(CH, LANES, dtype=F32),
    vm(CH, LANES, dtype=F32),
    vm(4 * COLS, LANES),
    vm(NW, 128, LANES),
    vm(128, LANES, dtype=F32),
    vm(NA, 8, LANES, dtype=F32),
    vm(8, LANES, dtype=F32),
    vm(NA, 8, LANES, dtype=F32),
    vm(128, LANES),
    vm(NW, 128, LANES),
    vm(6 * CH, LANES),
    vm(NW, 48, LANES),
    vm(48, LANES),
    vm(NA, 48, LANES),
    vm(48, LANES),
    vm(NW, 48, LANES),
    pltpu.SemaphoreType.DMA((GROUPS,)),
    pltpu.SemaphoreType.DMA((GROUPS,)),
    pltpu.SemaphoreType.DMA((7,)),
]


def body(frames, w_in, grid_mix, block_mix, w_out, conv_w, cotangent):
    vmem = pl.BlockSpec(memory_space=pltpu.VMEM)
    shape = jax.ShapeDtypeStruct
    rest, gframe, early, tail = pl.pallas_call(
        kernel,
        out_shape=(
            shape((2, ROWS * CH, LANES), F32),
            shape((2, ROWS * CH, LANES), F32),
            shape((NW, 128, LANES), BF),
            shape((NW, 48, LANES), BF),
        ),
        in_specs=[pl.BlockSpec(memory_space=pltpu.HBM)] * 7,
        out_specs=(vmem,) * 4,
        scratch_shapes=SCRATCH,
        compiler_params=pltpu.CompilerParams(
            collective_id=0, has_side_effects=True, vmem_limit_bytes=32 * 1024 * 1024
        ),
    )(frames, w_in.T, grid_mix, block_mix, w_out, conv_w, cotangent)
    restored, grad_frames, grad_w_in_t, grad_grid, grad_block, grad_w_out, grad_conv = pl.pallas_call(
        finish,
        out_shape=(
            shape((CH, ROWS, COLS), BF),
            shape((CH, ROWS, COLS), BF),
            shape((CH, 2 * CH), F32),
            shape((COLS, COLS), F32),
            shape((COLS, COLS), F32),
            shape((CH, CH), F32),
            shape((3, 3, CH, CH), F32),
        ),
        in_specs=[vmem] * 4,
        out_specs=(vmem,) * 7,
        compiler_params=pltpu.CompilerParams(vmem_limit_bytes=16 * 1024 * 1024),
    )(rest, gframe, early.reshape(4 * COLS, LANES), tail.reshape(6 * CH, LANES))
    return restored, grad_frames, grad_w_in_t.T, grad_grid, grad_block, grad_w_out, grad_conv


def solution(mesh):
    placed = (P(None, "ha", "wa"), P(), P(), P(), P(), P(), P(None, "ha", "wa"))
    return jax.shard_map(
        body,
        mesh=mesh,
        in_specs=placed,
        out_specs=(P(None, "ha", "wa"), P(None, "ha", "wa"), P(), P(), P(), P(), P()),
        check_vma=False,
    )
```

```python
import jax
import jax.numpy as jnp
from jax import lax
from jax.experimental import pallas as pl
from jax.experimental.pallas import tpu as pltpu
from jax.sharding import PartitionSpec as P

BF = jnp.bfloat16
F32 = jnp.float32
EPS = 1e-06
MESH = pl.DeviceIdType.MESH

CH = 64
HC = 32
ROWS = 16
COLS = 256
LANES = 128
NA = 16
NW = 8

(G_ROW0, G_PACK0, G_ROW1, G_PACK1, G_VA, G_VB, G_VC, G_VD, G_GA, G_GB, G_GC, G_GD) = range(12)
(G_E1, G_E2, G_E3, G_E4, G_T1, G_T2, G_T3) = range(12, 19)
GROUPS = 19


def dot(a, b):
    return lax.dot_general(a, b, (((1,), (0,)), ((), ())), preferred_element_type=F32)


def dot_nt(a, b):
    return lax.dot_general(a, b, (((1,), (1,)), ((), ())), preferred_element_type=F32)


def dot_tn(a, b):
    return lax.dot_general(a, b, (((0,), (0,)), ((), ())), preferred_element_type=F32)


def swap_granules(load, store, depth):
    lane = lax.broadcasted_iota(jnp.int32, (depth, LANES), 1)
    for row_half in range(2):
        for col_half in range(2):
            held = [load(row_half * 8 + k, col_half) for k in range(8)]
            for s in range(3):
                width = 16 << s
                low = (lane & width) == 0
                for k in range(8):
                    if not k & (1 << s):
                        a, b = held[k], held[k | (1 << s)]
                        held[k] = jnp.where(low, a, pltpu.roll(b, width, 1))
                        held[k | (1 << s)] = jnp.where(low, pltpu.roll(a, LANES - width, 1), b)
            for k in range(8):
                store(col_half * 8 + k, row_half, held[k])


def half(t):
    return slice(t * LANES, (t + 1) * LANES)


def loop(count, step, carry=0, unroll=1):
    return lax.fori_loop(0, count, step, carry, unroll=unroll)


def gelu_parts(x):
    root = 0.7978845608028654
    cube = root * 0.044715
    square = x * x
    h = 0.5 * jnp.tanh(x * (cube * square + root)) + 0.5
    value = x * h
    return value, h + value * (1.0 - h) * ((6.0 * cube) * square + 2.0 * root)


def kernel(
    frames_hbm, w_in_t_hbm, grid_mix_hbm, block_mix_hbm, w_out_hbm, conv_w_hbm, cot_hbm,
    rest_out, gframe_out, early_out, tail_out,
    frames, w_in_t, grid_mix, block_mix, w_out, conv_w, cot, w_in,
    turn, xb, nb, unit, inv, dgelu, gates, bval, u3, v3, gj, gg, bback, xt, bt, bm, gbv,
    va, va_in, vx, vb, vb_in, vc, vc_in, vd, vd_in,
    ga, ga_in, gx, gb, gb_in, gc, gc_in, gd, gd_in,
    gated, gbef, jp, row_in, pack_out, pack_in, edge_l, edge_r,
    se, re1, e1, re2, e2, re3, e4, re4, st, rt1, t1, rt2, t2, rt3,
    ssem, rsem, isem,
):
    ia = lax.axis_index("ha")
    iw = lax.axis_index("wa")
    up, down = lax.rem(ia + NA - 1, NA), lax.rem(ia + 1, NA)
    left, right = lax.rem(iw + NW - 1, NW), lax.rem(iw + 1, NW)
    lane = lax.broadcasted_iota(jnp.int32, (CH, LANES), 1)

    loads = [
        pltpu.make_async_copy(src, dst, isem.at[k])
        for k, (src, dst) in enumerate(
            [
                (frames_hbm, frames),
                (w_in_t_hbm, w_in_t),
                (cot_hbm, cot),
                (conv_w_hbm, conv_w),
                (w_out_hbm, w_out),
                (block_mix_hbm, block_mix),
                (grid_mix_hbm, grid_mix),
            ]
        )
    ]
    for load in loads:
        load.start()

    def push(src, dst, g, where):
        pltpu.make_async_remote_copy(
            src_ref=src, dst_ref=dst, send_sem=ssem.at[g], recv_sem=rsem.at[g], device_id=where, device_id_type=MESH
        ).start()

    def over_w(src_of, dst, g):
        for k in range(1, NW):
            peer = lax.rem(iw + k, NW)
            push(src_of(peer), dst, g, (ia, peer))

    def over_a(src_of, dst, g):
        for k in range(1, NA):
            peer = lax.rem(ia + k, NA)
            push(src_of(peer), dst, g, (peer, iw))

    def arrived(ref, g):
        pltpu.make_async_copy(ref, ref, rsem.at[g]).wait()

    def gone(ref, g):
        pltpu.make_async_copy(ref, ref, ssem.at[g]).wait()

    def from_w(ref, g):
        arrived(ref.at[pl.ds(0, NW - 1)], g)

    def from_a(ref, g):
        arrived(ref.at[pl.ds(0, NA - 1)], g)

    barrier = pltpu.get_barrier_semaphore()
    peers = [(ia, lax.rem(iw + k, NW)) for k in range(1, NW)]
    peers += [(lax.rem(ia + k, NA), iw) for k in range(1, NA)]
    peers += [(a, b) for a in (up, down) for b in (left, right)]
    for peer in peers:
        pl.semaphore_signal(barrier, inc=1, device_id=peer, device_id_type=MESH)

    def turn_in(src):
        for t in range(2):
            turn[t] = src[:, :, half(t)].astype(F32).reshape(CH * ROWS, LANES)

    def turned(r, t):
        return turn[t, pl.ds(r, CH, stride=ROWS), :]

    def edges(pack, t0, t1, r):
        pack = jnp.where(lane == r, pltpu.roll(t0, r, 1), pack)
        return jnp.where(lane == ROWS + r, pltpu.roll(t1, r + 17, 1), pack)

    def send_halo(field, pack, which, g_row, g_pack):
        pack_out[which] = pack.astype(BF)
        push(field.at[1, CH : 2 * CH], row_in.at[which, 1], g_row, (up, iw))
        push(field.at[ROWS, CH : 2 * CH], row_in.at[which, 0], g_row, (down, iw))
        for slot, where in enumerate(
            [(ia, right), (ia, left), (down, right), (down, left), (up, right), (up, left)]
        ):
            push(pack_out.at[which], pack_in.at[which, slot], g_pack, where)

    def take_halo(field, which, g_row, g_pack):
        arrived(row_in.at[which], g_row)
        arrived(pack_in.at[which], g_pack)
        top = row_in[which, 0].astype(F32) * jnp.where(ia > 0, 1.0, 0.0)
        field[0, CH : 2 * CH] = top.astype(BF)
        bottom = row_in[which, 1].astype(F32) * jnp.where(ia < NA - 1, 1.0, 0.0)
        field[ROWS + 1, CH : 2 * CH] = bottom.astype(BF)
        first = jnp.where(ia > 0, 0, 1)
        last = jnp.where(ia < NA - 1, ROWS + 2, ROWS + 1)
        got = [pack_in[which, k].astype(F32) for k in range(6)]

        def assemble(middle, above, below, has):
            joined = jnp.where(lane == 0, above, jnp.where(lane == ROWS + 1, below, middle))
            return jnp.where((lane >= first) & (lane < jnp.where(has, last, 0)), joined, 0.0)

        edge_l[...] = assemble(
            pltpu.roll(got[0], 113, 1), pltpu.roll(got[2], 97, 1), pltpu.roll(got[4], 1, 1), iw > 0
        )
        edge_r[...] = assemble(
            pltpu.roll(got[1], 1, 1), pltpu.roll(got[3], 113, 1), pltpu.roll(got[5], 17, 1), iw < NW - 1
        )

        def shifts(p, carry):
            t0 = field[p, CH : 2 * CH, half(0)].astype(F32)
            t1 = field[p, CH : 2 * CH, half(1)].astype(F32)
            a0, a1 = pltpu.roll(t0, 1, 1), pltpu.roll(t1, 1, 1)
            b0, b1 = pltpu.roll(t0, LANES - 1, 1), pltpu.roll(t1, LANES - 1, 1)
            lh = pltpu.roll(edge_l[...], lax.rem(LANES - p, LANES), 1)
            rh = pltpu.roll(edge_r[...], LANES - 1 - p, 1)
            field[p, 0:CH, half(0)] = jnp.where(lane == 0, lh, a0).astype(BF)
            field[p, 0:CH, half(1)] = jnp.where(lane == 0, a0, a1).astype(BF)
            field[p, 2 * CH :, half(0)] = jnp.where(lane == LANES - 1, b1, b0).astype(BF)
            field[p, 2 * CH :, half(1)] = jnp.where(lane == LANES - 1, rh, b1).astype(BF)
            return carry

        loop(ROWS + 2, shifts, unroll=3)

    def conv_start(w, field):
        y = dot(w, field[0])
        z = dot(w, field[1])
        return z[0:CH], y[0:CH] + z[CH : 2 * CH]

    def conv_step(w, field, r, carry):
        later, now = carry
        y = dot(w, field[r + 2])
        return now + y[2 * CH :], (y[0:CH], later + y[CH : 2 * CH])

    def step_a(a, a_in, g):
        over_w(lambda peer: a.at[peer], a_in.at[iw], g)
        a_in[iw] = a[iw]

    def step_b(a_in, x, b, b_in, g_a, g_b):
        from_w(a_in, g_a)

        def widen(j, carry):
            for t in range(2):
                for r in range(2):
                    x[pl.ds((r * 16 + j * 2 + t) * HC, HC), :] = a_in[j, t, r].astype(F32)
            return carry

        loop(NW, widen, unroll=4)

        def pick(q, carry):
            for r in range(2):
                for c in range(4):
                    b[r * 8 + q, :, half(c)] = x[pl.ds(r * 16 * HC + q * 4 + c, 16, stride=HC), :].astype(BF)
            return carry

        loop(8, pick, unroll=4)
        over_a(lambda peer: b.at[peer], b_in.at[ia], g_b)
        b_in[ia] = b[ia]

    def step_c(mixed, c, c_in, g):
        c[...] = mixed.astype(BF).reshape(NA, 16, 512)
        over_a(lambda peer: c.at[peer], c_in.at[ia], g)
        c_in[ia] = c[ia]

    def step_d(c_in, x, d, d_in, g_c, g_d):
        from_a(c_in, g_c)

        def unpick(q, carry):
            for r in range(2):
                for c in range(4):
                    x[pl.ds((r * HC + q * 4 + c) * 16, 16), :] = c_in[r * 8 + q, :, half(c)].astype(F32)
            return carry

        loop(8, unpick, unroll=4)

        def narrow(j, carry):
            for t in range(2):
                for r in range(2):
                    d[j, t, r] = x[pl.ds(r * HC * 16 + j * 2 + t, HC, stride=16), :].astype(BF)
            return carry

        loop(NW, narrow, unroll=4)
        over_w(lambda peer: d.at[peer], d_in.at[iw], g_d)
        d_in[iw] = d[iw]

    loads[0].wait()
    loads[1].wait()
    turn_in(frames)
    w_in[...] = w_in_t[...].astype(F32).T.astype(BF)

    def value_row(r, carry):
        for t in range(2):
            x = turned(r, t)
            xb[r, :, half(t)] = x.astype(BF)
            off = x - jnp.mean(x, axis=0, keepdims=True)
            rstd = lax.rsqrt(jnp.mean(off * off, axis=0, keepdims=True) + EPS)
            u = off * rstd
            unit[r, :, half(t)] = u
            inv[r, :, half(t)] = jnp.broadcast_to(rstd, (8, LANES))
            nb[r, :, half(t)] = u.astype(BF)
        value, slope = gelu_parts(dot(w_in[HC:CH], nb[r]))
        dgelu[r, HC:CH] = slope
        value = value.astype(BF)
        va[r // 2, 0, lax.rem(r, 2)] = value[:, half(0)]
        va[r // 2, 1, lax.rem(r, 2)] = value[:, half(1)]
        return carry

    loop(ROWS, value_row, unroll=4)
    pl.semaphore_wait(barrier, len(peers))
    step_a(va, va_in, G_VA)

    loads[2].wait()
    turn_in(cot)

    def cot_row(r, pack):
        t0, t1 = turned(r, 0), turned(r, 1)
        u3[r + 1, CH : 2 * CH, half(0)] = t0.astype(BF)
        u3[r + 1, CH : 2 * CH, half(1)] = t1.astype(BF)
        return edges(pack, t0, t1, r)

    pack = loop(ROWS, cot_row, jnp.zeros((CH, LANES), F32), unroll=4)
    send_halo(u3, pack, 0, G_ROW0, G_PACK0)

    def gate_row(r, carry):
        before = dot(w_in[...], nb[r])
        value, slope = gelu_parts(before[0:HC])
        gates[r, 0:HC] = value.astype(BF)
        dgelu[r, 0:HC] = slope
        value, slope = gelu_parts(before[CH:])
        dgelu[r, CH:] = slope
        value = value.astype(BF)
        gates[r, HC:CH] = value[0:HC]
        bval[r] = value[HC:]
        return carry

    loop(ROWS, gate_row, unroll=4)
    step_b(va_in, vx, vb, vb_in, G_VA, G_VB)

    take_halo(u3, 0, G_ROW0, G_PACK0)
    for load in loads[3:]:
        load.wait()
    back_w = jnp.concatenate(
        [jnp.concatenate([conv_w[2 - a, 2 - b] for a in range(3)], axis=1) for b in range(3)], axis=0
    ).astype(F32).T.astype(BF)
    w_out_t = w_out[...].astype(F32).T.astype(BF)

    def back_row(r, carry):
        total, carry = conv_step(back_w, u3, r, carry)
        g = (total + u3[r + 1, CH : 2 * CH].astype(F32)).astype(BF)
        gj[r] = g
        up_gated = dot(w_out_t, g)
        gg[r] = up_gated
        mixed = (up_gated * gates[r].astype(F32)).astype(BF)
        ga[r // 2, 0, lax.rem(r, 2)] = mixed[0:HC, half(0)]
        ga[r // 2, 1, lax.rem(r, 2)] = mixed[0:HC, half(1)]
        bback[r] = mixed[HC:]
        return carry

    loop(ROWS, back_row, conv_start(back_w, u3), unroll=4)
    step_a(ga, ga_in, G_GA)

    mix = grid_mix[...]
    from_a(vb_in, G_VB)
    step_c(dot(mix, vb_in[...].reshape(256, 512)), vc, vc_in, G_VC)

    def put(ref):
        def store(k, t, value):
            ref[k, :, half(t)] = value.astype(ref.dtype)

        return store

    swap_granules(lambda k, t: bval[k, :, half(t)].astype(F32), put(xt), HC)
    values = xt[...].reshape(ROWS * HC, COLS)
    mixed = dot_nt(values, block_mix[...])
    swap_granules(lambda k, t: mixed[k * HC : (k + 1) * HC, half(t)], put(bm), HC)

    step_b(ga_in, gx, gb, gb_in, G_GA, G_GB)
    step_d(vc_in, vx, vd, vd_in, G_VC, G_VD)

    swap_granules(lambda k, t: bback[k, :, half(t)].astype(F32), put(bt), HC)
    backs = bt[...].reshape(ROWS * HC, COLS)
    unmixed = dot(backs, block_mix[...])
    swap_granules(lambda k, t: unmixed[k * HC : (k + 1) * HC, half(t)], put(gbv), HC)
    part_block = dot_tn(backs, values).astype(BF)
    se[2 * COLS : 3 * COLS] = part_block[:, half(0)]
    se[3 * COLS :] = part_block[:, half(1)]

    from_a(gb_in, G_GB)
    back = gb_in[...].reshape(256, 512)
    step_c(dot_tn(mix, back), gc, gc_in, G_GC)
    part_grid = dot_nt(back, vb_in[...].reshape(256, 512)).astype(BF)
    se[0:COLS] = part_grid[:, half(0)]
    se[COLS : 2 * COLS] = part_grid[:, half(1)]
    over_w(lambda peer: se.at[pl.ds(pl.multiple_of(peer * 128, 128), 128)], re1.at[iw], G_E1)
    re1[iw] = se[pl.ds(pl.multiple_of(iw * 128, 128), 128)]

    for k in (0, 1, ROWS + 2, ROWS + 3):
        jp[k] = jnp.zeros((CH, COLS), BF)
    from_w(vd_in, G_VD)

    def returned(ref, r):
        return [ref[r // 2, t, lax.rem(r, 2)].astype(F32) for t in range(2)]

    def joined_row(r, pack):
        grid_mixed = returned(vd_in, r)
        for t in range(2):
            gates_t = gates[r, :, half(t)].astype(F32)
            gated[r, 0:HC, half(t)] = (gates_t[0:HC] * (grid_mixed[t] + 1.0)).astype(BF)
            gated[r, HC:, half(t)] = (gates_t[HC:] * (bm[r, :, half(t)] + 1.0)).astype(BF)
        j = (xb[r].astype(F32) + dot(w_out[...], gated[r])).astype(BF)
        jp[r + 2] = j
        v3[r + 1, CH : 2 * CH] = j
        jf = j.astype(F32)
        return edges(pack, jf[:, half(0)], jf[:, half(1)], r)

    pack = loop(ROWS, joined_row, jnp.zeros((CH, LANES), F32), unroll=4)
    send_halo(v3, pack, 1, G_ROW1, G_PACK1)

    step_d(gc_in, gx, gd, gd_in, G_GC, G_GD)

    from_w(re1, G_E1)
    total = re1[0].astype(F32)
    for k in range(1, NW):
        total = total + re1[k].astype(F32)
    e1[...] = total
    over_a(lambda peer: e1.at[pl.ds(pl.multiple_of(peer * 8, 8), 8)], re2.at[ia], G_E2)
    re2[ia] = e1[pl.ds(pl.multiple_of(ia * 8, 8), 8)]

    def conv_row(p, total):
        return total + dot_nt(u3[p], jp[pl.ds(p, 3)].reshape(3 * CH, COLS))

    p_conv = loop(ROWS + 2, conv_row, jnp.zeros((3 * CH, 3 * CH), F32), unroll=6)

    from_a(re2, G_E2)
    total = re2[0]
    for k in range(1, NA):
        total = total + re2[k]
    e2[...] = total
    over_a(lambda peer: e2, re3.at[ia], G_E3)
    re3[ia] = e2[...]

    from_w(gd_in, G_GD)

    def before_row(r, carry):
        p_in, p_out = carry
        grid_mixed = returned(vd_in, r)
        grid_back = returned(gd_in, r)
        for t in range(2):
            g = gg[r, :, half(t)]
            d = dgelu[r, :, half(t)]
            gbef[r, 0:HC, half(t)] = (d[0:HC] * (g[0:HC] * (grid_mixed[t] + 1.0))).astype(BF)
            gbef[r, HC:CH, half(t)] = (d[HC:CH] * grid_back[t]).astype(BF)
            gbef[r, CH : CH + HC, half(t)] = (d[CH : CH + HC] * (g[HC:] * (bm[r, :, half(t)] + 1.0))).astype(BF)
            gbef[r, CH + HC :, half(t)] = (d[CH + HC :] * gbv[r, :, half(t)]).astype(BF)
        return p_in + dot_nt(nb[r], gbef[r]), p_out + dot_nt(gj[r], gated[r])

    p_in, p_out = loop(
        ROWS, before_row, (jnp.zeros((CH, 2 * CH), F32), jnp.zeros((CH, CH), F32)), unroll=4
    )
    st[0 : 3 * CH] = p_conv[:, half(0)].astype(BF)
    st[3 * CH : 4 * CH] = p_in.astype(BF)
    third = p_conv[:, 2 * CH :]
    st[4 * CH :] = jnp.concatenate(
        [third[: 2 * CH], jnp.concatenate([third[2 * CH :], p_out], axis=0)], axis=1
    ).astype(BF)
    over_w(lambda peer: st.at[pl.ds(pl.multiple_of(peer * 48, 16), 48)], rt1.at[iw], G_T1)
    rt1[iw] = st[pl.ds(pl.multiple_of(iw * 48, 16), 48)]

    from_a(re3, G_E3)
    e4[...] = re3[...].reshape(128, LANES).astype(BF)
    over_w(lambda peer: e4, re4.at[iw], G_E4)
    re4[iw] = e4[...]

    def frame_row(r, carry):
        normed = dot(w_in_t[...], gbef[r])
        u = unit[r]
        mean_grad = jnp.mean(normed, axis=0, keepdims=True)
        mean_proj = jnp.mean(normed * u, axis=0, keepdims=True)
        source = gj[r].astype(F32) + inv[r, 0:1] * (normed - mean_grad - u * mean_proj)
        for t in range(2):
            gframe_out[t, pl.ds(r * CH, CH), :] = source[:, half(t)]
        return carry

    loop(ROWS, frame_row, unroll=4)

    from_w(rt1, G_T1)
    total = rt1[0].astype(F32)
    for k in range(1, NW):
        total = total + rt1[k].astype(F32)
    t1[...] = total.astype(BF)
    over_a(lambda peer: t1, rt2.at[ia], G_T2)
    rt2[ia] = t1[...]

    take_halo(v3, 1, G_ROW1, G_PACK1)
    from_a(rt2, G_T2)
    total = rt2[0].astype(F32)
    for k in range(1, NA):
        total = total + rt2[k].astype(F32)
    t2[...] = total.astype(BF)
    over_w(lambda peer: t2, rt3.at[iw], G_T3)
    rt3[iw] = t2[...]

    conv_k = jnp.concatenate(
        [jnp.concatenate([conv_w[a, b] for b in range(3)], axis=1) for a in range(3)], axis=0
    )

    def out_row(r, carry):
        total, carry = conv_step(conv_k, v3, r, carry)
        total = total + v3[r + 1, CH : 2 * CH].astype(F32)
        for t in range(2):
            rest_out[t, pl.ds(r * CH, CH), :] = total[:, half(t)]
        return carry

    loop(ROWS, out_row, conv_start(conv_k, v3), unroll=4)

    from_w(re4, G_E4)
    early_out[...] = re4[...]
    from_w(rt3, G_T3)
    tail_out[...] = rt3[...]

    for which, g_row, g_pack in ((0, G_ROW0, G_PACK0), (1, G_ROW1, G_PACK1)):
        gone(row_in.at[which], g_row)
        gone(pack_in.at[which], g_pack)
    for ref, g in (
        (va_in, G_VA), (vd_in, G_VD), (ga_in, G_GA), (gd_in, G_GD),
        (re1, G_E1), (re4, G_E4), (rt1, G_T1), (rt3, G_T3),
    ):
        gone(ref.at[pl.ds(0, NW - 1)], g)
    for ref, g in (
        (vb_in, G_VB), (vc_in, G_VC), (gb_in, G_GB), (gc_in, G_GC), (re2, G_E2), (re3, G_E3), (rt2, G_T2),
    ):
        gone(ref.at[pl.ds(0, NA - 1)], g)


def finish(rest, gframe, early, tail, restored, grad_frames, grad_w_in_t, grad_grid, grad_block, grad_w_out, grad_conv):
    scale = float(ROWS * NA * COLS * NW) ** (-0.5)

    def channel(c, carry):
        for src, dst in ((rest, restored), (gframe, grad_frames)):
            for t in range(2):
                dst[c, :, half(t)] = src[t, pl.ds(c, ROWS, stride=CH), :].astype(BF)
        return carry

    loop(CH, channel, unroll=8)

    for k in range(2):
        grad_grid[:, half(k)] = early[k * COLS : (k + 1) * COLS].astype(F32) * scale
        grad_block[:, half(k)] = early[(2 + k) * COLS : (3 + k) * COLS].astype(F32) * scale
    grad_w_in_t[...] = tail[3 * CH : 4 * CH].astype(F32) * scale
    last = tail[4 * CH :].astype(F32) * scale
    grad_w_out[...] = last[CH:, CH:]
    for b in range(3):
        rows = slice((2 - b) * CH, (3 - b) * CH)
        pair = tail[rows].astype(F32) * scale
        grad_conv[0, b] = pair[:, :CH]
        grad_conv[1, b] = pair[:, CH:]
    grad_conv[2, 2] = last[:CH, :CH]
    grad_conv[2, 1] = last[CH:, :CH]
    grad_conv[2, 0] = last[:CH, CH:]


def vm(*shape, dtype=BF):
    return pltpu.VMEM(shape, dtype)


def exchange():
    message_w = vm(NW, 2, 2, HC, LANES)
    message_a = vm(NA, 16, 512)
    return [message_w, message_w, vm(2 * 16 * HC, LANES, dtype=F32)] + [message_a] * 4 + [message_w] * 2


SCRATCH = [
    vm(CH, ROWS, COLS),
    vm(CH, 2 * CH),
    vm(COLS, COLS),
    vm(COLS, COLS),
    vm(CH, CH),
    vm(3, 3, CH, CH),
    vm(CH, ROWS, COLS),
    vm(2 * CH, CH),
    vm(2, CH * ROWS, LANES, dtype=F32),
    vm(ROWS, CH, COLS),
    vm(ROWS, CH, COLS),
    vm(ROWS, CH, COLS, dtype=F32),
    vm(ROWS, 8, COLS, dtype=F32),
    vm(ROWS, 2 * CH, COLS, dtype=F32),
    vm(ROWS, CH, COLS),
    vm(ROWS, HC, COLS),
    vm(ROWS + 2, 3 * CH, COLS),
    vm(ROWS + 2, 3 * CH, COLS),
    vm(ROWS, CH, COLS),
    vm(ROWS, CH, COLS, dtype=F32),
    vm(ROWS, HC, COLS),
    vm(ROWS, HC, COLS),
    vm(ROWS, HC, COLS),
    vm(ROWS, HC, COLS, dtype=F32),
    vm(ROWS, HC, COLS, dtype=F32),
    *exchange(),
    *exchange(),
    vm(ROWS, CH, COLS),
    vm(ROWS, 2 * CH, COLS),
    vm(ROWS + 4, CH, COLS),
    vm(2, 2, CH, COLS),
    vm(2, CH, LANES),
    vm(2, 6, CH, LANES),
    vm(CH, LANES, dtype=F32),
    vm(CH, LANES, dtype=F32),
    vm(4 * COLS, LANES),
    vm(NW, 128, LANES),
    vm(128, LANES, dtype=F32),
    vm(NA, 8, LANES, dtype=F32),
    vm(8, LANES, dtype=F32),
    vm(NA, 8, LANES, dtype=F32),
    vm(128, LANES),
    vm(NW, 128, LANES),
    vm(6 * CH, LANES),
    vm(NW, 48, LANES),
    vm(48, LANES),
    vm(NA, 48, LANES),
    vm(48, LANES),
    vm(NW, 48, LANES),
    pltpu.SemaphoreType.DMA((GROUPS,)),
    pltpu.SemaphoreType.DMA((GROUPS,)),
    pltpu.SemaphoreType.DMA((7,)),
]


def body(frames, w_in, grid_mix, block_mix, w_out, conv_w, cotangent):
    operands = (frames, w_in.T, grid_mix, block_mix, w_out, conv_w, cotangent)
    vmem = pl.BlockSpec(memory_space=pltpu.VMEM)
    shape = jax.ShapeDtypeStruct
    rest, gframe, early, tail = pl.pallas_call(
        kernel,
        out_shape=(
            shape((2, ROWS * CH, LANES), F32),
            shape((2, ROWS * CH, LANES), F32),
            shape((NW, 128, LANES), BF),
            shape((NW, 48, LANES), BF),
        ),
        in_specs=[pl.BlockSpec(memory_space=pltpu.HBM)] * 7,
        out_specs=(vmem,) * 4,
        scratch_shapes=SCRATCH,
        compiler_params=pltpu.CompilerParams(
            collective_id=0, has_side_effects=True, vmem_limit_bytes=32 * 1024 * 1024
        ),
    )(*[pltpu.with_memory_space_constraint(x, pltpu.HBM) for x in operands])
    restored, grad_frames, grad_w_in_t, grad_grid, grad_block, grad_w_out, grad_conv = pl.pallas_call(
        finish,
        out_shape=(
            shape((CH, ROWS, COLS), BF),
            shape((CH, ROWS, COLS), BF),
            shape((CH, 2 * CH), F32),
            shape((COLS, COLS), F32),
            shape((COLS, COLS), F32),
            shape((CH, CH), F32),
            shape((3, 3, CH, CH), F32),
        ),
        in_specs=[vmem] * 4,
        out_specs=(vmem,) * 7,
        compiler_params=pltpu.CompilerParams(vmem_limit_bytes=16 * 1024 * 1024),
    )(rest, gframe, early.reshape(4 * COLS, LANES), tail.reshape(6 * CH, LANES))
    return restored, grad_frames, grad_w_in_t.T, grad_grid, grad_block, grad_w_out, grad_conv


def solution(mesh):
    placed = (P(None, "ha", "wa"), P(), P(), P(), P(), P(), P(None, "ha", "wa"))
    return jax.shard_map(
        body,
        mesh=mesh,
        in_specs=placed,
        out_specs=(P(None, "ha", "wa"), P(None, "ha", "wa"), P(), P(), P(), P(), P()),
        check_vma=False,
    )
```

```python
import jax
import jax.numpy as jnp
from jax import lax
from jax.experimental import pallas as pl
from jax.experimental.pallas import tpu as pltpu
from jax.sharding import PartitionSpec as P

BF = jnp.bfloat16
F32 = jnp.float32
EPS = 1e-06
MESH = pl.DeviceIdType.MESH

CH = 64
HC = 32
ROWS = 16
COLS = 256
LANES = 128
NA = 16
NW = 8

(G_ROW0, G_PACK0, G_ROW1, G_PACK1, G_VA, G_VB, G_VC, G_VD, G_GA, G_GB, G_GC, G_GD) = range(12)
(G_E1, G_E2, G_E3, G_E4, G_T1, G_T2, G_T3) = range(12, 19)
GROUPS = 19


def dot(a, b):
    return lax.dot_general(a, b, (((1,), (0,)), ((), ())), preferred_element_type=F32)


def dot_nt(a, b):
    return lax.dot_general(a, b, (((1,), (1,)), ((), ())), preferred_element_type=F32)


def dot_tn(a, b):
    return lax.dot_general(a, b, (((0,), (0,)), ((), ())), preferred_element_type=F32)


def swap_granules(load, store, depth):
    lane = lax.broadcasted_iota(jnp.int32, (depth, LANES), 1)
    for row_half in range(2):
        for col_half in range(2):
            held = [load(row_half * 8 + k, col_half) for k in range(8)]
            for s in range(3):
                width = 16 << s
                low = (lane & width) == 0
                for k in range(8):
                    if not k & (1 << s):
                        a, b = held[k], held[k | (1 << s)]
                        held[k] = jnp.where(low, a, pltpu.roll(b, width, 1))
                        held[k | (1 << s)] = jnp.where(low, pltpu.roll(a, LANES - width, 1), b)
            for k in range(8):
                store(col_half * 8 + k, row_half, held[k])


def half(t):
    return slice(t * LANES, (t + 1) * LANES)


def loop(count, step, carry=0, unroll=1):
    return lax.fori_loop(0, count, step, carry, unroll=unroll)


def gelu_parts(x):
    root = 0.7978845608028654
    cube = root * 0.044715
    square = x * x
    h = 0.5 * jnp.tanh(x * (cube * square + root)) + 0.5
    value = x * h
    return value, h + value * (1.0 - h) * ((6.0 * cube) * square + 2.0 * root)


def kernel(
    frames_hbm, w_in_t_hbm, grid_mix_hbm, block_mix_hbm, w_out_hbm, conv_w_hbm, cot_hbm,
    rest_out, gframe_out, early_out, tail_out,
    frames, w_in_t, grid_mix, block_mix, w_out, conv_w, cot, w_in,
    turn, xb, nb, unit, inv, dgelu, gates, bval, u3, v3, gj, gg, bback, xt, bt, bm, gbv,
    va, va_in, vx, vb, vb_in, vc, vc_in, vd, vd_in,
    ga, ga_in, gx, gb, gb_in, gc, gc_in, gd, gd_in,
    gated, gbef, jp, row_in, pack_out, pack_in, edge_l, edge_r,
    se, re1, e1, re2, e2, re3, e4, re4, st, rt1, t1, rt2, t2, rt3,
    ssem, rsem, isem,
):
    ia = lax.axis_index("ha")
    iw = lax.axis_index("wa")
    up, down = lax.rem(ia + NA - 1, NA), lax.rem(ia + 1, NA)
    left, right = lax.rem(iw + NW - 1, NW), lax.rem(iw + 1, NW)
    lane = lax.broadcasted_iota(jnp.int32, (CH, LANES), 1)

    loads = [
        pltpu.make_async_copy(src, dst, isem.at[k])
        for k, (src, dst) in enumerate(
            [
                (frames_hbm, frames),
                (w_in_t_hbm, w_in_t),
                (cot_hbm, cot),
                (conv_w_hbm, conv_w),
                (w_out_hbm, w_out),
                (block_mix_hbm, block_mix),
                (grid_mix_hbm, grid_mix),
            ]
        )
    ]
    for load in loads:
        load.start()

    def push(src, dst, g, where):
        pltpu.make_async_remote_copy(
            src_ref=src, dst_ref=dst, send_sem=ssem.at[g], recv_sem=rsem.at[g], device_id=where, device_id_type=MESH
        ).start()

    def over_w(src_of, dst, g):
        for k in range(1, NW):
            peer = lax.rem(iw + k, NW)
            push(src_of(peer), dst, g, (ia, peer))

    def over_a(src_of, dst, g):
        for k in range(1, NA):
            peer = lax.rem(ia + k, NA)
            push(src_of(peer), dst, g, (peer, iw))

    def arrived(ref, g):
        pltpu.make_async_copy(ref, ref, rsem.at[g]).wait()

    def gone(ref, g):
        pltpu.make_async_copy(ref, ref, ssem.at[g]).wait()

    def from_w(ref, g):
        arrived(ref.at[pl.ds(0, NW - 1)], g)

    def from_a(ref, g):
        arrived(ref.at[pl.ds(0, NA - 1)], g)

    barrier = pltpu.get_barrier_semaphore()
    peers = [(ia, lax.rem(iw + k, NW)) for k in range(1, NW)]
    peers += [(lax.rem(ia + k, NA), iw) for k in range(1, NA)]
    peers += [(a, b) for a in (up, down) for b in (left, right)]
    for peer in peers:
        pl.semaphore_signal(barrier, inc=1, device_id=peer, device_id_type=MESH)

    def turn_in(src):
        for t in range(2):
            turn[t] = src[:, :, half(t)].astype(F32).reshape(CH * ROWS, LANES)

    def turned(r, t):
        return turn[t, pl.ds(r, CH, stride=ROWS), :]

    def edges(pack, t0, t1, r):
        pack = jnp.where(lane == r, pltpu.roll(t0, r, 1), pack)
        return jnp.where(lane == ROWS + r, pltpu.roll(t1, r + 17, 1), pack)

    def send_halo(field, pack, which, g_row, g_pack):
        pack_out[which] = pack.astype(BF)
        push(field.at[1, CH : 2 * CH], row_in.at[which, 1], g_row, (up, iw))
        push(field.at[ROWS, CH : 2 * CH], row_in.at[which, 0], g_row, (down, iw))
        for slot, where in enumerate(
            [(ia, right), (ia, left), (down, right), (down, left), (up, right), (up, left)]
        ):
            push(pack_out.at[which], pack_in.at[which, slot], g_pack, where)

    def take_halo(field, which, g_row, g_pack):
        arrived(row_in.at[which], g_row)
        arrived(pack_in.at[which], g_pack)
        top = row_in[which, 0].astype(F32) * jnp.where(ia > 0, 1.0, 0.0)
        field[0, CH : 2 * CH] = top.astype(BF)
        bottom = row_in[which, 1].astype(F32) * jnp.where(ia < NA - 1, 1.0, 0.0)
        field[ROWS + 1, CH : 2 * CH] = bottom.astype(BF)
        first = jnp.where(ia > 0, 0, 1)
        last = jnp.where(ia < NA - 1, ROWS + 2, ROWS + 1)
        got = [pack_in[which, k].astype(F32) for k in range(6)]

        def assemble(middle, above, below, has):
            joined = jnp.where(lane == 0, above, jnp.where(lane == ROWS + 1, below, middle))
            return jnp.where((lane >= first) & (lane < jnp.where(has, last, 0)), joined, 0.0)

        edge_l[...] = assemble(
            pltpu.roll(got[0], 113, 1), pltpu.roll(got[2], 97, 1), pltpu.roll(got[4], 1, 1), iw > 0
        )
        edge_r[...] = assemble(
            pltpu.roll(got[1], 1, 1), pltpu.roll(got[3], 113, 1), pltpu.roll(got[5], 17, 1), iw < NW - 1
        )

        def shifts(p, carry):
            t0 = field[p, CH : 2 * CH, half(0)].astype(F32)
            t1 = field[p, CH : 2 * CH, half(1)].astype(F32)
            a0, a1 = pltpu.roll(t0, 1, 1), pltpu.roll(t1, 1, 1)
            b0, b1 = pltpu.roll(t0, LANES - 1, 1), pltpu.roll(t1, LANES - 1, 1)
            lh = pltpu.roll(edge_l[...], lax.rem(LANES - p, LANES), 1)
            rh = pltpu.roll(edge_r[...], LANES - 1 - p, 1)
            field[p, 0:CH, half(0)] = jnp.where(lane == 0, lh, a0).astype(BF)
            field[p, 0:CH, half(1)] = jnp.where(lane == 0, a0, a1).astype(BF)
            field[p, 2 * CH :, half(0)] = jnp.where(lane == LANES - 1, b1, b0).astype(BF)
            field[p, 2 * CH :, half(1)] = jnp.where(lane == LANES - 1, rh, b1).astype(BF)
            return carry

        loop(ROWS + 2, shifts, unroll=9)

    def conv_start(w, field):
        y = dot(w, field[0])
        z = dot(w, field[1])
        return z[0:CH], y[0:CH] + z[CH : 2 * CH]

    def conv_step(w, field, r, carry):
        later, now = carry
        y = dot(w, field[r + 2])
        return now + y[2 * CH :], (y[0:CH], later + y[CH : 2 * CH])

    def step_a(a, a_in, g):
        over_w(lambda peer: a.at[peer], a_in.at[iw], g)
        a_in[iw] = a[iw]

    def step_b(a_in, x, b, b_in, g_a, g_b):
        from_w(a_in, g_a)

        def widen(j, carry):
            for t in range(2):
                for r in range(2):
                    x[pl.ds((r * 16 + j * 2 + t) * HC, HC), :] = a_in[j, t, r].astype(F32)
            return carry

        loop(NW, widen, unroll=8)

        def pick(q, carry):
            for r in range(2):
                for c in range(4):
                    b[r * 8 + q, :, half(c)] = x[pl.ds(r * 16 * HC + q * 4 + c, 16, stride=HC), :].astype(BF)
            return carry

        loop(8, pick, unroll=8)
        over_a(lambda peer: b.at[peer], b_in.at[ia], g_b)
        b_in[ia] = b[ia]

    def step_c(mixed, c, c_in, g):
        c[...] = mixed.astype(BF).reshape(NA, 16, 512)
        over_a(lambda peer: c.at[peer], c_in.at[ia], g)
        c_in[ia] = c[ia]

    def step_d(c_in, x, d, d_in, g_c, g_d):
        from_a(c_in, g_c)

        def unpick(q, carry):
            for r in range(2):
                for c in range(4):
                    x[pl.ds((r * HC + q * 4 + c) * 16, 16), :] = c_in[r * 8 + q, :, half(c)].astype(F32)
            return carry

        loop(8, unpick, unroll=8)

        def narrow(j, carry):
            for t in range(2):
                for r in range(2):
                    d[j, t, r] = x[pl.ds(r * HC * 16 + j * 2 + t, HC, stride=16), :].astype(BF)
            return carry

        loop(NW, narrow, unroll=8)
        over_w(lambda peer: d.at[peer], d_in.at[iw], g_d)
        d_in[iw] = d[iw]

    loads[0].wait()
    loads[1].wait()
    turn_in(frames)
    w_in[...] = w_in_t[...].astype(F32).T.astype(BF)

    def value_row(r, carry):
        for t in range(2):
            x = turned(r, t)
            xb[r, :, half(t)] = x.astype(BF)
            off = x - jnp.mean(x, axis=0, keepdims=True)
            rstd = lax.rsqrt(jnp.mean(off * off, axis=0, keepdims=True) + EPS)
            u = off * rstd
            unit[r, :, half(t)] = u
            inv[r, :, half(t)] = jnp.broadcast_to(rstd, (8, LANES))
            nb[r, :, half(t)] = u.astype(BF)
        value, slope = gelu_parts(dot(w_in[HC:CH], nb[r]))
        dgelu[r, HC:CH] = slope
        value = value.astype(BF)
        va[r // 2, 0, lax.rem(r, 2)] = value[:, half(0)]
        va[r // 2, 1, lax.rem(r, 2)] = value[:, half(1)]
        return carry

    loop(ROWS, value_row, unroll=8)
    pl.semaphore_wait(barrier, len(peers))
    step_a(va, va_in, G_VA)

    loads[2].wait()
    turn_in(cot)

    def cot_row(r, pack):
        t0, t1 = turned(r, 0), turned(r, 1)
        u3[r + 1, CH : 2 * CH, half(0)] = t0.astype(BF)
        u3[r + 1, CH : 2 * CH, half(1)] = t1.astype(BF)
        return edges(pack, t0, t1, r)

    pack = loop(ROWS, cot_row, jnp.zeros((CH, LANES), F32), unroll=8)
    send_halo(u3, pack, 0, G_ROW0, G_PACK0)

    def gate_row(r, carry):
        before = dot(w_in[...], nb[r])
        value, slope = gelu_parts(before[0:HC])
        gates[r, 0:HC] = value.astype(BF)
        dgelu[r, 0:HC] = slope
        value, slope = gelu_parts(before[CH:])
        dgelu[r, CH:] = slope
        value = value.astype(BF)
        gates[r, HC:CH] = value[0:HC]
        bval[r] = value[HC:]
        return carry

    loop(ROWS, gate_row, unroll=8)
    step_b(va_in, vx, vb, vb_in, G_VA, G_VB)

    take_halo(u3, 0, G_ROW0, G_PACK0)
    for load in loads[3:]:
        load.wait()
    back_w = jnp.concatenate(
        [jnp.concatenate([conv_w[2 - a, 2 - b] for a in range(3)], axis=1) for b in range(3)], axis=0
    ).astype(F32).T.astype(BF)
    w_out_t = w_out[...].astype(F32).T.astype(BF)

    def back_row(r, carry):
        total, carry = conv_step(back_w, u3, r, carry)
        g = (total + u3[r + 1, CH : 2 * CH].astype(F32)).astype(BF)
        gj[r] = g
        up_gated = dot(w_out_t, g)
        gg[r] = up_gated
        mixed = (up_gated * gates[r].astype(F32)).astype(BF)
        ga[r // 2, 0, lax.rem(r, 2)] = mixed[0:HC, half(0)]
        ga[r // 2, 1, lax.rem(r, 2)] = mixed[0:HC, half(1)]
        bback[r] = mixed[HC:]
        return carry

    loop(ROWS, back_row, conv_start(back_w, u3), unroll=8)
    step_a(ga, ga_in, G_GA)

    mix = grid_mix[...]
    from_a(vb_in, G_VB)
    step_c(dot(mix, vb_in[...].reshape(256, 512)), vc, vc_in, G_VC)

    def put(ref):
        def store(k, t, value):
            ref[k, :, half(t)] = value.astype(ref.dtype)

        return store

    swap_granules(lambda k, t: bval[k, :, half(t)].astype(F32), put(xt), HC)
    values = xt[...].reshape(ROWS * HC, COLS)
    mixed = dot_nt(values, block_mix[...])
    swap_granules(lambda k, t: mixed[k * HC : (k + 1) * HC, half(t)], put(bm), HC)

    step_b(ga_in, gx, gb, gb_in, G_GA, G_GB)
    step_d(vc_in, vx, vd, vd_in, G_VC, G_VD)

    swap_granules(lambda k, t: bback[k, :, half(t)].astype(F32), put(bt), HC)
    backs = bt[...].reshape(ROWS * HC, COLS)
    unmixed = dot(backs, block_mix[...])
    swap_granules(lambda k, t: unmixed[k * HC : (k + 1) * HC, half(t)], put(gbv), HC)
    part_block = dot_tn(backs, values).astype(BF)
    se[2 * COLS : 3 * COLS] = part_block[:, half(0)]
    se[3 * COLS :] = part_block[:, half(1)]

    from_a(gb_in, G_GB)
    back = gb_in[...].reshape(256, 512)
    step_c(dot_tn(mix, back), gc, gc_in, G_GC)
    part_grid = dot_nt(back, vb_in[...].reshape(256, 512)).astype(BF)
    se[0:COLS] = part_grid[:, half(0)]
    se[COLS : 2 * COLS] = part_grid[:, half(1)]
    over_w(lambda peer: se.at[pl.ds(pl.multiple_of(peer * 128, 128), 128)], re1.at[iw], G_E1)
    re1[iw] = se[pl.ds(pl.multiple_of(iw * 128, 128), 128)]

    for k in (0, 1, ROWS + 2, ROWS + 3):
        jp[k] = jnp.zeros((CH, COLS), BF)
    from_w(vd_in, G_VD)

    def returned(ref, r):
        return [ref[r // 2, t, lax.rem(r, 2)].astype(F32) for t in range(2)]

    def joined_row(r, pack):
        grid_mixed = returned(vd_in, r)
        for t in range(2):
            gates_t = gates[r, :, half(t)].astype(F32)
            gated[r, 0:HC, half(t)] = (gates_t[0:HC] * (grid_mixed[t] + 1.0)).astype(BF)
            gated[r, HC:, half(t)] = (gates_t[HC:] * (bm[r, :, half(t)] + 1.0)).astype(BF)
        j = (xb[r].astype(F32) + dot(w_out[...], gated[r])).astype(BF)
        jp[r + 2] = j
        v3[r + 1, CH : 2 * CH] = j
        jf = j.astype(F32)
        return edges(pack, jf[:, half(0)], jf[:, half(1)], r)

    pack = loop(ROWS, joined_row, jnp.zeros((CH, LANES), F32), unroll=8)
    send_halo(v3, pack, 1, G_ROW1, G_PACK1)

    step_d(gc_in, gx, gd, gd_in, G_GC, G_GD)

    from_w(re1, G_E1)
    total = re1[0].astype(F32)
    for k in range(1, NW):
        total = total + re1[k].astype(F32)
    e1[...] = total
    over_a(lambda peer: e1.at[pl.ds(pl.multiple_of(peer * 8, 8), 8)], re2.at[ia], G_E2)
    re2[ia] = e1[pl.ds(pl.multiple_of(ia * 8, 8), 8)]

    def conv_row(p, total):
        return total + dot_nt(u3[p], jp[pl.ds(p, 3)].reshape(3 * CH, COLS))

    p_conv = loop(ROWS + 2, conv_row, jnp.zeros((3 * CH, 3 * CH), F32), unroll=9)

    from_a(re2, G_E2)
    total = re2[0]
    for k in range(1, NA):
        total = total + re2[k]
    e2[...] = total
    over_a(lambda peer: e2, re3.at[ia], G_E3)
    re3[ia] = e2[...]

    from_w(gd_in, G_GD)

    def before_row(r, carry):
        p_in, p_out = carry
        grid_mixed = returned(vd_in, r)
        grid_back = returned(gd_in, r)
        for t in range(2):
            g = gg[r, :, half(t)]
            d = dgelu[r, :, half(t)]
            gbef[r, 0:HC, half(t)] = (d[0:HC] * (g[0:HC] * (grid_mixed[t] + 1.0))).astype(BF)
            gbef[r, HC:CH, half(t)] = (d[HC:CH] * grid_back[t]).astype(BF)
            gbef[r, CH : CH + HC, half(t)] = (d[CH : CH + HC] * (g[HC:] * (bm[r, :, half(t)] + 1.0))).astype(BF)
            gbef[r, CH + HC :, half(t)] = (d[CH + HC :] * gbv[r, :, half(t)]).astype(BF)
        return p_in + dot_nt(nb[r], gbef[r]), p_out + dot_nt(gj[r], gated[r])

    p_in, p_out = loop(
        ROWS, before_row, (jnp.zeros((CH, 2 * CH), F32), jnp.zeros((CH, CH), F32)), unroll=4
    )
    st[0 : 3 * CH] = p_conv[:, half(0)].astype(BF)
    st[3 * CH : 4 * CH] = p_in.astype(BF)
    third = p_conv[:, 2 * CH :]
    st[4 * CH :] = jnp.concatenate(
        [third[: 2 * CH], jnp.concatenate([third[2 * CH :], p_out], axis=0)], axis=1
    ).astype(BF)
    over_w(lambda peer: st.at[pl.ds(pl.multiple_of(peer * 48, 16), 48)], rt1.at[iw], G_T1)
    rt1[iw] = st[pl.ds(pl.multiple_of(iw * 48, 16), 48)]

    from_a(re3, G_E3)
    e4[...] = re3[...].reshape(128, LANES).astype(BF)
    over_w(lambda peer: e4, re4.at[iw], G_E4)
    re4[iw] = e4[...]

    def frame_row(r, carry):
        normed = dot(w_in_t[...], gbef[r])
        u = unit[r]
        mean_grad = jnp.mean(normed, axis=0, keepdims=True)
        mean_proj = jnp.mean(normed * u, axis=0, keepdims=True)
        source = gj[r].astype(F32) + inv[r, 0:1] * (normed - mean_grad - u * mean_proj)
        for t in range(2):
            gframe_out[t, pl.ds(r * CH, CH), :] = source[:, half(t)]
        return carry

    loop(ROWS, frame_row, unroll=8)

    from_w(rt1, G_T1)
    total = rt1[0].astype(F32)
    for k in range(1, NW):
        total = total + rt1[k].astype(F32)
    t1[...] = total.astype(BF)
    over_a(lambda peer: t1, rt2.at[ia], G_T2)
    rt2[ia] = t1[...]

    take_halo(v3, 1, G_ROW1, G_PACK1)
    from_a(rt2, G_T2)
    total = rt2[0].astype(F32)
    for k in range(1, NA):
        total = total + rt2[k].astype(F32)
    t2[...] = total.astype(BF)
    over_w(lambda peer: t2, rt3.at[iw], G_T3)
    rt3[iw] = t2[...]

    conv_k = jnp.concatenate(
        [jnp.concatenate([conv_w[a, b] for b in range(3)], axis=1) for a in range(3)], axis=0
    )

    def out_row(r, carry):
        total, carry = conv_step(conv_k, v3, r, carry)
        total = total + v3[r + 1, CH : 2 * CH].astype(F32)
        for t in range(2):
            rest_out[t, pl.ds(r * CH, CH), :] = total[:, half(t)]
        return carry

    loop(ROWS, out_row, conv_start(conv_k, v3), unroll=8)

    from_w(re4, G_E4)
    early_out[...] = re4[...]
    from_w(rt3, G_T3)
    tail_out[...] = rt3[...]

    for which, g_row, g_pack in ((0, G_ROW0, G_PACK0), (1, G_ROW1, G_PACK1)):
        gone(row_in.at[which], g_row)
        gone(pack_in.at[which], g_pack)
    for ref, g in (
        (va_in, G_VA), (vd_in, G_VD), (ga_in, G_GA), (gd_in, G_GD),
        (re1, G_E1), (re4, G_E4), (rt1, G_T1), (rt3, G_T3),
    ):
        gone(ref.at[pl.ds(0, NW - 1)], g)
    for ref, g in (
        (vb_in, G_VB), (vc_in, G_VC), (gb_in, G_GB), (gc_in, G_GC), (re2, G_E2), (re3, G_E3), (rt2, G_T2),
    ):
        gone(ref.at[pl.ds(0, NA - 1)], g)


def finish(rest, gframe, early, tail, restored, grad_frames, grad_w_in_t, grad_grid, grad_block, grad_w_out, grad_conv):
    scale = float(ROWS * NA * COLS * NW) ** (-0.5)

    def channel(c, carry):
        for src, dst in ((rest, restored), (gframe, grad_frames)):
            for t in range(2):
                dst[c, :, half(t)] = src[t, pl.ds(c, ROWS, stride=CH), :].astype(BF)
        return carry

    loop(CH, channel, unroll=8)

    for k in range(2):
        grad_grid[:, half(k)] = early[k * COLS : (k + 1) * COLS].astype(F32) * scale
        grad_block[:, half(k)] = early[(2 + k) * COLS : (3 + k) * COLS].astype(F32) * scale
    grad_w_in_t[...] = tail[3 * CH : 4 * CH].astype(F32) * scale
    last = tail[4 * CH :].astype(F32) * scale
    grad_w_out[...] = last[CH:, CH:]
    for b in range(3):
        rows = slice((2 - b) * CH, (3 - b) * CH)
        pair = tail[rows].astype(F32) * scale
        grad_conv[0, b] = pair[:, :CH]
        grad_conv[1, b] = pair[:, CH:]
    grad_conv[2, 2] = last[:CH, :CH]
    grad_conv[2, 1] = last[CH:, :CH]
    grad_conv[2, 0] = last[:CH, CH:]


def vm(*shape, dtype=BF):
    return pltpu.VMEM(shape, dtype)


def exchange():
    message_w = vm(NW, 2, 2, HC, LANES)
    message_a = vm(NA, 16, 512)
    return [message_w, message_w, vm(2 * 16 * HC, LANES, dtype=F32)] + [message_a] * 4 + [message_w] * 2


SCRATCH = [
    vm(CH, ROWS, COLS),
    vm(CH, 2 * CH),
    vm(COLS, COLS),
    vm(COLS, COLS),
    vm(CH, CH),
    vm(3, 3, CH, CH),
    vm(CH, ROWS, COLS),
    vm(2 * CH, CH),
    vm(2, CH * ROWS, LANES, dtype=F32),
    vm(ROWS, CH, COLS),
    vm(ROWS, CH, COLS),
    vm(ROWS, CH, COLS, dtype=F32),
    vm(ROWS, 8, COLS, dtype=F32),
    vm(ROWS, 2 * CH, COLS, dtype=F32),
    vm(ROWS, CH, COLS),
    vm(ROWS, HC, COLS),
    vm(ROWS + 2, 3 * CH, COLS),
    vm(ROWS + 2, 3 * CH, COLS),
    vm(ROWS, CH, COLS),
    vm(ROWS, CH, COLS, dtype=F32),
    vm(ROWS, HC, COLS),
    vm(ROWS, HC, COLS),
    vm(ROWS, HC, COLS),
    vm(ROWS, HC, COLS, dtype=F32),
    vm(ROWS, HC, COLS, dtype=F32),
    *exchange(),
    *exchange(),
    vm(ROWS, CH, COLS),
    vm(ROWS, 2 * CH, COLS),
    vm(ROWS + 4, CH, COLS),
    vm(2, 2, CH, COLS),
    vm(2, CH, LANES),
    vm(2, 6, CH, LANES),
    vm(CH, LANES, dtype=F32),
    vm(CH, LANES, dtype=F32),
    vm(4 * COLS, LANES),
    vm(NW, 128, LANES),
    vm(128, LANES, dtype=F32),
    vm(NA, 8, LANES, dtype=F32),
    vm(8, LANES, dtype=F32),
    vm(NA, 8, LANES, dtype=F32),
    vm(128, LANES),
    vm(NW, 128, LANES),
    vm(6 * CH, LANES),
    vm(NW, 48, LANES),
    vm(48, LANES),
    vm(NA, 48, LANES),
    vm(48, LANES),
    vm(NW, 48, LANES),
    pltpu.SemaphoreType.DMA((GROUPS,)),
    pltpu.SemaphoreType.DMA((GROUPS,)),
    pltpu.SemaphoreType.DMA((7,)),
]


def body(frames, w_in, grid_mix, block_mix, w_out, conv_w, cotangent):
    operands = (frames, w_in.T, grid_mix, block_mix, w_out, conv_w, cotangent)
    vmem = pl.BlockSpec(memory_space=pltpu.VMEM)
    shape = jax.ShapeDtypeStruct
    rest, gframe, early, tail = pl.pallas_call(
        kernel,
        out_shape=(
            shape((2, ROWS * CH, LANES), F32),
            shape((2, ROWS * CH, LANES), F32),
            shape((NW, 128, LANES), BF),
            shape((NW, 48, LANES), BF),
        ),
        in_specs=[pl.BlockSpec(memory_space=pltpu.HBM)] * 7,
        out_specs=(vmem,) * 4,
        scratch_shapes=SCRATCH,
        compiler_params=pltpu.CompilerParams(
            collective_id=0, has_side_effects=True, vmem_limit_bytes=32 * 1024 * 1024
        ),
    )(*[pltpu.with_memory_space_constraint(x, pltpu.HBM) for x in operands])
    restored, grad_frames, grad_w_in_t, grad_grid, grad_block, grad_w_out, grad_conv = pl.pallas_call(
        finish,
        out_shape=(
            shape((CH, ROWS, COLS), BF),
            shape((CH, ROWS, COLS), BF),
            shape((CH, 2 * CH), F32),
            shape((COLS, COLS), F32),
            shape((COLS, COLS), F32),
            shape((CH, CH), F32),
            shape((3, 3, CH, CH), F32),
        ),
        in_specs=[vmem] * 4,
        out_specs=(vmem,) * 7,
        compiler_params=pltpu.CompilerParams(vmem_limit_bytes=16 * 1024 * 1024),
    )(rest, gframe, early.reshape(4 * COLS, LANES), tail.reshape(6 * CH, LANES))
    return restored, grad_frames, grad_w_in_t.T, grad_grid, grad_block, grad_w_out, grad_conv


def solution(mesh):
    placed = (P(None, "ha", "wa"), P(), P(), P(), P(), P(), P(None, "ha", "wa"))
    return jax.shard_map(
        body,
        mesh=mesh,
        in_specs=placed,
        out_specs=(P(None, "ha", "wa"), P(None, "ha", "wa"), P(), P(), P(), P(), P()),
        check_vma=False,
    )
```

```python
import jax
import jax.numpy as jnp
from jax import lax
from jax.experimental import pallas as pl
from jax.experimental.pallas import tpu as pltpu
from jax.sharding import PartitionSpec as P

BF = jnp.bfloat16
F32 = jnp.float32
EPS = 1e-06
MESH = pl.DeviceIdType.MESH

CH = 64
HC = 32
ROWS = 16
COLS = 256
LANES = 128
NA = 16
NW = 8
NEAR = 8
FAR = 16

(G_ROW0, G_PACK0, G_ROW1, G_PACK1, G_VA, G_VB, G_VC, G_VD, G_GA, G_GB, G_GC, G_GD) = range(12)
(G_E0, G_E1, G_E2, G_E3, G_E4, G_E5, G_T1, G_T2, G_T3) = range(12, 21)
GROUPS = 21


def dot(a, b):
    return lax.dot_general(a, b, (((1,), (0,)), ((), ())), preferred_element_type=F32)


def dot_nt(a, b):
    return lax.dot_general(a, b, (((1,), (1,)), ((), ())), preferred_element_type=F32)


def dot_tn(a, b):
    return lax.dot_general(a, b, (((0,), (0,)), ((), ())), preferred_element_type=F32)


def swap_granules(load, store, depth):
    lane = lax.broadcasted_iota(jnp.int32, (depth, LANES), 1)
    for row_half in range(2):
        for col_half in range(2):
            held = [load(row_half * 8 + k, col_half) for k in range(8)]
            for s in range(3):
                width = 16 << s
                low = (lane & width) == 0
                for k in range(8):
                    if not k & (1 << s):
                        a, b = held[k], held[k | (1 << s)]
                        held[k] = jnp.where(low, a, pltpu.roll(b, width, 1))
                        held[k | (1 << s)] = jnp.where(low, pltpu.roll(a, LANES - width, 1), b)
            for k in range(8):
                store(col_half * 8 + k, row_half, held[k])


def half(t):
    return slice(t * LANES, (t + 1) * LANES)


def loop(count, step, carry=0, unroll=1):
    return lax.fori_loop(0, count, step, carry, unroll=unroll)


def gelu_parts(x):
    root = 0.7978845608028654
    cube = root * 0.044715
    square = x * x
    h = 0.5 * jnp.tanh(x * (cube * square + root)) + 0.5
    value = x * h
    return value, h + value * (1.0 - h) * ((6.0 * cube) * square + 2.0 * root)


def kernel(
    frames_hbm, w_in_t_hbm, grid_mix_hbm, block_mix_hbm, w_out_hbm, conv_w_hbm, cot_hbm,
    rest_out, gframe_out, early_out, tail_out,
    frames, w_in_t, grid_mix, block_mix, w_out, conv_w, cot, w_in,
    turn, xb, nb, unit, inv, dgelu, gates, bval, u3, v3, gj, gg, bback, xt, bt, bm, gbv,
    va, va_in, vx, vb, vb_in, vc, vc_in, vd, vd_in,
    ga, ga_in, gx, gb, gb_in, gc, gc_in, gd, gd_in,
    gated, gbef, jp, row_in, pack_out, pack_in, edge_l, edge_r,
    mixp, se, re0, e0, re1, e1, re2, e2, re3, e4, re4, e5, st, rt1, t1, rt2, t2, rt3,
    ssem, rsem, isem,
):
    ia = lax.axis_index("ha")
    iw = lax.axis_index("wa")
    up, down = lax.rem(ia + NA - 1, NA), lax.rem(ia + 1, NA)
    left, right = lax.rem(iw + NW - 1, NW), lax.rem(iw + 1, NW)
    lane = lax.broadcasted_iota(jnp.int32, (CH, LANES), 1)

    loads = [
        pltpu.make_async_copy(src, dst, isem.at[k])
        for k, (src, dst) in enumerate(
            [
                (frames_hbm, frames),
                (w_in_t_hbm, w_in_t),
                (cot_hbm, cot),
                (conv_w_hbm, conv_w),
                (w_out_hbm, w_out),
                (block_mix_hbm, block_mix),
                (grid_mix_hbm, grid_mix),
            ]
        )
    ]
    for load in loads:
        load.start()

    def push(src, dst, g, where):
        pltpu.make_async_remote_copy(
            src_ref=src, dst_ref=dst, send_sem=ssem.at[g], recv_sem=rsem.at[g], device_id=where, device_id_type=MESH
        ).start()

    near = lax.rem(iw, 2) * 4 + lax.rem(ia, 4)
    far = ia // 4 * 4 + iw // 2

    def near_device(peer):
        return ia // 4 * 4 + lax.rem(peer, 4), iw // 2 * 2 + peer // 4

    def far_device(peer):
        return peer // 4 * 4 + lax.rem(ia, 4), lax.rem(peer, 4) * 2 + lax.rem(iw, 2)

    near_peers = [lax.rem(near + k, NEAR) for k in range(1, NEAR)]
    far_peers = [lax.rem(far + k, FAR) for k in range(1, FAR)]
    twin = near + 1 - 2 * lax.rem(near, 2)

    def over_near(src_of, dst, g):
        for peer in near_peers:
            push(src_of(peer), dst, g, near_device(peer))

    def over_far(src_of, dst, g):
        for peer in far_peers:
            push(src_of(peer), dst, g, far_device(peer))

    def over_y(src_of, dst, g):
        for k in range(1, 4):
            peer = lax.rem(near + 2 * k, NEAR)
            push(src_of(peer // 2), dst, g, near_device(peer))

    def arrived(ref, g):
        pltpu.make_async_copy(ref, ref, rsem.at[g]).wait()

    def gone(ref, g):
        pltpu.make_async_copy(ref, ref, ssem.at[g]).wait()

    def from_near(ref, g):
        arrived(ref.at[pl.ds(0, NEAR - 1)], g)

    def from_far(ref, g):
        arrived(ref.at[pl.ds(0, FAR - 1)], g)

    mine = lax.rem(near, 2) * 512
    level = near // 2

    barrier = pltpu.get_barrier_semaphore()
    peers = [near_device(peer) for peer in near_peers]
    peers += [far_device(peer) for peer in far_peers]
    peers += [(a, b) for a in (up, ia, down) for b in (left, right)] + [(up, iw), (down, iw)]
    for peer in peers:
        pl.semaphore_signal(barrier, inc=1, device_id=peer, device_id_type=MESH)

    def turn_in(src):
        for t in range(2):
            turn[t] = src[:, :, half(t)].astype(F32).reshape(CH * ROWS, LANES)

    def turned(r, t):
        return turn[t, pl.ds(r, CH, stride=ROWS), :]

    def edges(pack, t0, t1, r):
        pack = jnp.where(lane == r, pltpu.roll(t0, r, 1), pack)
        return jnp.where(lane == ROWS + r, pltpu.roll(t1, r + 17, 1), pack)

    def send_halo(field, pack, which, g_row, g_pack):
        pack_out[which] = pack.astype(BF)
        push(field.at[1, CH : 2 * CH], row_in.at[which, 1], g_row, (up, iw))
        push(field.at[ROWS, CH : 2 * CH], row_in.at[which, 0], g_row, (down, iw))
        for slot, where in enumerate(
            [(ia, right), (ia, left), (down, right), (down, left), (up, right), (up, left)]
        ):
            push(pack_out.at[which], pack_in.at[which, slot], g_pack, where)

    def take_halo(field, which, g_row, g_pack):
        arrived(row_in.at[which], g_row)
        arrived(pack_in.at[which], g_pack)
        top = row_in[which, 0].astype(F32) * jnp.where(ia > 0, 1.0, 0.0)
        field[0, CH : 2 * CH] = top.astype(BF)
        bottom = row_in[which, 1].astype(F32) * jnp.where(ia < NA - 1, 1.0, 0.0)
        field[ROWS + 1, CH : 2 * CH] = bottom.astype(BF)
        first = jnp.where(ia > 0, 0, 1)
        last = jnp.where(ia < NA - 1, ROWS + 2, ROWS + 1)
        got = [pack_in[which, k].astype(F32) for k in range(6)]

        def assemble(middle, above, below, has):
            joined = jnp.where(lane == 0, above, jnp.where(lane == ROWS + 1, below, middle))
            return jnp.where((lane >= first) & (lane < jnp.where(has, last, 0)), joined, 0.0)

        edge_l[...] = assemble(
            pltpu.roll(got[0], 113, 1), pltpu.roll(got[2], 97, 1), pltpu.roll(got[4], 1, 1), iw > 0
        )
        edge_r[...] = assemble(
            pltpu.roll(got[1], 1, 1), pltpu.roll(got[3], 113, 1), pltpu.roll(got[5], 17, 1), iw < NW - 1
        )

        def shifts(p, carry):
            t0 = field[p, CH : 2 * CH, half(0)].astype(F32)
            t1 = field[p, CH : 2 * CH, half(1)].astype(F32)
            a0, a1 = pltpu.roll(t0, 1, 1), pltpu.roll(t1, 1, 1)
            b0, b1 = pltpu.roll(t0, LANES - 1, 1), pltpu.roll(t1, LANES - 1, 1)
            lh = pltpu.roll(edge_l[...], lax.rem(LANES - p, LANES), 1)
            rh = pltpu.roll(edge_r[...], LANES - 1 - p, 1)
            field[p, 0:CH, half(0)] = jnp.where(lane == 0, lh, a0).astype(BF)
            field[p, 0:CH, half(1)] = jnp.where(lane == 0, a0, a1).astype(BF)
            field[p, 2 * CH :, half(0)] = jnp.where(lane == LANES - 1, b1, b0).astype(BF)
            field[p, 2 * CH :, half(1)] = jnp.where(lane == LANES - 1, rh, b1).astype(BF)
            return carry

        loop(ROWS + 2, shifts, unroll=9)

    def conv_start(w, field):
        y = dot(w, field[0])
        z = dot(w, field[1])
        return z[0:CH], y[0:CH] + z[CH : 2 * CH]

    def conv_step(w, field, r, carry):
        later, now = carry
        y = dot(w, field[r + 2])
        return now + y[2 * CH :], (y[0:CH], later + y[CH : 2 * CH])

    def step_a(a, a_in, g):
        over_near(lambda peer: a.at[peer], a_in.at[near], g)
        a_in[near] = a[near]

    def step_b(a_in, x, b, b_in, g_a, g_b):
        from_near(a_in, g_a)

        def widen(j, carry):
            for t in range(2):
                for r in range(2):
                    x[pl.ds((r * 16 + j * 2 + t) * HC, HC), :] = a_in[j, t, r].astype(F32)
            return carry

        loop(NEAR, widen, unroll=8)

        def pick(q, carry):
            for r in range(2):
                for c in range(4):
                    b[r * 8 + q, :, half(c)] = x[pl.ds(r * 16 * HC + q * 4 + c, 16, stride=HC), :].astype(BF)
            return carry

        loop(8, pick, unroll=8)
        over_far(lambda peer: b.at[peer], b_in.at[far], g_b)
        b_in[far] = b[far]

    def step_c(mixed, c, c_in, g):
        c[...] = mixed.astype(BF).reshape(FAR, 16, 512)
        over_far(lambda peer: c.at[peer], c_in.at[far], g)
        c_in[far] = c[far]

    def step_d(c_in, x, d, d_in, g_c, g_d):
        from_far(c_in, g_c)

        def unpick(q, carry):
            for r in range(2):
                for c in range(4):
                    x[pl.ds((r * HC + q * 4 + c) * 16, 16), :] = c_in[r * 8 + q, :, half(c)].astype(F32)
            return carry

        loop(8, unpick, unroll=8)

        def narrow(j, carry):
            for t in range(2):
                for r in range(2):
                    d[j, t, r] = x[pl.ds(r * HC * 16 + j * 2 + t, HC, stride=16), :].astype(BF)
            return carry

        loop(NEAR, narrow, unroll=8)
        over_near(lambda peer: d.at[peer], d_in.at[near], g_d)
        d_in[near] = d[near]

    loads[0].wait()
    loads[1].wait()
    turn_in(frames)
    w_in[...] = w_in_t[...].astype(F32).T.astype(BF)

    def value_row(r, carry):
        for t in range(2):
            x = turned(r, t)
            xb[r, :, half(t)] = x.astype(BF)
            off = x - jnp.mean(x, axis=0, keepdims=True)
            rstd = lax.rsqrt(jnp.mean(off * off, axis=0, keepdims=True) + EPS)
            u = off * rstd
            unit[r, :, half(t)] = u
            inv[r, :, half(t)] = jnp.broadcast_to(rstd, (8, LANES))
            nb[r, :, half(t)] = u.astype(BF)
        value, slope = gelu_parts(dot(w_in[HC:CH], nb[r]))
        dgelu[r, HC:CH] = slope
        value = value.astype(BF)
        va[r // 2, 0, lax.rem(r, 2)] = value[:, half(0)]
        va[r // 2, 1, lax.rem(r, 2)] = value[:, half(1)]
        return carry

    loop(ROWS, value_row, unroll=8)
    pl.semaphore_wait(barrier, len(peers))
    step_a(va, va_in, G_VA)

    def order():
        row = lax.broadcasted_iota(jnp.int32, (COLS, COLS), 0)
        cell = lax.broadcasted_iota(jnp.int32, (COLS, COLS), 1)
        found = (row & 0xC1) | ((row & 6) << 3) | ((row & 48) >> 2) | ((row & 8) >> 2)
        return jnp.where(cell == found, 1.0, 0.0).astype(BF)

    def mix_in_order():
        swap = order()
        return dot_nt(dot(swap, grid_mix[...]).astype(BF), swap).astype(BF)


    loads[2].wait()
    turn_in(cot)

    def cot_row(r, pack):
        t0, t1 = turned(r, 0), turned(r, 1)
        u3[r + 1, CH : 2 * CH, half(0)] = t0.astype(BF)
        u3[r + 1, CH : 2 * CH, half(1)] = t1.astype(BF)
        return edges(pack, t0, t1, r)

    pack = loop(ROWS, cot_row, jnp.zeros((CH, LANES), F32), unroll=8)
    send_halo(u3, pack, 0, G_ROW0, G_PACK0)

    def gate_row(r, carry):
        before = dot(w_in[...], nb[r])
        value, slope = gelu_parts(before[0:HC])
        gates[r, 0:HC] = value.astype(BF)
        dgelu[r, 0:HC] = slope
        value, slope = gelu_parts(before[CH:])
        dgelu[r, CH:] = slope
        value = value.astype(BF)
        gates[r, HC:CH] = value[0:HC]
        bval[r] = value[HC:]
        return carry

    loop(ROWS, gate_row, unroll=8)
    for load in loads[3:]:
        load.wait()
    mixp[...] = mix_in_order()
    step_b(va_in, vx, vb, vb_in, G_VA, G_VB)

    take_halo(u3, 0, G_ROW0, G_PACK0)
    back_w = jnp.concatenate(
        [jnp.concatenate([conv_w[2 - a, 2 - b] for a in range(3)], axis=1) for b in range(3)], axis=0
    ).astype(F32).T.astype(BF)
    w_out_t = w_out[...].astype(F32).T.astype(BF)

    def back_row(r, carry):
        total, carry = conv_step(back_w, u3, r, carry)
        g = (total + u3[r + 1, CH : 2 * CH].astype(F32)).astype(BF)
        gj[r] = g
        up_gated = dot(w_out_t, g)
        gg[r] = up_gated
        mixed = (up_gated * gates[r].astype(F32)).astype(BF)
        ga[r // 2, 0, lax.rem(r, 2)] = mixed[0:HC, half(0)]
        ga[r // 2, 1, lax.rem(r, 2)] = mixed[0:HC, half(1)]
        bback[r] = mixed[HC:]
        return carry

    loop(ROWS, back_row, conv_start(back_w, u3), unroll=8)
    step_a(ga, ga_in, G_GA)

    from_far(vb_in, G_VB)
    step_c(dot(mixp[...], vb_in[...].reshape(256, 512)), vc, vc_in, G_VC)

    def put(ref):
        def store(k, t, value):
            ref[k, :, half(t)] = value.astype(ref.dtype)

        return store

    swap_granules(lambda k, t: bval[k, :, half(t)].astype(F32), put(xt), HC)
    values = xt[...].reshape(ROWS * HC, COLS)
    mixed = dot_nt(values, block_mix[...])
    swap_granules(lambda k, t: mixed[k * HC : (k + 1) * HC, half(t)], put(bm), HC)

    step_b(ga_in, gx, gb, gb_in, G_GA, G_GB)
    step_d(vc_in, vx, vd, vd_in, G_VC, G_VD)

    swap_granules(lambda k, t: bback[k, :, half(t)].astype(F32), put(bt), HC)
    backs = bt[...].reshape(ROWS * HC, COLS)
    unmixed = dot(backs, block_mix[...])
    swap_granules(lambda k, t: unmixed[k * HC : (k + 1) * HC, half(t)], put(gbv), HC)
    part_block = dot_tn(backs, values).astype(BF)
    se[2 * COLS : 3 * COLS] = part_block[:, half(0)]
    se[3 * COLS :] = part_block[:, half(1)]

    from_far(gb_in, G_GB)
    back = gb_in[...].reshape(256, 512)
    step_c(dot_tn(mixp[...], back), gc, gc_in, G_GC)
    part_grid = dot_nt(back, vb_in[...].reshape(256, 512)).astype(BF)
    part_grid = dot(dot_tn(order(), part_grid).astype(BF), order()).astype(BF)
    se[0:COLS] = part_grid[:, half(0)]
    se[COLS : 2 * COLS] = part_grid[:, half(1)]
    push(se.at[pl.ds(pl.multiple_of(512 - mine, 512), 512)], re0, G_E0, near_device(twin))

    for k in (0, 1, ROWS + 2, ROWS + 3):
        jp[k] = jnp.zeros((CH, COLS), BF)
    from_near(vd_in, G_VD)

    def returned(ref, r):
        return [ref[r // 2, t, lax.rem(r, 2)].astype(F32) for t in range(2)]

    def joined_row(r, pack):
        grid_mixed = returned(vd_in, r)
        for t in range(2):
            gates_t = gates[r, :, half(t)].astype(F32)
            gated[r, 0:HC, half(t)] = (gates_t[0:HC] * (grid_mixed[t] + 1.0)).astype(BF)
            gated[r, HC:, half(t)] = (gates_t[HC:] * (bm[r, :, half(t)] + 1.0)).astype(BF)
        j = (xb[r].astype(F32) + dot(w_out[...], gated[r])).astype(BF)
        jp[r + 2] = j
        v3[r + 1, CH : 2 * CH] = j
        jf = j.astype(F32)
        return edges(pack, jf[:, half(0)], jf[:, half(1)], r)

    pack = loop(ROWS, joined_row, jnp.zeros((CH, LANES), F32), unroll=8)
    send_halo(v3, pack, 1, G_ROW1, G_PACK1)

    arrived(re0, G_E0)
    e0[...] = (se[pl.ds(pl.multiple_of(mine, 512), 512)].astype(F32) + re0[...].astype(F32)).astype(BF)
    over_y(lambda peer: e0.at[pl.ds(pl.multiple_of(peer * 128, 128), 128)], re1.at[level], G_E1)
    re1[level] = e0[pl.ds(pl.multiple_of(level * 128, 128), 128)]

    step_d(gc_in, gx, gd, gd_in, G_GC, G_GD)

    arrived(re1.at[pl.ds(0, 3)], G_E1)
    total = re1[0].astype(F32)
    for k in range(1, 4):
        total = total + re1[k].astype(F32)
    e1[...] = total
    over_far(lambda peer: e1.at[pl.ds(pl.multiple_of(peer * 8, 8), 8)], re2.at[far], G_E2)
    re2[far] = e1[pl.ds(pl.multiple_of(far * 8, 8), 8)]

    def conv_row(p, total):
        return total + dot_nt(u3[p], jp[pl.ds(p, 3)].reshape(3 * CH, COLS))

    p_conv = loop(ROWS + 2, conv_row, jnp.zeros((3 * CH, 3 * CH), F32), unroll=9)

    from_far(re2, G_E2)
    total = re2[0]
    for k in range(1, NA):
        total = total + re2[k]
    e2[...] = total
    over_far(lambda peer: e2, re3.at[far], G_E3)
    re3[far] = e2[...]

    from_near(gd_in, G_GD)

    def before_row(r, carry):
        p_in, p_out = carry
        grid_mixed = returned(vd_in, r)
        grid_back = returned(gd_in, r)
        for t in range(2):
            g = gg[r, :, half(t)]
            d = dgelu[r, :, half(t)]
            gbef[r, 0:HC, half(t)] = (d[0:HC] * (g[0:HC] * (grid_mixed[t] + 1.0))).astype(BF)
            gbef[r, HC:CH, half(t)] = (d[HC:CH] * grid_back[t]).astype(BF)
            gbef[r, CH : CH + HC, half(t)] = (d[CH : CH + HC] * (g[HC:] * (bm[r, :, half(t)] + 1.0))).astype(BF)
            gbef[r, CH + HC :, half(t)] = (d[CH + HC :] * gbv[r, :, half(t)]).astype(BF)
        return p_in + dot_nt(nb[r], gbef[r]), p_out + dot_nt(gj[r], gated[r])

    p_in, p_out = loop(
        ROWS, before_row, (jnp.zeros((CH, 2 * CH), F32), jnp.zeros((CH, CH), F32)), unroll=4
    )
    st[0 : 3 * CH] = p_conv[:, half(0)].astype(BF)
    st[3 * CH : 4 * CH] = p_in.astype(BF)
    third = p_conv[:, 2 * CH :]
    st[4 * CH :] = jnp.concatenate(
        [third[: 2 * CH], jnp.concatenate([third[2 * CH :], p_out], axis=0)], axis=1
    ).astype(BF)
    over_near(lambda peer: st.at[pl.ds(pl.multiple_of(peer * 48, 16), 48)], rt1.at[near], G_T1)
    rt1[near] = st[pl.ds(pl.multiple_of(near * 48, 16), 48)]

    from_far(re3, G_E3)
    e4[...] = re3[...].reshape(128, LANES).astype(BF)
    over_y(lambda peer: e4, re4.at[level], G_E4)
    re4[level] = e4[...]

    def frame_row(r, carry):
        normed = dot(w_in_t[...], gbef[r])
        u = unit[r]
        mean_grad = jnp.mean(normed, axis=0, keepdims=True)
        mean_proj = jnp.mean(normed * u, axis=0, keepdims=True)
        source = gj[r].astype(F32) + inv[r, 0:1] * (normed - mean_grad - u * mean_proj)
        for t in range(2):
            gframe_out[t, pl.ds(r * CH, CH), :] = source[:, half(t)]
        return carry

    loop(ROWS, frame_row, unroll=8)

    from_near(rt1, G_T1)
    total = rt1[0].astype(F32)
    for k in range(1, NW):
        total = total + rt1[k].astype(F32)
    t1[...] = total.astype(BF)
    over_far(lambda peer: t1, rt2.at[far], G_T2)
    rt2[far] = t1[...]

    arrived(re4.at[pl.ds(0, 3)], G_E4)
    push(re4, e5, G_E5, near_device(twin))
    early_out[pl.ds(pl.multiple_of(mine, 512), 512)] = re4[...].reshape(512, LANES)

    take_halo(v3, 1, G_ROW1, G_PACK1)
    from_far(rt2, G_T2)
    total = rt2[0].astype(F32)
    for k in range(1, NA):
        total = total + rt2[k].astype(F32)
    t2[...] = total.astype(BF)
    over_near(lambda peer: t2, rt3.at[near], G_T3)
    rt3[near] = t2[...]

    conv_k = jnp.concatenate(
        [jnp.concatenate([conv_w[a, b] for b in range(3)], axis=1) for a in range(3)], axis=0
    )

    def out_row(r, carry):
        total, carry = conv_step(conv_k, v3, r, carry)
        total = total + v3[r + 1, CH : 2 * CH].astype(F32)
        for t in range(2):
            rest_out[t, pl.ds(r * CH, CH), :] = total[:, half(t)]
        return carry

    loop(ROWS, out_row, conv_start(conv_k, v3), unroll=8)

    arrived(e5, G_E5)
    early_out[pl.ds(pl.multiple_of(512 - mine, 512), 512)] = e5[...].reshape(512, LANES)
    from_near(rt3, G_T3)
    tail_out[...] = rt3[...]

    for which, g_row, g_pack in ((0, G_ROW0, G_PACK0), (1, G_ROW1, G_PACK1)):
        gone(row_in.at[which], g_row)
        gone(pack_in.at[which], g_pack)
    for ref, g in (
        (va_in, G_VA), (vd_in, G_VD), (ga_in, G_GA), (gd_in, G_GD),
        (rt1, G_T1), (rt3, G_T3),
    ):
        gone(ref.at[pl.ds(0, NEAR - 1)], g)
    for ref, g in (
        (vb_in, G_VB), (vc_in, G_VC), (gb_in, G_GB), (gc_in, G_GC), (re2, G_E2), (re3, G_E3), (rt2, G_T2),
    ):
        gone(ref.at[pl.ds(0, FAR - 1)], g)
    gone(re0, G_E0)
    gone(re1.at[pl.ds(0, 3)], G_E1)
    gone(re4.at[pl.ds(0, 3)], G_E4)
    gone(e5, G_E5)


def finish(rest, gframe, early, tail, restored, grad_frames, grad_w_in_t, grad_grid, grad_block, grad_w_out, grad_conv):
    scale = float(ROWS * NA * COLS * NW) ** (-0.5)

    def channel(c, carry):
        for src, dst in ((rest, restored), (gframe, grad_frames)):
            for t in range(2):
                dst[c, :, half(t)] = src[t, pl.ds(c, ROWS, stride=CH), :].astype(BF)
        return carry

    loop(CH, channel, unroll=8)

    for k in range(2):
        grad_grid[:, half(k)] = early[k * COLS : (k + 1) * COLS].astype(F32) * scale
        grad_block[:, half(k)] = early[(2 + k) * COLS : (3 + k) * COLS].astype(F32) * scale
    grad_w_in_t[...] = tail[3 * CH : 4 * CH].astype(F32) * scale
    last = tail[4 * CH :].astype(F32) * scale
    grad_w_out[...] = last[CH:, CH:]
    for b in range(3):
        rows = slice((2 - b) * CH, (3 - b) * CH)
        pair = tail[rows].astype(F32) * scale
        grad_conv[0, b] = pair[:, :CH]
        grad_conv[1, b] = pair[:, CH:]
    grad_conv[2, 2] = last[:CH, :CH]
    grad_conv[2, 1] = last[CH:, :CH]
    grad_conv[2, 0] = last[:CH, CH:]


def vm(*shape, dtype=BF):
    return pltpu.VMEM(shape, dtype)


def exchange():
    message_w = vm(NW, 2, 2, HC, LANES)
    message_a = vm(NA, 16, 512)
    return [message_w, message_w, vm(2 * 16 * HC, LANES, dtype=F32)] + [message_a] * 4 + [message_w] * 2


SCRATCH = [
    vm(CH, ROWS, COLS),
    vm(CH, 2 * CH),
    vm(COLS, COLS),
    vm(COLS, COLS),
    vm(CH, CH),
    vm(3, 3, CH, CH),
    vm(CH, ROWS, COLS),
    vm(2 * CH, CH),
    vm(2, CH * ROWS, LANES, dtype=F32),
    vm(ROWS, CH, COLS),
    vm(ROWS, CH, COLS),
    vm(ROWS, CH, COLS, dtype=F32),
    vm(ROWS, 8, COLS, dtype=F32),
    vm(ROWS, 2 * CH, COLS, dtype=F32),
    vm(ROWS, CH, COLS),
    vm(ROWS, HC, COLS),
    vm(ROWS + 2, 3 * CH, COLS),
    vm(ROWS + 2, 3 * CH, COLS),
    vm(ROWS, CH, COLS),
    vm(ROWS, CH, COLS, dtype=F32),
    vm(ROWS, HC, COLS),
    vm(ROWS, HC, COLS),
    vm(ROWS, HC, COLS),
    vm(ROWS, HC, COLS, dtype=F32),
    vm(ROWS, HC, COLS, dtype=F32),
    *exchange(),
    *exchange(),
    vm(ROWS, CH, COLS),
    vm(ROWS, 2 * CH, COLS),
    vm(ROWS + 4, CH, COLS),
    vm(2, 2, CH, COLS),
    vm(2, CH, LANES),
    vm(2, 6, CH, LANES),
    vm(CH, LANES, dtype=F32),
    vm(CH, LANES, dtype=F32),
    vm(COLS, COLS),
    vm(4 * COLS, LANES),
    vm(512, LANES),
    vm(512, LANES),
    vm(4, 128, LANES),
    vm(128, LANES, dtype=F32),
    vm(NA, 8, LANES, dtype=F32),
    vm(8, LANES, dtype=F32),
    vm(NA, 8, LANES, dtype=F32),
    vm(128, LANES),
    vm(4, 128, LANES),
    vm(4, 128, LANES),
    vm(6 * CH, LANES),
    vm(NW, 48, LANES),
    vm(48, LANES),
    vm(NA, 48, LANES),
    vm(48, LANES),
    vm(NW, 48, LANES),
    pltpu.SemaphoreType.DMA((GROUPS,)),
    pltpu.SemaphoreType.DMA((GROUPS,)),
    pltpu.SemaphoreType.DMA((7,)),
]


def body(frames, w_in, grid_mix, block_mix, w_out, conv_w, cotangent):
    operands = (frames, w_in.T, grid_mix, block_mix, w_out, conv_w, cotangent)
    vmem = pl.BlockSpec(memory_space=pltpu.VMEM)
    shape = jax.ShapeDtypeStruct
    rest, gframe, early, tail = pl.pallas_call(
        kernel,
        out_shape=(
            shape((2, ROWS * CH, LANES), F32),
            shape((2, ROWS * CH, LANES), F32),
            shape((4 * COLS, LANES), BF),
            shape((NW, 48, LANES), BF),
        ),
        in_specs=[pl.BlockSpec(memory_space=pltpu.HBM)] * 7,
        out_specs=(vmem,) * 4,
        scratch_shapes=SCRATCH,
        compiler_params=pltpu.CompilerParams(
            collective_id=0, has_side_effects=True, vmem_limit_bytes=32 * 1024 * 1024
        ),
    )(*[pltpu.with_memory_space_constraint(x, pltpu.HBM) for x in operands])
    restored, grad_frames, grad_w_in_t, grad_grid, grad_block, grad_w_out, grad_conv = pl.pallas_call(
        finish,
        out_shape=(
            shape((CH, ROWS, COLS), BF),
            shape((CH, ROWS, COLS), BF),
            shape((CH, 2 * CH), F32),
            shape((COLS, COLS), F32),
            shape((COLS, COLS), F32),
            shape((CH, CH), F32),
            shape((3, 3, CH, CH), F32),
        ),
        in_specs=[vmem] * 4,
        out_specs=(vmem,) * 7,
        compiler_params=pltpu.CompilerParams(vmem_limit_bytes=16 * 1024 * 1024),
    )(rest, gframe, early, tail.reshape(6 * CH, LANES))
    return restored, grad_frames, grad_w_in_t.T, grad_grid, grad_block, grad_w_out, grad_conv


def solution(mesh):
    placed = (P(None, "ha", "wa"), P(), P(), P(), P(), P(), P(None, "ha", "wa"))
    return jax.shard_map(
        body,
        mesh=mesh,
        in_specs=placed,
        out_specs=(P(None, "ha", "wa"), P(None, "ha", "wa"), P(), P(), P(), P(), P()),
        check_vma=False,
    )
```

```python
import jax
import jax.numpy as jnp
from jax import lax
from jax.experimental import pallas as pl
from jax.experimental.pallas import tpu as pltpu
from jax.sharding import PartitionSpec as P

BF = jnp.bfloat16
F32 = jnp.float32
EPS = 1e-06
MESH = pl.DeviceIdType.MESH

CH = 64
HC = 32
ROWS = 16
COLS = 256
LANES = 128
NA = 16
NW = 8
NEAR = 8
FAR = 16

(G_ROW0, G_PACK0, G_ROW1, G_PACK1, G_VA, G_VB, G_VC, G_VD, G_GA, G_GB, G_GC, G_GD) = range(12)
(G_E0, G_E1, G_E2, G_E3, G_E4, G_E5, G_E6, G_T1, G_T2, G_T3) = range(12, 22)
GROUPS = 22


def dot(a, b):
    return lax.dot_general(a, b, (((1,), (0,)), ((), ())), preferred_element_type=F32)


def dot_nt(a, b):
    return lax.dot_general(a, b, (((1,), (1,)), ((), ())), preferred_element_type=F32)


def dot_tn(a, b):
    return lax.dot_general(a, b, (((0,), (0,)), ((), ())), preferred_element_type=F32)


def swap_granules(load, store, depth):
    lane = lax.broadcasted_iota(jnp.int16, (depth, LANES), 1)
    for row_half in range(2):
        for col_half in range(2):
            held = [load(row_half * 8 + k, col_half) for k in range(8)]
            for s in range(3):
                width = 16 << s
                low = (lane & width) == 0
                for k in range(8):
                    if not k & (1 << s):
                        a, b = held[k], held[k | (1 << s)]
                        held[k] = jnp.where(low, a, pltpu.roll(b, width, 1))
                        held[k | (1 << s)] = jnp.where(low, pltpu.roll(a, LANES - width, 1), b)
            for k in range(8):
                store(col_half * 8 + k, row_half, held[k])


def half(t):
    return slice(t * LANES, (t + 1) * LANES)


def loop(count, step, carry=0, unroll=1):
    return lax.fori_loop(0, count, step, carry, unroll=unroll)


def gelu_parts(x):
    root = 0.7978845608028654
    cube = root * 0.044715
    square = x * x
    h = 0.5 * jnp.tanh(x * (cube * square + root)) + 0.5
    value = x * h
    return value, h + value * (1.0 - h) * ((6.0 * cube) * square + 2.0 * root)


def kernel(
    frames_hbm, w_in_t_hbm, grid_mix_hbm, block_mix_hbm, w_out_hbm, conv_w_hbm, cot_hbm,
    rest_out, gframe_out, early_out, tail_out,
    frames, w_in_t, grid_mix, block_mix, w_out, conv_w, cot, w_in,
    turn, xb, nb, unit, inv, dgelu, gates, bval, u3, v3, gj, gg, bback, xt, bt, bm, gbv,
    va, va_in, vx, vb, vb_in, vc, vc_in, vd, vd_in,
    ga, ga_in, gx, gb, gb_in, gc, gc_in, gd, gd_in,
    gated, gbef, jp, row_in, pack_out, pack_in, edge_l, edge_r,
    mixp, se, re0, e0, re1, e1, re2, e2, re3, e3, re4, re5, re6, st, rt1, t1, rt2, t2, rt3,
    ssem, rsem, isem,
):
    ia = lax.axis_index("ha")
    iw = lax.axis_index("wa")
    up, down = lax.rem(ia + NA - 1, NA), lax.rem(ia + 1, NA)
    left, right = lax.rem(iw + NW - 1, NW), lax.rem(iw + 1, NW)
    lane = lax.broadcasted_iota(jnp.int16, (CH, LANES), 1)
    lane_wide = lax.broadcasted_iota(jnp.int32, (CH, LANES), 1)

    loads = [
        pltpu.make_async_copy(src, dst, isem.at[k])
        for k, (src, dst) in enumerate(
            [
                (frames_hbm, frames),
                (w_in_t_hbm, w_in_t),
                (cot_hbm, cot),
                (conv_w_hbm, conv_w),
                (w_out_hbm, w_out),
                (block_mix_hbm, block_mix),
                (grid_mix_hbm, grid_mix),
            ]
        )
    ]
    for load in loads:
        load.start()

    def push(src, dst, g, where):
        pltpu.make_async_remote_copy(
            src_ref=src, dst_ref=dst, send_sem=ssem.at[g], recv_sem=rsem.at[g], device_id=where, device_id_type=MESH
        ).start()

    near = lax.rem(iw, 2) * 4 + lax.rem(ia, 4)
    far = ia // 4 * 4 + iw // 2

    def near_device(peer):
        return ia // 4 * 4 + lax.rem(peer, 4), iw // 2 * 2 + peer // 4

    def far_device(peer):
        return peer // 4 * 4 + lax.rem(ia, 4), lax.rem(peer, 4) * 2 + lax.rem(iw, 2)

    near_peers = [lax.rem(near + k, NEAR) for k in range(1, NEAR)]
    far_peers = [lax.rem(far + k, FAR) for k in range(1, FAR)]
    twin = near + 1 - 2 * lax.rem(near, 2)

    def over_near(src_of, dst, g):
        for peer in near_peers:
            push(src_of(peer), dst, g, near_device(peer))

    def over_far(src_of, dst, g):
        for peer in far_peers:
            push(src_of(peer), dst, g, far_device(peer))

    def over_x(src_of, dst, g):
        for k in range(1, 4):
            peer = lax.rem(iw // 2 + k, 4)
            push(src_of(peer), dst, g, (ia, peer * 2 + lax.rem(iw, 2)))

    def over_z(src_of, dst, g):
        for k in range(1, 4):
            peer = lax.rem(ia // 4 + k, 4)
            push(src_of(peer), dst, g, (peer * 4 + lax.rem(ia, 4), iw))

    def over_y(src_of, dst, g):
        for k in range(1, 4):
            peer = lax.rem(near + 2 * k, NEAR)
            push(src_of(peer // 2), dst, g, near_device(peer))

    def arrived(ref, g):
        pltpu.make_async_copy(ref, ref, rsem.at[g]).wait()

    def gone(ref, g):
        pltpu.make_async_copy(ref, ref, ssem.at[g]).wait()

    def from_near(ref, g):
        arrived(ref.at[pl.ds(0, NEAR - 1)], g)

    def from_far(ref, g):
        arrived(ref.at[pl.ds(0, FAR - 1)], g)

    mine = lax.rem(near, 2) * 512
    level, across, deep = near // 2, iw // 2, ia // 4

    barrier = pltpu.get_barrier_semaphore()
    peers = [near_device(peer) for peer in near_peers]
    peers += [far_device(peer) for peer in far_peers]
    peers += [(a, b) for a in (up, ia, down) for b in (left, right)] + [(up, iw), (down, iw)]
    for peer in peers:
        pl.semaphore_signal(barrier, inc=1, device_id=peer, device_id_type=MESH)

    def turn_in(src):
        for t in range(2):
            turn[t] = src[:, :, half(t)].astype(F32).reshape(CH * ROWS, LANES)

    def turned(r, t):
        return turn[t, pl.ds(r, CH, stride=ROWS), :]

    def edges(pack, t0, t1, r):
        pack = jnp.where(lane_wide == r, pltpu.roll(t0, r, 1), pack)
        return jnp.where(lane_wide == ROWS + r, pltpu.roll(t1, r + 17, 1), pack)

    def send_halo(field, pack, which, g_row, g_pack):
        pack_out[which] = pack
        push(field.at[1, CH : 2 * CH], row_in.at[which, 1], g_row, (up, iw))
        push(field.at[ROWS, CH : 2 * CH], row_in.at[which, 0], g_row, (down, iw))
        for slot, where in enumerate(
            [(ia, right), (ia, left), (down, right), (down, left), (up, right), (up, left)]
        ):
            push(pack_out.at[which], pack_in.at[which, slot], g_pack, where)

    def take_halo(field, which, g_row, g_pack):
        arrived(row_in.at[which], g_row)
        arrived(pack_in.at[which], g_pack)
        field[0, CH : 2 * CH] = jnp.where(ia > 0, row_in[which, 0], jnp.zeros((CH, COLS), BF))
        field[ROWS + 1, CH : 2 * CH] = jnp.where(ia < NA - 1, row_in[which, 1], jnp.zeros((CH, COLS), BF))
        first = jnp.where(ia > 0, 0, 1)
        last = jnp.where(ia < NA - 1, ROWS + 2, ROWS + 1)
        got = [pack_in[which, k] for k in range(6)]

        def assemble(middle, above, below, has):
            joined = jnp.where(lane == 0, above, jnp.where(lane == ROWS + 1, below, middle))
            inside = (lane_wide >= first) & (lane_wide < jnp.where(has, last, 0))
            return jnp.where(inside, joined, jnp.zeros_like(joined))

        edge_l[...] = assemble(
            pltpu.roll(got[0], 113, 1), pltpu.roll(got[2], 97, 1), pltpu.roll(got[4], 1, 1), iw > 0
        )
        edge_r[...] = assemble(
            pltpu.roll(got[1], 1, 1), pltpu.roll(got[3], 113, 1), pltpu.roll(got[5], 17, 1), iw < NW - 1
        )

        def shifts(p, carry):
            t0 = field[p, CH : 2 * CH, half(0)]
            t1 = field[p, CH : 2 * CH, half(1)]
            a0, a1 = pltpu.roll(t0, 1, 1), pltpu.roll(t1, 1, 1)
            b0, b1 = pltpu.roll(t0, LANES - 1, 1), pltpu.roll(t1, LANES - 1, 1)
            lh = pltpu.roll(edge_l[...], lax.rem(LANES - p, LANES), 1)
            rh = pltpu.roll(edge_r[...], LANES - 1 - p, 1)
            field[p, 0:CH, half(0)] = jnp.where(lane == 0, lh, a0)
            field[p, 0:CH, half(1)] = jnp.where(lane == 0, a0, a1)
            field[p, 2 * CH :, half(0)] = jnp.where(lane == LANES - 1, b1, b0)
            field[p, 2 * CH :, half(1)] = jnp.where(lane == LANES - 1, rh, b1)
            return carry

        loop(ROWS + 2, shifts, unroll=9)

    def conv_start(w, field):
        y = dot(w, field[0])
        z = dot(w, field[1])
        return z[0:CH], y[0:CH] + z[CH : 2 * CH]

    def conv_step(w, field, r, carry):
        later, now = carry
        y = dot(w, field[r + 2])
        return now + y[2 * CH :], (y[0:CH], later + y[CH : 2 * CH])

    def step_b(a_in, x, b, b_in, g_a, g_b):
        from_near(a_in, g_a)

        def widen(j, carry):
            for t in range(2):
                for r in range(2):
                    x[pl.ds((r * 16 + j * 2 + t) * HC, HC), :] = a_in[j, t, r].astype(F32)
            return carry

        loop(NEAR, widen, unroll=8)

        for peer in [*far_peers, far]:
            base = peer // 8 * (16 * HC) + lax.rem(peer, 8) * 4
            slot = b_in if peer is far else b
            for c in range(4):
                slot[peer, :, half(c)] = x[pl.ds(base + c, 16, stride=HC), :].astype(BF)
            if peer is not far:
                push(b.at[peer], b_in.at[far], g_b, far_device(peer))

    def step_c(mixed, c, c_in, g):
        c[...] = mixed.astype(BF).reshape(FAR, 16, 512)
        over_far(lambda peer: c.at[peer], c_in.at[far], g)
        c_in[far] = c[far]

    def step_d(c_in, x, d, d_in, g_c, g_d):
        from_far(c_in, g_c)

        def unpick(q, carry):
            for r in range(2):
                for c in range(4):
                    x[pl.ds((r * HC + q * 4 + c) * 16, 16), :] = c_in[r * 8 + q, :, half(c)].astype(F32)
            return carry

        loop(8, unpick, unroll=8)

        for peer in [*near_peers, near]:
            slot = d_in if peer is near else d
            for t in range(2):
                for r in range(2):
                    slot[peer, t, r] = x[pl.ds(r * HC * 16 + peer * 2 + t, HC, stride=16), :].astype(BF)
            if peer is not near:
                push(d.at[peer], d_in.at[near], g_d, near_device(peer))

    loads[0].wait()
    loads[1].wait()
    turn_in(frames)
    w_in[...] = w_in_t[...].astype(F32).T.astype(BF)

    def value_row(slot, peer, low):
        r = peer * 2 + low
        for t in range(2):
            x = turned(r, t)
            xb[r, :, half(t)] = x.astype(BF)
            off = x - jnp.mean(x, axis=0, keepdims=True)
            rstd = lax.rsqrt(jnp.mean(off * off, axis=0, keepdims=True) + EPS)
            u = off * rstd
            unit[r, :, half(t)] = u
            inv[r, :, half(t)] = jnp.broadcast_to(rstd, (8, LANES))
            nb[r, :, half(t)] = u.astype(BF)
        value, slope = gelu_parts(dot(w_in[HC:CH], nb[r]))
        dgelu[r, HC:CH] = slope
        value = value.astype(BF)
        slot[peer, 0, low] = value[:, half(0)]
        slot[peer, 1, low] = value[:, half(1)]

    for first in range(0, NEAR, 2):
        group = [*near_peers, near][first : first + 2]
        for peer in group:
            for low in range(2):
                value_row(va_in if peer is near else va, peer, low)
        if first == 0:
            pl.semaphore_wait(barrier, len(peers))
        for peer in group:
            if peer is not near:
                push(va.at[peer], va_in.at[near], G_VA, near_device(peer))

    def order():
        row = lax.broadcasted_iota(jnp.int32, (COLS, COLS), 0)
        cell = lax.broadcasted_iota(jnp.int32, (COLS, COLS), 1)
        found = (row & 0xC1) | ((row & 6) << 3) | ((row & 48) >> 2) | ((row & 8) >> 2)
        return jnp.where(cell == found, 1.0, 0.0).astype(BF)

    def mix_in_order():
        swap = order()
        return dot_nt(dot(swap, grid_mix[...]).astype(BF), swap).astype(BF)


    loads[2].wait()
    turn_in(cot)

    def cot_row(r, pack):
        t0, t1 = turned(r, 0).astype(BF), turned(r, 1).astype(BF)
        u3[r + 1, CH : 2 * CH, half(0)] = t0
        u3[r + 1, CH : 2 * CH, half(1)] = t1
        return edges(pack, t0, t1, r)

    pack = loop(ROWS, cot_row, jnp.zeros((CH, LANES), BF), unroll=8)
    send_halo(u3, pack, 0, G_ROW0, G_PACK0)

    def gate_row(r, carry):
        before = dot(w_in[...], nb[r])
        value, slope = gelu_parts(before[0:HC])
        gates[r, 0:HC] = value.astype(BF)
        dgelu[r, 0:HC] = slope
        value, slope = gelu_parts(before[CH:])
        dgelu[r, CH:] = slope
        value = value.astype(BF)
        gates[r, HC:CH] = value[0:HC]
        bval[r] = value[HC:]
        return carry

    loop(ROWS, gate_row, unroll=8)
    for load in loads[3:]:
        load.wait()
    mixp[...] = mix_in_order()
    step_b(va_in, vx, vb, vb_in, G_VA, G_VB)

    take_halo(u3, 0, G_ROW0, G_PACK0)
    back_w = jnp.concatenate(
        [jnp.concatenate([conv_w[2 - a, 2 - b] for a in range(3)], axis=1) for b in range(3)], axis=0
    ).astype(F32).T.astype(BF)
    w_out_t = w_out[...].astype(F32).T.astype(BF)

    def back_row(r, carry):
        total, carry = conv_step(back_w, u3, r, carry)
        g = (total + u3[r + 1, CH : 2 * CH].astype(F32)).astype(BF)
        gj[r] = g
        up_gated = dot(w_out_t, g)
        gg[r] = up_gated
        mixed = (up_gated * gates[r].astype(F32)).astype(BF)
        ga[r // 2, 0, r % 2] = mixed[0:HC, half(0)]
        ga[r // 2, 1, r % 2] = mixed[0:HC, half(1)]
        bback[r] = mixed[HC:]
        return carry

    carry = conv_start(back_w, u3)
    for first in range(0, NEAR, 2):
        for r in range(2 * first, 2 * first + 4):
            carry = back_row(r, carry)
        for peer in (first, first + 1):

            @pl.when(peer != near)
            def _():
                push(ga.at[peer], ga_in.at[near], G_GA, near_device(peer))

    ga_in[near] = ga[near]

    from_far(vb_in, G_VB)
    step_c(dot(mixp[...], vb_in[...].reshape(256, 512)), vc, vc_in, G_VC)

    def put(ref):
        def store(k, t, value):
            ref[k, :, half(t)] = value

        return store

    swap_granules(lambda k, t: bval[k, :, half(t)], put(xt), HC)
    values = xt[...].reshape(ROWS * HC, COLS)
    mixed = dot_nt(values, block_mix[...]).astype(BF)
    swap_granules(lambda k, t: mixed[k * HC : (k + 1) * HC, half(t)], put(bm), HC)

    step_b(ga_in, gx, gb, gb_in, G_GA, G_GB)
    step_d(vc_in, vx, vd, vd_in, G_VC, G_VD)

    swap_granules(lambda k, t: bback[k, :, half(t)], put(bt), HC)
    backs = bt[...].reshape(ROWS * HC, COLS)
    unmixed = dot(backs, block_mix[...]).astype(BF)
    swap_granules(lambda k, t: unmixed[k * HC : (k + 1) * HC, half(t)], put(gbv), HC)
    part_block = dot_tn(backs, values).astype(BF)
    se[2 * COLS : 3 * COLS] = part_block[:, half(0)]
    se[3 * COLS :] = part_block[:, half(1)]

    from_far(gb_in, G_GB)
    back = gb_in[...].reshape(256, 512)
    step_c(dot_tn(mixp[...], back), gc, gc_in, G_GC)
    part_grid = dot_nt(back, vb_in[...].reshape(256, 512)).astype(BF)
    part_grid = dot(dot_tn(order(), part_grid).astype(BF), order()).astype(BF)
    se[0:COLS] = part_grid[:, half(0)]
    se[COLS : 2 * COLS] = part_grid[:, half(1)]
    push(se.at[pl.ds(pl.multiple_of(512 - mine, 512), 512)], re0, G_E0, near_device(twin))

    for k in (0, 1, ROWS + 2, ROWS + 3):
        jp[k] = jnp.zeros((CH, COLS), BF)
    from_near(vd_in, G_VD)

    def returned(ref, r):
        return [ref[r // 2, t, lax.rem(r, 2)].astype(F32) for t in range(2)]

    def joined_row(r, pack):
        grid_mixed = returned(vd_in, r)
        for t in range(2):
            gates_t = gates[r, :, half(t)].astype(F32)
            gated[r, 0:HC, half(t)] = (gates_t[0:HC] * (grid_mixed[t] + 1.0)).astype(BF)
            gated[r, HC:, half(t)] = (gates_t[HC:] * (bm[r, :, half(t)].astype(F32) + 1.0)).astype(BF)
        j = (xb[r].astype(F32) + dot(w_out[...], gated[r])).astype(BF)
        jp[r + 2] = j
        v3[r + 1, CH : 2 * CH] = j
        return edges(pack, j[:, half(0)], j[:, half(1)], r)

    pack = loop(ROWS, joined_row, jnp.zeros((CH, LANES), BF), unroll=8)
    send_halo(v3, pack, 1, G_ROW1, G_PACK1)

    arrived(re0, G_E0)
    e0[...] = (se[pl.ds(pl.multiple_of(mine, 512), 512)].astype(F32) + re0[...].astype(F32)).astype(BF)
    over_y(lambda peer: e0.at[pl.ds(pl.multiple_of(peer * 128, 128), 128)], re1.at[level], G_E1)
    re1[level] = e0[pl.ds(pl.multiple_of(level * 128, 128), 128)]

    step_d(gc_in, gx, gd, gd_in, G_GC, G_GD)

    arrived(re1.at[pl.ds(0, 3)], G_E1)
    total = re1[0].astype(F32)
    for k in range(1, 4):
        total = total + re1[k].astype(F32)
    e1[...] = total
    over_x(lambda peer: e1.at[pl.ds(pl.multiple_of(peer * 32, 32), 32)], re2.at[across], G_E2)
    re2[across] = e1[pl.ds(pl.multiple_of(across * 32, 32), 32)]

    def conv_row(p, total):
        return total + dot_nt(u3[p], jp[pl.ds(p, 3)].reshape(3 * CH, COLS))

    p_conv = loop(ROWS + 2, conv_row, jnp.zeros((3 * CH, 3 * CH), F32), unroll=9)

    arrived(re2.at[pl.ds(0, 3)], G_E2)
    e2[...] = re2[0] + re2[1] + re2[2] + re2[3]
    over_z(lambda peer: e2, re3.at[deep], G_E3)
    re3[deep] = e2[...]

    from_near(gd_in, G_GD)

    def before_row(r, carry):
        p_in, p_out = carry
        grid_mixed = returned(vd_in, r)
        grid_back = returned(gd_in, r)
        for t in range(2):
            g = gg[r, :, half(t)]
            d = dgelu[r, :, half(t)]
            gbef[r, 0:HC, half(t)] = (d[0:HC] * (g[0:HC] * (grid_mixed[t] + 1.0))).astype(BF)
            gbef[r, HC:CH, half(t)] = (d[HC:CH] * grid_back[t]).astype(BF)
            gbef[r, CH : CH + HC, half(t)] = (d[CH : CH + HC] * (g[HC:] * (bm[r, :, half(t)].astype(F32) + 1.0))).astype(BF)
            gbef[r, CH + HC :, half(t)] = (d[CH + HC :] * gbv[r, :, half(t)].astype(F32)).astype(BF)
        return p_in + dot_nt(nb[r], gbef[r]), p_out + dot_nt(gj[r], gated[r])

    p_in, p_out = loop(
        ROWS, before_row, (jnp.zeros((CH, 2 * CH), F32), jnp.zeros((CH, CH), F32)), unroll=4
    )
    st[0 : 3 * CH] = p_conv[:, half(0)].astype(BF)
    st[3 * CH : 4 * CH] = p_in.astype(BF)
    third = p_conv[:, 2 * CH :]
    st[4 * CH :] = jnp.concatenate(
        [third[: 2 * CH], jnp.concatenate([third[2 * CH :], p_out], axis=0)], axis=1
    ).astype(BF)
    over_near(lambda peer: st.at[pl.ds(pl.multiple_of(peer * 48, 16), 48)], rt1.at[near], G_T1)
    rt1[near] = st[pl.ds(pl.multiple_of(near * 48, 16), 48)]

    arrived(re3.at[pl.ds(0, 3)], G_E3)
    e3[...] = (re3[0] + re3[1] + re3[2] + re3[3]).astype(BF)
    over_x(lambda peer: e3, re4.at[across], G_E4)
    re4[across] = e3[...]

    def frame_row(r, carry):
        normed = dot(w_in_t[...], gbef[r])
        u = unit[r]
        mean_grad = jnp.mean(normed, axis=0, keepdims=True)
        mean_proj = jnp.mean(normed * u, axis=0, keepdims=True)
        source = gj[r].astype(F32) + inv[r, 0:1] * (normed - mean_grad - u * mean_proj)
        for t in range(2):
            gframe_out[t, pl.ds(r * CH, CH), :] = source[:, half(t)]
        return carry

    loop(ROWS, frame_row, unroll=8)

    from_near(rt1, G_T1)
    total = rt1[0].astype(F32)
    for k in range(1, NW):
        total = total + rt1[k].astype(F32)
    t1[...] = total.astype(BF)
    over_far(lambda peer: t1, rt2.at[far], G_T2)
    rt2[far] = t1[...]

    arrived(re4.at[pl.ds(0, 3)], G_E4)
    over_y(lambda peer: re4, re5.at[level], G_E5)
    re5[level] = re4[...]

    take_halo(v3, 1, G_ROW1, G_PACK1)
    from_far(rt2, G_T2)
    total = rt2[0].astype(F32)
    for k in range(1, NA):
        total = total + rt2[k].astype(F32)
    t2[...] = total.astype(BF)
    over_near(lambda peer: t2, rt3.at[near], G_T3)
    rt3[near] = t2[...]

    arrived(re5.at[pl.ds(0, 3)], G_E5)
    push(re5, re6, G_E6, near_device(twin))
    early_out[pl.ds(pl.multiple_of(mine, 512), 512)] = re5[...].reshape(512, LANES)

    conv_k = jnp.concatenate(
        [jnp.concatenate([conv_w[a, b] for b in range(3)], axis=1) for a in range(3)], axis=0
    )

    def out_row(r, carry):
        total, carry = conv_step(conv_k, v3, r, carry)
        total = total + v3[r + 1, CH : 2 * CH].astype(F32)
        for t in range(2):
            rest_out[t, pl.ds(r * CH, CH), :] = total[:, half(t)]
        return carry

    loop(ROWS, out_row, conv_start(conv_k, v3), unroll=8)

    arrived(re6, G_E6)
    early_out[pl.ds(pl.multiple_of(512 - mine, 512), 512)] = re6[...].reshape(512, LANES)
    from_near(rt3, G_T3)
    tail_out[...] = rt3[...]

    for which, g_row, g_pack in ((0, G_ROW0, G_PACK0), (1, G_ROW1, G_PACK1)):
        gone(row_in.at[which], g_row)
        gone(pack_in.at[which], g_pack)
    for ref, g in (
        (va_in, G_VA), (vd_in, G_VD), (ga_in, G_GA), (gd_in, G_GD),
        (rt1, G_T1), (rt3, G_T3),
    ):
        gone(ref.at[pl.ds(0, NEAR - 1)], g)
    for ref, g in (
        (vb_in, G_VB), (vc_in, G_VC), (gb_in, G_GB), (gc_in, G_GC), (rt2, G_T2),
    ):
        gone(ref.at[pl.ds(0, FAR - 1)], g)
    gone(re0, G_E0)
    for ref, g in ((re1, G_E1), (re2, G_E2), (re3, G_E3), (re4, G_E4), (re5, G_E5)):
        gone(ref.at[pl.ds(0, 3)], g)
    gone(re6, G_E6)


def finish(rest, gframe, early, tail, restored, grad_frames, grad_w_in_t, grad_grid, grad_block, grad_w_out, grad_conv):
    scale = float(ROWS * NA * COLS * NW) ** (-0.5)

    def channel(c, carry):
        for src, dst in ((rest, restored), (gframe, grad_frames)):
            for t in range(2):
                dst[c, :, half(t)] = src[t, pl.ds(c, ROWS, stride=CH), :].astype(BF)
        return carry

    loop(CH, channel, unroll=8)

    for k in range(2):
        grad_grid[:, half(k)] = early[k * COLS : (k + 1) * COLS].astype(F32) * scale
        grad_block[:, half(k)] = early[(2 + k) * COLS : (3 + k) * COLS].astype(F32) * scale
    grad_w_in_t[...] = tail[3 * CH : 4 * CH].astype(F32) * scale
    last = tail[4 * CH :].astype(F32) * scale
    grad_w_out[...] = last[CH:, CH:]
    for b in range(3):
        rows = slice((2 - b) * CH, (3 - b) * CH)
        pair = tail[rows].astype(F32) * scale
        grad_conv[0, b] = pair[:, :CH]
        grad_conv[1, b] = pair[:, CH:]
    grad_conv[2, 2] = last[:CH, :CH]
    grad_conv[2, 1] = last[CH:, :CH]
    grad_conv[2, 0] = last[:CH, CH:]


def vm(*shape, dtype=BF):
    return pltpu.VMEM(shape, dtype)


def exchange():
    message_w = vm(NW, 2, 2, HC, LANES)
    message_a = vm(NA, 16, 512)
    return [message_w, message_w, vm(2 * 16 * HC, LANES, dtype=F32)] + [message_a] * 4 + [message_w] * 2


SCRATCH = [
    vm(CH, ROWS, COLS),
    vm(CH, 2 * CH),
    vm(COLS, COLS),
    vm(COLS, COLS),
    vm(CH, CH),
    vm(3, 3, CH, CH),
    vm(CH, ROWS, COLS),
    vm(2 * CH, CH),
    vm(2, CH * ROWS, LANES, dtype=F32),
    vm(ROWS, CH, COLS),
    vm(ROWS, CH, COLS),
    vm(ROWS, CH, COLS, dtype=F32),
    vm(ROWS, 8, COLS, dtype=F32),
    vm(ROWS, 2 * CH, COLS, dtype=F32),
    vm(ROWS, CH, COLS),
    vm(ROWS, HC, COLS),
    vm(ROWS + 2, 3 * CH, COLS),
    vm(ROWS + 2, 3 * CH, COLS),
    vm(ROWS, CH, COLS),
    vm(ROWS, CH, COLS, dtype=F32),
    vm(ROWS, HC, COLS),
    vm(ROWS, HC, COLS),
    vm(ROWS, HC, COLS),
    vm(ROWS, HC, COLS),
    vm(ROWS, HC, COLS),
    *exchange(),
    *exchange(),
    vm(ROWS, CH, COLS),
    vm(ROWS, 2 * CH, COLS),
    vm(ROWS + 4, CH, COLS),
    vm(2, 2, CH, COLS),
    vm(2, CH, LANES),
    vm(2, 6, CH, LANES),
    vm(CH, LANES),
    vm(CH, LANES),
    vm(COLS, COLS),
    vm(4 * COLS, LANES),
    vm(512, LANES),
    vm(512, LANES),
    vm(4, 128, LANES),
    vm(128, LANES, dtype=F32),
    vm(4, 32, LANES, dtype=F32),
    vm(32, LANES, dtype=F32),
    vm(4, 32, LANES, dtype=F32),
    vm(32, LANES),
    vm(4, 32, LANES),
    vm(4, 4, 32, LANES),
    vm(4, 4, 32, LANES),
    vm(6 * CH, LANES),
    vm(NW, 48, LANES),
    vm(48, LANES),
    vm(NA, 48, LANES),
    vm(48, LANES),
    vm(NW, 48, LANES),
    pltpu.SemaphoreType.DMA((GROUPS,)),
    pltpu.SemaphoreType.DMA((GROUPS,)),
    pltpu.SemaphoreType.DMA((7,)),
]


def body(frames, w_in, grid_mix, block_mix, w_out, conv_w, cotangent):
    operands = (frames, w_in.T, grid_mix, block_mix, w_out, conv_w, cotangent)
    vmem = pl.BlockSpec(memory_space=pltpu.VMEM)
    shape = jax.ShapeDtypeStruct
    rest, gframe, early, tail = pl.pallas_call(
        kernel,
        out_shape=(
            shape((2, ROWS * CH, LANES), F32),
            shape((2, ROWS * CH, LANES), F32),
            shape((4 * COLS, LANES), BF),
            shape((NW, 48, LANES), BF),
        ),
        in_specs=[pl.BlockSpec(memory_space=pltpu.HBM)] * 7,
        out_specs=(vmem,) * 4,
        scratch_shapes=SCRATCH,
        compiler_params=pltpu.CompilerParams(
            collective_id=0, has_side_effects=True, vmem_limit_bytes=32 * 1024 * 1024
        ),
    )(*[pltpu.with_memory_space_constraint(x, pltpu.HBM) for x in operands])
    restored, grad_frames, grad_w_in_t, grad_grid, grad_block, grad_w_out, grad_conv = pl.pallas_call(
        finish,
        out_shape=(
            shape((CH, ROWS, COLS), BF),
            shape((CH, ROWS, COLS), BF),
            shape((CH, 2 * CH), F32),
            shape((COLS, COLS), F32),
            shape((COLS, COLS), F32),
            shape((CH, CH), F32),
            shape((3, 3, CH, CH), F32),
        ),
        in_specs=[vmem] * 4,
        out_specs=(vmem,) * 7,
        compiler_params=pltpu.CompilerParams(vmem_limit_bytes=16 * 1024 * 1024),
    )(rest, gframe, early, tail.reshape(6 * CH, LANES))
    return restored, grad_frames, grad_w_in_t.T, grad_grid, grad_block, grad_w_out, grad_conv


def solution(mesh):
    placed = (P(None, "ha", "wa"), P(), P(), P(), P(), P(), P(None, "ha", "wa"))
    return jax.shard_map(
        body,
        mesh=mesh,
        in_specs=placed,
        out_specs=(P(None, "ha", "wa"), P(None, "ha", "wa"), P(), P(), P(), P(), P()),
        check_vma=False,
    )
```

```python
import jax
import jax.numpy as jnp
from jax import lax
from jax.experimental import pallas as pl
from jax.experimental.pallas import tpu as pltpu
from jax.sharding import PartitionSpec as P

BF = jnp.bfloat16
F32 = jnp.float32
EPS = 1e-06
MESH = pl.DeviceIdType.MESH

CH = 64
HC = 32
ROWS = 16
COLS = 256
LANES = 128
NA = 16
NW = 8
NEAR = 8
FAR = 16

(G_ROW0, G_PACK0, G_ROW1, G_PACK1, G_VA, G_VB, G_VC, G_VD, G_GA, G_GB, G_GC, G_GD) = range(12)
(G_E0, G_E1, G_E2, G_E3, G_E4, G_E5, G_E6, G_T1, G_T2, G_T3, G_T4, G_Q1, G_Q2) = range(12, 25)
GROUPS = 25


def dot(a, b):
    return lax.dot_general(a, b, (((1,), (0,)), ((), ())), preferred_element_type=F32)


def dot_nt(a, b):
    return lax.dot_general(a, b, (((1,), (1,)), ((), ())), preferred_element_type=F32)


def dot_tn(a, b):
    return lax.dot_general(a, b, (((0,), (0,)), ((), ())), preferred_element_type=F32)


def swap_granules(load, store, depth):
    lane = lax.broadcasted_iota(jnp.int16, (depth, LANES), 1)
    for row_half in range(2):
        for col_half in range(2):
            held = [load(row_half * 8 + k, col_half) for k in range(8)]
            for s in range(3):
                width = 16 << s
                low = (lane & width) == 0
                for k in range(8):
                    if not k & (1 << s):
                        a, b = held[k], held[k | (1 << s)]
                        held[k] = jnp.where(low, a, pltpu.roll(b, width, 1))
                        held[k | (1 << s)] = jnp.where(low, pltpu.roll(a, LANES - width, 1), b)
            for k in range(8):
                store(col_half * 8 + k, row_half, held[k])


def half(t):
    return slice(t * LANES, (t + 1) * LANES)


def loop(count, step, carry=0, unroll=1):
    return lax.fori_loop(0, count, step, carry, unroll=unroll)


def gelu_parts(x):
    root = 0.7978845608028654
    cube = root * 0.044715
    square = x * x
    h = 0.5 * jnp.tanh(x * (cube * square + root)) + 0.5
    value = x * h
    return value, h + value * (1.0 - h) * ((6.0 * cube) * square + 2.0 * root)


def kernel(
    frames_hbm, w_in_t_hbm, grid_mix_hbm, block_mix_hbm, w_out_hbm, conv_w_hbm, cot_hbm,
    rest_out, gframe_out, early_out, tail_out, value_out,
    frames, w_in_t, grid_mix, block_mix, w_out, conv_w, cot, w_in,
    turn, xb, nb, unit, inv, dgelu, gates, bval, u3, v3, gj, gg, xt, bt, bm, gbv,
    va, va_in, vx, vb, vb_in, vc, vc_in, vd, vd_in,
    ga, ga_in, gx, gb, gb_in, gc, gc_in, gd, gd_in,
    gated, gbef, jp, row_in, pack_out, pack_in, edge_l, edge_r,
    mixp, se, re0, e0, re1, e1, re2, e2, re3, e3, re4, re5, re6,
    st, rt1, t1, rt2, t2, rt3, t3, rt4, sq, rq1, q1, rq2,
    ssem, rsem, isem,
):
    ia = lax.axis_index("ha")
    iw = lax.axis_index("wa")
    up, down = lax.rem(ia + NA - 1, NA), lax.rem(ia + 1, NA)
    left, right = lax.rem(iw + NW - 1, NW), lax.rem(iw + 1, NW)
    lane = lax.broadcasted_iota(jnp.int16, (CH, LANES), 1)
    lane_wide = lax.broadcasted_iota(jnp.int32, (CH, LANES), 1)

    loads = [
        pltpu.make_async_copy(src, dst, isem.at[k])
        for k, (src, dst) in enumerate(
            [
                (cot_hbm, cot),
                (frames_hbm, frames),
                (w_in_t_hbm, w_in_t),
                (conv_w_hbm, conv_w),
                (w_out_hbm, w_out),
                (block_mix_hbm, block_mix),
                (grid_mix_hbm, grid_mix),
            ]
        )
    ]
    for load in loads:
        load.start()

    def push(src, dst, g, where):
        pltpu.make_async_remote_copy(
            src_ref=src, dst_ref=dst, send_sem=ssem.at[g], recv_sem=rsem.at[g], device_id=where, device_id_type=MESH
        ).start()

    near = lax.rem(iw, 2) * 4 + lax.rem(ia, 4)
    far = ia // 4 * 4 + iw // 2

    def near_device(peer):
        return ia // 4 * 4 + lax.rem(peer, 4), iw // 2 * 2 + peer // 4

    def far_device(peer):
        return peer // 4 * 4 + lax.rem(ia, 4), lax.rem(peer, 4) * 2 + lax.rem(iw, 2)

    near_peers = [lax.rem(near + k, NEAR) for k in range(1, NEAR)]
    far_peers = [lax.rem(far + k, FAR) for k in range(1, FAR)]
    twin = near + 1 - 2 * lax.rem(near, 2)

    def over_near(src_of, dst, g):
        for peer in near_peers:
            push(src_of(peer), dst, g, near_device(peer))

    def over_far(src_of, dst, g):
        for peer in far_peers:
            push(src_of(peer), dst, g, far_device(peer))

    def over_x(src_of, dst, g):
        for k in range(1, 4):
            peer = lax.rem(iw // 2 + k, 4)
            push(src_of(peer), dst, g, (ia, peer * 2 + lax.rem(iw, 2)))

    def over_z(src_of, dst, g):
        for k in range(1, 4):
            peer = lax.rem(ia // 4 + k, 4)
            push(src_of(peer), dst, g, (peer * 4 + lax.rem(ia, 4), iw))

    def over_y(src_of, dst, g):
        for k in range(1, 4):
            peer = lax.rem(near + 2 * k, NEAR)
            push(src_of(peer // 2), dst, g, near_device(peer))

    def arrived(ref, g):
        pltpu.make_async_copy(ref, ref, rsem.at[g]).wait()

    def gone(ref, g):
        pltpu.make_async_copy(ref, ref, ssem.at[g]).wait()

    def from_near(ref, g):
        arrived(ref.at[pl.ds(0, NEAR - 1)], g)

    def from_far(ref, g):
        arrived(ref.at[pl.ds(0, FAR - 1)], g)

    mine = lax.rem(near, 2) * 512
    level, across, deep = near // 2, iw // 2, ia // 4

    barrier = pltpu.get_barrier_semaphore()
    peers = [near_device(peer) for peer in near_peers]
    peers += [far_device(peer) for peer in far_peers]
    peers += [(a, b) for a in (up, ia, down) for b in (left, right)] + [(up, iw), (down, iw)]
    for peer in peers:
        pl.semaphore_signal(barrier, inc=1, device_id=peer, device_id_type=MESH)

    def turn_in(src):
        for t in range(2):
            turn[t] = src[:, :, half(t)].astype(F32).reshape(CH * ROWS, LANES)

    def turned(r, t):
        return turn[t, pl.ds(r, CH, stride=ROWS), :]

    def edges(pack, t0, t1, r):
        pack = jnp.where(lane_wide == r, pltpu.roll(t0, r, 1), pack)
        return jnp.where(lane_wide == ROWS + r, pltpu.roll(t1, r + 17, 1), pack)

    def send_halo(field, pack, which, g_row, g_pack):
        pack_out[which] = pack
        push(field.at[1, CH : 2 * CH], row_in.at[which, 1], g_row, (up, iw))
        push(field.at[ROWS, CH : 2 * CH], row_in.at[which, 0], g_row, (down, iw))
        for slot, where in enumerate(
            [(ia, right), (ia, left), (down, right), (down, left), (up, right), (up, left)]
        ):
            push(pack_out.at[which], pack_in.at[which, slot], g_pack, where)

    def take_halo(field, which, g_row, g_pack):
        arrived(row_in.at[which], g_row)
        arrived(pack_in.at[which], g_pack)
        field[0, CH : 2 * CH] = jnp.where(ia > 0, row_in[which, 0], jnp.zeros((CH, COLS), BF))
        field[ROWS + 1, CH : 2 * CH] = jnp.where(ia < NA - 1, row_in[which, 1], jnp.zeros((CH, COLS), BF))
        first = jnp.where(ia > 0, 0, 1)
        last = jnp.where(ia < NA - 1, ROWS + 2, ROWS + 1)
        got = [pack_in[which, k] for k in range(6)]

        def assemble(middle, above, below, has):
            joined = jnp.where(lane == 0, above, jnp.where(lane == ROWS + 1, below, middle))
            inside = (lane_wide >= first) & (lane_wide < jnp.where(has, last, 0))
            return jnp.where(inside, joined, jnp.zeros_like(joined))

        edge_l[...] = assemble(
            pltpu.roll(got[0], 113, 1), pltpu.roll(got[2], 97, 1), pltpu.roll(got[4], 1, 1), iw > 0
        )
        edge_r[...] = assemble(
            pltpu.roll(got[1], 1, 1), pltpu.roll(got[3], 113, 1), pltpu.roll(got[5], 17, 1), iw < NW - 1
        )

        def shifts(p, carry):
            t0 = field[p, CH : 2 * CH, half(0)]
            t1 = field[p, CH : 2 * CH, half(1)]
            a0, a1 = pltpu.roll(t0, 1, 1), pltpu.roll(t1, 1, 1)
            b0, b1 = pltpu.roll(t0, LANES - 1, 1), pltpu.roll(t1, LANES - 1, 1)
            lh = pltpu.roll(edge_l[...], lax.rem(LANES - p, LANES), 1)
            rh = pltpu.roll(edge_r[...], LANES - 1 - p, 1)
            field[p, 0:CH, half(0)] = jnp.where(lane == 0, lh, a0)
            field[p, 0:CH, half(1)] = jnp.where(lane == 0, a0, a1)
            field[p, 2 * CH :, half(0)] = jnp.where(lane == LANES - 1, b1, b0)
            field[p, 2 * CH :, half(1)] = jnp.where(lane == LANES - 1, rh, b1)
            return carry

        loop(ROWS + 2, shifts, unroll=9)

    def conv_start(w, field):
        y = dot(w, field[0])
        z = dot(w, field[1])
        return z[0:CH], y[0:CH] + z[CH : 2 * CH]

    def conv_step(w, field, r, carry):
        later, now = carry
        y = dot(w, field[r + 2])
        return now + y[2 * CH :], (y[0:CH], later + y[CH : 2 * CH])

    def step_b(a_in, x, b, b_in, g_a, g_b):
        from_near(a_in, g_a)

        def widen(j, carry):
            for t in range(2):
                for r in range(2):
                    x[pl.ds((r * 16 + j * 2 + t) * HC, HC), :] = a_in[j, t, r].astype(F32)
            return carry

        loop(NEAR, widen, unroll=8)

        for peer in [*far_peers, far]:
            base = peer // 8 * (16 * HC) + lax.rem(peer, 8) * 4
            slot = b_in if peer is far else b
            for c in range(4):
                slot[peer, :, half(c)] = x[pl.ds(base + c, 16, stride=HC), :].astype(BF)
            if peer is not far:
                push(b.at[peer], b_in.at[far], g_b, far_device(peer))

    def step_c(mixed, c, c_in, g):
        c[...] = mixed.astype(BF).reshape(FAR, 16, 512)
        over_far(lambda peer: c.at[peer], c_in.at[far], g)
        c_in[far] = c[far]

    def step_d(c_in, x, d, d_in, g_c, g_d):
        from_far(c_in, g_c)

        def unpick(q, carry):
            for r in range(2):
                for c in range(4):
                    x[pl.ds((r * HC + q * 4 + c) * 16, 16), :] = c_in[r * 8 + q, :, half(c)].astype(F32)
            return carry

        loop(8, unpick, unroll=8)

        for peer in [*near_peers, near]:
            slot = d_in if peer is near else d
            for t in range(2):
                for r in range(2):
                    slot[peer, t, r] = x[pl.ds(r * HC * 16 + peer * 2 + t, HC, stride=16), :].astype(BF)
            if peer is not near:
                push(d.at[peer], d_in.at[near], g_d, near_device(peer))

    def order():
        row = lax.broadcasted_iota(jnp.int32, (COLS, COLS), 0)
        cell = lax.broadcasted_iota(jnp.int32, (COLS, COLS), 1)
        found = (row & 0xC1) | ((row & 6) << 3) | ((row & 48) >> 2) | ((row & 8) >> 2)
        return jnp.where(cell == found, 1.0, 0.0).astype(BF)

    def mix_in_order():
        swap = order()
        return dot_nt(dot(swap, grid_mix[...]).astype(BF), swap).astype(BF)

    loads[0].wait()
    turn_in(cot)

    def cot_row(r, pack):
        t0, t1 = turned(r, 0).astype(BF), turned(r, 1).astype(BF)
        u3[r + 1, CH : 2 * CH, half(0)] = t0
        u3[r + 1, CH : 2 * CH, half(1)] = t1
        return edges(pack, t0, t1, r)

    pack = loop(ROWS, cot_row, jnp.zeros((CH, LANES), BF), unroll=8)
    pl.semaphore_wait(barrier, len(peers))
    send_halo(u3, pack, 0, G_ROW0, G_PACK0)

    loads[1].wait()
    loads[2].wait()
    turn_in(frames)
    w_in[...] = w_in_t[...].astype(F32).T.astype(BF)

    def value_row(slot, peer, low):
        r = peer * 2 + low
        for t in range(2):
            x = turned(r, t)
            xb[r, :, half(t)] = x.astype(BF)
            off = x - jnp.mean(x, axis=0, keepdims=True)
            rstd = lax.rsqrt(jnp.mean(off * off, axis=0, keepdims=True) + EPS)
            u = off * rstd
            unit[r, :, half(t)] = u
            inv[r, :, half(t)] = jnp.broadcast_to(rstd, (8, LANES))
            nb[r, :, half(t)] = u.astype(BF)
        value, slope = gelu_parts(dot(w_in[HC:CH], nb[r]))
        dgelu[r, HC:CH] = slope
        value = value.astype(BF)
        slot[peer, 0, low] = value[:, half(0)]
        slot[peer, 1, low] = value[:, half(1)]

    for first in range(0, NEAR, 2):
        group = [*near_peers, near][first : first + 2]
        for peer in group:
            for low in range(2):
                value_row(va_in if peer is near else va, peer, low)
        for peer in group:
            if peer is not near:
                push(va.at[peer], va_in.at[near], G_VA, near_device(peer))

    def grid_gate_row(r, carry):
        value, slope = gelu_parts(dot(w_in[0:HC], nb[r]))
        gates[r, 0:HC] = value.astype(BF)
        dgelu[r, 0:HC] = slope
        return carry

    loop(ROWS, grid_gate_row, unroll=8)

    for load in loads[3:]:
        load.wait()
    back_w = jnp.concatenate(
        [jnp.concatenate([conv_w[2 - a, 2 - b] for a in range(3)], axis=1) for b in range(3)], axis=0
    ).astype(F32).T.astype(BF)
    w_out_t = w_out[...].astype(F32).T.astype(BF)
    take_halo(u3, 0, G_ROW0, G_PACK0)

    def back_row(r, carry):
        total, carry = conv_step(back_w, u3, r, carry)
        g = (total + u3[r + 1, CH : 2 * CH].astype(F32)).astype(BF)
        gj[r] = g
        up_gated = dot(w_out_t, g)
        gg[r] = up_gated
        mixed = (up_gated[0:HC] * gates[r, 0:HC].astype(F32)).astype(BF)
        ga[r // 2, 0, r % 2] = mixed[:, half(0)]
        ga[r // 2, 1, r % 2] = mixed[:, half(1)]
        return carry

    carry = conv_start(back_w, u3)
    for first in range(0, NEAR, 2):
        for r in range(2 * first, 2 * first + 4):
            carry = back_row(r, carry)
        for peer in (first, first + 1):

            @pl.when(peer != near)
            def _():
                push(ga.at[peer], ga_in.at[near], G_GA, near_device(peer))

    ga_in[near] = ga[near]

    step_b(va_in, vx, vb, vb_in, G_VA, G_VB)

    def block_gate_row(r, carry):
        value, slope = gelu_parts(dot(w_in[CH:], nb[r]))
        dgelu[r, CH:] = slope
        value = value.astype(BF)
        gates[r, HC:CH] = value[0:HC]
        bval[r] = value[HC:]
        return carry

    loop(ROWS, block_gate_row, unroll=8)
    mixp[...] = mix_in_order()

    def put(ref):
        def store(k, t, value):
            ref[k, :, half(t)] = value

        return store

    swap_granules(lambda k, t: bval[k, :, half(t)], put(xt), HC)
    values = xt[...].reshape(ROWS * HC, COLS)
    mixed = dot_nt(values, block_mix[...]).astype(BF)
    swap_granules(lambda k, t: mixed[k * HC : (k + 1) * HC, half(t)], put(bm), HC)

    step_b(ga_in, gx, gb, gb_in, G_GA, G_GB)
    from_far(vb_in, G_VB)
    step_c(dot(mixp[...], vb_in[...].reshape(256, 512)), vc, vc_in, G_VC)

    def block_back(k, t):
        return (gg[k, HC:, half(t)] * gates[k, HC:, half(t)].astype(F32)).astype(BF)

    swap_granules(block_back, put(bt), HC)
    backs = bt[...].reshape(ROWS * HC, COLS)
    unmixed = dot(backs, block_mix[...]).astype(BF)
    swap_granules(lambda k, t: unmixed[k * HC : (k + 1) * HC, half(t)], put(gbv), HC)
    part_block = dot_tn(backs, values).astype(BF)
    se[2 * COLS : 3 * COLS] = part_block[:, half(0)]
    se[3 * COLS :] = part_block[:, half(1)]

    def block_before_row(r, carry):
        d = dgelu[r, CH:]
        gbef[r, CH : CH + HC] = (d[0:HC] * (gg[r, HC:] * (bm[r].astype(F32) + 1.0))).astype(BF)
        gbef[r, CH + HC :] = (d[HC:] * gbv[r].astype(F32)).astype(BF)
        gbef[r, HC:CH] = jnp.zeros((HC, COLS), BF)
        return carry

    loop(ROWS, block_before_row, unroll=4)
    for k in (0, 1, ROWS + 2, ROWS + 3):
        jp[k] = jnp.zeros((CH, COLS), BF)

    from_far(gb_in, G_GB)
    back = gb_in[...].reshape(256, 512)
    step_c(dot_tn(mixp[...], back), gc, gc_in, G_GC)
    step_d(vc_in, vx, vd, vd_in, G_VC, G_VD)

    part_grid = dot_nt(back, vb_in[...].reshape(256, 512)).astype(BF)
    part_grid = dot(dot_tn(order(), part_grid).astype(BF), order()).astype(BF)
    se[0:COLS] = part_grid[:, half(0)]
    se[COLS : 2 * COLS] = part_grid[:, half(1)]
    push(se.at[pl.ds(pl.multiple_of(512 - mine, 512), 512)], re0, G_E0, near_device(twin))

    step_d(gc_in, gx, gd, gd_in, G_GC, G_GD)

    from_near(vd_in, G_VD)

    def returned(ref, r):
        return [ref[r // 2, t, lax.rem(r, 2)].astype(F32) for t in range(2)]

    def joined_row(r, pack):
        grid_mixed = returned(vd_in, r)
        for t in range(2):
            gates_t = gates[r, :, half(t)].astype(F32)
            gated[r, 0:HC, half(t)] = (gates_t[0:HC] * (grid_mixed[t] + 1.0)).astype(BF)
            gated[r, HC:, half(t)] = (gates_t[HC:] * (bm[r, :, half(t)].astype(F32) + 1.0)).astype(BF)
        j = (xb[r].astype(F32) + dot(w_out[...], gated[r])).astype(BF)
        jp[r + 2] = j
        v3[r + 1, CH : 2 * CH] = j
        return edges(pack, j[:, half(0)], j[:, half(1)], r)

    pack = loop(ROWS, joined_row, jnp.zeros((CH, LANES), BF), unroll=8)
    send_halo(v3, pack, 1, G_ROW1, G_PACK1)

    arrived(re0, G_E0)
    e0[...] = (se[pl.ds(pl.multiple_of(mine, 512), 512)].astype(F32) + re0[...].astype(F32)).astype(BF)
    over_y(lambda peer: e0.at[pl.ds(pl.multiple_of(peer * 128, 128), 128)], re1.at[level], G_E1)
    re1[level] = e0[pl.ds(pl.multiple_of(level * 128, 128), 128)]

    def conv_row(p, total):
        return total + dot_nt(u3[p], jp[pl.ds(p, 3)].reshape(3 * CH, COLS))

    p_conv = loop(ROWS + 2, conv_row, jnp.zeros((3 * CH, 3 * CH), F32), unroll=9)

    def gate_before_row(r, carry):
        p_in, p_out = carry
        grid_mixed = returned(vd_in, r)
        for t in range(2):
            slope = dgelu[r, 0:HC, half(t)]
            gbef[r, 0:HC, half(t)] = (slope * (gg[r, 0:HC, half(t)] * (grid_mixed[t] + 1.0))).astype(BF)
        return p_in + dot_nt(nb[r], gbef[r]), p_out + dot_nt(gj[r], gated[r])

    p_in, p_out = loop(
        ROWS, gate_before_row, (jnp.zeros((CH, 2 * CH), F32), jnp.zeros((CH, CH), F32)), unroll=4
    )
    st[0 : 3 * CH] = p_conv[:, half(0)].astype(BF)
    st[3 * CH : 4 * CH] = p_in.astype(BF)
    third = p_conv[:, 2 * CH :]
    st[4 * CH :] = jnp.concatenate(
        [third[: 2 * CH], jnp.concatenate([third[2 * CH :], p_out], axis=0)], axis=1
    ).astype(BF)
    over_near(lambda peer: st.at[pl.ds(pl.multiple_of(peer * 48, 16), 48)], rt1.at[near], G_T1)
    rt1[near] = st[pl.ds(pl.multiple_of(near * 48, 16), 48)]

    from_near(gd_in, G_GD)

    def value_before_row(r, total):
        grid_back = returned(gd_in, r)
        for t in range(2):
            gbef[r, HC:CH, half(t)] = (dgelu[r, HC:CH, half(t)] * grid_back[t]).astype(BF)
        return total + dot_nt(gbef[r, HC:CH], nb[r])

    p_value = loop(ROWS, value_before_row, jnp.zeros((HC, CH), F32), unroll=4)
    sq[...] = jnp.concatenate([p_value[0:16], p_value[16:]], axis=1).astype(BF)
    over_near(lambda peer: sq, rq1.at[near], G_Q1)
    rq1[near] = sq[...]

    arrived(re1.at[pl.ds(0, 3)], G_E1)
    total = re1[0].astype(F32)
    for k in range(1, 4):
        total = total + re1[k].astype(F32)
    e1[...] = total
    over_x(lambda peer: e1.at[pl.ds(pl.multiple_of(peer * 32, 32), 32)], re2.at[across], G_E2)
    re2[across] = e1[pl.ds(pl.multiple_of(across * 32, 32), 32)]

    def frame_row(r, carry):
        normed = dot(w_in_t[...], gbef[r])
        u = unit[r]
        mean_grad = jnp.mean(normed, axis=0, keepdims=True)
        mean_proj = jnp.mean(normed * u, axis=0, keepdims=True)
        source = gj[r].astype(F32) + inv[r, 0:1] * (normed - mean_grad - u * mean_proj)
        for t in range(2):
            gframe_out[t, pl.ds(r * CH, CH), :] = source[:, half(t)]
        return carry

    loop(ROWS, frame_row, unroll=8)

    from_near(rt1, G_T1)
    total = rt1[0].astype(F32)
    for k in range(1, NEAR):
        total = total + rt1[k].astype(F32)
    t1[...] = total.astype(BF)
    over_x(lambda peer: t1, rt2.at[across], G_T2)
    rt2[across] = t1[...]

    from_near(rq1, G_Q1)
    total = rq1[0].astype(F32)
    for k in range(1, NEAR):
        total = total + rq1[k].astype(F32)
    q1[...] = total.astype(BF)
    over_far(lambda peer: q1, rq2.at[far], G_Q2)
    rq2[far] = q1[...]

    arrived(re2.at[pl.ds(0, 3)], G_E2)
    e2[...] = re2[0] + re2[1] + re2[2] + re2[3]
    over_z(lambda peer: e2, re3.at[deep], G_E3)
    re3[deep] = e2[...]

    take_halo(v3, 1, G_ROW1, G_PACK1)

    arrived(rt2.at[pl.ds(0, 3)], G_T2)
    total = rt2[0].astype(F32)
    for k in range(1, 4):
        total = total + rt2[k].astype(F32)
    t2[...] = total.astype(BF)
    over_z(lambda peer: t2, rt3.at[deep], G_T3)
    rt3[deep] = t2[...]

    arrived(re3.at[pl.ds(0, 3)], G_E3)
    e3[...] = (re3[0] + re3[1] + re3[2] + re3[3]).astype(BF)
    over_x(lambda peer: e3, re4.at[across], G_E4)
    re4[across] = e3[...]

    conv_k = jnp.concatenate(
        [jnp.concatenate([conv_w[a, b] for b in range(3)], axis=1) for a in range(3)], axis=0
    )

    def out_row(r, carry):
        total, carry = conv_step(conv_k, v3, r, carry)
        total = total + v3[r + 1, CH : 2 * CH].astype(F32)
        for t in range(2):
            rest_out[t, pl.ds(r * CH, CH), :] = total[:, half(t)]
        return carry

    carry = loop(ROWS // 2, out_row, conv_start(conv_k, v3), unroll=8)

    arrived(re4.at[pl.ds(0, 3)], G_E4)
    over_y(lambda peer: re4, re5.at[level], G_E5)
    re5[level] = re4[...]
    arrived(rt3.at[pl.ds(0, 3)], G_T3)
    total = rt3[0].astype(F32)
    for k in range(1, 4):
        total = total + rt3[k].astype(F32)
    t3[...] = total.astype(BF)
    over_near(lambda peer: t3, rt4.at[near], G_T4)
    rt4[near] = t3[...]

    loop(ROWS // 2, lambda r, carry: out_row(r + ROWS // 2, carry), carry, unroll=8)

    arrived(re5.at[pl.ds(0, 3)], G_E5)
    push(re5, re6, G_E6, near_device(twin))
    early_out[pl.ds(pl.multiple_of(mine, 512), 512)] = re5[...].reshape(512, LANES)

    from_far(rq2, G_Q2)
    total = rq2[0].astype(F32)
    for k in range(1, FAR):
        total = total + rq2[k].astype(F32)
    value_out[...] = total
    from_near(rt4, G_T4)
    tail_out[...] = rt4[...]
    arrived(re6, G_E6)
    early_out[pl.ds(pl.multiple_of(512 - mine, 512), 512)] = re6[...].reshape(512, LANES)

    for which, g_row, g_pack in ((0, G_ROW0, G_PACK0), (1, G_ROW1, G_PACK1)):
        gone(row_in.at[which], g_row)
        gone(pack_in.at[which], g_pack)
    for ref, g in (
        (va_in, G_VA), (vd_in, G_VD), (ga_in, G_GA), (gd_in, G_GD),
        (rt1, G_T1), (rt4, G_T4), (rq1, G_Q1),
    ):
        gone(ref.at[pl.ds(0, NEAR - 1)], g)
    for ref, g in (
        (vb_in, G_VB), (vc_in, G_VC), (gb_in, G_GB), (gc_in, G_GC), (rq2, G_Q2),
    ):
        gone(ref.at[pl.ds(0, FAR - 1)], g)
    gone(re0, G_E0)
    for ref, g in ((re1, G_E1), (re2, G_E2), (re3, G_E3), (re4, G_E4), (re5, G_E5), (rt2, G_T2), (rt3, G_T3)):
        gone(ref.at[pl.ds(0, 3)], g)
    gone(re6, G_E6)


def finish(
    rest, gframe, early, tail, value,
    restored, grad_frames, grad_w_in_t, grad_grid, grad_block, grad_w_out, grad_conv,
):
    scale = float(ROWS * NA * COLS * NW) ** (-0.5)

    def channel(c, carry):
        for src, dst in ((rest, restored), (gframe, grad_frames)):
            for t in range(2):
                dst[c, :, half(t)] = src[t, pl.ds(c, ROWS, stride=CH), :].astype(BF)
        return carry

    loop(CH, channel, unroll=8)

    for k in range(2):
        grad_grid[:, half(k)] = early[k * COLS : (k + 1) * COLS].astype(F32) * scale
        grad_block[:, half(k)] = early[(2 + k) * COLS : (3 + k) * COLS].astype(F32) * scale
    quarter = value[...] * scale
    zeros = jnp.zeros((HC, CH), F32)
    quarter = jnp.concatenate([zeros, quarter[:, :CH], quarter[:, CH:], zeros, zeros], axis=0)
    grad_w_in_t[...] = tail[3 * CH : 4 * CH].astype(F32) * scale + quarter.T
    last = tail[4 * CH :].astype(F32) * scale
    grad_w_out[...] = last[CH:, CH:]
    for b in range(3):
        rows = slice((2 - b) * CH, (3 - b) * CH)
        pair = tail[rows].astype(F32) * scale
        grad_conv[0, b] = pair[:, :CH]
        grad_conv[1, b] = pair[:, CH:]
    grad_conv[2, 2] = last[:CH, :CH]
    grad_conv[2, 1] = last[CH:, :CH]
    grad_conv[2, 0] = last[:CH, CH:]


def vm(*shape, dtype=BF):
    return pltpu.VMEM(shape, dtype)


def exchange():
    message_w = vm(NW, 2, 2, HC, LANES)
    message_a = vm(NA, 16, 512)
    return [message_w, message_w, vm(2 * 16 * HC, LANES, dtype=F32)] + [message_a] * 4 + [message_w] * 2


SCRATCH = [
    vm(CH, ROWS, COLS),
    vm(CH, 2 * CH),
    vm(COLS, COLS),
    vm(COLS, COLS),
    vm(CH, CH),
    vm(3, 3, CH, CH),
    vm(CH, ROWS, COLS),
    vm(2 * CH, CH),
    vm(2, CH * ROWS, LANES, dtype=F32),
    vm(ROWS, CH, COLS),
    vm(ROWS, CH, COLS),
    vm(ROWS, CH, COLS, dtype=F32),
    vm(ROWS, 8, COLS, dtype=F32),
    vm(ROWS, 2 * CH, COLS, dtype=F32),
    vm(ROWS, CH, COLS),
    vm(ROWS, HC, COLS),
    vm(ROWS + 2, 3 * CH, COLS),
    vm(ROWS + 2, 3 * CH, COLS),
    vm(ROWS, CH, COLS),
    vm(ROWS, CH, COLS, dtype=F32),
    vm(ROWS, HC, COLS),
    vm(ROWS, HC, COLS),
    vm(ROWS, HC, COLS),
    vm(ROWS, HC, COLS),
    *exchange(),
    *exchange(),
    vm(ROWS, CH, COLS),
    vm(ROWS, 2 * CH, COLS),
    vm(ROWS + 4, CH, COLS),
    vm(2, 2, CH, COLS),
    vm(2, CH, LANES),
    vm(2, 6, CH, LANES),
    vm(CH, LANES),
    vm(CH, LANES),
    vm(COLS, COLS),
    vm(4 * COLS, LANES),
    vm(512, LANES),
    vm(512, LANES),
    vm(4, 128, LANES),
    vm(128, LANES, dtype=F32),
    vm(4, 32, LANES, dtype=F32),
    vm(32, LANES, dtype=F32),
    vm(4, 32, LANES, dtype=F32),
    vm(32, LANES),
    vm(4, 32, LANES),
    vm(4, 4, 32, LANES),
    vm(4, 4, 32, LANES),
    vm(6 * CH, LANES),
    vm(NW, 48, LANES),
    vm(48, LANES),
    vm(4, 48, LANES),
    vm(48, LANES),
    vm(4, 48, LANES),
    vm(48, LANES),
    vm(NEAR, 48, LANES),
    vm(16, LANES),
    vm(NEAR, 16, LANES),
    vm(16, LANES),
    vm(FAR, 16, LANES),
    pltpu.SemaphoreType.DMA((GROUPS,)),
    pltpu.SemaphoreType.DMA((GROUPS,)),
    pltpu.SemaphoreType.DMA((7,)),
]


def body(frames, w_in, grid_mix, block_mix, w_out, conv_w, cotangent):
    operands = (frames, w_in.T, grid_mix, block_mix, w_out, conv_w, cotangent)
    vmem = pl.BlockSpec(memory_space=pltpu.VMEM)
    shape = jax.ShapeDtypeStruct
    rest, gframe, early, tail, value = pl.pallas_call(
        kernel,
        out_shape=(
            shape((2, ROWS * CH, LANES), F32),
            shape((2, ROWS * CH, LANES), F32),
            shape((4 * COLS, LANES), BF),
            shape((NEAR, 48, LANES), BF),
            shape((16, LANES), F32),
        ),
        in_specs=[pl.BlockSpec(memory_space=pltpu.HBM)] * 7,
        out_specs=(vmem,) * 5,
        scratch_shapes=SCRATCH,
        compiler_params=pltpu.CompilerParams(
            collective_id=0, has_side_effects=True, vmem_limit_bytes=32 * 1024 * 1024
        ),
    )(*[pltpu.with_memory_space_constraint(x, pltpu.HBM) for x in operands])
    restored, grad_frames, grad_w_in_t, grad_grid, grad_block, grad_w_out, grad_conv = pl.pallas_call(
        finish,
        out_shape=(
            shape((CH, ROWS, COLS), BF),
            shape((CH, ROWS, COLS), BF),
            shape((CH, 2 * CH), F32),
            shape((COLS, COLS), F32),
            shape((COLS, COLS), F32),
            shape((CH, CH), F32),
            shape((3, 3, CH, CH), F32),
        ),
        in_specs=[vmem] * 5,
        out_specs=(vmem,) * 7,
        compiler_params=pltpu.CompilerParams(vmem_limit_bytes=16 * 1024 * 1024),
    )(rest, gframe, early, tail.reshape(6 * CH, LANES), value)
    return restored, grad_frames, grad_w_in_t.T, grad_grid, grad_block, grad_w_out, grad_conv


def solution(mesh):
    placed = (P(None, "ha", "wa"), P(), P(), P(), P(), P(), P(None, "ha", "wa"))
    return jax.shard_map(
        body,
        mesh=mesh,
        in_specs=placed,
        out_specs=(P(None, "ha", "wa"), P(None, "ha", "wa"), P(), P(), P(), P(), P()),
        check_vma=False,
    )
```

```python
import jax
import jax.numpy as jnp
from jax import lax
from jax.experimental import pallas as pl
from jax.experimental.pallas import tpu as pltpu
from jax.sharding import PartitionSpec as P

BF = jnp.bfloat16
F32 = jnp.float32
EPS = 1e-06
LOGICAL = pl.DeviceIdType.LOGICAL

CH = 64
HC = 32
ROWS = 16
COLS = 256
LANES = 128
NA = 16
NW = 8
NEAR = 8
FAR = 16

(G_ROW0, G_PACK0, G_ROW1, G_PACK1, G_VA, G_VB, G_VC, G_VD, G_GA, G_GB, G_GC, G_GD) = range(12)
(G_E0, G_E1, G_E2, G_E3, G_E4, G_E5, G_E6, G_T1, G_T2, G_T3) = range(12, 22)
GROUPS = 22


def dot(a, b):
    return lax.dot_general(a, b, (((1,), (0,)), ((), ())), preferred_element_type=F32)


def dot_nt(a, b):
    return lax.dot_general(a, b, (((1,), (1,)), ((), ())), preferred_element_type=F32)


def dot_tn(a, b):
    return lax.dot_general(a, b, (((0,), (0,)), ((), ())), preferred_element_type=F32)


def swap_granules(load, store, depth):
    lane = lax.broadcasted_iota(jnp.int16, (depth, LANES), 1)
    for row_half in range(2):
        for col_half in range(2):
            held = [load(row_half * 8 + k, col_half) for k in range(8)]
            for s in range(3):
                width = 16 << s
                low = (lane & width) == 0
                for k in range(8):
                    if not k & (1 << s):
                        a, b = held[k], held[k | (1 << s)]
                        held[k] = jnp.where(low, a, pltpu.roll(b, width, 1))
                        held[k | (1 << s)] = jnp.where(low, pltpu.roll(a, LANES - width, 1), b)
            for k in range(8):
                store(col_half * 8 + k, row_half, held[k])


def half(t):
    return slice(t * LANES, (t + 1) * LANES)


def loop(count, step, carry=0, unroll=1):
    return lax.fori_loop(0, count, step, carry, unroll=unroll)


def gelu_parts(x):
    root = 0.7978845608028654
    cube = root * 0.044715
    square = x * x
    h = 0.5 * jnp.tanh(x * (cube * square + root)) + 0.5
    value = x * h
    return value, h + value * (1.0 - h) * ((6.0 * cube) * square + 2.0 * root)


def kernel(
    frames_hbm, w_in_t_hbm, grid_mix_hbm, block_mix_hbm, w_out_hbm, conv_w_hbm, cot_hbm,
    rest_out, gframe_out, early_out, tail_out,
    frames, w_in_t, grid_mix, block_mix, w_out, conv_w, cot, w_in,
    turn, xb, nb, unit, inv, dgelu, gates, bval, u3, v3, gj, gg, xt, bt, bm, gbv,
    va, va_in, vx, vb, vb_in, vc, vc_in, vd, vd_in,
    ga, ga_in, gx, gb, gb_in, gc, gc_in, gd, gd_in,
    gated, gbef, jp, row_in, pack_out, pack_in, edge_l, edge_r,
    mixp, mixp_t, gather, spread, se, re0, e0, re1, e1, re2, e2, re3, e3, re4, re5, re6,
    st, rt1, t1, rt2, t2, rt3,
    ssem, rsem, isem,
):
    ia = lax.axis_index("ha")
    iw = lax.axis_index("wa")
    up, down = lax.rem(ia + NA - 1, NA), lax.rem(ia + 1, NA)
    left, right = lax.rem(iw + NW - 1, NW), lax.rem(iw + 1, NW)
    lane = lax.broadcasted_iota(jnp.int16, (CH, LANES), 1)
    lane_wide = lax.broadcasted_iota(jnp.int32, (CH, LANES), 1)

    loads = [
        pltpu.make_async_copy(src, dst, isem.at[k])
        for k, (src, dst) in enumerate(
            [
                (cot_hbm, cot),
                (frames_hbm, frames),
                (w_in_t_hbm, w_in_t),
                (conv_w_hbm, conv_w),
                (w_out_hbm, w_out),
                (block_mix_hbm, block_mix),
                (grid_mix_hbm, grid_mix),
            ]
        )
    ]
    for load in loads:
        load.start()

    def push(src, dst, g, where):
        pltpu.make_async_remote_copy(
            src_ref=src, dst_ref=dst, send_sem=ssem.at[g], recv_sem=rsem.at[g], device_id=where, device_id_type=LOGICAL
        ).start()

    deep, across = ia // 4, iw // 2
    here, high = lax.rem(ia, 4), lax.rem(iw, 2)
    near = high * 4 + here
    far = deep * 4 + across
    level = near // 2
    core = lax.rem(ia, 2)
    low = here - core
    column = deep * (4 * NW) + across * 2
    spot = here * NW + high
    cores = (core, 1 - core)
    lows = (low, 2 - low)
    highs = (high, 1 - high)
    near_peers, near_ids = [], []
    for k in range(NEAR):
        place = lows[k // 2 % 2] + cores[k % 2]
        near_peers.append(highs[k // 4] * 4 + place)
        near_ids.append(column + place * NW + highs[k // 4])
    rings = []
    for index in (deep, across):
        last = lax.rem(index, 2)
        first = index - last
        rings.append([(first, 2 - first)[k // 2] + (last, 1 - last)[k % 2] for k in range(4)])
    far_peers = [rings[0][k // 4] * 4 + rings[1][k % 4] for k in range(FAR)]
    far_ids = [rings[0][k // 4] * (4 * NW) + rings[1][k % 4] * 2 + spot for k in range(FAR)]

    def over_near(src_of, dst, g):
        for k in range(1, NEAR):
            push(src_of(near_peers[k]), dst, g, near_ids[k])

    def over_far(src_of, dst, g):
        for k in range(1, FAR):
            push(src_of(far_peers[k]), dst, g, far_ids[k])

    def over_x(src_of, dst, g):
        for k in range(1, 4):
            push(src_of(rings[1][k]), dst, g, far_ids[k])

    def over_z(src_of, dst, g):
        for k in range(1, 4):
            push(src_of(rings[0][k]), dst, g, far_ids[4 * k])

    def over_y(src_of, dst, g):
        for k in range(1, 4):
            push(src_of(near_peers[2 * k] // 2), dst, g, near_ids[2 * k])

    def arrived(ref, g):
        pltpu.make_async_copy(ref, ref, rsem.at[g]).wait()

    def gone(ref, g):
        pltpu.make_async_copy(ref, ref, ssem.at[g]).wait()

    def from_near(ref, g):
        arrived(ref.at[pl.ds(0, NEAR - 1)], g)

    def from_far(ref, g):
        arrived(ref.at[pl.ds(0, FAR - 1)], g)

    mine = core * 512
    sides = {
        (a, b): (ia, up, down)[a] * NW + (iw, left, right)[b] for a in range(3) for b in range(3)
    }
    halo_ids = [sides[1, 0], sides[2, 0]]
    halo_ids += [sides[a, b] for a, b in ((0, 2), (0, 1), (2, 2), (2, 1), (1, 2), (1, 1))]

    barrier = pltpu.get_barrier_semaphore()
    peers = near_ids[1:] + far_ids[1:] + halo_ids
    for peer in peers:
        pl.semaphore_signal(barrier, inc=1, device_id=peer, device_id_type=LOGICAL)

    def turn_in(src):
        for t in range(2):
            turn[t] = src[:, :, half(t)].astype(F32).reshape(CH * ROWS, LANES)

    def turned(r, t):
        return turn[t, pl.ds(r, CH, stride=ROWS), :]

    def edges(pack, t0, t1, r):
        pack = jnp.where(lane_wide == r, pltpu.roll(t0, r, 1), pack)
        return jnp.where(lane_wide == ROWS + r, pltpu.roll(t1, r + 17, 1), pack)

    def send_halo(field, pack, which, g_row, g_pack):
        pack_out[which] = pack
        push(field.at[1, CH : 2 * CH], row_in.at[which, 1], g_row, halo_ids[0])
        push(field.at[ROWS, CH : 2 * CH], row_in.at[which, 0], g_row, halo_ids[1])
        for slot in range(6):
            push(pack_out.at[which], pack_in.at[which, slot], g_pack, halo_ids[2 + slot])

    def take_halo(field, which, g_row, g_pack):
        arrived(row_in.at[which], g_row)
        arrived(pack_in.at[which], g_pack)
        field[0, CH : 2 * CH] = jnp.where(ia > 0, row_in[which, 0], jnp.zeros((CH, COLS), BF))
        field[ROWS + 1, CH : 2 * CH] = jnp.where(ia < NA - 1, row_in[which, 1], jnp.zeros((CH, COLS), BF))
        first = jnp.where(ia > 0, 0, 1)
        last = jnp.where(ia < NA - 1, ROWS + 2, ROWS + 1)
        got = [pack_in[which, k] for k in range(6)]

        def assemble(middle, above, below, has):
            joined = jnp.where(lane == 0, above, jnp.where(lane == ROWS + 1, below, middle))
            inside = (lane_wide >= first) & (lane_wide < jnp.where(has, last, 0))
            return jnp.where(inside, joined, jnp.zeros_like(joined))

        edge_l[...] = assemble(
            pltpu.roll(got[0], 113, 1), pltpu.roll(got[2], 97, 1), pltpu.roll(got[4], 1, 1), iw > 0
        )
        edge_r[...] = assemble(
            pltpu.roll(got[1], 1, 1), pltpu.roll(got[3], 113, 1), pltpu.roll(got[5], 17, 1), iw < NW - 1
        )

        def shifts(p, carry):
            t0 = field[p, CH : 2 * CH, half(0)]
            t1 = field[p, CH : 2 * CH, half(1)]
            a0, a1 = pltpu.roll(t0, 1, 1), pltpu.roll(t1, 1, 1)
            b0, b1 = pltpu.roll(t0, LANES - 1, 1), pltpu.roll(t1, LANES - 1, 1)
            lh = pltpu.roll(edge_l[...], lax.rem(LANES - p, LANES), 1)
            rh = pltpu.roll(edge_r[...], LANES - 1 - p, 1)
            field[p, 0:CH, half(0)] = jnp.where(lane == 0, lh, a0)
            field[p, 0:CH, half(1)] = jnp.where(lane == 0, a0, a1)
            field[p, 2 * CH :, half(0)] = jnp.where(lane == LANES - 1, b1, b0)
            field[p, 2 * CH :, half(1)] = jnp.where(lane == LANES - 1, rh, b1)
            return carry

        loop(ROWS + 2, shifts, unroll=9)

    def conv_start(w, field):
        y = dot(w, field[0])
        z = dot(w, field[1])
        return z[0:CH], y[0:CH] + z[CH : 2 * CH]

    def conv_step(w, field, r, carry):
        later, now = carry
        y = dot(w, field[r + 2])
        return now + y[2 * CH :], (y[0:CH], later + y[CH : 2 * CH])

    def step_b(a_in, x, b, b_in, g_a, g_b):
        from_near(a_in, g_a)

        def widen(j, carry):
            for t in range(2):
                for r in range(2):
                    x[pl.ds((r * 16 + j * 2 + t) * HC, HC), :] = a_in[j, t, r].astype(F32)
            return carry

        loop(NEAR, widen, unroll=8)

        for k in [*range(1, FAR), 0]:
            peer = far_peers[k]
            base = peer // 8 * (16 * HC) + lax.rem(peer, 8) * 4
            slot = b if k else b_in
            for c in range(4):
                slot[peer, :, half(c)] = x[pl.ds(base + c, 16, stride=HC), :].astype(BF)
            if k:
                push(b.at[peer], b_in.at[far], g_b, far_ids[k])

    def step_c(mixed, c, c_in, g):
        c[...] = mixed.astype(BF).reshape(FAR, 16, 512)
        over_far(lambda peer: c.at[peer], c_in.at[far], g)
        c_in[far] = c[far]

    def step_d(c_in, x, d, d_in, g_c, g_d):
        from_far(c_in, g_c)

        def unpick(q, carry):
            for r in range(2):
                for c in range(4):
                    x[pl.ds((r * HC + q * 4 + c) * 16, 16), :] = c_in[r * 8 + q, :, half(c)].astype(F32)
            return carry

        loop(8, unpick, unroll=8)

        for k in [*range(1, NEAR), 0]:
            peer = near_peers[k]
            slot = d if k else d_in
            for t in range(2):
                for r in range(2):
                    slot[peer, t, r] = x[pl.ds(r * HC * 16 + peer * 2 + t, HC, stride=16), :].astype(BF)
            if k:
                push(d.at[peer], d_in.at[near], g_d, near_ids[k])

    def order(cell, row):
        found = (row & 0xC1) | ((row & 6) << 3) | ((row & 48) >> 2) | ((row & 8) >> 2)
        return jnp.where(cell == found, 1.0, 0.0).astype(BF)

    loads[0].wait()
    turn_in(cot)

    def cot_row(r, pack):
        t0, t1 = turned(r, 0).astype(BF), turned(r, 1).astype(BF)
        u3[r + 1, CH : 2 * CH, half(0)] = t0
        u3[r + 1, CH : 2 * CH, half(1)] = t1
        return edges(pack, t0, t1, r)

    pack = loop(ROWS, cot_row, jnp.zeros((CH, LANES), BF), unroll=8)
    pl.semaphore_wait(barrier, len(peers))
    send_halo(u3, pack, 0, G_ROW0, G_PACK0)

    loads[1].wait()
    loads[2].wait()
    turn_in(frames)
    w_in[...] = w_in_t[...].astype(F32).T.astype(BF)

    def value_row(slot, peer, odd):
        r = peer * 2 + odd
        for t in range(2):
            x = turned(r, t)
            xb[r, :, half(t)] = x.astype(BF)
            off = x - jnp.mean(x, axis=0, keepdims=True)
            rstd = lax.rsqrt(jnp.mean(off * off, axis=0, keepdims=True) + EPS)
            u = off * rstd
            unit[r, :, half(t)] = u
            inv[r, :, half(t)] = jnp.broadcast_to(rstd, (8, LANES))
            nb[r, :, half(t)] = u.astype(BF)
        value, slope = gelu_parts(dot(w_in[HC:CH], nb[r]))
        dgelu[r, HC:CH] = slope
        value = value.astype(BF)
        slot[peer, 0, odd] = value[:, half(0)]
        slot[peer, 1, odd] = value[:, half(1)]

    for first in range(0, NEAR, 2):
        group = [*range(1, NEAR), 0][first : first + 2]
        for k in group:
            for odd in range(2):
                value_row(va if k else va_in, near_peers[k], odd)
        for k in group:
            if k:
                push(va.at[near_peers[k]], va_in.at[near], G_VA, near_ids[k])

    def grid_gate_row(r, carry):
        value, slope = gelu_parts(dot(w_in[0:HC], nb[r]))
        gates[r, 0:HC] = value.astype(BF)
        dgelu[r, 0:HC] = slope
        return carry

    loop(ROWS, grid_gate_row, unroll=8)

    for load in loads[3:]:
        load.wait()
    back_w = jnp.concatenate(
        [jnp.concatenate([conv_w[2 - a, 2 - b] for a in range(3)], axis=1) for b in range(3)], axis=0
    ).astype(F32).T.astype(BF)
    w_out_t = w_out[...].astype(F32).T.astype(BF)
    take_halo(u3, 0, G_ROW0, G_PACK0)

    def back_row(r, carry):
        total, carry = conv_step(back_w, u3, r, carry)
        g = (total + u3[r + 1, CH : 2 * CH].astype(F32)).astype(BF)
        gj[r] = g
        up_gated = dot(w_out_t, g)
        gg[r] = up_gated
        mixed = (up_gated[0:HC] * gates[r, 0:HC].astype(F32)).astype(BF)
        ga[r // 2, 0, r % 2] = mixed[:, half(0)]
        ga[r // 2, 1, r % 2] = mixed[:, half(1)]
        return carry

    carry = conv_start(back_w, u3)
    for first in range(0, NEAR, 2):
        for r in range(2 * first, 2 * first + 4):
            carry = back_row(r, carry)
        for peer in (first, first + 1):

            @pl.when(peer != near)
            def _():
                push(ga.at[peer], ga_in.at[near], G_GA, column + (peer % 4) * NW + peer // 4)

    ga_in[near] = ga[near]

    step_b(va_in, vx, vb, vb_in, G_VA, G_VB)

    def block_gate_row(r, carry):
        value, slope = gelu_parts(dot(w_in[CH:], nb[r]))
        dgelu[r, CH:] = slope
        value = value.astype(BF)
        gates[r, HC:CH] = value[0:HC]
        bval[r] = value[HC:]
        return carry

    loop(ROWS, block_gate_row, unroll=8)
    down_axis = lax.broadcasted_iota(jnp.int32, (COLS, COLS), 0)
    along_axis = lax.broadcasted_iota(jnp.int32, (COLS, COLS), 1)
    gather[...] = order(along_axis, down_axis)
    spread[...] = order(down_axis, along_axis)
    mixp[...] = dot(dot(gather[...], grid_mix[...]).astype(BF), spread[...]).astype(BF)
    mixp_t[...] = dot(dot_nt(gather[...], grid_mix[...]).astype(BF), spread[...]).astype(BF)

    def put(ref):
        def store(k, t, value):
            ref[k, :, half(t)] = value

        return store

    swap_granules(lambda k, t: bval[k, :, half(t)], put(xt), HC)
    values = xt[...].reshape(ROWS * HC, COLS)
    mixed = dot_nt(values, block_mix[...]).astype(BF)
    swap_granules(lambda k, t: mixed[k * HC : (k + 1) * HC, half(t)], put(bm), HC)

    step_b(ga_in, gx, gb, gb_in, G_GA, G_GB)
    from_far(vb_in, G_VB)
    step_c(dot(mixp[...], vb_in[...].reshape(256, 512)), vc, vc_in, G_VC)

    def block_back(k, t):
        return (gg[k, HC:, half(t)] * gates[k, HC:, half(t)].astype(F32)).astype(BF)

    swap_granules(block_back, put(bt), HC)
    backs = bt[...].reshape(ROWS * HC, COLS)
    unmixed = dot(backs, block_mix[...]).astype(BF)
    swap_granules(lambda k, t: unmixed[k * HC : (k + 1) * HC, half(t)], put(gbv), HC)
    part_block = dot_tn(backs, values).astype(BF)
    se[2 * COLS : 3 * COLS] = part_block[:, half(0)]
    se[3 * COLS :] = part_block[:, half(1)]

    def block_before_row(r, carry):
        d = dgelu[r, CH:]
        gbef[r, CH : CH + HC] = (d[0:HC] * (gg[r, HC:] * (bm[r].astype(F32) + 1.0))).astype(BF)
        gbef[r, CH + HC :] = (d[HC:] * gbv[r].astype(F32)).astype(BF)
        return carry

    loop(ROWS, block_before_row, unroll=4)
    for k in (0, 1, ROWS + 2, ROWS + 3):
        jp[k] = jnp.zeros((CH, COLS), BF)

    from_far(gb_in, G_GB)
    back = gb_in[...].reshape(256, 512)
    step_c(dot(mixp_t[...], back), gc, gc_in, G_GC)
    step_d(vc_in, vx, vd, vd_in, G_VC, G_VD)

    part_grid = dot_nt(back, vb_in[...].reshape(256, 512)).astype(BF)
    part_grid = dot(dot(spread[...], part_grid).astype(BF), gather[...]).astype(BF)
    se[0:COLS] = part_grid[:, half(0)]
    se[COLS : 2 * COLS] = part_grid[:, half(1)]
    push(se.at[pl.ds(pl.multiple_of(512 - mine, 512), 512)], re0, G_E0, near_ids[1])

    step_d(gc_in, gx, gd, gd_in, G_GC, G_GD)

    from_near(vd_in, G_VD)

    def returned(ref, r):
        return [ref[r // 2, t, lax.rem(r, 2)].astype(F32) for t in range(2)]

    def joined_row(r, pack):
        grid_mixed = returned(vd_in, r)
        for t in range(2):
            gates_t = gates[r, :, half(t)].astype(F32)
            gated[r, 0:HC, half(t)] = (gates_t[0:HC] * (grid_mixed[t] + 1.0)).astype(BF)
            gated[r, HC:, half(t)] = (gates_t[HC:] * (bm[r, :, half(t)].astype(F32) + 1.0)).astype(BF)
        j = (xb[r].astype(F32) + dot(w_out[...], gated[r])).astype(BF)
        jp[r + 2] = j
        v3[r + 1, CH : 2 * CH] = j
        return edges(pack, j[:, half(0)], j[:, half(1)], r)

    pack = loop(ROWS, joined_row, jnp.zeros((CH, LANES), BF), unroll=8)
    send_halo(v3, pack, 1, G_ROW1, G_PACK1)

    arrived(re0, G_E0)
    e0[...] = (se[pl.ds(pl.multiple_of(mine, 512), 512)].astype(F32) + re0[...].astype(F32)).astype(BF)
    over_y(lambda peer: e0.at[pl.ds(pl.multiple_of(peer * 128, 128), 128)], re1.at[level], G_E1)
    re1[level] = e0[pl.ds(pl.multiple_of(level * 128, 128), 128)]

    def conv_row(p, total):
        return total + dot_nt(u3[p], jp[pl.ds(p, 3)].reshape(3 * CH, COLS))

    p_conv = loop(ROWS + 2, conv_row, jnp.zeros((3 * CH, 3 * CH), F32), unroll=9)

    from_near(gd_in, G_GD)

    def gate_before_row(r, carry):
        p_in, p_out = carry
        grid_mixed, grid_back = returned(vd_in, r), returned(gd_in, r)
        for t in range(2):
            slope = dgelu[r, 0:HC, half(t)]
            gbef[r, 0:HC, half(t)] = (slope * (gg[r, 0:HC, half(t)] * (grid_mixed[t] + 1.0))).astype(BF)
            gbef[r, HC:CH, half(t)] = (dgelu[r, HC:CH, half(t)] * grid_back[t]).astype(BF)
        return p_in + dot_nt(nb[r], gbef[r]), p_out + dot_nt(gj[r], gated[r])

    p_in, p_out = loop(
        ROWS, gate_before_row, (jnp.zeros((CH, 2 * CH), F32), jnp.zeros((CH, CH), F32)), unroll=4
    )
    st[0 : 3 * CH] = p_conv[:, half(0)].astype(BF)
    st[3 * CH : 4 * CH] = p_in.astype(BF)
    third = p_conv[:, 2 * CH :]
    st[4 * CH :] = jnp.concatenate(
        [third[: 2 * CH], jnp.concatenate([third[2 * CH :], p_out], axis=0)], axis=1
    ).astype(BF)
    over_near(lambda peer: st.at[pl.ds(pl.multiple_of(peer * 48, 16), 48)], rt1.at[near], G_T1)
    rt1[near] = st[pl.ds(pl.multiple_of(near * 48, 16), 48)]

    arrived(re1.at[pl.ds(0, 3)], G_E1)
    total = re1[0].astype(F32)
    for k in range(1, 4):
        total = total + re1[k].astype(F32)
    e1[...] = total
    over_x(lambda peer: e1.at[pl.ds(pl.multiple_of(peer * 32, 32), 32)], re2.at[across], G_E2)
    re2[across] = e1[pl.ds(pl.multiple_of(across * 32, 32), 32)]

    def frame_row(r, carry):
        normed = dot(w_in_t[...], gbef[r])
        u = unit[r]
        mean_grad = jnp.mean(normed, axis=0, keepdims=True)
        mean_proj = jnp.mean(normed * u, axis=0, keepdims=True)
        source = gj[r].astype(F32) + inv[r, 0:1] * (normed - mean_grad - u * mean_proj)
        for t in range(2):
            gframe_out[t, pl.ds(r * CH, CH), :] = source[:, half(t)]
        return carry

    loop(ROWS, frame_row, unroll=8)

    from_near(rt1, G_T1)
    total = rt1[0].astype(F32)
    for k in range(1, NEAR):
        total = total + rt1[k].astype(F32)
    t1[...] = total.astype(BF)
    over_far(lambda peer: t1, rt2.at[far], G_T2)
    rt2[far] = t1[...]

    arrived(re2.at[pl.ds(0, 3)], G_E2)
    e2[...] = re2[0] + re2[1] + re2[2] + re2[3]
    over_z(lambda peer: e2, re3.at[deep], G_E3)
    re3[deep] = e2[...]

    take_halo(v3, 1, G_ROW1, G_PACK1)

    from_far(rt2, G_T2)
    total = rt2[0].astype(F32)
    for k in range(1, FAR):
        total = total + rt2[k].astype(F32)
    t2[...] = total.astype(BF)
    over_near(lambda peer: t2, rt3.at[near], G_T3)
    rt3[near] = t2[...]

    arrived(re3.at[pl.ds(0, 3)], G_E3)
    e3[...] = (re3[0] + re3[1] + re3[2] + re3[3]).astype(BF)
    over_x(lambda peer: e3, re4.at[across], G_E4)
    re4[across] = e3[...]

    conv_k = jnp.concatenate(
        [jnp.concatenate([conv_w[a, b] for b in range(3)], axis=1) for a in range(3)], axis=0
    )

    def out_row(r, carry):
        total, carry = conv_step(conv_k, v3, r, carry)
        total = total + v3[r + 1, CH : 2 * CH].astype(F32)
        for t in range(2):
            rest_out[t, pl.ds(r * CH, CH), :] = total[:, half(t)]
        return carry

    carry = loop(ROWS // 2, out_row, conv_start(conv_k, v3), unroll=8)

    arrived(re4.at[pl.ds(0, 3)], G_E4)
    over_y(lambda peer: re4, re5.at[level], G_E5)
    re5[level] = re4[...]

    loop(ROWS // 2, lambda r, carry: out_row(r + ROWS // 2, carry), carry, unroll=8)

    arrived(re5.at[pl.ds(0, 3)], G_E5)
    push(re5, re6, G_E6, near_ids[1])
    early_out[pl.ds(pl.multiple_of(mine, 512), 512)] = re5[...].reshape(512, LANES)

    from_near(rt3, G_T3)
    tail_out[...] = rt3[...]
    arrived(re6, G_E6)
    early_out[pl.ds(pl.multiple_of(512 - mine, 512), 512)] = re6[...].reshape(512, LANES)

    for which, g_row, g_pack in ((0, G_ROW0, G_PACK0), (1, G_ROW1, G_PACK1)):
        gone(row_in.at[which], g_row)
        gone(pack_in.at[which], g_pack)
    for ref, g in (
        (va_in, G_VA), (vd_in, G_VD), (ga_in, G_GA), (gd_in, G_GD),
        (rt1, G_T1), (rt3, G_T3),
    ):
        gone(ref.at[pl.ds(0, NEAR - 1)], g)
    for ref, g in (
        (vb_in, G_VB), (vc_in, G_VC), (gb_in, G_GB), (gc_in, G_GC), (rt2, G_T2),
    ):
        gone(ref.at[pl.ds(0, FAR - 1)], g)
    gone(re0, G_E0)
    for ref, g in ((re1, G_E1), (re2, G_E2), (re3, G_E3), (re4, G_E4), (re5, G_E5)):
        gone(ref.at[pl.ds(0, 3)], g)
    gone(re6, G_E6)


def finish(
    rest, gframe, early, tail,
    restored, grad_frames, grad_w_in_t, grad_grid, grad_block, grad_w_out, grad_conv,
):
    scale = float(ROWS * NA * COLS * NW) ** (-0.5)

    def channel(c, carry):
        for src, dst in ((rest, restored), (gframe, grad_frames)):
            for t in range(2):
                dst[c, :, half(t)] = src[t, pl.ds(c, ROWS, stride=CH), :].astype(BF)
        return carry

    loop(CH, channel, unroll=8)

    for k in range(2):
        grad_grid[:, half(k)] = early[k * COLS : (k + 1) * COLS].astype(F32) * scale
        grad_block[:, half(k)] = early[(2 + k) * COLS : (3 + k) * COLS].astype(F32) * scale
    grad_w_in_t[...] = tail[3 * CH : 4 * CH].astype(F32) * scale
    last = tail[4 * CH :].astype(F32) * scale
    grad_w_out[...] = last[CH:, CH:]
    for b in range(3):
        rows = slice((2 - b) * CH, (3 - b) * CH)
        pair = tail[rows].astype(F32) * scale
        grad_conv[0, b] = pair[:, :CH]
        grad_conv[1, b] = pair[:, CH:]
    grad_conv[2, 2] = last[:CH, :CH]
    grad_conv[2, 1] = last[CH:, :CH]
    grad_conv[2, 0] = last[:CH, CH:]


def vm(*shape, dtype=BF):
    return pltpu.VMEM(shape, dtype)


def exchange():
    message_w = vm(NW, 2, 2, HC, LANES)
    message_a = vm(NA, 16, 512)
    return [message_w, message_w, vm(2 * 16 * HC, LANES, dtype=F32)] + [message_a] * 4 + [message_w] * 2


SCRATCH = [
    vm(CH, ROWS, COLS),
    vm(CH, 2 * CH),
    vm(COLS, COLS),
    vm(COLS, COLS),
    vm(CH, CH),
    vm(3, 3, CH, CH),
    vm(CH, ROWS, COLS),
    vm(2 * CH, CH),
    vm(2, CH * ROWS, LANES, dtype=F32),
    vm(ROWS, CH, COLS),
    vm(ROWS, CH, COLS),
    vm(ROWS, CH, COLS, dtype=F32),
    vm(ROWS, 8, COLS, dtype=F32),
    vm(ROWS, 2 * CH, COLS, dtype=F32),
    vm(ROWS, CH, COLS),
    vm(ROWS, HC, COLS),
    vm(ROWS + 2, 3 * CH, COLS),
    vm(ROWS + 2, 3 * CH, COLS),
    vm(ROWS, CH, COLS),
    vm(ROWS, CH, COLS, dtype=F32),
    vm(ROWS, HC, COLS),
    vm(ROWS, HC, COLS),
    vm(ROWS, HC, COLS),
    vm(ROWS, HC, COLS),
    *exchange(),
    *exchange(),
    vm(ROWS, CH, COLS),
    vm(ROWS, 2 * CH, COLS),
    vm(ROWS + 4, CH, COLS),
    vm(2, 2, CH, COLS),
    vm(2, CH, LANES),
    vm(2, 6, CH, LANES),
    vm(CH, LANES),
    vm(CH, LANES),
    vm(COLS, COLS),
    vm(COLS, COLS),
    vm(COLS, COLS),
    vm(COLS, COLS),
    vm(4 * COLS, LANES),
    vm(512, LANES),
    vm(512, LANES),
    vm(4, 128, LANES),
    vm(128, LANES, dtype=F32),
    vm(4, 32, LANES, dtype=F32),
    vm(32, LANES, dtype=F32),
    vm(4, 32, LANES, dtype=F32),
    vm(32, LANES),
    vm(4, 32, LANES),
    vm(4, 4, 32, LANES),
    vm(4, 4, 32, LANES),
    vm(6 * CH, LANES),
    vm(NW, 48, LANES),
    vm(48, LANES),
    vm(FAR, 48, LANES),
    vm(48, LANES),
    vm(NEAR, 48, LANES),
    pltpu.SemaphoreType.DMA((GROUPS,)),
    pltpu.SemaphoreType.DMA((GROUPS,)),
    pltpu.SemaphoreType.DMA((7,)),
]


def body(frames, w_in, grid_mix, block_mix, w_out, conv_w, cotangent):
    operands = (frames, w_in.T, grid_mix, block_mix, w_out, conv_w, cotangent)
    vmem = pl.BlockSpec(memory_space=pltpu.VMEM)
    shape = jax.ShapeDtypeStruct
    rest, gframe, early, tail = pl.pallas_call(
        kernel,
        out_shape=(
            shape((2, ROWS * CH, LANES), F32),
            shape((2, ROWS * CH, LANES), F32),
            shape((4 * COLS, LANES), BF),
            shape((NEAR, 48, LANES), BF),
        ),
        in_specs=[pl.BlockSpec(memory_space=pltpu.HBM)] * 7,
        out_specs=(vmem,) * 4,
        scratch_shapes=SCRATCH,
        compiler_params=pltpu.CompilerParams(
            collective_id=0, has_side_effects=True, vmem_limit_bytes=32 * 1024 * 1024
        ),
    )(*[pltpu.with_memory_space_constraint(x, pltpu.HBM) for x in operands])
    restored, grad_frames, grad_w_in_t, grad_grid, grad_block, grad_w_out, grad_conv = pl.pallas_call(
        finish,
        out_shape=(
            shape((CH, ROWS, COLS), BF),
            shape((CH, ROWS, COLS), BF),
            shape((CH, 2 * CH), F32),
            shape((COLS, COLS), F32),
            shape((COLS, COLS), F32),
            shape((CH, CH), F32),
            shape((3, 3, CH, CH), F32),
        ),
        in_specs=[vmem] * 4,
        out_specs=(vmem,) * 7,
        compiler_params=pltpu.CompilerParams(vmem_limit_bytes=16 * 1024 * 1024),
    )(rest, gframe, early, tail.reshape(6 * CH, LANES))
    return restored, grad_frames, grad_w_in_t.T, grad_grid, grad_block, grad_w_out, grad_conv


def solution(mesh):
    placed = (P(None, "ha", "wa"), P(), P(), P(), P(), P(), P(None, "ha", "wa"))
    return jax.shard_map(
        body,
        mesh=mesh,
        in_specs=placed,
        out_specs=(P(None, "ha", "wa"), P(None, "ha", "wa"), P(), P(), P(), P(), P()),
        check_vma=False,
    )
```

```python
import jax
import jax.numpy as jnp
from jax import lax
from jax.experimental import pallas as pl
from jax.experimental.pallas import tpu as pltpu
from jax.sharding import PartitionSpec as P

BF = jnp.bfloat16
F32 = jnp.float32
EPS = 1e-06
MESH = pl.DeviceIdType.MESH

CH = 64
HC = 32
ROWS = 16
COLS = 256
LANES = 128
NA = 16
NW = 8
NEAR = 8
FAR = 16

(G_ROW0, G_PACK0, G_ROW1, G_PACK1, G_VA, G_VB, G_VC, G_VD, G_GA, G_GB, G_GC, G_GD) = range(12)
(G_E0, G_E1, G_E2, G_E3, G_E4, G_E5, G_E6, G_T1, G_T2, G_T3, G_T4, G_Q1, G_Q2) = range(12, 25)
GROUPS = 25


def dot(a, b):
    return lax.dot_general(a, b, (((1,), (0,)), ((), ())), preferred_element_type=F32)


def dot_nt(a, b):
    return lax.dot_general(a, b, (((1,), (1,)), ((), ())), preferred_element_type=F32)


def dot_tn(a, b):
    return lax.dot_general(a, b, (((0,), (0,)), ((), ())), preferred_element_type=F32)


def swap_granules(load, store, depth):
    lane = lax.broadcasted_iota(jnp.int16, (depth, LANES), 1)
    for row_half in range(2):
        for col_half in range(2):
            held = [load(row_half * 8 + k, col_half) for k in range(8)]
            for s in range(3):
                width = 16 << s
                low = (lane & width) == 0
                for k in range(8):
                    if not k & (1 << s):
                        a, b = held[k], held[k | (1 << s)]
                        held[k] = jnp.where(low, a, pltpu.roll(b, width, 1))
                        held[k | (1 << s)] = jnp.where(low, pltpu.roll(a, LANES - width, 1), b)
            for k in range(8):
                store(col_half * 8 + k, row_half, held[k])


def half(t):
    return slice(t * LANES, (t + 1) * LANES)


def loop(count, step, carry=0, unroll=1):
    return lax.fori_loop(0, count, step, carry, unroll=unroll)


def gelu_parts(x):
    root = 0.7978845608028654
    cube = root * 0.044715
    square = x * x
    h = 0.5 * jnp.tanh(x * (cube * square + root)) + 0.5
    value = x * h
    return value, h + value * (1.0 - h) * ((6.0 * cube) * square + 2.0 * root)


def kernel(
    frames_hbm, w_in_t_hbm, grid_mix_hbm, block_mix_hbm, w_out_hbm, conv_w_hbm, cot_hbm,
    rest_out, gframe_out, early_out, tail_out, value_out,
    frames, w_in_t, grid_mix, block_mix, w_out, conv_w, cot, w_in,
    turn, xb, nb, unit, inv, dgelu, gates, bval, u3, v3, gj, gg, xt, bt, bm, gbv,
    va, va_in, vx, vb, vb_in, vc, vc_in, vd, vd_in,
    ga, ga_in, gx, gb, gb_in, gc, gc_in, gd, gd_in,
    gated, gbef, jp, row_in, pack_out, pack_in, edge_l, edge_r,
    mixp, se, re0, e0, re1, e1, re2, e2, re3, e3, re4, re5, re6,
    st, rt1, t1, rt2, t2, rt3, t3, rt4, sq, rq1, q1, rq2,
    ssem, rsem, isem,
):
    ia = lax.axis_index("ha")
    iw = lax.axis_index("wa")
    up, down = lax.rem(ia + NA - 1, NA), lax.rem(ia + 1, NA)
    left, right = lax.rem(iw + NW - 1, NW), lax.rem(iw + 1, NW)
    lane = lax.broadcasted_iota(jnp.int16, (CH, LANES), 1)
    lane_wide = lax.broadcasted_iota(jnp.int32, (CH, LANES), 1)

    loads = [
        pltpu.make_async_copy(src, dst, isem.at[k])
        for k, (src, dst) in enumerate(
            [
                (cot_hbm, cot),
                (frames_hbm, frames),
                (w_in_t_hbm, w_in_t),
                (conv_w_hbm, conv_w),
                (w_out_hbm, w_out),
                (block_mix_hbm, block_mix),
                (grid_mix_hbm, grid_mix),
            ]
        )
    ]
    for load in loads:
        load.start()

    def push(src, dst, g, where):
        pltpu.make_async_remote_copy(
            src_ref=src, dst_ref=dst, send_sem=ssem.at[g], recv_sem=rsem.at[g], device_id=where, device_id_type=MESH
        ).start()

    near = lax.rem(iw, 2) * 4 + lax.rem(ia, 4)
    far = ia // 4 * 4 + iw // 2

    def near_device(peer):
        return ia // 4 * 4 + lax.rem(peer, 4), iw // 2 * 2 + peer // 4

    def far_device(peer):
        return peer // 4 * 4 + lax.rem(ia, 4), lax.rem(peer, 4) * 2 + lax.rem(iw, 2)

    near_peers = [lax.rem(near + k, NEAR) for k in range(1, NEAR)]
    far_peers = [lax.rem(far + k, FAR) for k in range(1, FAR)]
    twin = near + 1 - 2 * lax.rem(near, 2)

    def over_near(src_of, dst, g):
        for peer in near_peers:
            push(src_of(peer), dst, g, near_device(peer))

    def over_far(src_of, dst, g):
        for peer in far_peers:
            push(src_of(peer), dst, g, far_device(peer))

    def over_x(src_of, dst, g):
        for k in range(1, 4):
            peer = lax.rem(iw // 2 + k, 4)
            push(src_of(peer), dst, g, (ia, peer * 2 + lax.rem(iw, 2)))

    def over_z(src_of, dst, g):
        for k in range(1, 4):
            peer = lax.rem(ia // 4 + k, 4)
            push(src_of(peer), dst, g, (peer * 4 + lax.rem(ia, 4), iw))

    def over_y(src_of, dst, g):
        for k in range(1, 4):
            peer = lax.rem(near + 2 * k, NEAR)
            push(src_of(peer // 2), dst, g, near_device(peer))

    def arrived(ref, g):
        pltpu.make_async_copy(ref, ref, rsem.at[g]).wait()

    def gone(ref, g):
        pltpu.make_async_copy(ref, ref, ssem.at[g]).wait()

    def from_near(ref, g):
        arrived(ref.at[pl.ds(0, NEAR - 1)], g)

    def from_far(ref, g):
        arrived(ref.at[pl.ds(0, FAR - 1)], g)

    mine = lax.rem(near, 2) * 512
    level, across, deep = near // 2, iw // 2, ia // 4

    barrier = pltpu.get_barrier_semaphore()
    peers = [near_device(peer) for peer in near_peers]
    peers += [far_device(peer) for peer in far_peers]
    peers += [(a, b) for a in (up, ia, down) for b in (left, right)] + [(up, iw), (down, iw)]
    for peer in peers:
        pl.semaphore_signal(barrier, inc=1, device_id=peer, device_id_type=MESH)

    def turn_in(src):
        for t in range(2):
            turn[t] = src[:, :, half(t)].astype(F32).reshape(CH * ROWS, LANES)

    def turned(r, t):
        return turn[t, pl.ds(r, CH, stride=ROWS), :]

    def edges(pack, t0, t1, r):
        pack = jnp.where(lane_wide == r, pltpu.roll(t0, r, 1), pack)
        return jnp.where(lane_wide == ROWS + r, pltpu.roll(t1, r + 17, 1), pack)

    def send_halo(field, pack, which, g_row, g_pack):
        pack_out[which] = jnp.concatenate([pack, jnp.zeros_like(pack)], axis=0).T[0:32]
        push(field.at[1, CH : 2 * CH], row_in.at[which, 1], g_row, (up, iw))
        push(field.at[ROWS, CH : 2 * CH], row_in.at[which, 0], g_row, (down, iw))
        for slot, where in enumerate(
            [(ia, right), (down, right), (up, right), (ia, left), (down, left), (up, left)]
        ):
            part = pack_out.at[which, pl.ds(16 if slot < 3 else 0, 16)]
            push(part, pack_in.at[which, pl.ds(16 * slot, 16)], g_pack, where)

    def take_halo(field, which, g_row, g_pack):
        arrived(row_in.at[which], g_row)
        arrived(pack_in.at[which], g_pack)
        field[0, CH : 2 * CH] = jnp.where(ia > 0, row_in[which, 0], jnp.zeros((CH, COLS), BF))
        field[ROWS + 1, CH : 2 * CH] = jnp.where(ia < NA - 1, row_in[which, 1], jnp.zeros((CH, COLS), BF))
        first = jnp.where(ia > 0, 0, 1)
        last = jnp.where(ia < NA - 1, ROWS + 2, ROWS + 1)
        got = jnp.concatenate([pack_in[which], jnp.zeros((32, LANES), BF)], axis=0).T[0:CH]

        def assemble(middle, above, below, has):
            joined = jnp.where(lane == 0, above, jnp.where(lane == ROWS + 1, below, middle))
            inside = (lane_wide >= first) & (lane_wide < jnp.where(has, last, 0))
            return jnp.where(inside, joined, jnp.zeros_like(joined))

        edge_l[...] = assemble(pltpu.roll(got, 1, 1), pltpu.roll(got, 97, 1), pltpu.roll(got, 113, 1), iw > 0)
        edge_r[...] = assemble(pltpu.roll(got, 81, 1), pltpu.roll(got, 49, 1), pltpu.roll(got, 65, 1), iw < NW - 1)

        def shifts(p, carry):
            t0 = field[p, CH : 2 * CH, half(0)]
            t1 = field[p, CH : 2 * CH, half(1)]
            a0, a1 = pltpu.roll(t0, 1, 1), pltpu.roll(t1, 1, 1)
            b0, b1 = pltpu.roll(t0, LANES - 1, 1), pltpu.roll(t1, LANES - 1, 1)
            lh = pltpu.roll(edge_l[...], lax.rem(LANES - p, LANES), 1)
            rh = pltpu.roll(edge_r[...], LANES - 1 - p, 1)
            field[p, 0:CH, half(0)] = jnp.where(lane == 0, lh, a0)
            field[p, 0:CH, half(1)] = jnp.where(lane == 0, a0, a1)
            field[p, 2 * CH :, half(0)] = jnp.where(lane == LANES - 1, b1, b0)
            field[p, 2 * CH :, half(1)] = jnp.where(lane == LANES - 1, rh, b1)
            return carry

        loop(ROWS + 2, shifts, unroll=9)

    def conv_start(w, field):
        y = dot(w, field[0])
        z = dot(w, field[1])
        return z[0:CH], y[0:CH] + z[CH : 2 * CH]

    def conv_step(w, field, r, carry):
        later, now = carry
        y = dot(w, field[r + 2])
        return now + y[2 * CH :], (y[0:CH], later + y[CH : 2 * CH])

    def step_b(a_in, x, b, b_in, g_a, g_b):
        from_near(a_in, g_a)

        def widen(j, carry):
            for t in range(2):
                for r in range(2):
                    x[pl.ds((r * 16 + j * 2 + t) * HC, HC), :] = a_in[j, t, r].astype(F32)
            return carry

        loop(NEAR, widen, unroll=8)

        for peer in [*far_peers, far]:
            base = peer // 8 * (16 * HC) + lax.rem(peer, 8) * 4
            slot = b_in if peer is far else b
            for c in range(4):
                slot[peer, :, half(c)] = x[pl.ds(base + c, 16, stride=HC), :].astype(BF)
            if peer is not far:
                push(b.at[peer], b_in.at[far], g_b, far_device(peer))

    def step_c(mixed, c, c_in, g):
        c[...] = mixed.astype(BF).reshape(FAR, 16, 512)
        over_far(lambda peer: c.at[peer], c_in.at[far], g)
        c_in[far] = c[far]

    def step_d(c_in, x, d, d_in, g_c, g_d):
        from_far(c_in, g_c)

        def unpick(q, carry):
            for r in range(2):
                for c in range(4):
                    x[pl.ds((r * HC + q * 4 + c) * 16, 16), :] = c_in[r * 8 + q, :, half(c)].astype(F32)
            return carry

        loop(8, unpick, unroll=8)

        for peer in [*near_peers, near]:
            slot = d_in if peer is near else d
            for t in range(2):
                for r in range(2):
                    slot[peer, t, r] = x[pl.ds(r * HC * 16 + peer * 2 + t, HC, stride=16), :].astype(BF)
            if peer is not near:
                push(d.at[peer], d_in.at[near], g_d, near_device(peer))

    def order():
        row = lax.broadcasted_iota(jnp.int32, (COLS, COLS), 0)
        cell = lax.broadcasted_iota(jnp.int32, (COLS, COLS), 1)
        found = (row & 0xC1) | ((row & 6) << 3) | ((row & 48) >> 2) | ((row & 8) >> 2)
        return jnp.where(cell == found, 1.0, 0.0).astype(BF)

    def mix_in_order():
        swap = order()
        return dot_nt(dot(swap, grid_mix[...]).astype(BF), swap).astype(BF)

    loads[0].wait()
    turn_in(cot)

    def cot_row(r, pack):
        t0, t1 = turned(r, 0).astype(BF), turned(r, 1).astype(BF)
        u3[r + 1, CH : 2 * CH, half(0)] = t0
        u3[r + 1, CH : 2 * CH, half(1)] = t1
        return edges(pack, t0, t1, r)

    pack = loop(ROWS, cot_row, jnp.zeros((CH, LANES), BF), unroll=8)
    pl.semaphore_wait(barrier, len(peers))
    send_halo(u3, pack, 0, G_ROW0, G_PACK0)

    loads[1].wait()
    loads[2].wait()
    turn_in(frames)
    w_in[...] = w_in_t[...].astype(F32).T.astype(BF)

    def value_row(slot, peer, low):
        r = peer * 2 + low
        for t in range(2):
            x = turned(r, t)
            xb[r, :, half(t)] = x.astype(BF)
            off = x - jnp.mean(x, axis=0, keepdims=True)
            rstd = lax.rsqrt(jnp.mean(off * off, axis=0, keepdims=True) + EPS)
            u = off * rstd
            unit[r, :, half(t)] = u
            inv[r, :, half(t)] = jnp.broadcast_to(rstd, (8, LANES))
            nb[r, :, half(t)] = u.astype(BF)
        value, slope = gelu_parts(dot(w_in[HC:CH], nb[r]))
        dgelu[r, HC:CH] = slope
        value = value.astype(BF)
        slot[peer, 0, low] = value[:, half(0)]
        slot[peer, 1, low] = value[:, half(1)]

    for first in range(0, NEAR, 2):
        group = [*near_peers, near][first : first + 2]
        for peer in group:
            for low in range(2):
                value_row(va_in if peer is near else va, peer, low)
        for peer in group:
            if peer is not near:
                push(va.at[peer], va_in.at[near], G_VA, near_device(peer))

    def grid_gate_row(r, carry):
        value, slope = gelu_parts(dot(w_in[0:HC], nb[r]))
        gates[r, 0:HC] = value.astype(BF)
        dgelu[r, 0:HC] = slope
        return carry

    loop(ROWS, grid_gate_row, unroll=8)

    for load in loads[3:]:
        load.wait()
    back_w = jnp.concatenate(
        [jnp.concatenate([conv_w[2 - a, 2 - b] for a in range(3)], axis=1) for b in range(3)], axis=0
    ).astype(F32).T.astype(BF)
    w_out_t = w_out[...].astype(F32).T.astype(BF)
    take_halo(u3, 0, G_ROW0, G_PACK0)

    def back_row(r, carry):
        total, carry = conv_step(back_w, u3, r, carry)
        g = (total + u3[r + 1, CH : 2 * CH].astype(F32)).astype(BF)
        gj[r] = g
        up_gated = dot(w_out_t, g)
        gg[r] = up_gated
        mixed = (up_gated[0:HC] * gates[r, 0:HC].astype(F32)).astype(BF)
        ga[r // 2, 0, r % 2] = mixed[:, half(0)]
        ga[r // 2, 1, r % 2] = mixed[:, half(1)]
        return carry

    carry = conv_start(back_w, u3)
    for first in range(0, NEAR, 2):
        for r in range(2 * first, 2 * first + 4):
            carry = back_row(r, carry)
        for peer in (first, first + 1):

            @pl.when(peer != near)
            def _():
                push(ga.at[peer], ga_in.at[near], G_GA, near_device(peer))

    ga_in[near] = ga[near]

    step_b(va_in, vx, vb, vb_in, G_VA, G_VB)

    def block_gate_row(r, carry):
        value, slope = gelu_parts(dot(w_in[CH:], nb[r]))
        dgelu[r, CH:] = slope
        value = value.astype(BF)
        gates[r, HC:CH] = value[0:HC]
        bval[r] = value[HC:]
        return carry

    loop(ROWS, block_gate_row, unroll=8)
    mixp[...] = mix_in_order()

    def put(ref):
        def store(k, t, value):
            ref[k, :, half(t)] = value

        return store

    swap_granules(lambda k, t: bval[k, :, half(t)], put(xt), HC)
    values = xt[...].reshape(ROWS * HC, COLS)
    mixed = dot_nt(values, block_mix[...]).astype(BF)
    swap_granules(lambda k, t: mixed[k * HC : (k + 1) * HC, half(t)], put(bm), HC)

    step_b(ga_in, gx, gb, gb_in, G_GA, G_GB)
    from_far(vb_in, G_VB)
    step_c(dot(mixp[...], vb_in[...].reshape(256, 512)), vc, vc_in, G_VC)

    def block_back(k, t):
        return (gg[k, HC:, half(t)] * gates[k, HC:, half(t)].astype(F32)).astype(BF)

    swap_granules(block_back, put(bt), HC)
    backs = bt[...].reshape(ROWS * HC, COLS)
    unmixed = dot(backs, block_mix[...]).astype(BF)
    swap_granules(lambda k, t: unmixed[k * HC : (k + 1) * HC, half(t)], put(gbv), HC)
    part_block = dot_tn(backs, values).astype(BF)
    se[2 * COLS : 3 * COLS] = part_block[:, half(0)]
    se[3 * COLS :] = part_block[:, half(1)]

    def block_before_row(r, carry):
        d = dgelu[r, CH:]
        gbef[r, CH : CH + HC] = (d[0:HC] * (gg[r, HC:] * (bm[r].astype(F32) + 1.0))).astype(BF)
        gbef[r, CH + HC :] = (d[HC:] * gbv[r].astype(F32)).astype(BF)
        gbef[r, HC:CH] = jnp.zeros((HC, COLS), BF)
        return carry

    loop(ROWS, block_before_row, unroll=4)
    for k in (0, 1, ROWS + 2, ROWS + 3):
        jp[k] = jnp.zeros((CH, COLS), BF)

    from_far(gb_in, G_GB)
    back = gb_in[...].reshape(256, 512)
    step_c(dot_tn(mixp[...], back), gc, gc_in, G_GC)
    step_d(vc_in, vx, vd, vd_in, G_VC, G_VD)

    part_grid = dot_nt(back, vb_in[...].reshape(256, 512)).astype(BF)
    part_grid = dot(dot_tn(order(), part_grid).astype(BF), order()).astype(BF)
    se[0:COLS] = part_grid[:, half(0)]
    se[COLS : 2 * COLS] = part_grid[:, half(1)]
    push(se.at[pl.ds(pl.multiple_of(512 - mine, 512), 512)], re0, G_E0, near_device(twin))

    step_d(gc_in, gx, gd, gd_in, G_GC, G_GD)

    from_near(vd_in, G_VD)

    def returned(ref, r):
        return [ref[r // 2, t, lax.rem(r, 2)].astype(F32) for t in range(2)]

    def joined_row(r, pack):
        grid_mixed = returned(vd_in, r)
        for t in range(2):
            gates_t = gates[r, :, half(t)].astype(F32)
            gated[r, 0:HC, half(t)] = (gates_t[0:HC] * (grid_mixed[t] + 1.0)).astype(BF)
            gated[r, HC:, half(t)] = (gates_t[HC:] * (bm[r, :, half(t)].astype(F32) + 1.0)).astype(BF)
        j = (xb[r].astype(F32) + dot(w_out[...], gated[r])).astype(BF)
        jp[r + 2] = j
        v3[r + 1, CH : 2 * CH] = j
        return edges(pack, j[:, half(0)], j[:, half(1)], r)

    pack = loop(ROWS, joined_row, jnp.zeros((CH, LANES), BF), unroll=8)
    send_halo(v3, pack, 1, G_ROW1, G_PACK1)

    arrived(re0, G_E0)
    e0[...] = (se[pl.ds(pl.multiple_of(mine, 512), 512)].astype(F32) + re0[...].astype(F32)).astype(BF)
    over_y(lambda peer: e0.at[pl.ds(pl.multiple_of(peer * 128, 128), 128)], re1.at[level], G_E1)
    re1[level] = e0[pl.ds(pl.multiple_of(level * 128, 128), 128)]

    def conv_row(p, total):
        return total + dot_nt(u3[p], jp[pl.ds(p, 3)].reshape(3 * CH, COLS))

    p_conv = loop(ROWS + 2, conv_row, jnp.zeros((3 * CH, 3 * CH), F32), unroll=9)

    def gate_before_row(r, carry):
        p_in, p_out = carry
        grid_mixed = returned(vd_in, r)
        for t in range(2):
            slope = dgelu[r, 0:HC, half(t)]
            gbef[r, 0:HC, half(t)] = (slope * (gg[r, 0:HC, half(t)] * (grid_mixed[t] + 1.0))).astype(BF)
        return p_in + dot_nt(nb[r], gbef[r]), p_out + dot_nt(gj[r], gated[r])

    p_in, p_out = loop(
        ROWS, gate_before_row, (jnp.zeros((CH, 2 * CH), F32), jnp.zeros((CH, CH), F32)), unroll=4
    )
    st[0 : 3 * CH] = p_conv[:, half(0)].astype(BF)
    st[3 * CH : 4 * CH] = p_in.astype(BF)
    third = p_conv[:, 2 * CH :]
    st[4 * CH :] = jnp.concatenate(
        [third[: 2 * CH], jnp.concatenate([third[2 * CH :], p_out], axis=0)], axis=1
    ).astype(BF)
    over_near(lambda peer: st.at[pl.ds(pl.multiple_of(peer * 48, 16), 48)], rt1.at[near], G_T1)
    rt1[near] = st[pl.ds(pl.multiple_of(near * 48, 16), 48)]

    from_near(gd_in, G_GD)

    def value_before_row(r, total):
        grid_back = returned(gd_in, r)
        for t in range(2):
            gbef[r, HC:CH, half(t)] = (dgelu[r, HC:CH, half(t)] * grid_back[t]).astype(BF)
        return total + dot_nt(gbef[r, HC:CH], nb[r])

    p_value = loop(ROWS, value_before_row, jnp.zeros((HC, CH), F32), unroll=4)
    sq[...] = jnp.concatenate([p_value[0:16], p_value[16:]], axis=1).astype(BF)
    over_near(lambda peer: sq, rq1.at[near], G_Q1)
    rq1[near] = sq[...]

    arrived(re1.at[pl.ds(0, 3)], G_E1)
    total = re1[0].astype(F32)
    for k in range(1, 4):
        total = total + re1[k].astype(F32)
    e1[...] = total
    over_x(lambda peer: e1.at[pl.ds(pl.multiple_of(peer * 32, 32), 32)], re2.at[across], G_E2)
    re2[across] = e1[pl.ds(pl.multiple_of(across * 32, 32), 32)]

    def frame_row(r, carry):
        normed = dot(w_in_t[...], gbef[r])
        u = unit[r]
        mean_grad = jnp.mean(normed, axis=0, keepdims=True)
        mean_proj = jnp.mean(normed * u, axis=0, keepdims=True)
        source = gj[r].astype(F32) + inv[r, 0:1] * (normed - mean_grad - u * mean_proj)
        for t in range(2):
            gframe_out[t, pl.ds(r * CH, CH), :] = source[:, half(t)]
        return carry

    loop(ROWS, frame_row, unroll=8)

    from_near(rt1, G_T1)
    total = rt1[0].astype(F32)
    for k in range(1, NEAR):
        total = total + rt1[k].astype(F32)
    t1[...] = total.astype(BF)
    over_x(lambda peer: t1, rt2.at[across], G_T2)
    rt2[across] = t1[...]

    from_near(rq1, G_Q1)
    total = rq1[0].astype(F32)
    for k in range(1, NEAR):
        total = total + rq1[k].astype(F32)
    q1[...] = total.astype(BF)
    over_far(lambda peer: q1, rq2.at[far], G_Q2)
    rq2[far] = q1[...]

    arrived(re2.at[pl.ds(0, 3)], G_E2)
    e2[...] = re2[0] + re2[1] + re2[2] + re2[3]
    over_z(lambda peer: e2, re3.at[deep], G_E3)
    re3[deep] = e2[...]

    take_halo(v3, 1, G_ROW1, G_PACK1)

    arrived(rt2.at[pl.ds(0, 3)], G_T2)
    total = rt2[0].astype(F32)
    for k in range(1, 4):
        total = total + rt2[k].astype(F32)
    t2[...] = total.astype(BF)
    over_z(lambda peer: t2, rt3.at[deep], G_T3)
    rt3[deep] = t2[...]

    arrived(re3.at[pl.ds(0, 3)], G_E3)
    e3[...] = (re3[0] + re3[1] + re3[2] + re3[3]).astype(BF)
    over_x(lambda peer: e3, re4.at[across], G_E4)
    re4[across] = e3[...]

    conv_k = jnp.concatenate(
        [jnp.concatenate([conv_w[a, b] for b in range(3)], axis=1) for a in range(3)], axis=0
    )

    def out_row(r, carry):
        total, carry = conv_step(conv_k, v3, r, carry)
        total = total + v3[r + 1, CH : 2 * CH].astype(F32)
        for t in range(2):
            rest_out[t, pl.ds(r * CH, CH), :] = total[:, half(t)]
        return carry

    carry = loop(ROWS // 2, out_row, conv_start(conv_k, v3), unroll=8)

    arrived(re4.at[pl.ds(0, 3)], G_E4)
    over_y(lambda peer: re4, re5.at[level], G_E5)
    re5[level] = re4[...]
    arrived(rt3.at[pl.ds(0, 3)], G_T3)
    total = rt3[0].astype(F32)
    for k in range(1, 4):
        total = total + rt3[k].astype(F32)
    t3[...] = total.astype(BF)
    over_near(lambda peer: t3, rt4.at[near], G_T4)
    rt4[near] = t3[...]

    loop(ROWS // 2, lambda r, carry: out_row(r + ROWS // 2, carry), carry, unroll=8)

    arrived(re5.at[pl.ds(0, 3)], G_E5)
    push(re5, re6, G_E6, near_device(twin))
    early_out[pl.ds(pl.multiple_of(mine, 512), 512)] = re5[...].reshape(512, LANES)

    from_far(rq2, G_Q2)
    total = rq2[0].astype(F32)
    for k in range(1, FAR):
        total = total + rq2[k].astype(F32)
    value_out[...] = total
    from_near(rt4, G_T4)
    tail_out[...] = rt4[...]
    arrived(re6, G_E6)
    early_out[pl.ds(pl.multiple_of(512 - mine, 512), 512)] = re6[...].reshape(512, LANES)

    for which, g_row, g_pack in ((0, G_ROW0, G_PACK0), (1, G_ROW1, G_PACK1)):
        gone(row_in.at[which], g_row)
        gone(pack_in.at[which], g_pack)
    for ref, g in (
        (va_in, G_VA), (vd_in, G_VD), (ga_in, G_GA), (gd_in, G_GD),
        (rt1, G_T1), (rt4, G_T4), (rq1, G_Q1),
    ):
        gone(ref.at[pl.ds(0, NEAR - 1)], g)
    for ref, g in (
        (vb_in, G_VB), (vc_in, G_VC), (gb_in, G_GB), (gc_in, G_GC), (rq2, G_Q2),
    ):
        gone(ref.at[pl.ds(0, FAR - 1)], g)
    gone(re0, G_E0)
    for ref, g in ((re1, G_E1), (re2, G_E2), (re3, G_E3), (re4, G_E4), (re5, G_E5), (rt2, G_T2), (rt3, G_T3)):
        gone(ref.at[pl.ds(0, 3)], g)
    gone(re6, G_E6)


def finish(
    rest, gframe, early, tail, value,
    restored, grad_frames, grad_w_in_t, grad_grid, grad_block, grad_w_out, grad_conv,
):
    scale = float(ROWS * NA * COLS * NW) ** (-0.5)

    def channel(c, carry):
        for src, dst in ((rest, restored), (gframe, grad_frames)):
            for t in range(2):
                dst[c, :, half(t)] = src[t, pl.ds(c, ROWS, stride=CH), :].astype(BF)
        return carry

    loop(CH, channel, unroll=8)

    for k in range(2):
        grad_grid[:, half(k)] = early[k * COLS : (k + 1) * COLS].astype(F32) * scale
        grad_block[:, half(k)] = early[(2 + k) * COLS : (3 + k) * COLS].astype(F32) * scale
    quarter = value[...] * scale
    zeros = jnp.zeros((HC, CH), F32)
    quarter = jnp.concatenate([zeros, quarter[:, :CH], quarter[:, CH:], zeros, zeros], axis=0)
    grad_w_in_t[...] = tail[3 * CH : 4 * CH].astype(F32) * scale + quarter.T
    last = tail[4 * CH :].astype(F32) * scale
    grad_w_out[...] = last[CH:, CH:]
    for b in range(3):
        rows = slice((2 - b) * CH, (3 - b) * CH)
        pair = tail[rows].astype(F32) * scale
        grad_conv[0, b] = pair[:, :CH]
        grad_conv[1, b] = pair[:, CH:]
    grad_conv[2, 2] = last[:CH, :CH]
    grad_conv[2, 1] = last[CH:, :CH]
    grad_conv[2, 0] = last[:CH, CH:]


def vm(*shape, dtype=BF):
    return pltpu.VMEM(shape, dtype)


def exchange():
    message_w = vm(NW, 2, 2, HC, LANES)
    message_a = vm(NA, 16, 512)
    return [message_w, message_w, vm(2 * 16 * HC, LANES, dtype=F32)] + [message_a] * 4 + [message_w] * 2


SCRATCH = [
    vm(CH, ROWS, COLS),
    vm(CH, 2 * CH),
    vm(COLS, COLS),
    vm(COLS, COLS),
    vm(CH, CH),
    vm(3, 3, CH, CH),
    vm(CH, ROWS, COLS),
    vm(2 * CH, CH),
    vm(2, CH * ROWS, LANES, dtype=F32),
    vm(ROWS, CH, COLS),
    vm(ROWS, CH, COLS),
    vm(ROWS, CH, COLS, dtype=F32),
    vm(ROWS, 8, COLS, dtype=F32),
    vm(ROWS, 2 * CH, COLS, dtype=F32),
    vm(ROWS, CH, COLS),
    vm(ROWS, HC, COLS),
    vm(ROWS + 2, 3 * CH, COLS),
    vm(ROWS + 2, 3 * CH, COLS),
    vm(ROWS, CH, COLS),
    vm(ROWS, CH, COLS, dtype=F32),
    vm(ROWS, HC, COLS),
    vm(ROWS, HC, COLS),
    vm(ROWS, HC, COLS),
    vm(ROWS, HC, COLS),
    *exchange(),
    *exchange(),
    vm(ROWS, CH, COLS),
    vm(ROWS, 2 * CH, COLS),
    vm(ROWS + 4, CH, COLS),
    vm(2, 2, CH, COLS),
    vm(2, 32, LANES),
    vm(2, 96, LANES),
    vm(CH, LANES),
    vm(CH, LANES),
    vm(COLS, COLS),
    vm(4 * COLS, LANES),
    vm(512, LANES),
    vm(512, LANES),
    vm(4, 128, LANES),
    vm(128, LANES, dtype=F32),
    vm(4, 32, LANES, dtype=F32),
    vm(32, LANES, dtype=F32),
    vm(4, 32, LANES, dtype=F32),
    vm(32, LANES),
    vm(4, 32, LANES),
    vm(4, 4, 32, LANES),
    vm(4, 4, 32, LANES),
    vm(6 * CH, LANES),
    vm(NW, 48, LANES),
    vm(48, LANES),
    vm(4, 48, LANES),
    vm(48, LANES),
    vm(4, 48, LANES),
    vm(48, LANES),
    vm(NEAR, 48, LANES),
    vm(16, LANES),
    vm(NEAR, 16, LANES),
    vm(16, LANES),
    vm(FAR, 16, LANES),
    pltpu.SemaphoreType.DMA((GROUPS,)),
    pltpu.SemaphoreType.DMA((GROUPS,)),
    pltpu.SemaphoreType.DMA((7,)),
]


def body(frames, w_in, grid_mix, block_mix, w_out, conv_w, cotangent):
    operands = (frames, w_in.T, grid_mix, block_mix, w_out, conv_w, cotangent)
    vmem = pl.BlockSpec(memory_space=pltpu.VMEM)
    shape = jax.ShapeDtypeStruct
    rest, gframe, early, tail, value = pl.pallas_call(
        kernel,
        out_shape=(
            shape((2, ROWS * CH, LANES), F32),
            shape((2, ROWS * CH, LANES), F32),
            shape((4 * COLS, LANES), BF),
            shape((NEAR, 48, LANES), BF),
            shape((16, LANES), F32),
        ),
        in_specs=[pl.BlockSpec(memory_space=pltpu.HBM)] * 7,
        out_specs=(vmem,) * 5,
        scratch_shapes=SCRATCH,
        compiler_params=pltpu.CompilerParams(
            collective_id=0, has_side_effects=True, vmem_limit_bytes=32 * 1024 * 1024
        ),
    )(*[pltpu.with_memory_space_constraint(x, pltpu.HBM) for x in operands])
    restored, grad_frames, grad_w_in_t, grad_grid, grad_block, grad_w_out, grad_conv = pl.pallas_call(
        finish,
        out_shape=(
            shape((CH, ROWS, COLS), BF),
            shape((CH, ROWS, COLS), BF),
            shape((CH, 2 * CH), F32),
            shape((COLS, COLS), F32),
            shape((COLS, COLS), F32),
            shape((CH, CH), F32),
            shape((3, 3, CH, CH), F32),
        ),
        in_specs=[vmem] * 5,
        out_specs=(vmem,) * 7,
        compiler_params=pltpu.CompilerParams(vmem_limit_bytes=16 * 1024 * 1024),
    )(rest, gframe, early, tail.reshape(6 * CH, LANES), value)
    return restored, grad_frames, grad_w_in_t.T, grad_grid, grad_block, grad_w_out, grad_conv


def solution(mesh):
    placed = (P(None, "ha", "wa"), P(), P(), P(), P(), P(), P(None, "ha", "wa"))
    return jax.shard_map(
        body,
        mesh=mesh,
        in_specs=placed,
        out_specs=(P(None, "ha", "wa"), P(None, "ha", "wa"), P(), P(), P(), P(), P()),
        check_vma=False,
    )
```

```python
import jax
import jax.numpy as jnp
from jax import lax
from jax.experimental import pallas as pl
from jax.experimental.pallas import tpu as pltpu
from jax.sharding import PartitionSpec as P

BF = jnp.bfloat16
F32 = jnp.float32
EPS = 1e-06
MESH = pl.DeviceIdType.MESH

CH = 64
HC = 32
ROWS = 16
COLS = 256
LANES = 128
NA = 16
NW = 8
NEAR = 8
FAR = 16

(G_ROW0, G_PACK0, G_ROW1, G_PACK1) = range(4)
(G_E0, G_E1, G_E2, G_E3, G_E4, G_E5, G_E6, G_T1, G_T2, G_T3, G_T4, G_Q1, G_Q2) = range(4, 17)
VALUES, BACKS = (0, 1), (2, 3)
G_A, G_B, G_C, G_D = 17, 21, 25, 29
GROUPS = 33
QC = 16


def dot(a, b):
    return lax.dot_general(a, b, (((1,), (0,)), ((), ())), preferred_element_type=F32)


def dot_nt(a, b):
    return lax.dot_general(a, b, (((1,), (1,)), ((), ())), preferred_element_type=F32)


def dot_tn(a, b):
    return lax.dot_general(a, b, (((0,), (0,)), ((), ())), preferred_element_type=F32)


def swap_granules(load, store, depth):
    lane = lax.broadcasted_iota(jnp.int16, (depth, LANES), 1)
    for row_half in range(2):
        for col_half in range(2):
            held = [load(row_half * 8 + k, col_half) for k in range(8)]
            for s in range(3):
                width = 16 << s
                low = (lane & width) == 0
                for k in range(8):
                    if not k & (1 << s):
                        a, b = held[k], held[k | (1 << s)]
                        held[k] = jnp.where(low, a, pltpu.roll(b, width, 1))
                        held[k | (1 << s)] = jnp.where(low, pltpu.roll(a, LANES - width, 1), b)
            for k in range(8):
                store(col_half * 8 + k, row_half, held[k])


def half(t):
    return slice(t * LANES, (t + 1) * LANES)


def loop(count, step, carry=0, unroll=1):
    return lax.fori_loop(0, count, step, carry, unroll=unroll)


def gelu_parts(x):
    root = 0.7978845608028654
    cube = root * 0.044715
    square = x * x
    h = 0.5 * jnp.tanh(x * (cube * square + root)) + 0.5
    value = x * h
    return value, h + value * (1.0 - h) * ((6.0 * cube) * square + 2.0 * root)


def kernel(
    frames_hbm, w_in_t_hbm, grid_mix_hbm, block_mix_hbm, w_out_hbm, conv_w_hbm, cot_hbm,
    rest_out, gframe_out, early_out, tail_out, value_out,
    frames, w_in_t, grid_mix, block_mix, w_out, conv_w, cot, w_in,
    turn, xb, nb, unit, inv, dgelu, gates, bval, u3, v3, gj, gg, xt, bt, bm, gbv,
    a, a_in, x32, b, b_in, c, c_in, d, d_in,
    gated, gbef, jp, row_in, pack_out, pack_in, edge_l, edge_r,
    mixp, mixp_t, gather, spread, se, re0, e0, re1, e1, re2, e2, re3, e3, re4, re5, re6,
    st, rt1, t1, rt2, t2, rt3, t3, rt4, sq, rq1, q1, rq2,
    ssem, rsem, isem,
):
    ia = lax.axis_index("ha")
    iw = lax.axis_index("wa")
    up, down = lax.rem(ia + NA - 1, NA), lax.rem(ia + 1, NA)
    left, right = lax.rem(iw + NW - 1, NW), lax.rem(iw + 1, NW)
    lane = lax.broadcasted_iota(jnp.int16, (CH, LANES), 1)
    lane_wide = lax.broadcasted_iota(jnp.int32, (CH, LANES), 1)

    loads = [
        pltpu.make_async_copy(src, dst, isem.at[k])
        for k, (src, dst) in enumerate(
            [
                (cot_hbm, cot),
                (frames_hbm, frames),
                (w_in_t_hbm, w_in_t),
                (conv_w_hbm, conv_w),
                (w_out_hbm, w_out),
                (block_mix_hbm, block_mix),
                (grid_mix_hbm, grid_mix),
            ]
        )
    ]
    for load in loads:
        load.start()

    def push(src, dst, g, where):
        pltpu.make_async_remote_copy(
            src_ref=src, dst_ref=dst, send_sem=ssem.at[g], recv_sem=rsem.at[g], device_id=where, device_id_type=MESH
        ).start()

    near = lax.rem(iw, 2) * 4 + lax.rem(ia, 4)
    far = ia // 4 * 4 + iw // 2

    def near_device(peer):
        return ia // 4 * 4 + lax.rem(peer, 4), iw // 2 * 2 + peer // 4

    def far_device(peer):
        return peer // 4 * 4 + lax.rem(ia, 4), lax.rem(peer, 4) * 2 + lax.rem(iw, 2)

    near_peers = [lax.rem(near + k, NEAR) for k in range(1, NEAR)]
    far_peers = [lax.rem(far + k, FAR) for k in range(1, FAR)]
    twin = near + 1 - 2 * lax.rem(near, 2)

    def over_near(src_of, dst, g):
        for peer in near_peers:
            push(src_of(peer), dst, g, near_device(peer))

    def over_far(src_of, dst, g):
        for peer in far_peers:
            push(src_of(peer), dst, g, far_device(peer))

    def over_x(src_of, dst, g):
        for k in range(1, 4):
            peer = lax.rem(iw // 2 + k, 4)
            push(src_of(peer), dst, g, (ia, peer * 2 + lax.rem(iw, 2)))

    def over_z(src_of, dst, g):
        for k in range(1, 4):
            peer = lax.rem(ia // 4 + k, 4)
            push(src_of(peer), dst, g, (peer * 4 + lax.rem(ia, 4), iw))

    def over_y(src_of, dst, g):
        for k in range(1, 4):
            peer = lax.rem(near + 2 * k, NEAR)
            push(src_of(peer // 2), dst, g, near_device(peer))

    def arrived(ref, g):
        pltpu.make_async_copy(ref, ref, rsem.at[g]).wait()

    def gone(ref, g):
        pltpu.make_async_copy(ref, ref, ssem.at[g]).wait()

    def from_near(ref, g):
        arrived(ref.at[pl.ds(0, NEAR - 1)], g)

    def from_far(ref, g):
        arrived(ref.at[pl.ds(0, FAR - 1)], g)

    mine = lax.rem(near, 2) * 512
    level, across, deep = near // 2, iw // 2, ia // 4

    barrier = pltpu.get_barrier_semaphore()
    peers = [near_device(peer) for peer in near_peers]
    peers += [far_device(peer) for peer in far_peers]
    peers += [(a, b) for a in (up, ia, down) for b in (left, right)] + [(up, iw), (down, iw)]
    for peer in peers:
        pl.semaphore_signal(barrier, inc=1, device_id=peer, device_id_type=MESH)

    def turn_in(src):
        for t in range(2):
            turn[t] = src[:, :, half(t)].astype(F32).reshape(CH * ROWS, LANES)

    def turned(r, t):
        return turn[t, pl.ds(r, CH, stride=ROWS), :]

    def edges(pack, t0, t1, r):
        pack = jnp.where(lane_wide == r, pltpu.roll(t0, r, 1), pack)
        return jnp.where(lane_wide == ROWS + r, pltpu.roll(t1, r + 17, 1), pack)

    def send_halo(field, pack, which, g_row, g_pack):
        pack_out[which] = jnp.concatenate([pack, jnp.zeros_like(pack)], axis=0).T[0:32]
        push(field.at[1, CH : 2 * CH], row_in.at[which, 1], g_row, (up, iw))
        push(field.at[ROWS, CH : 2 * CH], row_in.at[which, 0], g_row, (down, iw))
        for slot, where in enumerate(
            [(ia, right), (down, right), (up, right), (ia, left), (down, left), (up, left)]
        ):
            part = pack_out.at[which, pl.ds(16 if slot < 3 else 0, 16)]
            push(part, pack_in.at[which, pl.ds(16 * slot, 16)], g_pack, where)

    def take_halo(field, which, g_row, g_pack):
        arrived(row_in.at[which], g_row)
        arrived(pack_in.at[which], g_pack)
        field[0, CH : 2 * CH] = jnp.where(ia > 0, row_in[which, 0], jnp.zeros((CH, COLS), BF))
        field[ROWS + 1, CH : 2 * CH] = jnp.where(ia < NA - 1, row_in[which, 1], jnp.zeros((CH, COLS), BF))
        first = jnp.where(ia > 0, 0, 1)
        last = jnp.where(ia < NA - 1, ROWS + 2, ROWS + 1)
        got = jnp.concatenate([pack_in[which], jnp.zeros((32, LANES), BF)], axis=0).T[0:CH]

        def assemble(middle, above, below, has):
            joined = jnp.where(lane == 0, above, jnp.where(lane == ROWS + 1, below, middle))
            inside = (lane_wide >= first) & (lane_wide < jnp.where(has, last, 0))
            return jnp.where(inside, joined, jnp.zeros_like(joined))

        edge_l[...] = assemble(pltpu.roll(got, 1, 1), pltpu.roll(got, 97, 1), pltpu.roll(got, 113, 1), iw > 0)
        edge_r[...] = assemble(pltpu.roll(got, 81, 1), pltpu.roll(got, 49, 1), pltpu.roll(got, 65, 1), iw < NW - 1)

        def shifts(p, carry):
            t0 = field[p, CH : 2 * CH, half(0)]
            t1 = field[p, CH : 2 * CH, half(1)]
            a0, a1 = pltpu.roll(t0, 1, 1), pltpu.roll(t1, 1, 1)
            b0, b1 = pltpu.roll(t0, LANES - 1, 1), pltpu.roll(t1, LANES - 1, 1)
            lh = pltpu.roll(edge_l[...], lax.rem(LANES - p, LANES), 1)
            rh = pltpu.roll(edge_r[...], LANES - 1 - p, 1)
            field[p, 0:CH, half(0)] = jnp.where(lane == 0, lh, a0)
            field[p, 0:CH, half(1)] = jnp.where(lane == 0, a0, a1)
            field[p, 2 * CH :, half(0)] = jnp.where(lane == LANES - 1, b1, b0)
            field[p, 2 * CH :, half(1)] = jnp.where(lane == LANES - 1, rh, b1)
            return carry

        loop(ROWS + 2, shifts, unroll=9)

    def conv_start(w, field):
        y = dot(w, field[0])
        z = dot(w, field[1])
        return z[0:CH], y[0:CH] + z[CH : 2 * CH]

    def conv_step(w, field, r, carry):
        later, now = carry
        y = dot(w, field[r + 2])
        return now + y[2 * CH :], (y[0:CH], later + y[CH : 2 * CH])

    def step_a(n):
        over_near(lambda peer: a.at[n, peer], a_in.at[n, near], G_A + n)

    def step_b(n):
        arrived(a_in.at[n, pl.ds(0, NEAR - 1)], G_A + n)

        def widen(j, carry):
            for t in range(2):
                for r in range(2):
                    x32[n, pl.ds((r * 16 + j * 2 + t) * QC, QC), :] = a_in[n, j, t, r].astype(F32)
            return carry

        loop(NEAR, widen, unroll=8)

        for peer in [*far_peers, far]:
            base = peer // 8 * (16 * QC) + lax.rem(peer, 8) * 2
            slot = b_in if peer is far else b
            for k in range(2):
                slot[n, peer, :, half(k)] = x32[n, pl.ds(base + k, 16, stride=QC), :].astype(BF)
            if peer is not far:
                push(b.at[n, peer], b_in.at[n, far], G_B + n, far_device(peer))

    def table(n):
        return b_in[n].reshape(256, 256)

    def step_c(n, mix):
        arrived(b_in.at[n, pl.ds(0, FAR - 1)], G_B + n)
        c[n] = dot(mix[...], table(n)).astype(BF).reshape(FAR, 16, 256)
        over_far(lambda peer: c.at[n, peer], c_in.at[n, far], G_C + n)
        c_in[n, far] = c[n, far]

    def step_d(n):
        arrived(c_in.at[n, pl.ds(0, FAR - 1)], G_C + n)

        def unpick(q, carry):
            for r in range(2):
                for k in range(2):
                    x32[n, pl.ds((r * QC + q * 2 + k) * 16, 16), :] = c_in[n, r * 8 + q, :, half(k)].astype(F32)
            return carry

        loop(8, unpick, unroll=8)

        for peer in [*near_peers, near]:
            slot = d_in if peer is near else d
            for t in range(2):
                for r in range(2):
                    slot[n, peer, t, r] = x32[n, pl.ds(r * QC * 16 + peer * 2 + t, QC, stride=16), :].astype(BF)
            if peer is not near:
                push(d.at[n, peer], d_in.at[n, near], G_D + n, near_device(peer))

    def step_e(n):
        arrived(d_in.at[n, pl.ds(0, NEAR - 1)], G_D + n)

    def order(cell, row):
        found = (row & 0xC1) | ((row & 6) << 3) | ((row & 48) >> 2) | ((row & 8) >> 2)
        return jnp.where(cell == found, 1.0, 0.0).astype(BF)

    loads[0].wait()
    turn_in(cot)

    def cot_row(r, pack):
        t0, t1 = turned(r, 0).astype(BF), turned(r, 1).astype(BF)
        u3[r + 1, CH : 2 * CH, half(0)] = t0
        u3[r + 1, CH : 2 * CH, half(1)] = t1
        return edges(pack, t0, t1, r)

    pack = loop(ROWS, cot_row, jnp.zeros((CH, LANES), BF), unroll=8)
    pl.semaphore_wait(barrier, len(peers))
    send_halo(u3, pack, 0, G_ROW0, G_PACK0)

    loads[1].wait()
    loads[2].wait()
    turn_in(frames)
    w_in[...] = w_in_t[...].astype(F32).T.astype(BF)

    def value_row(slot, peer, low):
        r = peer * 2 + low
        for t in range(2):
            x = turned(r, t)
            xb[r, :, half(t)] = x.astype(BF)
            off = x - jnp.mean(x, axis=0, keepdims=True)
            rstd = lax.rsqrt(jnp.mean(off * off, axis=0, keepdims=True) + EPS)
            u = off * rstd
            unit[r, :, half(t)] = u
            inv[r, :, half(t)] = jnp.broadcast_to(rstd, (8, LANES))
            nb[r, :, half(t)] = u.astype(BF)
        value, slope = gelu_parts(dot(w_in[HC:CH], nb[r]))
        dgelu[r, HC:CH] = slope
        value = value.astype(BF)
        for n in VALUES:
            for t in range(2):
                slot[n, peer, t, low] = value[n * QC : (n + 1) * QC, half(t)]

    for first in range(0, NEAR, 2):
        group = [*near_peers, near][first : first + 2]
        for peer in group:
            for low in range(2):
                value_row(a_in if peer is near else a, peer, low)
        for peer in group:
            if peer is not near:
                push(a.at[0, peer], a_in.at[0, near], G_A, near_device(peer))
    step_a(1)

    def grid_gate_row(r, carry):
        value, slope = gelu_parts(dot(w_in[0:HC], nb[r]))
        gates[r, 0:HC] = value.astype(BF)
        dgelu[r, 0:HC] = slope
        return carry

    loop(ROWS, grid_gate_row, unroll=8)

    for load in loads[3:]:
        load.wait()
    back_w = jnp.concatenate(
        [jnp.concatenate([conv_w[2 - a, 2 - b] for a in range(3)], axis=1) for b in range(3)], axis=0
    ).astype(F32).T.astype(BF)
    w_out_t = w_out[...].astype(F32).T.astype(BF)
    take_halo(u3, 0, G_ROW0, G_PACK0)

    def back_row(r, carry):
        total, carry = conv_step(back_w, u3, r, carry)
        g = (total + u3[r + 1, CH : 2 * CH].astype(F32)).astype(BF)
        gj[r] = g
        up_gated = dot(w_out_t, g)
        gg[r] = up_gated
        mixed = (up_gated[0:HC] * gates[r, 0:HC].astype(F32)).astype(BF)
        for n in range(2):
            for t in range(2):
                a[2 + n, r // 2, t, r % 2] = mixed[n * QC : (n + 1) * QC, half(t)]
        return carry

    carry = conv_start(back_w, u3)
    for first in range(0, NEAR, 2):
        for r in range(2 * first, 2 * first + 4):
            carry = back_row(r, carry)
        for peer in (first, first + 1):

            @pl.when(peer != near)
            def _():
                push(a.at[2, peer], a_in.at[2, near], G_A + 2, near_device(peer))

    step_a(3)
    for n in BACKS:
        a_in[n, near] = a[n, near]
    step_b(0)
    step_b(1)

    def block_gate_row(r, carry):
        value, slope = gelu_parts(dot(w_in[CH:], nb[r]))
        dgelu[r, CH:] = slope
        value = value.astype(BF)
        gates[r, HC:CH] = value[0:HC]
        bval[r] = value[HC:]
        return carry

    loop(ROWS, block_gate_row, unroll=8)
    down_axis = lax.broadcasted_iota(jnp.int32, (COLS, COLS), 0)
    along_axis = lax.broadcasted_iota(jnp.int32, (COLS, COLS), 1)
    gather[...] = order(along_axis, down_axis)
    spread[...] = order(down_axis, along_axis)
    mixp[...] = dot(dot(gather[...], grid_mix[...]).astype(BF), spread[...]).astype(BF)
    mixp_t[...] = dot(dot_nt(gather[...], grid_mix[...]).astype(BF), spread[...]).astype(BF)
    step_c(0, mixp)

    def put(ref):
        def store(k, t, value):
            ref[k, :, half(t)] = value

        return store

    swap_granules(lambda k, t: bval[k, :, half(t)], put(xt), HC)
    values = xt[...].reshape(ROWS * HC, COLS)
    mixed = dot_nt(values, block_mix[...]).astype(BF)
    swap_granules(lambda k, t: mixed[k * HC : (k + 1) * HC, half(t)], put(bm), HC)

    step_c(1, mixp)
    step_b(2)
    step_b(3)

    def block_back(k, t):
        return (gg[k, HC:, half(t)] * gates[k, HC:, half(t)].astype(F32)).astype(BF)

    swap_granules(block_back, put(bt), HC)
    backs = bt[...].reshape(ROWS * HC, COLS)
    unmixed = dot(backs, block_mix[...]).astype(BF)
    swap_granules(lambda k, t: unmixed[k * HC : (k + 1) * HC, half(t)], put(gbv), HC)
    part_block = dot_tn(backs, values).astype(BF)
    se[2 * COLS : 3 * COLS] = part_block[:, half(0)]
    se[3 * COLS :] = part_block[:, half(1)]

    def block_before_row(r, carry):
        d = dgelu[r, CH:]
        gbef[r, CH : CH + HC] = (d[0:HC] * (gg[r, HC:] * (bm[r].astype(F32) + 1.0))).astype(BF)
        gbef[r, CH + HC :] = (d[HC:] * gbv[r].astype(F32)).astype(BF)
        gbef[r, HC:CH] = jnp.zeros((HC, COLS), BF)
        return carry

    loop(ROWS, block_before_row, unroll=4)
    for k in (0, 1, ROWS + 2, ROWS + 3):
        jp[k] = jnp.zeros((CH, COLS), BF)

    step_d(0)
    step_d(1)
    step_c(2, mixp_t)
    step_c(3, mixp_t)

    part_grid = (dot_nt(table(2), table(0)) + dot_nt(table(3), table(1))).astype(BF)
    part_grid = dot(dot(spread[...], part_grid).astype(BF), gather[...]).astype(BF)
    se[0:COLS] = part_grid[:, half(0)]
    se[COLS : 2 * COLS] = part_grid[:, half(1)]
    push(se.at[pl.ds(pl.multiple_of(512 - mine, 512), 512)], re0, G_E0, near_device(twin))

    step_e(0)
    step_e(1)

    arrived(re0, G_E0)
    e0[...] = (se[pl.ds(pl.multiple_of(mine, 512), 512)].astype(F32) + re0[...].astype(F32)).astype(BF)
    over_y(lambda peer: e0.at[pl.ds(pl.multiple_of(peer * 128, 128), 128)], re1.at[level], G_E1)
    re1[level] = e0[pl.ds(pl.multiple_of(level * 128, 128), 128)]

    def returned(chains, r):
        return [
            jnp.concatenate([d_in[n, r // 2, t, lax.rem(r, 2)] for n in chains], axis=0).astype(F32) for t in range(2)
        ]

    def joined_row(r, carry):
        pack, p_in, p_out = carry
        grid_mixed = returned(VALUES, r)
        for t in range(2):
            gates_t = gates[r, :, half(t)].astype(F32)
            more = grid_mixed[t] + 1.0
            gated[r, 0:HC, half(t)] = (gates_t[0:HC] * more).astype(BF)
            gated[r, HC:, half(t)] = (gates_t[HC:] * (bm[r, :, half(t)].astype(F32) + 1.0)).astype(BF)
            gbef[r, 0:HC, half(t)] = (dgelu[r, 0:HC, half(t)] * (gg[r, 0:HC, half(t)] * more)).astype(BF)
        j = (xb[r].astype(F32) + dot(w_out[...], gated[r])).astype(BF)
        jp[r + 2] = j
        v3[r + 1, CH : 2 * CH] = j
        pack = edges(pack, j[:, half(0)], j[:, half(1)], r)
        return pack, p_in + dot_nt(nb[r], gbef[r]), p_out + dot_nt(gj[r], gated[r])

    pack, p_in, p_out = loop(
        ROWS,
        joined_row,
        (jnp.zeros((CH, LANES), BF), jnp.zeros((CH, 2 * CH), F32), jnp.zeros((CH, CH), F32)),
        unroll=8,
    )

    def conv_row(p, total):
        return total + dot_nt(u3[p], jp[pl.ds(p, 3)].reshape(3 * CH, COLS))

    p_conv = loop(ROWS + 2, conv_row, jnp.zeros((3 * CH, 3 * CH), F32), unroll=9)
    st[0 : 3 * CH] = p_conv[:, half(0)].astype(BF)
    st[3 * CH : 4 * CH] = p_in.astype(BF)
    third = p_conv[:, 2 * CH :]
    st[4 * CH :] = jnp.concatenate(
        [third[: 2 * CH], jnp.concatenate([third[2 * CH :], p_out], axis=0)], axis=1
    ).astype(BF)
    over_near(lambda peer: st.at[pl.ds(pl.multiple_of(peer * 48, 16), 48)], rt1.at[near], G_T1)
    rt1[near] = st[pl.ds(pl.multiple_of(near * 48, 16), 48)]
    send_halo(v3, pack, 1, G_ROW1, G_PACK1)

    step_d(2)
    step_d(3)

    arrived(re1.at[pl.ds(0, 3)], G_E1)
    total = re1[0].astype(F32)
    for k in range(1, 4):
        total = total + re1[k].astype(F32)
    e1[...] = total
    over_x(lambda peer: e1.at[pl.ds(pl.multiple_of(peer * 32, 32), 32)], re2.at[across], G_E2)
    re2[across] = e1[pl.ds(pl.multiple_of(across * 32, 32), 32)]

    take_halo(v3, 1, G_ROW1, G_PACK1)

    from_near(rt1, G_T1)
    total = rt1[0].astype(F32)
    for k in range(1, NEAR):
        total = total + rt1[k].astype(F32)
    t1[...] = total.astype(BF)
    over_x(lambda peer: t1, rt2.at[across], G_T2)
    rt2[across] = t1[...]

    conv_k = jnp.concatenate(
        [jnp.concatenate([conv_w[a, b] for b in range(3)], axis=1) for a in range(3)], axis=0
    )

    def out_row(r, carry):
        total, carry = conv_step(conv_k, v3, r, carry)
        total = total + v3[r + 1, CH : 2 * CH].astype(F32)
        for t in range(2):
            rest_out[t, pl.ds(r * CH, CH), :] = total[:, half(t)]
        return carry

    carry = loop(ROWS // 2, out_row, conv_start(conv_k, v3), unroll=8)

    arrived(re2.at[pl.ds(0, 3)], G_E2)
    e2[...] = re2[0] + re2[1] + re2[2] + re2[3]
    over_z(lambda peer: e2, re3.at[deep], G_E3)
    re3[deep] = e2[...]

    step_e(2)
    step_e(3)

    def value_before_row(r, total):
        grid_back = returned(BACKS, r)
        for t in range(2):
            gbef[r, HC:CH, half(t)] = (dgelu[r, HC:CH, half(t)] * grid_back[t]).astype(BF)
        return total + dot_nt(gbef[r, HC:CH], nb[r])

    p_value = loop(ROWS, value_before_row, jnp.zeros((HC, CH), F32), unroll=4)
    sq[...] = jnp.concatenate([p_value[0:16], p_value[16:]], axis=1).astype(BF)
    over_near(lambda peer: sq, rq1.at[near], G_Q1)
    rq1[near] = sq[...]

    arrived(rt2.at[pl.ds(0, 3)], G_T2)
    total = rt2[0].astype(F32)
    for k in range(1, 4):
        total = total + rt2[k].astype(F32)
    t2[...] = total.astype(BF)
    over_z(lambda peer: t2, rt3.at[deep], G_T3)
    rt3[deep] = t2[...]

    def frame_row(r, carry):
        normed = dot(w_in_t[...], gbef[r])
        u = unit[r]
        mean_grad = jnp.mean(normed, axis=0, keepdims=True)
        mean_proj = jnp.mean(normed * u, axis=0, keepdims=True)
        source = gj[r].astype(F32) + inv[r, 0:1] * (normed - mean_grad - u * mean_proj)
        for t in range(2):
            gframe_out[t, pl.ds(r * CH, CH), :] = source[:, half(t)]
        return carry

    loop(ROWS, frame_row, unroll=8)

    from_near(rq1, G_Q1)
    total = rq1[0].astype(F32)
    for k in range(1, NEAR):
        total = total + rq1[k].astype(F32)
    q1[...] = total.astype(BF)
    over_far(lambda peer: q1, rq2.at[far], G_Q2)
    rq2[far] = q1[...]

    arrived(re3.at[pl.ds(0, 3)], G_E3)
    e3[...] = (re3[0] + re3[1] + re3[2] + re3[3]).astype(BF)
    over_x(lambda peer: e3, re4.at[across], G_E4)
    re4[across] = e3[...]

    arrived(rt3.at[pl.ds(0, 3)], G_T3)
    total = rt3[0].astype(F32)
    for k in range(1, 4):
        total = total + rt3[k].astype(F32)
    t3[...] = total.astype(BF)
    over_near(lambda peer: t3, rt4.at[near], G_T4)
    rt4[near] = t3[...]


    arrived(re4.at[pl.ds(0, 3)], G_E4)
    over_y(lambda peer: re4, re5.at[level], G_E5)
    re5[level] = re4[...]

    loop(ROWS // 2, lambda r, carry: out_row(r + ROWS // 2, carry), carry, unroll=8)

    arrived(re5.at[pl.ds(0, 3)], G_E5)
    push(re5, re6, G_E6, near_device(twin))
    early_out[pl.ds(pl.multiple_of(mine, 512), 512)] = re5[...].reshape(512, LANES)

    from_far(rq2, G_Q2)
    total = rq2[0].astype(F32)
    for k in range(1, FAR):
        total = total + rq2[k].astype(F32)
    value_out[...] = total
    from_near(rt4, G_T4)
    tail_out[...] = rt4[...]
    arrived(re6, G_E6)
    early_out[pl.ds(pl.multiple_of(512 - mine, 512), 512)] = re6[...].reshape(512, LANES)

    for which, g_row, g_pack in ((0, G_ROW0, G_PACK0), (1, G_ROW1, G_PACK1)):
        gone(row_in.at[which], g_row)
        gone(pack_in.at[which], g_pack)
    for n in VALUES + BACKS:
        for ref, count, g in ((a_in, NEAR, G_A), (b_in, FAR, G_B), (c_in, FAR, G_C), (d_in, NEAR, G_D)):
            gone(ref.at[n, pl.ds(0, count - 1)], g + n)
    for ref, g in ((rt1, G_T1), (rt4, G_T4), (rq1, G_Q1)):
        gone(ref.at[pl.ds(0, NEAR - 1)], g)
    gone(rq2.at[pl.ds(0, FAR - 1)], G_Q2)
    gone(re0, G_E0)
    for ref, g in ((re1, G_E1), (re2, G_E2), (re3, G_E3), (re4, G_E4), (re5, G_E5), (rt2, G_T2), (rt3, G_T3)):
        gone(ref.at[pl.ds(0, 3)], g)
    gone(re6, G_E6)


def finish(
    rest, gframe, early, tail, value,
    restored, grad_frames, grad_w_in_t, grad_grid, grad_block, grad_w_out, grad_conv,
):
    scale = float(ROWS * NA * COLS * NW) ** (-0.5)

    def channel(c, carry):
        for src, dst in ((rest, restored), (gframe, grad_frames)):
            for t in range(2):
                dst[c, :, half(t)] = src[t, pl.ds(c, ROWS, stride=CH), :].astype(BF)
        return carry

    loop(CH, channel, unroll=8)

    for k in range(2):
        grad_grid[:, half(k)] = early[k * COLS : (k + 1) * COLS].astype(F32) * scale
        grad_block[:, half(k)] = early[(2 + k) * COLS : (3 + k) * COLS].astype(F32) * scale
    quarter = value[...] * scale
    zeros = jnp.zeros((HC, CH), F32)
    quarter = jnp.concatenate([zeros, quarter[:, :CH], quarter[:, CH:], zeros, zeros], axis=0)
    grad_w_in_t[...] = tail[3 * CH : 4 * CH].astype(F32) * scale + quarter.T
    last = tail[4 * CH :].astype(F32) * scale
    grad_w_out[...] = last[CH:, CH:]
    for b in range(3):
        rows = slice((2 - b) * CH, (3 - b) * CH)
        pair = tail[rows].astype(F32) * scale
        grad_conv[0, b] = pair[:, :CH]
        grad_conv[1, b] = pair[:, CH:]
    grad_conv[2, 2] = last[:CH, :CH]
    grad_conv[2, 1] = last[CH:, :CH]
    grad_conv[2, 0] = last[:CH, CH:]


def vm(*shape, dtype=BF):
    return pltpu.VMEM(shape, dtype)


def exchange():
    message_w = vm(4, NEAR, 2, 2, QC, LANES)
    message_a = vm(4, FAR, 16, 256)
    return [message_w, message_w, vm(4, 2 * 16 * QC, LANES, dtype=F32)] + [message_a] * 4 + [message_w] * 2


SCRATCH = [
    vm(CH, ROWS, COLS),
    vm(CH, 2 * CH),
    vm(COLS, COLS),
    vm(COLS, COLS),
    vm(CH, CH),
    vm(3, 3, CH, CH),
    vm(CH, ROWS, COLS),
    vm(2 * CH, CH),
    vm(2, CH * ROWS, LANES, dtype=F32),
    vm(ROWS, CH, COLS),
    vm(ROWS, CH, COLS),
    vm(ROWS, CH, COLS, dtype=F32),
    vm(ROWS, 8, COLS, dtype=F32),
    vm(ROWS, 2 * CH, COLS, dtype=F32),
    vm(ROWS, CH, COLS),
    vm(ROWS, HC, COLS),
    vm(ROWS + 2, 3 * CH, COLS),
    vm(ROWS + 2, 3 * CH, COLS),
    vm(ROWS, CH, COLS),
    vm(ROWS, CH, COLS, dtype=F32),
    vm(ROWS, HC, COLS),
    vm(ROWS, HC, COLS),
    vm(ROWS, HC, COLS),
    vm(ROWS, HC, COLS),
    *exchange(),
    vm(ROWS, CH, COLS),
    vm(ROWS, 2 * CH, COLS),
    vm(ROWS + 4, CH, COLS),
    vm(2, 2, CH, COLS),
    vm(2, 32, LANES),
    vm(2, 96, LANES),
    vm(CH, LANES),
    vm(CH, LANES),
    vm(COLS, COLS),
    vm(COLS, COLS),
    vm(COLS, COLS),
    vm(COLS, COLS),
    vm(4 * COLS, LANES),
    vm(512, LANES),
    vm(512, LANES),
    vm(4, 128, LANES),
    vm(128, LANES, dtype=F32),
    vm(4, 32, LANES, dtype=F32),
    vm(32, LANES, dtype=F32),
    vm(4, 32, LANES, dtype=F32),
    vm(32, LANES),
    vm(4, 32, LANES),
    vm(4, 4, 32, LANES),
    vm(4, 4, 32, LANES),
    vm(6 * CH, LANES),
    vm(NW, 48, LANES),
    vm(48, LANES),
    vm(4, 48, LANES),
    vm(48, LANES),
    vm(4, 48, LANES),
    vm(48, LANES),
    vm(NEAR, 48, LANES),
    vm(16, LANES),
    vm(NEAR, 16, LANES),
    vm(16, LANES),
    vm(FAR, 16, LANES),
    pltpu.SemaphoreType.DMA((GROUPS,)),
    pltpu.SemaphoreType.DMA((GROUPS,)),
    pltpu.SemaphoreType.DMA((7,)),
]


def body(frames, w_in, grid_mix, block_mix, w_out, conv_w, cotangent):
    operands = (frames, w_in.T, grid_mix, block_mix, w_out, conv_w, cotangent)
    vmem = pl.BlockSpec(memory_space=pltpu.VMEM)
    shape = jax.ShapeDtypeStruct
    rest, gframe, early, tail, value = pl.pallas_call(
        kernel,
        out_shape=(
            shape((2, ROWS * CH, LANES), F32),
            shape((2, ROWS * CH, LANES), F32),
            shape((4 * COLS, LANES), BF),
            shape((NEAR, 48, LANES), BF),
            shape((16, LANES), F32),
        ),
        in_specs=[pl.BlockSpec(memory_space=pltpu.HBM)] * 7,
        out_specs=(vmem,) * 5,
        scratch_shapes=SCRATCH,
        compiler_params=pltpu.CompilerParams(
            collective_id=0, has_side_effects=True, vmem_limit_bytes=32 * 1024 * 1024
        ),
    )(*[pltpu.with_memory_space_constraint(x, pltpu.HBM) for x in operands])
    restored, grad_frames, grad_w_in_t, grad_grid, grad_block, grad_w_out, grad_conv = pl.pallas_call(
        finish,
        out_shape=(
            shape((CH, ROWS, COLS), BF),
            shape((CH, ROWS, COLS), BF),
            shape((CH, 2 * CH), F32),
            shape((COLS, COLS), F32),
            shape((COLS, COLS), F32),
            shape((CH, CH), F32),
            shape((3, 3, CH, CH), F32),
        ),
        in_specs=[vmem] * 5,
        out_specs=(vmem,) * 7,
        compiler_params=pltpu.CompilerParams(vmem_limit_bytes=16 * 1024 * 1024),
    )(rest, gframe, early, tail.reshape(6 * CH, LANES), value)
    return restored, grad_frames, grad_w_in_t.T, grad_grid, grad_block, grad_w_out, grad_conv


def solution(mesh):
    placed = (P(None, "ha", "wa"), P(), P(), P(), P(), P(), P(None, "ha", "wa"))
    return jax.shard_map(
        body,
        mesh=mesh,
        in_specs=placed,
        out_specs=(P(None, "ha", "wa"), P(None, "ha", "wa"), P(), P(), P(), P(), P()),
        check_vma=False,
    )
```

```python
import jax
import jax.numpy as jnp
from jax import lax
from jax.experimental import pallas as pl
from jax.experimental.pallas import tpu as pltpu
from jax.sharding import PartitionSpec as P

BF = jnp.bfloat16
F32 = jnp.float32
EPS = 1e-06
MESH = pl.DeviceIdType.MESH

CH = 64
HC = 32
ROWS = 16
COLS = 256
LANES = 128
NA = 16
NW = 8
NEAR = 8
FAR = 16

(G_ROW0, G_PACK0, G_ROW1, G_PACK1) = range(4)
(G_E0, G_E1, G_E2, G_E3, G_E4, G_E5, G_E6, G_T1, G_T2, G_T3, G_T4, G_Q1, G_Q2) = range(4, 17)
VALUES, BACKS = (0, 1), (2, 3)
G_A, G_B, G_C, G_D = 17, 21, 25, 29
GROUPS = 33
QC = 16


def dot(a, b):
    return lax.dot_general(a, b, (((1,), (0,)), ((), ())), preferred_element_type=F32)


def dot_nt(a, b):
    return lax.dot_general(a, b, (((1,), (1,)), ((), ())), preferred_element_type=F32)


def dot_tn(a, b):
    return lax.dot_general(a, b, (((0,), (0,)), ((), ())), preferred_element_type=F32)


def swap_granules(load, store, depth):
    lane = lax.broadcasted_iota(jnp.int16, (depth, LANES), 1)
    for row_half in range(2):
        for col_half in range(2):
            held = [load(row_half * 8 + k, col_half) for k in range(8)]
            for s in range(3):
                width = 16 << s
                low = (lane & width) == 0
                for k in range(8):
                    if not k & (1 << s):
                        a, b = held[k], held[k | (1 << s)]
                        held[k] = jnp.where(low, a, pltpu.roll(b, width, 1))
                        held[k | (1 << s)] = jnp.where(low, pltpu.roll(a, LANES - width, 1), b)
            for k in range(8):
                store(col_half * 8 + k, row_half, held[k])


def half(t):
    return slice(t * LANES, (t + 1) * LANES)


def loop(count, step, carry=0, unroll=1):
    return lax.fori_loop(0, count, step, carry, unroll=unroll)


def gelu_parts(x):
    root = 0.7978845608028654
    cube = root * 0.044715
    square = x * x
    h = 0.5 * jnp.tanh(x * (cube * square + root)) + 0.5
    value = x * h
    return value, h + value * (1.0 - h) * ((6.0 * cube) * square + 2.0 * root)


def kernel(
    frames_hbm, w_in_t_hbm, grid_mix_hbm, block_mix_hbm, w_out_hbm, conv_w_hbm, cot_hbm,
    rest_out, gframe_out, early_out, tail_out, value_out,
    frames, w_in_t, grid_mix, block_mix, w_out, conv_w, cot, w_in,
    turn, xb, nb, unit, inv, dgelu, gates, bval, u3, v3, gj, gg, xt, bt, bm, gbv,
    a, a_in, x32, b, b_in, c, c_in, d, d_in,
    gated, gbef, jp, row_in, pack_out, pack_in, edge_l, edge_r,
    mixp, mixp_t, gather, spread, se, re0, e0, re1, e1, re2, e2, re3, e3, re4, re5, re6,
    st, rt1, t1, rt2, t2, rt3, t3, rt4, sq, rq1, q1, rq2,
    ssem, rsem, isem,
):
    ia = lax.axis_index("ha")
    iw = lax.axis_index("wa")
    up, down = lax.rem(ia + NA - 1, NA), lax.rem(ia + 1, NA)
    left, right = lax.rem(iw + NW - 1, NW), lax.rem(iw + 1, NW)
    lane = lax.broadcasted_iota(jnp.int16, (CH, LANES), 1)
    lane_wide = lax.broadcasted_iota(jnp.int32, (CH, LANES), 1)

    loads = [
        pltpu.make_async_copy(src, dst, isem.at[k])
        for k, (src, dst) in enumerate(
            [
                (cot_hbm, cot),
                (frames_hbm, frames),
                (w_in_t_hbm, w_in_t),
                (conv_w_hbm, conv_w),
                (w_out_hbm, w_out),
                (block_mix_hbm, block_mix),
                (grid_mix_hbm, grid_mix),
            ]
        )
    ]
    for load in loads:
        load.start()

    def push(src, dst, g, where):
        pltpu.make_async_remote_copy(
            src_ref=src, dst_ref=dst, send_sem=ssem.at[g], recv_sem=rsem.at[g], device_id=where, device_id_type=MESH
        ).start()

    near = lax.rem(iw, 2) * 4 + lax.rem(ia, 4)
    far = ia // 4 * 4 + iw // 2

    def near_device(peer):
        return ia // 4 * 4 + lax.rem(peer, 4), iw // 2 * 2 + peer // 4

    def far_device(peer):
        return peer // 4 * 4 + lax.rem(ia, 4), lax.rem(peer, 4) * 2 + lax.rem(iw, 2)

    near_peers = [lax.rem(near + k, NEAR) for k in range(1, NEAR)]
    far_peers = [lax.rem(far + k, FAR) for k in range(1, FAR)]
    twin = near + 1 - 2 * lax.rem(near, 2)

    near_places = [near_device(peer) for peer in near_peers]
    far_places = [far_device(peer) for peer in far_peers]

    def over_near(src_of, dst, g):
        for peer, place in zip(near_peers, near_places):
            push(src_of(peer), dst, g, place)

    def over_far(src_of, dst, g):
        for peer, place in zip(far_peers, far_places):
            push(src_of(peer), dst, g, place)

    def over_x(src_of, dst, g):
        for k in range(1, 4):
            peer = lax.rem(iw // 2 + k, 4)
            push(src_of(peer), dst, g, (ia, peer * 2 + lax.rem(iw, 2)))

    def over_z(src_of, dst, g):
        for k in range(1, 4):
            peer = lax.rem(ia // 4 + k, 4)
            push(src_of(peer), dst, g, (peer * 4 + lax.rem(ia, 4), iw))

    def over_y(src_of, dst, g):
        for k in range(1, 4):
            peer = lax.rem(near + 2 * k, NEAR)
            push(src_of(peer // 2), dst, g, near_device(peer))

    def arrived(ref, g):
        pltpu.make_async_copy(ref, ref, rsem.at[g]).wait()

    def gone(ref, g):
        pltpu.make_async_copy(ref, ref, ssem.at[g]).wait()

    def from_near(ref, g):
        arrived(ref.at[pl.ds(0, NEAR - 1)], g)

    def from_far(ref, g):
        arrived(ref.at[pl.ds(0, FAR - 1)], g)

    mine = lax.rem(near, 2) * 512
    level, across, deep = near // 2, iw // 2, ia // 4

    barrier = pltpu.get_barrier_semaphore()
    peers = [near_device(peer) for peer in near_peers]
    peers += [far_device(peer) for peer in far_peers]
    peers += [(a, b) for a in (up, ia, down) for b in (left, right)] + [(up, iw), (down, iw)]
    for peer in peers:
        pl.semaphore_signal(barrier, inc=1, device_id=peer, device_id_type=MESH)

    def turn_in(src):
        for t in range(2):
            turn[t] = src[:, :, half(t)].astype(F32).reshape(CH * ROWS, LANES)

    def turned(r, t):
        return turn[t, pl.ds(r, CH, stride=ROWS), :]

    def edges(pack, t0, t1, r):
        pack = jnp.where(lane_wide == r, pltpu.roll(t0, r, 1), pack)
        return jnp.where(lane_wide == ROWS + r, pltpu.roll(t1, r + 17, 1), pack)

    def send_halo(field, pack, which, g_row, g_pack):
        pack_out[which] = jnp.concatenate([pack, jnp.zeros_like(pack)], axis=0).T[0:32]
        push(field.at[1, CH : 2 * CH], row_in.at[which, 1], g_row, (up, iw))
        push(field.at[ROWS, CH : 2 * CH], row_in.at[which, 0], g_row, (down, iw))
        for slot, where in enumerate(
            [(ia, right), (down, right), (up, right), (ia, left), (down, left), (up, left)]
        ):
            part = pack_out.at[which, pl.ds(16 if slot < 3 else 0, 16)]
            push(part, pack_in.at[which, pl.ds(16 * slot, 16)], g_pack, where)

    def take_halo(field, which, g_row, g_pack):
        arrived(row_in.at[which], g_row)
        arrived(pack_in.at[which], g_pack)
        field[0, CH : 2 * CH] = jnp.where(ia > 0, row_in[which, 0], jnp.zeros((CH, COLS), BF))
        field[ROWS + 1, CH : 2 * CH] = jnp.where(ia < NA - 1, row_in[which, 1], jnp.zeros((CH, COLS), BF))
        first = jnp.where(ia > 0, 0, 1)
        last = jnp.where(ia < NA - 1, ROWS + 2, ROWS + 1)
        got = jnp.concatenate([pack_in[which], jnp.zeros((32, LANES), BF)], axis=0).T[0:CH]

        def assemble(middle, above, below, has):
            joined = jnp.where(lane == 0, above, jnp.where(lane == ROWS + 1, below, middle))
            inside = (lane_wide >= first) & (lane_wide < jnp.where(has, last, 0))
            return jnp.where(inside, joined, jnp.zeros_like(joined))

        edge_l[...] = assemble(pltpu.roll(got, 1, 1), pltpu.roll(got, 97, 1), pltpu.roll(got, 113, 1), iw > 0)
        edge_r[...] = assemble(pltpu.roll(got, 81, 1), pltpu.roll(got, 49, 1), pltpu.roll(got, 65, 1), iw < NW - 1)

        def shifts(p, carry):
            t0 = field[p, CH : 2 * CH, half(0)]
            t1 = field[p, CH : 2 * CH, half(1)]
            a0, a1 = pltpu.roll(t0, 1, 1), pltpu.roll(t1, 1, 1)
            b0, b1 = pltpu.roll(t0, LANES - 1, 1), pltpu.roll(t1, LANES - 1, 1)
            lh = pltpu.roll(edge_l[...], lax.rem(LANES - p, LANES), 1)
            rh = pltpu.roll(edge_r[...], LANES - 1 - p, 1)
            field[p, 0:CH, half(0)] = jnp.where(lane == 0, lh, a0)
            field[p, 0:CH, half(1)] = jnp.where(lane == 0, a0, a1)
            field[p, 2 * CH :, half(0)] = jnp.where(lane == LANES - 1, b1, b0)
            field[p, 2 * CH :, half(1)] = jnp.where(lane == LANES - 1, rh, b1)
            return carry

        loop(ROWS + 2, shifts, unroll=9)

    def conv_start(w, field):
        y = dot(w, field[0])
        z = dot(w, field[1])
        return z[0:CH], y[0:CH] + z[CH : 2 * CH]

    def conv_step(w, field, r, carry):
        later, now = carry
        y = dot(w, field[r + 2])
        return now + y[2 * CH :], (y[0:CH], later + y[CH : 2 * CH])

    def step_a(n):
        over_near(lambda peer: a.at[n, peer], a_in.at[n, near], G_A + n)

    def step_b(n):
        arrived(a_in.at[n, pl.ds(0, NEAR - 1)], G_A + n)

        def widen(j, carry):
            for t in range(2):
                for r in range(2):
                    x32[n, pl.ds((r * 16 + j * 2 + t) * QC, QC), :] = a_in[n, j, t, r].astype(F32)
            return carry

        loop(NEAR, widen, unroll=8)

        for peer, place in zip([*far_peers, far], [*far_places, None]):
            base = peer // 8 * (16 * QC) + lax.rem(peer, 8) * 2
            slot = b_in if peer is far else b
            for k in range(2):
                slot[n, peer, :, half(k)] = x32[n, pl.ds(base + k, 16, stride=QC), :].astype(BF)
            if peer is not far:
                push(b.at[n, peer], b_in.at[n, far], G_B + n, place)

    def table(n):
        return b_in[n].reshape(256, 256)

    def step_c(n, mix):
        arrived(b_in.at[n, pl.ds(0, FAR - 1)], G_B + n)
        c[n] = dot(mix[...], table(n)).astype(BF).reshape(FAR, 16, 256)
        over_far(lambda peer: c.at[n, peer], c_in.at[n, far], G_C + n)
        c_in[n, far] = c[n, far]

    def step_d(n):
        arrived(c_in.at[n, pl.ds(0, FAR - 1)], G_C + n)

        def unpick(q, carry):
            for r in range(2):
                for k in range(2):
                    x32[n, pl.ds((r * QC + q * 2 + k) * 16, 16), :] = c_in[n, r * 8 + q, :, half(k)].astype(F32)
            return carry

        loop(8, unpick, unroll=8)

        for peer, place in zip([*near_peers, near], [*near_places, None]):
            slot = d_in if peer is near else d
            for t in range(2):
                for r in range(2):
                    slot[n, peer, t, r] = x32[n, pl.ds(r * QC * 16 + peer * 2 + t, QC, stride=16), :].astype(BF)
            if peer is not near:
                push(d.at[n, peer], d_in.at[n, near], G_D + n, place)

    def step_e(n):
        arrived(d_in.at[n, pl.ds(0, NEAR - 1)], G_D + n)

    def order(cell, row):
        found = (row & 0xC1) | ((row & 6) << 3) | ((row & 48) >> 2) | ((row & 8) >> 2)
        return jnp.where(cell == found, 1.0, 0.0).astype(BF)

    loads[0].wait()
    turn_in(cot)

    def cot_row(r, pack):
        t0, t1 = turned(r, 0).astype(BF), turned(r, 1).astype(BF)
        u3[r + 1, CH : 2 * CH, half(0)] = t0
        u3[r + 1, CH : 2 * CH, half(1)] = t1
        return edges(pack, t0, t1, r)

    pack = loop(ROWS, cot_row, jnp.zeros((CH, LANES), BF), unroll=8)
    pl.semaphore_wait(barrier, len(peers))
    send_halo(u3, pack, 0, G_ROW0, G_PACK0)

    loads[1].wait()
    loads[2].wait()
    turn_in(frames)
    w_in[...] = w_in_t[...].astype(F32).T.astype(BF)

    def value_row(slot, peer, low):
        r = peer * 2 + low
        for t in range(2):
            x = turned(r, t)
            xb[r, :, half(t)] = x.astype(BF)
            off = x - jnp.mean(x, axis=0, keepdims=True)
            rstd = lax.rsqrt(jnp.mean(off * off, axis=0, keepdims=True) + EPS)
            u = off * rstd
            unit[r, :, half(t)] = u
            inv[r, :, half(t)] = jnp.broadcast_to(rstd, (8, LANES))
            nb[r, :, half(t)] = u.astype(BF)
        value, slope = gelu_parts(dot(w_in[HC:CH], nb[r]))
        dgelu[r, HC:CH] = slope
        value = value.astype(BF)
        for n in VALUES:
            for t in range(2):
                slot[n, peer, t, low] = value[n * QC : (n + 1) * QC, half(t)]

    for first in range(0, NEAR, 2):
        group = [*near_peers, near][first : first + 2]
        for peer in group:
            for low in range(2):
                value_row(a_in if peer is near else a, peer, low)
        for peer in group:
            if peer is not near:
                push(a.at[0, peer], a_in.at[0, near], G_A, near_device(peer))
    step_a(1)

    def grid_gate_row(r, carry):
        value, slope = gelu_parts(dot(w_in[0:HC], nb[r]))
        gates[r, 0:HC] = value.astype(BF)
        dgelu[r, 0:HC] = slope
        return carry

    loop(ROWS, grid_gate_row, unroll=8)

    for load in loads[3:]:
        load.wait()
    back_w = jnp.concatenate(
        [jnp.concatenate([conv_w[2 - a, 2 - b] for a in range(3)], axis=1) for b in range(3)], axis=0
    ).astype(F32).T.astype(BF)
    w_out_t = w_out[...].astype(F32).T.astype(BF)
    take_halo(u3, 0, G_ROW0, G_PACK0)

    def back_row(r, carry):
        total, carry = conv_step(back_w, u3, r, carry)
        g = (total + u3[r + 1, CH : 2 * CH].astype(F32)).astype(BF)
        gj[r] = g
        up_gated = dot(w_out_t, g)
        gg[r] = up_gated
        mixed = (up_gated[0:HC] * gates[r, 0:HC].astype(F32)).astype(BF)
        for n in range(2):
            for t in range(2):
                a[2 + n, r // 2, t, r % 2] = mixed[n * QC : (n + 1) * QC, half(t)]
        return carry

    carry = conv_start(back_w, u3)
    for first in range(0, NEAR, 2):
        for r in range(2 * first, 2 * first + 4):
            carry = back_row(r, carry)
        for peer in (first, first + 1):

            @pl.when(peer != near)
            def _():
                push(a.at[2, peer], a_in.at[2, near], G_A + 2, near_device(peer))

    step_a(3)
    for n in BACKS:
        a_in[n, near] = a[n, near]
    step_b(0)
    step_b(1)

    def block_gate_row(r, carry):
        value, slope = gelu_parts(dot(w_in[CH:], nb[r]))
        dgelu[r, CH:] = slope
        value = value.astype(BF)
        gates[r, HC:CH] = value[0:HC]
        bval[r] = value[HC:]
        return carry

    loop(ROWS, block_gate_row, unroll=8)
    down_axis = lax.broadcasted_iota(jnp.int32, (COLS, COLS), 0)
    along_axis = lax.broadcasted_iota(jnp.int32, (COLS, COLS), 1)
    gather[...] = order(along_axis, down_axis)
    spread[...] = order(down_axis, along_axis)
    mixp[...] = dot(dot(gather[...], grid_mix[...]).astype(BF), spread[...]).astype(BF)
    mixp_t[...] = dot(dot_nt(gather[...], grid_mix[...]).astype(BF), spread[...]).astype(BF)
    step_c(0, mixp)

    def put(ref):
        def store(k, t, value):
            ref[k, :, half(t)] = value

        return store

    swap_granules(lambda k, t: bval[k, :, half(t)], put(xt), HC)
    values = xt[...].reshape(ROWS * HC, COLS)
    mixed = dot_nt(values, block_mix[...]).astype(BF)
    swap_granules(lambda k, t: mixed[k * HC : (k + 1) * HC, half(t)], put(bm), HC)

    step_c(1, mixp)
    step_b(2)
    step_b(3)

    def block_back(k, t):
        return (gg[k, HC:, half(t)] * gates[k, HC:, half(t)].astype(F32)).astype(BF)

    swap_granules(block_back, put(bt), HC)
    backs = bt[...].reshape(ROWS * HC, COLS)
    unmixed = dot(backs, block_mix[...]).astype(BF)
    swap_granules(lambda k, t: unmixed[k * HC : (k + 1) * HC, half(t)], put(gbv), HC)
    part_block = dot_tn(backs, values).astype(BF)
    se[2 * COLS : 3 * COLS] = part_block[:, half(0)]
    se[3 * COLS :] = part_block[:, half(1)]

    def block_before_row(r, carry):
        d = dgelu[r, CH:]
        gbef[r, CH : CH + HC] = (d[0:HC] * (gg[r, HC:] * (bm[r].astype(F32) + 1.0))).astype(BF)
        gbef[r, CH + HC :] = (d[HC:] * gbv[r].astype(F32)).astype(BF)
        gbef[r, HC:CH] = jnp.zeros((HC, COLS), BF)
        return carry

    loop(ROWS, block_before_row, unroll=4)
    for k in (0, 1, ROWS + 2, ROWS + 3):
        jp[k] = jnp.zeros((CH, COLS), BF)

    step_d(0)
    step_d(1)
    step_c(2, mixp_t)
    step_c(3, mixp_t)

    part_grid = (dot_nt(table(2), table(0)) + dot_nt(table(3), table(1))).astype(BF)
    part_grid = dot(dot(spread[...], part_grid).astype(BF), gather[...]).astype(BF)
    se[0:COLS] = part_grid[:, half(0)]
    se[COLS : 2 * COLS] = part_grid[:, half(1)]
    push(se.at[pl.ds(pl.multiple_of(512 - mine, 512), 512)], re0, G_E0, near_device(twin))

    step_e(0)
    step_e(1)

    arrived(re0, G_E0)
    e0[...] = (se[pl.ds(pl.multiple_of(mine, 512), 512)].astype(F32) + re0[...].astype(F32)).astype(BF)
    over_y(lambda peer: e0.at[pl.ds(pl.multiple_of(peer * 128, 128), 128)], re1.at[level], G_E1)
    re1[level] = e0[pl.ds(pl.multiple_of(level * 128, 128), 128)]

    def returned(chains, r):
        return [
            jnp.concatenate([d_in[n, r // 2, t, lax.rem(r, 2)] for n in chains], axis=0).astype(F32) for t in range(2)
        ]

    def joined_row(r, carry):
        pack, p_in, p_out, p_conv = carry
        grid_mixed = returned(VALUES, r)
        for t in range(2):
            gates_t = gates[r, :, half(t)].astype(F32)
            more = grid_mixed[t] + 1.0
            gated[r, 0:HC, half(t)] = (gates_t[0:HC] * more).astype(BF)
            gated[r, HC:, half(t)] = (gates_t[HC:] * (bm[r, :, half(t)].astype(F32) + 1.0)).astype(BF)
            gbef[r, 0:HC, half(t)] = (dgelu[r, 0:HC, half(t)] * (gg[r, 0:HC, half(t)] * more)).astype(BF)
        j = (xb[r].astype(F32) + dot(w_out[...], gated[r])).astype(BF)
        jp[r + 2] = j
        v3[r + 1, CH : 2 * CH] = j
        pack = edges(pack, j[:, half(0)], j[:, half(1)], r)
        return pack, p_in + dot_nt(nb[r], gbef[r]), p_out + dot_nt(gj[r], gated[r]), p_conv + conv_plane(r)

    def conv_plane(p):
        return dot_nt(u3[p], jp[pl.ds(p, 3)].reshape(3 * CH, COLS))

    pack, p_in, p_out, p_conv = loop(
        ROWS,
        joined_row,
        (
            jnp.zeros((CH, LANES), BF),
            jnp.zeros((CH, 2 * CH), F32),
            jnp.zeros((CH, CH), F32),
            jnp.zeros((3 * CH, 3 * CH), F32),
        ),
        unroll=8,
    )
    p_conv = p_conv + conv_plane(ROWS) + conv_plane(ROWS + 1)
    st[0 : 3 * CH] = p_conv[:, half(0)].astype(BF)
    st[3 * CH : 4 * CH] = p_in.astype(BF)
    third = p_conv[:, 2 * CH :]
    st[4 * CH :] = jnp.concatenate(
        [third[: 2 * CH], jnp.concatenate([third[2 * CH :], p_out], axis=0)], axis=1
    ).astype(BF)
    over_near(lambda peer: st.at[pl.ds(pl.multiple_of(peer * 48, 16), 48)], rt1.at[near], G_T1)
    rt1[near] = st[pl.ds(pl.multiple_of(near * 48, 16), 48)]
    send_halo(v3, pack, 1, G_ROW1, G_PACK1)

    arrived(re1.at[pl.ds(0, 3)], G_E1)
    total = re1[0].astype(F32)
    for k in range(1, 4):
        total = total + re1[k].astype(F32)
    e1[...] = total
    over_x(lambda peer: e1.at[pl.ds(pl.multiple_of(peer * 32, 32), 32)], re2.at[across], G_E2)
    re2[across] = e1[pl.ds(pl.multiple_of(across * 32, 32), 32)]

    step_d(2)
    step_d(3)

    take_halo(v3, 1, G_ROW1, G_PACK1)

    arrived(re2.at[pl.ds(0, 3)], G_E2)
    e2[...] = re2[0] + re2[1] + re2[2] + re2[3]
    over_z(lambda peer: e2, re3.at[deep], G_E3)
    re3[deep] = e2[...]

    from_near(rt1, G_T1)
    total = rt1[0].astype(F32)
    for k in range(1, NEAR):
        total = total + rt1[k].astype(F32)
    t1[...] = total.astype(BF)
    over_x(lambda peer: t1, rt2.at[across], G_T2)
    rt2[across] = t1[...]

    conv_k = jnp.concatenate(
        [jnp.concatenate([conv_w[a, b] for b in range(3)], axis=1) for a in range(3)], axis=0
    )

    def out_row(r, carry):
        total, carry = conv_step(conv_k, v3, r, carry)
        total = total + v3[r + 1, CH : 2 * CH].astype(F32)
        for t in range(2):
            rest_out[t, pl.ds(r * CH, CH), :] = total[:, half(t)]
        return carry

    carry = loop(ROWS // 2, out_row, conv_start(conv_k, v3), unroll=8)

    arrived(re3.at[pl.ds(0, 3)], G_E3)
    e3[...] = (re3[0] + re3[1] + re3[2] + re3[3]).astype(BF)
    over_x(lambda peer: e3, re4.at[across], G_E4)
    re4[across] = e3[...]

    step_e(2)
    step_e(3)

    def value_before_row(r, total):
        grid_back = returned(BACKS, r)
        for t in range(2):
            gbef[r, HC:CH, half(t)] = (dgelu[r, HC:CH, half(t)] * grid_back[t]).astype(BF)
        return total + dot_nt(gbef[r, HC:CH], nb[r])

    p_value = loop(ROWS, value_before_row, jnp.zeros((HC, CH), F32), unroll=4)
    sq[...] = jnp.concatenate([p_value[0:16], p_value[16:]], axis=1).astype(BF)
    over_near(lambda peer: sq, rq1.at[near], G_Q1)
    rq1[near] = sq[...]

    arrived(re4.at[pl.ds(0, 3)], G_E4)
    over_y(lambda peer: re4, re5.at[level], G_E5)
    re5[level] = re4[...]

    arrived(rt2.at[pl.ds(0, 3)], G_T2)
    total = rt2[0].astype(F32)
    for k in range(1, 4):
        total = total + rt2[k].astype(F32)
    t2[...] = total.astype(BF)
    over_z(lambda peer: t2, rt3.at[deep], G_T3)
    rt3[deep] = t2[...]

    def frame_row(r, carry):
        normed = dot(w_in_t[...], gbef[r])
        u = unit[r]
        mean_grad = jnp.mean(normed, axis=0, keepdims=True)
        mean_proj = jnp.mean(normed * u, axis=0, keepdims=True)
        source = gj[r].astype(F32) + inv[r, 0:1] * (normed - mean_grad - u * mean_proj)
        for t in range(2):
            gframe_out[t, pl.ds(r * CH, CH), :] = source[:, half(t)]
        return carry

    loop(ROWS, frame_row, unroll=8)

    from_near(rq1, G_Q1)
    total = rq1[0].astype(F32)
    for k in range(1, NEAR):
        total = total + rq1[k].astype(F32)
    q1[...] = total.astype(BF)
    over_far(lambda peer: q1, rq2.at[far], G_Q2)
    rq2[far] = q1[...]

    arrived(rt3.at[pl.ds(0, 3)], G_T3)
    total = rt3[0].astype(F32)
    for k in range(1, 4):
        total = total + rt3[k].astype(F32)
    t3[...] = total.astype(BF)
    over_near(lambda peer: t3, rt4.at[near], G_T4)
    rt4[near] = t3[...]


    arrived(re5.at[pl.ds(0, 3)], G_E5)
    push(re5, re6, G_E6, near_device(twin))
    early_out[pl.ds(pl.multiple_of(mine, 512), 512)] = re5[...].reshape(512, LANES)

    loop(ROWS // 2, lambda r, carry: out_row(r + ROWS // 2, carry), carry, unroll=8)

    from_far(rq2, G_Q2)
    total = rq2[0].astype(F32)
    for k in range(1, FAR):
        total = total + rq2[k].astype(F32)
    value_out[...] = total
    from_near(rt4, G_T4)
    tail_out[...] = rt4[...]
    arrived(re6, G_E6)
    early_out[pl.ds(pl.multiple_of(512 - mine, 512), 512)] = re6[...].reshape(512, LANES)

    for which, g_row, g_pack in ((0, G_ROW0, G_PACK0), (1, G_ROW1, G_PACK1)):
        gone(row_in.at[which], g_row)
        gone(pack_in.at[which], g_pack)
    for n in VALUES + BACKS:
        for ref, count, g in ((a_in, NEAR, G_A), (b_in, FAR, G_B), (c_in, FAR, G_C), (d_in, NEAR, G_D)):
            gone(ref.at[n, pl.ds(0, count - 1)], g + n)
    for ref, g in ((rt1, G_T1), (rt4, G_T4), (rq1, G_Q1)):
        gone(ref.at[pl.ds(0, NEAR - 1)], g)
    gone(rq2.at[pl.ds(0, FAR - 1)], G_Q2)
    gone(re0, G_E0)
    for ref, g in ((re1, G_E1), (re2, G_E2), (re3, G_E3), (re4, G_E4), (re5, G_E5), (rt2, G_T2), (rt3, G_T3)):
        gone(ref.at[pl.ds(0, 3)], g)
    gone(re6, G_E6)


def finish(rest, gframe, early, tail, value, *refs):
    outs, sem = (refs[:7], refs[7:14]), refs[14]
    restored, grad_frames, grad_w_in_t, grad_grid, grad_block, grad_w_out, grad_conv = outs[1]
    copies = []

    def leave(k, part=None):
        src, dst = outs[1][k], outs[0][k]
        if part is not None:
            src, dst = src.at[part], dst.at[part]
        copies.append(pltpu.make_async_copy(src, dst, sem.at[len(copies)]))
        copies[-1].start()

    def turn_out(src, dst, k):
        for first in range(0, CH, CH // 2):

            def channel(c, carry):
                for t in range(2):
                    dst[first + c, :, half(t)] = src[t, pl.ds(first + c, ROWS, stride=CH), :].astype(BF)
                return carry

            loop(CH // 2, channel, unroll=16)
            leave(k, pl.ds(first, CH // 2))

    scale = float(ROWS * NA * COLS * NW) ** (-0.5)
    for k in range(2):
        grad_grid[:, half(k)] = early[k * COLS : (k + 1) * COLS].astype(F32) * scale
        grad_block[:, half(k)] = early[(2 + k) * COLS : (3 + k) * COLS].astype(F32) * scale
    leave(3)
    leave(4)
    turn_out(gframe, grad_frames, 1)
    turn_out(rest, restored, 0)
    quarter = value[...] * scale
    zeros = jnp.zeros((HC, CH), F32)
    quarter = jnp.concatenate([zeros, quarter[:, :CH], quarter[:, CH:], zeros, zeros], axis=0)
    grad_w_in_t[...] = tail[3 * CH : 4 * CH].astype(F32) * scale + quarter.T
    leave(2)
    last = tail[4 * CH :].astype(F32) * scale
    grad_w_out[...] = last[CH:, CH:]
    leave(5)
    for b in range(3):
        rows = slice((2 - b) * CH, (3 - b) * CH)
        pair = tail[rows].astype(F32) * scale
        grad_conv[0, b] = pair[:, :CH]
        grad_conv[1, b] = pair[:, CH:]
    grad_conv[2, 2] = last[:CH, :CH]
    grad_conv[2, 1] = last[CH:, :CH]
    grad_conv[2, 0] = last[:CH, CH:]
    leave(6)
    for copy in copies:
        copy.wait()


def vm(*shape, dtype=BF):
    return pltpu.VMEM(shape, dtype)


def exchange():
    message_w = vm(4, NEAR, 2, 2, QC, LANES)
    message_a = vm(4, FAR, 16, 256)
    return [message_w, message_w, vm(4, 2 * 16 * QC, LANES, dtype=F32)] + [message_a] * 4 + [message_w] * 2


SCRATCH = [
    vm(CH, ROWS, COLS),
    vm(CH, 2 * CH),
    vm(COLS, COLS),
    vm(COLS, COLS),
    vm(CH, CH),
    vm(3, 3, CH, CH),
    vm(CH, ROWS, COLS),
    vm(2 * CH, CH),
    vm(2, CH * ROWS, LANES, dtype=F32),
    vm(ROWS, CH, COLS),
    vm(ROWS, CH, COLS),
    vm(ROWS, CH, COLS, dtype=F32),
    vm(ROWS, 8, COLS, dtype=F32),
    vm(ROWS, 2 * CH, COLS, dtype=F32),
    vm(ROWS, CH, COLS),
    vm(ROWS, HC, COLS),
    vm(ROWS + 2, 3 * CH, COLS),
    vm(ROWS + 2, 3 * CH, COLS),
    vm(ROWS, CH, COLS),
    vm(ROWS, CH, COLS, dtype=F32),
    vm(ROWS, HC, COLS),
    vm(ROWS, HC, COLS),
    vm(ROWS, HC, COLS),
    vm(ROWS, HC, COLS),
    *exchange(),
    vm(ROWS, CH, COLS),
    vm(ROWS, 2 * CH, COLS),
    vm(ROWS + 4, CH, COLS),
    vm(2, 2, CH, COLS),
    vm(2, 32, LANES),
    vm(2, 96, LANES),
    vm(CH, LANES),
    vm(CH, LANES),
    vm(COLS, COLS),
    vm(COLS, COLS),
    vm(COLS, COLS),
    vm(COLS, COLS),
    vm(4 * COLS, LANES),
    vm(512, LANES),
    vm(512, LANES),
    vm(4, 128, LANES),
    vm(128, LANES, dtype=F32),
    vm(4, 32, LANES, dtype=F32),
    vm(32, LANES, dtype=F32),
    vm(4, 32, LANES, dtype=F32),
    vm(32, LANES),
    vm(4, 32, LANES),
    vm(4, 4, 32, LANES),
    vm(4, 4, 32, LANES),
    vm(6 * CH, LANES),
    vm(NW, 48, LANES),
    vm(48, LANES),
    vm(4, 48, LANES),
    vm(48, LANES),
    vm(4, 48, LANES),
    vm(48, LANES),
    vm(NEAR, 48, LANES),
    vm(16, LANES),
    vm(NEAR, 16, LANES),
    vm(16, LANES),
    vm(FAR, 16, LANES),
    pltpu.SemaphoreType.DMA((GROUPS,)),
    pltpu.SemaphoreType.DMA((GROUPS,)),
    pltpu.SemaphoreType.DMA((7,)),
]


def body(frames, w_in, grid_mix, block_mix, w_out, conv_w, cotangent):
    operands = (frames, w_in.T, grid_mix, block_mix, w_out, conv_w, cotangent)
    vmem = pl.BlockSpec(memory_space=pltpu.VMEM)
    shape = jax.ShapeDtypeStruct
    rest, gframe, early, tail, value = pl.pallas_call(
        kernel,
        out_shape=(
            shape((2, ROWS * CH, LANES), F32),
            shape((2, ROWS * CH, LANES), F32),
            shape((4 * COLS, LANES), BF),
            shape((NEAR, 48, LANES), BF),
            shape((16, LANES), F32),
        ),
        in_specs=[pl.BlockSpec(memory_space=pltpu.HBM)] * 7,
        out_specs=(vmem,) * 5,
        scratch_shapes=SCRATCH,
        compiler_params=pltpu.CompilerParams(
            collective_id=0, has_side_effects=True, vmem_limit_bytes=32 * 1024 * 1024
        ),
    )(*[pltpu.with_memory_space_constraint(x, pltpu.HBM) for x in operands])
    restored, grad_frames, grad_w_in_t, grad_grid, grad_block, grad_w_out, grad_conv = pl.pallas_call(
        finish,
        out_shape=(
            shape((CH, ROWS, COLS), BF),
            shape((CH, ROWS, COLS), BF),
            shape((CH, 2 * CH), F32),
            shape((COLS, COLS), F32),
            shape((COLS, COLS), F32),
            shape((CH, CH), F32),
            shape((3, 3, CH, CH), F32),
        ),
        in_specs=[vmem] * 5,
        out_specs=(pl.BlockSpec(memory_space=pl.ANY),) * 7,
        scratch_shapes=[
            vm(CH, ROWS, COLS),
            vm(CH, ROWS, COLS),
            vm(CH, 2 * CH, dtype=F32),
            vm(COLS, COLS, dtype=F32),
            vm(COLS, COLS, dtype=F32),
            vm(CH, CH, dtype=F32),
            vm(3, 3, CH, CH, dtype=F32),
            pltpu.SemaphoreType.DMA((9,)),
        ],
        compiler_params=pltpu.CompilerParams(vmem_limit_bytes=16 * 1024 * 1024),
    )(rest, gframe, early, tail.reshape(6 * CH, LANES), value)
    return restored, grad_frames, grad_w_in_t.T, grad_grid, grad_block, grad_w_out, grad_conv


def solution(mesh):
    placed = (P(None, "ha", "wa"), P(), P(), P(), P(), P(), P(None, "ha", "wa"))
    return jax.shard_map(
        body,
        mesh=mesh,
        in_specs=placed,
        out_specs=(P(None, "ha", "wa"), P(None, "ha", "wa"), P(), P(), P(), P(), P()),
        check_vma=False,
    )
```

```python
import jax
import jax.numpy as jnp
from jax import lax
from jax.experimental import pallas as pl
from jax.experimental.pallas import tpu as pltpu
from jax.sharding import PartitionSpec as P

BF = jnp.bfloat16
F32 = jnp.float32
EPS = 1e-06
MESH = pl.DeviceIdType.MESH

CH = 64
HC = 32
ROWS = 16
COLS = 256
LANES = 128
NA = 16
NW = 8
NEAR = 8
FAR = 16

(G_ROW0, G_PACK0, G_ROW1, G_PACK1) = range(4)
(G_E0, G_E1, G_E2, G_E3, G_E4, G_E5, G_E6, G_T1, G_T2, G_T3, G_T4, G_Q1, G_Q2) = range(4, 17)
VALUES, BACKS = (0, 1), (2, 3)
G_A, G_B, G_C, G_D = 17, 21, 25, 29
GROUPS = 33
QC = 16


def dot(a, b):
    return lax.dot_general(a, b, (((1,), (0,)), ((), ())), preferred_element_type=F32)


def dot_nt(a, b):
    return lax.dot_general(a, b, (((1,), (1,)), ((), ())), preferred_element_type=F32)


def dot_tn(a, b):
    return lax.dot_general(a, b, (((0,), (0,)), ((), ())), preferred_element_type=F32)


def swap_granules(load, store, depth):
    lane = lax.broadcasted_iota(jnp.int16, (depth, LANES), 1)
    for row_half in range(2):
        for col_half in range(2):
            held = [load(row_half * 8 + k, col_half) for k in range(8)]
            for s in range(3):
                width = 16 << s
                low = (lane & width) == 0
                for k in range(8):
                    if not k & (1 << s):
                        a, b = held[k], held[k | (1 << s)]
                        held[k] = jnp.where(low, a, pltpu.roll(b, width, 1))
                        held[k | (1 << s)] = jnp.where(low, pltpu.roll(a, LANES - width, 1), b)
            for k in range(8):
                store(col_half * 8 + k, row_half, held[k])


def half(t):
    return slice(t * LANES, (t + 1) * LANES)


def loop(count, step, carry=0, unroll=1):
    return lax.fori_loop(0, count, step, carry, unroll=unroll)


def gelu_parts(x):
    root = 0.7978845608028654
    cube = root * 0.044715
    square = x * x
    h = 0.5 * jnp.tanh(x * (cube * square + root)) + 0.5
    value = x * h
    return value, h + value * (1.0 - h) * ((6.0 * cube) * square + 2.0 * root)


def kernel(
    frames_hbm, w_in_t_hbm, grid_mix_hbm, block_mix_hbm, w_out_hbm, conv_w_hbm, cot_hbm,
    rest_out, gframe_out, early_out, tail_out, value_out,
    frames, w_in_t, grid_mix, block_mix, w_out, conv_w, cot, w_in,
    turn, xb, nb, unit, inv, dgelu, gates, bval, u3, v3, gj, gg, xt, bt, bm, gbv,
    a, a_in, x32, b, b_in, c, c_in, d, d_in,
    gated, gbef, jp, row_in, pack_out, pack_in, edge_l, edge_r,
    mixp, mixp_t, gather, spread, se, re0, e0, re1, e1, re2, e2, re3, e3, re4, re5, re6,
    st, rt1, t1, rt2, t2, rt3, t3, rt4, sq, rq1, q1, rq2,
    ssem, rsem, isem,
):
    ia = lax.axis_index("ha")
    iw = lax.axis_index("wa")
    up, down = lax.rem(ia + NA - 1, NA), lax.rem(ia + 1, NA)
    left, right = lax.rem(iw + NW - 1, NW), lax.rem(iw + 1, NW)
    lane = lax.broadcasted_iota(jnp.int16, (CH, LANES), 1)
    lane_wide = lax.broadcasted_iota(jnp.int32, (CH, LANES), 1)

    loads = [
        pltpu.make_async_copy(src, dst, isem.at[k])
        for k, (src, dst) in enumerate(
            [
                (frames_hbm, frames),
                (w_in_t_hbm, w_in_t),
                (cot_hbm, cot),
                (conv_w_hbm, conv_w),
                (w_out_hbm, w_out),
                (block_mix_hbm, block_mix),
                (grid_mix_hbm, grid_mix),
            ]
        )
    ]
    for load in loads:
        load.start()

    def push(src, dst, g, where):
        pltpu.make_async_remote_copy(
            src_ref=src, dst_ref=dst, send_sem=ssem.at[g], recv_sem=rsem.at[g], device_id=where, device_id_type=MESH
        ).start()

    near = lax.rem(iw, 2) * 4 + lax.rem(ia, 4)
    far = ia // 4 * 4 + iw // 2

    def near_device(peer):
        return ia // 4 * 4 + lax.rem(peer, 4), iw // 2 * 2 + peer // 4

    def far_device(peer):
        return peer // 4 * 4 + lax.rem(ia, 4), lax.rem(peer, 4) * 2 + lax.rem(iw, 2)

    near_peers = [lax.rem(near + k, NEAR) for k in range(1, NEAR)]
    far_peers = [lax.rem(far + k, FAR) for k in range(1, FAR)]
    twin = near + 1 - 2 * lax.rem(near, 2)

    near_places = [near_device(peer) for peer in near_peers]
    far_places = [far_device(peer) for peer in far_peers]

    def over_near(src_of, dst, g):
        for peer, place in zip(near_peers, near_places):
            push(src_of(peer), dst, g, place)

    def over_far(src_of, dst, g):
        for peer, place in zip(far_peers, far_places):
            push(src_of(peer), dst, g, place)

    def over_x(src_of, dst, g):
        for k in range(1, 4):
            peer = lax.rem(iw // 2 + k, 4)
            push(src_of(peer), dst, g, (ia, peer * 2 + lax.rem(iw, 2)))

    def over_z(src_of, dst, g):
        for k in range(1, 4):
            peer = lax.rem(ia // 4 + k, 4)
            push(src_of(peer), dst, g, (peer * 4 + lax.rem(ia, 4), iw))

    def over_y(src_of, dst, g):
        for k in range(1, 4):
            peer = lax.rem(near + 2 * k, NEAR)
            push(src_of(peer // 2), dst, g, near_device(peer))

    def arrived(ref, g):
        pltpu.make_async_copy(ref, ref, rsem.at[g]).wait()

    def gone(ref, g):
        pltpu.make_async_copy(ref, ref, ssem.at[g]).wait()

    def from_near(ref, g):
        arrived(ref.at[pl.ds(0, NEAR - 1)], g)

    def from_far(ref, g):
        arrived(ref.at[pl.ds(0, FAR - 1)], g)

    mine = lax.rem(near, 2) * 512
    level, across, deep = near // 2, iw // 2, ia // 4

    barrier = pltpu.get_barrier_semaphore()
    peers = [near_device(peer) for peer in near_peers]
    peers += [far_device(peer) for peer in far_peers]
    peers += [(a, b) for a in (up, ia, down) for b in (left, right)] + [(up, iw), (down, iw)]
    for peer in peers:
        pl.semaphore_signal(barrier, inc=1, device_id=peer, device_id_type=MESH)

    def turn_in(src):
        for t in range(2):
            turn[t] = src[:, :, half(t)].astype(F32).reshape(CH * ROWS, LANES)

    def turned(r, t):
        return turn[t, pl.ds(r, CH, stride=ROWS), :]

    def edges(pack, t0, t1, r):
        pack = jnp.where(lane_wide == r, pltpu.roll(t0, r, 1), pack)
        return jnp.where(lane_wide == ROWS + r, pltpu.roll(t1, r + 17, 1), pack)

    def send_halo(field, pack, which, g_row, g_pack):
        pack_out[which] = jnp.concatenate([pack, jnp.zeros_like(pack)], axis=0).T[0:32]
        push(field.at[1, CH : 2 * CH], row_in.at[which, 1], g_row, (up, iw))
        push(field.at[ROWS, CH : 2 * CH], row_in.at[which, 0], g_row, (down, iw))
        for slot, where in enumerate(
            [(ia, right), (down, right), (up, right), (ia, left), (down, left), (up, left)]
        ):
            part = pack_out.at[which, pl.ds(16 if slot < 3 else 0, 16)]
            push(part, pack_in.at[which, pl.ds(16 * slot, 16)], g_pack, where)

    def take_halo(field, which, g_row, g_pack):
        arrived(row_in.at[which], g_row)
        arrived(pack_in.at[which], g_pack)
        field[0, CH : 2 * CH] = jnp.where(ia > 0, row_in[which, 0], jnp.zeros((CH, COLS), BF))
        field[ROWS + 1, CH : 2 * CH] = jnp.where(ia < NA - 1, row_in[which, 1], jnp.zeros((CH, COLS), BF))
        first = jnp.where(ia > 0, 0, 1)
        last = jnp.where(ia < NA - 1, ROWS + 2, ROWS + 1)
        got = jnp.concatenate([pack_in[which], jnp.zeros((32, LANES), BF)], axis=0).T[0:CH]

        def assemble(middle, above, below, has):
            joined = jnp.where(lane == 0, above, jnp.where(lane == ROWS + 1, below, middle))
            inside = (lane_wide >= first) & (lane_wide < jnp.where(has, last, 0))
            return jnp.where(inside, joined, jnp.zeros_like(joined))

        edge_l[...] = assemble(pltpu.roll(got, 1, 1), pltpu.roll(got, 97, 1), pltpu.roll(got, 113, 1), iw > 0)
        edge_r[...] = assemble(pltpu.roll(got, 81, 1), pltpu.roll(got, 49, 1), pltpu.roll(got, 65, 1), iw < NW - 1)

        def shifts(p, carry):
            t0 = field[p, CH : 2 * CH, half(0)]
            t1 = field[p, CH : 2 * CH, half(1)]
            a0, a1 = pltpu.roll(t0, 1, 1), pltpu.roll(t1, 1, 1)
            b0, b1 = pltpu.roll(t0, LANES - 1, 1), pltpu.roll(t1, LANES - 1, 1)
            lh = pltpu.roll(edge_l[...], lax.rem(LANES - p, LANES), 1)
            rh = pltpu.roll(edge_r[...], LANES - 1 - p, 1)
            field[p, 0:CH, half(0)] = jnp.where(lane == 0, lh, a0)
            field[p, 0:CH, half(1)] = jnp.where(lane == 0, a0, a1)
            field[p, 2 * CH :, half(0)] = jnp.where(lane == LANES - 1, b1, b0)
            field[p, 2 * CH :, half(1)] = jnp.where(lane == LANES - 1, rh, b1)
            return carry

        loop(ROWS + 2, shifts, unroll=9)

    def conv_start(w, field):
        y = dot(w, field[0])
        z = dot(w, field[1])
        return z[0:CH], y[0:CH] + z[CH : 2 * CH]

    def conv_step(w, field, r, carry):
        later, now = carry
        y = dot(w, field[r + 2])
        return now + y[2 * CH :], (y[0:CH], later + y[CH : 2 * CH])

    def step_a(n):
        over_near(lambda peer: a.at[n, peer], a_in.at[n, near], G_A + n)

    def step_b(n):
        arrived(a_in.at[n, pl.ds(0, NEAR - 1)], G_A + n)

        def widen(j, carry):
            for t in range(2):
                for r in range(2):
                    x32[n, pl.ds((r * 16 + j * 2 + t) * QC, QC), :] = a_in[n, j, t, r].astype(F32)
            return carry

        loop(NEAR, widen, unroll=8)

        for peer, place in zip([*far_peers, far], [*far_places, None]):
            base = peer // 8 * (16 * QC) + lax.rem(peer, 8) * 2
            slot = b_in if peer is far else b
            for k in range(2):
                slot[n, peer, :, half(k)] = x32[n, pl.ds(base + k, 16, stride=QC), :].astype(BF)
            if peer is not far:
                push(b.at[n, peer], b_in.at[n, far], G_B + n, place)

    def table(n):
        return b_in[n].reshape(256, 256)

    def step_c(n, mix):
        arrived(b_in.at[n, pl.ds(0, FAR - 1)], G_B + n)
        c[n] = dot(mix[...], table(n)).astype(BF).reshape(FAR, 16, 256)
        over_far(lambda peer: c.at[n, peer], c_in.at[n, far], G_C + n)
        c_in[n, far] = c[n, far]

    def step_d(n):
        arrived(c_in.at[n, pl.ds(0, FAR - 1)], G_C + n)

        def unpick(q, carry):
            for r in range(2):
                for k in range(2):
                    x32[n, pl.ds((r * QC + q * 2 + k) * 16, 16), :] = c_in[n, r * 8 + q, :, half(k)].astype(F32)
            return carry

        loop(8, unpick, unroll=8)

        for peer, place in zip([*near_peers, near], [*near_places, None]):
            slot = d_in if peer is near else d
            for t in range(2):
                for r in range(2):
                    slot[n, peer, t, r] = x32[n, pl.ds(r * QC * 16 + peer * 2 + t, QC, stride=16), :].astype(BF)
            if peer is not near:
                push(d.at[n, peer], d_in.at[n, near], G_D + n, place)

    def step_e(n):
        arrived(d_in.at[n, pl.ds(0, NEAR - 1)], G_D + n)

    def order(cell, row):
        found = (row & 0xC1) | ((row & 6) << 3) | ((row & 48) >> 2) | ((row & 8) >> 2)
        return jnp.where(cell == found, 1.0, 0.0).astype(BF)

    loads[0].wait()
    loads[1].wait()
    turn_in(frames)
    w_in[...] = w_in_t[...].astype(F32).T.astype(BF)

    def value_row(slot, peer, low):
        r = peer * 2 + low
        for t in range(2):
            x = turned(r, t)
            xb[r, :, half(t)] = x.astype(BF)
            off = x - jnp.mean(x, axis=0, keepdims=True)
            rstd = lax.rsqrt(jnp.mean(off * off, axis=0, keepdims=True) + EPS)
            u = off * rstd
            unit[r, :, half(t)] = u
            inv[r, :, half(t)] = jnp.broadcast_to(rstd, (8, LANES))
            nb[r, :, half(t)] = u.astype(BF)
        value, slope = gelu_parts(dot(w_in[HC:CH], nb[r]))
        dgelu[r, HC:CH] = slope
        value = value.astype(BF)
        for n in VALUES:
            for t in range(2):
                slot[n, peer, t, low] = value[n * QC : (n + 1) * QC, half(t)]

    for first in range(0, NEAR, 2):
        group = [*near_peers, near][first : first + 2]
        for peer in group:
            for low in range(2):
                value_row(a_in if peer is near else a, peer, low)
        if first == 0:
            pl.semaphore_wait(barrier, len(peers))
        for peer in group:
            if peer is not near:
                push(a.at[0, peer], a_in.at[0, near], G_A, near_device(peer))
    step_a(1)

    loads[2].wait()
    turn_in(cot)

    def cot_row(r, pack):
        t0, t1 = turned(r, 0).astype(BF), turned(r, 1).astype(BF)
        u3[r + 1, CH : 2 * CH, half(0)] = t0
        u3[r + 1, CH : 2 * CH, half(1)] = t1
        return edges(pack, t0, t1, r)

    pack = loop(ROWS, cot_row, jnp.zeros((CH, LANES), BF), unroll=8)
    send_halo(u3, pack, 0, G_ROW0, G_PACK0)

    def grid_gate_row(r, carry):
        value, slope = gelu_parts(dot(w_in[0:HC], nb[r]))
        gates[r, 0:HC] = value.astype(BF)
        dgelu[r, 0:HC] = slope
        return carry

    loop(ROWS, grid_gate_row, unroll=8)

    def block_gate_row(r, carry):
        value, slope = gelu_parts(dot(w_in[CH:], nb[r]))
        dgelu[r, CH:] = slope
        value = value.astype(BF)
        gates[r, HC:CH] = value[0:HC]
        bval[r] = value[HC:]
        return carry

    loop(ROWS, block_gate_row, unroll=8)
    for load in loads[3:]:
        load.wait()
    down_axis = lax.broadcasted_iota(jnp.int32, (COLS, COLS), 0)
    along_axis = lax.broadcasted_iota(jnp.int32, (COLS, COLS), 1)
    gather[...] = order(along_axis, down_axis)
    spread[...] = order(down_axis, along_axis)
    mixp[...] = dot(dot(gather[...], grid_mix[...]).astype(BF), spread[...]).astype(BF)
    mixp_t[...] = dot(dot_nt(gather[...], grid_mix[...]).astype(BF), spread[...]).astype(BF)

    back_w = jnp.concatenate(
        [jnp.concatenate([conv_w[2 - a, 2 - b] for a in range(3)], axis=1) for b in range(3)], axis=0
    ).astype(F32).T.astype(BF)
    w_out_t = w_out[...].astype(F32).T.astype(BF)
    take_halo(u3, 0, G_ROW0, G_PACK0)

    def back_row(r, carry):
        total, carry = conv_step(back_w, u3, r, carry)
        g = (total + u3[r + 1, CH : 2 * CH].astype(F32)).astype(BF)
        gj[r] = g
        up_gated = dot(w_out_t, g)
        gg[r] = up_gated
        mixed = (up_gated[0:HC] * gates[r, 0:HC].astype(F32)).astype(BF)
        for n in range(2):
            for t in range(2):
                a[2 + n, r // 2, t, r % 2] = mixed[n * QC : (n + 1) * QC, half(t)]
        return carry

    step_b(0)
    carry = conv_start(back_w, u3)
    for first in range(0, NEAR, 2):
        if first == NEAR // 2:
            step_b(1)
        for r in range(2 * first, 2 * first + 4):
            carry = back_row(r, carry)
        for peer in (first, first + 1):

            @pl.when(peer != near)
            def _():
                push(a.at[2, peer], a_in.at[2, near], G_A + 2, near_device(peer))

    step_a(3)
    for n in BACKS:
        a_in[n, near] = a[n, near]


    def put(ref):
        def store(k, t, value):
            ref[k, :, half(t)] = value

        return store

    swap_granules(lambda k, t: bval[k, :, half(t)], put(xt), HC)
    values = xt[...].reshape(ROWS * HC, COLS)
    mixed = dot_nt(values, block_mix[...]).astype(BF)
    swap_granules(lambda k, t: mixed[k * HC : (k + 1) * HC, half(t)], put(bm), HC)

    step_c(0, mixp)
    step_b(2)
    step_c(1, mixp)
    step_b(3)

    def block_back(k, t):
        return (gg[k, HC:, half(t)] * gates[k, HC:, half(t)].astype(F32)).astype(BF)

    swap_granules(block_back, put(bt), HC)
    backs = bt[...].reshape(ROWS * HC, COLS)
    unmixed = dot(backs, block_mix[...]).astype(BF)
    swap_granules(lambda k, t: unmixed[k * HC : (k + 1) * HC, half(t)], put(gbv), HC)
    part_block = dot_tn(backs, values).astype(BF)
    se[2 * COLS : 3 * COLS] = part_block[:, half(0)]
    se[3 * COLS :] = part_block[:, half(1)]

    def block_before_row(r, carry):
        d = dgelu[r, CH:]
        gbef[r, CH : CH + HC] = (d[0:HC] * (gg[r, HC:] * (bm[r].astype(F32) + 1.0))).astype(BF)
        gbef[r, CH + HC :] = (d[HC:] * gbv[r].astype(F32)).astype(BF)
        gbef[r, HC:CH] = jnp.zeros((HC, COLS), BF)
        return carry

    loop(ROWS, block_before_row, unroll=4)
    for k in (0, 1, ROWS + 2, ROWS + 3):
        jp[k] = jnp.zeros((CH, COLS), BF)

    step_d(0)
    step_d(1)
    step_c(2, mixp_t)
    step_c(3, mixp_t)

    part_grid = (dot_nt(table(2), table(0)) + dot_nt(table(3), table(1))).astype(BF)
    part_grid = dot(dot(spread[...], part_grid).astype(BF), gather[...]).astype(BF)
    se[0:COLS] = part_grid[:, half(0)]
    se[COLS : 2 * COLS] = part_grid[:, half(1)]
    push(se.at[pl.ds(pl.multiple_of(512 - mine, 512), 512)], re0, G_E0, near_device(twin))

    step_e(0)
    step_e(1)

    arrived(re0, G_E0)
    e0[...] = (se[pl.ds(pl.multiple_of(mine, 512), 512)].astype(F32) + re0[...].astype(F32)).astype(BF)
    over_y(lambda peer: e0.at[pl.ds(pl.multiple_of(peer * 128, 128), 128)], re1.at[level], G_E1)
    re1[level] = e0[pl.ds(pl.multiple_of(level * 128, 128), 128)]

    def returned(chains, r):
        return [
            jnp.concatenate([d_in[n, r // 2, t, lax.rem(r, 2)] for n in chains], axis=0).astype(F32) for t in range(2)
        ]

    def joined_row(r, carry):
        pack, p_in, p_out = carry
        grid_mixed = returned(VALUES, r)
        for t in range(2):
            gates_t = gates[r, :, half(t)].astype(F32)
            more = grid_mixed[t] + 1.0
            gated[r, 0:HC, half(t)] = (gates_t[0:HC] * more).astype(BF)
            gated[r, HC:, half(t)] = (gates_t[HC:] * (bm[r, :, half(t)].astype(F32) + 1.0)).astype(BF)
            gbef[r, 0:HC, half(t)] = (dgelu[r, 0:HC, half(t)] * (gg[r, 0:HC, half(t)] * more)).astype(BF)
        j = (xb[r].astype(F32) + dot(w_out[...], gated[r])).astype(BF)
        jp[r + 2] = j
        v3[r + 1, CH : 2 * CH] = j
        pack = edges(pack, j[:, half(0)], j[:, half(1)], r)
        return pack, p_in + dot_nt(nb[r], gbef[r]), p_out + dot_nt(gj[r], gated[r])

    pack, p_in, p_out = loop(
        ROWS,
        joined_row,
        (jnp.zeros((CH, LANES), BF), jnp.zeros((CH, 2 * CH), F32), jnp.zeros((CH, CH), F32)),
        unroll=8,
    )

    def conv_row(p, total):
        return total + dot_nt(u3[p], jp[pl.ds(p, 3)].reshape(3 * CH, COLS))

    p_conv = loop(ROWS + 2, conv_row, jnp.zeros((3 * CH, 3 * CH), F32), unroll=9)
    st[0 : 3 * CH] = p_conv[:, half(0)].astype(BF)
    st[3 * CH : 4 * CH] = p_in.astype(BF)
    third = p_conv[:, 2 * CH :]
    st[4 * CH :] = jnp.concatenate(
        [third[: 2 * CH], jnp.concatenate([third[2 * CH :], p_out], axis=0)], axis=1
    ).astype(BF)
    over_near(lambda peer: st.at[pl.ds(pl.multiple_of(peer * 48, 16), 48)], rt1.at[near], G_T1)
    rt1[near] = st[pl.ds(pl.multiple_of(near * 48, 16), 48)]
    send_halo(v3, pack, 1, G_ROW1, G_PACK1)

    arrived(re1.at[pl.ds(0, 3)], G_E1)
    total = re1[0].astype(F32)
    for k in range(1, 4):
        total = total + re1[k].astype(F32)
    e1[...] = total
    over_x(lambda peer: e1.at[pl.ds(pl.multiple_of(peer * 32, 32), 32)], re2.at[across], G_E2)
    re2[across] = e1[pl.ds(pl.multiple_of(across * 32, 32), 32)]

    step_d(2)
    step_d(3)

    take_halo(v3, 1, G_ROW1, G_PACK1)

    for n in VALUES + BACKS:
        for ref, count, g in ((a_in, NEAR, G_A), (b_in, FAR, G_B), (c_in, FAR, G_C)):
            gone(ref.at[n, pl.ds(0, count - 1)], g + n)
    for n in VALUES:
        gone(d_in.at[n, pl.ds(0, NEAR - 1)], G_D + n)

    from_near(rt1, G_T1)
    total = rt1[0].astype(F32)
    for k in range(1, NEAR):
        total = total + rt1[k].astype(F32)
    t1[...] = total.astype(BF)
    over_x(lambda peer: t1, rt2.at[across], G_T2)
    rt2[across] = t1[...]

    arrived(re2.at[pl.ds(0, 3)], G_E2)
    e2[...] = re2[0] + re2[1] + re2[2] + re2[3]
    over_z(lambda peer: e2, re3.at[deep], G_E3)
    re3[deep] = e2[...]

    conv_k = jnp.concatenate(
        [jnp.concatenate([conv_w[a, b] for b in range(3)], axis=1) for a in range(3)], axis=0
    )

    def out_row(r, carry):
        total, carry = conv_step(conv_k, v3, r, carry)
        total = total + v3[r + 1, CH : 2 * CH].astype(F32)
        for t in range(2):
            rest_out[t, pl.ds(r * CH, CH), :] = total[:, half(t)]
        return carry

    carry = loop(ROWS // 2, out_row, conv_start(conv_k, v3), unroll=8)

    step_e(2)
    step_e(3)

    def value_before_row(r, total):
        grid_back = returned(BACKS, r)
        for t in range(2):
            gbef[r, HC:CH, half(t)] = (dgelu[r, HC:CH, half(t)] * grid_back[t]).astype(BF)
        return total + dot_nt(gbef[r, HC:CH], nb[r])

    p_value = loop(ROWS, value_before_row, jnp.zeros((HC, CH), F32), unroll=4)
    sq[...] = jnp.concatenate([p_value[0:16], p_value[16:]], axis=1).astype(BF)
    over_near(lambda peer: sq, rq1.at[near], G_Q1)
    rq1[near] = sq[...]

    arrived(re3.at[pl.ds(0, 3)], G_E3)
    e3[...] = (re3[0] + re3[1] + re3[2] + re3[3]).astype(BF)
    over_x(lambda peer: e3, re4.at[across], G_E4)
    re4[across] = e3[...]

    arrived(rt2.at[pl.ds(0, 3)], G_T2)
    total = rt2[0].astype(F32)
    for k in range(1, 4):
        total = total + rt2[k].astype(F32)
    t2[...] = total.astype(BF)
    over_z(lambda peer: t2, rt3.at[deep], G_T3)
    rt3[deep] = t2[...]

    def frame_row(r, carry):
        normed = dot(w_in_t[...], gbef[r])
        u = unit[r]
        mean_grad = jnp.mean(normed, axis=0, keepdims=True)
        mean_proj = jnp.mean(normed * u, axis=0, keepdims=True)
        source = gj[r].astype(F32) + inv[r, 0:1] * (normed - mean_grad - u * mean_proj)
        for t in range(2):
            gframe_out[t, pl.ds(r * CH, CH), :] = source[:, half(t)]
        return carry

    loop(ROWS, frame_row, unroll=8)

    from_near(rq1, G_Q1)
    total = rq1[0].astype(F32)
    for k in range(1, NEAR):
        total = total + rq1[k].astype(F32)
    q1[...] = total.astype(BF)
    over_far(lambda peer: q1, rq2.at[far], G_Q2)
    rq2[far] = q1[...]

    arrived(re4.at[pl.ds(0, 3)], G_E4)
    over_y(lambda peer: re4, re5.at[level], G_E5)
    re5[level] = re4[...]

    arrived(rt3.at[pl.ds(0, 3)], G_T3)
    total = rt3[0].astype(F32)
    for k in range(1, 4):
        total = total + rt3[k].astype(F32)
    t3[...] = total.astype(BF)
    over_near(lambda peer: t3, rt4.at[near], G_T4)
    rt4[near] = t3[...]


    loop(ROWS // 2, lambda r, carry: out_row(r + ROWS // 2, carry), carry, unroll=8)

    arrived(re5.at[pl.ds(0, 3)], G_E5)
    push(re5, re6, G_E6, near_device(twin))
    early_out[pl.ds(pl.multiple_of(mine, 512), 512)] = re5[...].reshape(512, LANES)

    from_far(rq2, G_Q2)
    total = rq2[0].astype(F32)
    for k in range(1, FAR):
        total = total + rq2[k].astype(F32)
    value_out[...] = total
    from_near(rt4, G_T4)
    tail_out[...] = rt4[...]
    arrived(re6, G_E6)
    early_out[pl.ds(pl.multiple_of(512 - mine, 512), 512)] = re6[...].reshape(512, LANES)

    for which, g_row, g_pack in ((0, G_ROW0, G_PACK0), (1, G_ROW1, G_PACK1)):
        gone(row_in.at[which], g_row)
        gone(pack_in.at[which], g_pack)
    for n in BACKS:
        gone(d_in.at[n, pl.ds(0, NEAR - 1)], G_D + n)
    for ref, g in ((rt1, G_T1), (rt4, G_T4), (rq1, G_Q1)):
        gone(ref.at[pl.ds(0, NEAR - 1)], g)
    gone(rq2.at[pl.ds(0, FAR - 1)], G_Q2)
    gone(re0, G_E0)
    for ref, g in ((re1, G_E1), (re2, G_E2), (re3, G_E3), (re4, G_E4), (re5, G_E5), (rt2, G_T2), (rt3, G_T3)):
        gone(ref.at[pl.ds(0, 3)], g)
    gone(re6, G_E6)


def finish(rest, gframe, early, tail, value, *refs):
    outs, sem = (refs[:7], refs[7:14]), refs[14]
    restored, grad_frames, grad_w_in_t, grad_grid, grad_block, grad_w_out, grad_conv = outs[1]
    copies = []

    def leave(k, part=None):
        src, dst = outs[1][k], outs[0][k]
        if part is not None:
            src, dst = src.at[part], dst.at[part]
        copies.append(pltpu.make_async_copy(src, dst, sem.at[len(copies)]))
        copies[-1].start()

    def turn_out(src, dst, k):
        for first in range(0, CH, CH // 2):

            def channel(c, carry):
                for t in range(2):
                    dst[first + c, :, half(t)] = src[t, pl.ds(first + c, ROWS, stride=CH), :].astype(BF)
                return carry

            loop(CH // 2, channel, unroll=16)
            leave(k, pl.ds(first, CH // 2))

    scale = float(ROWS * NA * COLS * NW) ** (-0.5)
    for k in range(2):
        grad_grid[:, half(k)] = early[k * COLS : (k + 1) * COLS].astype(F32) * scale
        grad_block[:, half(k)] = early[(2 + k) * COLS : (3 + k) * COLS].astype(F32) * scale
    leave(3)
    leave(4)
    turn_out(gframe, grad_frames, 1)
    turn_out(rest, restored, 0)
    quarter = value[...] * scale
    zeros = jnp.zeros((HC, CH), F32)
    quarter = jnp.concatenate([zeros, quarter[:, :CH], quarter[:, CH:], zeros, zeros], axis=0)
    grad_w_in_t[...] = tail[3 * CH : 4 * CH].astype(F32) * scale + quarter.T
    leave(2)
    last = tail[4 * CH :].astype(F32) * scale
    grad_w_out[...] = last[CH:, CH:]
    leave(5)
    for b in range(3):
        rows = slice((2 - b) * CH, (3 - b) * CH)
        pair = tail[rows].astype(F32) * scale
        grad_conv[0, b] = pair[:, :CH]
        grad_conv[1, b] = pair[:, CH:]
    grad_conv[2, 2] = last[:CH, :CH]
    grad_conv[2, 1] = last[CH:, :CH]
    grad_conv[2, 0] = last[:CH, CH:]
    leave(6)
    for copy in copies:
        copy.wait()


def vm(*shape, dtype=BF):
    return pltpu.VMEM(shape, dtype)


def exchange():
    message_w = vm(4, NEAR, 2, 2, QC, LANES)
    message_a = vm(4, FAR, 16, 256)
    return [message_w, message_w, vm(4, 2 * 16 * QC, LANES, dtype=F32)] + [message_a] * 4 + [message_w] * 2


SCRATCH = [
    vm(CH, ROWS, COLS),
    vm(CH, 2 * CH),
    vm(COLS, COLS),
    vm(COLS, COLS),
    vm(CH, CH),
    vm(3, 3, CH, CH),
    vm(CH, ROWS, COLS),
    vm(2 * CH, CH),
    vm(2, CH * ROWS, LANES, dtype=F32),
    vm(ROWS, CH, COLS),
    vm(ROWS, CH, COLS),
    vm(ROWS, CH, COLS, dtype=F32),
    vm(ROWS, 8, COLS, dtype=F32),
    vm(ROWS, 2 * CH, COLS, dtype=F32),
    vm(ROWS, CH, COLS),
    vm(ROWS, HC, COLS),
    vm(ROWS + 2, 3 * CH, COLS),
    vm(ROWS + 2, 3 * CH, COLS),
    vm(ROWS, CH, COLS),
    vm(ROWS, CH, COLS, dtype=F32),
    vm(ROWS, HC, COLS),
    vm(ROWS, HC, COLS),
    vm(ROWS, HC, COLS),
    vm(ROWS, HC, COLS),
    *exchange(),
    vm(ROWS, CH, COLS),
    vm(ROWS, 2 * CH, COLS),
    vm(ROWS + 4, CH, COLS),
    vm(2, 2, CH, COLS),
    vm(2, 32, LANES),
    vm(2, 96, LANES),
    vm(CH, LANES),
    vm(CH, LANES),
    vm(COLS, COLS),
    vm(COLS, COLS),
    vm(COLS, COLS),
    vm(COLS, COLS),
    vm(4 * COLS, LANES),
    vm(512, LANES),
    vm(512, LANES),
    vm(4, 128, LANES),
    vm(128, LANES, dtype=F32),
    vm(4, 32, LANES, dtype=F32),
    vm(32, LANES, dtype=F32),
    vm(4, 32, LANES, dtype=F32),
    vm(32, LANES),
    vm(4, 32, LANES),
    vm(4, 4, 32, LANES),
    vm(4, 4, 32, LANES),
    vm(6 * CH, LANES),
    vm(NW, 48, LANES),
    vm(48, LANES),
    vm(4, 48, LANES),
    vm(48, LANES),
    vm(4, 48, LANES),
    vm(48, LANES),
    vm(NEAR, 48, LANES),
    vm(16, LANES),
    vm(NEAR, 16, LANES),
    vm(16, LANES),
    vm(FAR, 16, LANES),
    pltpu.SemaphoreType.DMA((GROUPS,)),
    pltpu.SemaphoreType.DMA((GROUPS,)),
    pltpu.SemaphoreType.DMA((7,)),
]


def body(frames, w_in, grid_mix, block_mix, w_out, conv_w, cotangent):
    operands = (frames, w_in.T, grid_mix, block_mix, w_out, conv_w, cotangent)
    vmem = pl.BlockSpec(memory_space=pltpu.VMEM)
    shape = jax.ShapeDtypeStruct
    rest, gframe, early, tail, value = pl.pallas_call(
        kernel,
        out_shape=(
            shape((2, ROWS * CH, LANES), F32),
            shape((2, ROWS * CH, LANES), F32),
            shape((4 * COLS, LANES), BF),
            shape((NEAR, 48, LANES), BF),
            shape((16, LANES), F32),
        ),
        in_specs=[pl.BlockSpec(memory_space=pltpu.HBM)] * 7,
        out_specs=(vmem,) * 5,
        scratch_shapes=SCRATCH,
        compiler_params=pltpu.CompilerParams(
            collective_id=0, has_side_effects=True, vmem_limit_bytes=32 * 1024 * 1024
        ),
    )(*[pltpu.with_memory_space_constraint(x, pltpu.HBM) for x in operands])
    restored, grad_frames, grad_w_in_t, grad_grid, grad_block, grad_w_out, grad_conv = pl.pallas_call(
        finish,
        out_shape=(
            shape((CH, ROWS, COLS), BF),
            shape((CH, ROWS, COLS), BF),
            shape((CH, 2 * CH), F32),
            shape((COLS, COLS), F32),
            shape((COLS, COLS), F32),
            shape((CH, CH), F32),
            shape((3, 3, CH, CH), F32),
        ),
        in_specs=[vmem] * 5,
        out_specs=(pl.BlockSpec(memory_space=pl.ANY),) * 7,
        scratch_shapes=[
            vm(CH, ROWS, COLS),
            vm(CH, ROWS, COLS),
            vm(CH, 2 * CH, dtype=F32),
            vm(COLS, COLS, dtype=F32),
            vm(COLS, COLS, dtype=F32),
            vm(CH, CH, dtype=F32),
            vm(3, 3, CH, CH, dtype=F32),
            pltpu.SemaphoreType.DMA((9,)),
        ],
        compiler_params=pltpu.CompilerParams(vmem_limit_bytes=16 * 1024 * 1024),
    )(rest, gframe, early, tail.reshape(6 * CH, LANES), value)
    return restored, grad_frames, grad_w_in_t.T, grad_grid, grad_block, grad_w_out, grad_conv


def solution(mesh):
    placed = (P(None, "ha", "wa"), P(), P(), P(), P(), P(), P(None, "ha", "wa"))
    return jax.shard_map(
        body,
        mesh=mesh,
        in_specs=placed,
        out_specs=(P(None, "ha", "wa"), P(None, "ha", "wa"), P(), P(), P(), P(), P()),
        check_vma=False,
    )
```

```python
import jax
import jax.numpy as jnp
from jax import lax
from jax.experimental import pallas as pl
from jax.experimental.pallas import tpu as pltpu
from jax.sharding import PartitionSpec as P

BF = jnp.bfloat16
F32 = jnp.float32
EPS = 1e-06
MESH = pl.DeviceIdType.MESH

CH = 64
HC = 32
ROWS = 16
COLS = 256
LANES = 128
NA = 16
NW = 8
NEAR = 8
FAR = 16

(G_ROW0, G_PACK0, G_ROW1, G_PACK1) = range(4)
(G_E0, G_E1, G_E2, G_E3, G_E4, G_E5, G_E6, G_T1, G_T2, G_T3, G_T4, G_Q1, G_Q2) = range(4, 17)
VALUES, BACKS = (0, 1), (2, 3)
G_A, G_B, G_C, G_D = 17, 21, 25, 29
GROUPS = 33
QC = 16


def dot(a, b):
    return lax.dot_general(a, b, (((1,), (0,)), ((), ())), preferred_element_type=F32)


def dot_nt(a, b):
    return lax.dot_general(a, b, (((1,), (1,)), ((), ())), preferred_element_type=F32)


def dot_tn(a, b):
    return lax.dot_general(a, b, (((0,), (0,)), ((), ())), preferred_element_type=F32)


def swap_granules(load, store, depth):
    lane = lax.broadcasted_iota(jnp.int16, (depth, LANES), 1)
    for row_half in range(2):
        for col_half in range(2):
            held = [load(row_half * 8 + k, col_half) for k in range(8)]
            for s in range(3):
                width = 16 << s
                low = (lane & width) == 0
                for k in range(8):
                    if not k & (1 << s):
                        a, b = held[k], held[k | (1 << s)]
                        held[k] = jnp.where(low, a, pltpu.roll(b, width, 1))
                        held[k | (1 << s)] = jnp.where(low, pltpu.roll(a, LANES - width, 1), b)
            for k in range(8):
                store(col_half * 8 + k, row_half, held[k])


def half(t):
    return slice(t * LANES, (t + 1) * LANES)


def loop(count, step, carry=0, unroll=1):
    return lax.fori_loop(0, count, step, carry, unroll=unroll)


def gelu_parts(x):
    root = 0.7978845608028654
    cube = root * 0.044715
    square = x * x
    h = 0.5 * jnp.tanh(x * (cube * square + root)) + 0.5
    value = x * h
    return value, h + value * (1.0 - h) * ((6.0 * cube) * square + 2.0 * root)


def kernel(
    frames_hbm, w_in_t_hbm, grid_mix_hbm, block_mix_hbm, w_out_hbm, conv_w_hbm, cot_hbm,
    rest_out, gframe_out, early_out, tail_out, value_out,
    frames, w_in_t, grid_mix, block_mix, w_out, conv_w, cot, w_in,
    turn, xb, nb, unit, inv, dgelu, gates, bval, u3, v3, gj, gg, xt, bt, bm, gbv,
    a, a_in, x32, b, b_in, c, c_in, d, d_in,
    gated, gbef, jp, row_in, pack_out, pack_in, edge_l, edge_r,
    mixp, mixp_t, gather, spread, se, re0, e0, re1, e1, re2, e2, re3, e3, re4, re5, re6,
    st, rt1, t1, rt2, t2, rt3, t3, rt4, sq, rq1, q1, rq2,
    ssem, rsem, isem,
):
    ia = lax.axis_index("ha")
    iw = lax.axis_index("wa")
    up, down = lax.rem(ia + NA - 1, NA), lax.rem(ia + 1, NA)
    left, right = lax.rem(iw + NW - 1, NW), lax.rem(iw + 1, NW)
    lane = lax.broadcasted_iota(jnp.int16, (CH, LANES), 1)
    lane_wide = lax.broadcasted_iota(jnp.int32, (CH, LANES), 1)

    loads = [
        pltpu.make_async_copy(src, dst, isem.at[k])
        for k, (src, dst) in enumerate(
            [
                (frames_hbm, frames),
                (w_in_t_hbm, w_in_t),
                (cot_hbm, cot),
                (conv_w_hbm, conv_w),
                (w_out_hbm, w_out),
                (block_mix_hbm, block_mix),
                (grid_mix_hbm, grid_mix),
            ]
        )
    ]
    for load in loads:
        load.start()

    def push(src, dst, g, where):
        pltpu.make_async_remote_copy(
            src_ref=src, dst_ref=dst, send_sem=ssem.at[g], recv_sem=rsem.at[g], device_id=where, device_id_type=MESH
        ).start()

    near = lax.rem(iw, 2) * 4 + lax.rem(ia, 4)
    far = ia // 4 * 4 + iw // 2

    def near_device(peer):
        return ia // 4 * 4 + lax.rem(peer, 4), iw // 2 * 2 + peer // 4

    def far_device(peer):
        return peer // 4 * 4 + lax.rem(ia, 4), lax.rem(peer, 4) * 2 + lax.rem(iw, 2)

    near_peers = [lax.rem(near + k, NEAR) for k in range(1, NEAR)]
    far_peers = [lax.rem(far + k, FAR) for k in range(1, FAR)]
    twin = near + 1 - 2 * lax.rem(near, 2)

    near_places = [near_device(peer) for peer in near_peers]
    far_places = [far_device(peer) for peer in far_peers]

    def over_near(src_of, dst, g):
        for peer, place in zip(near_peers, near_places):
            push(src_of(peer), dst, g, place)

    def over_far(src_of, dst, g):
        for peer, place in zip(far_peers, far_places):
            push(src_of(peer), dst, g, place)

    def over_x(src_of, dst, g):
        for k in range(1, 4):
            peer = lax.rem(iw // 2 + k, 4)
            push(src_of(peer), dst, g, (ia, peer * 2 + lax.rem(iw, 2)))

    def over_z(src_of, dst, g):
        for k in range(1, 4):
            peer = lax.rem(ia // 4 + k, 4)
            push(src_of(peer), dst, g, (peer * 4 + lax.rem(ia, 4), iw))

    def over_y(src_of, dst, g):
        for k in range(1, 4):
            peer = lax.rem(near + 2 * k, NEAR)
            push(src_of(peer // 2), dst, g, near_device(peer))

    def arrived(ref, g):
        pltpu.make_async_copy(ref, ref, rsem.at[g]).wait()

    def gone(ref, g):
        pltpu.make_async_copy(ref, ref, ssem.at[g]).wait()

    def from_near(ref, g):
        arrived(ref.at[pl.ds(0, NEAR - 1)], g)

    def from_far(ref, g):
        arrived(ref.at[pl.ds(0, FAR - 1)], g)

    mine = lax.rem(near, 2) * 512
    level, across, deep = near // 2, iw // 2, ia // 4

    barrier = pltpu.get_barrier_semaphore()
    peers = [near_device(peer) for peer in near_peers]
    peers += [far_device(peer) for peer in far_peers]
    peers += [(a, b) for a in (up, ia, down) for b in (left, right)] + [(up, iw), (down, iw)]
    for peer in peers:
        pl.semaphore_signal(barrier, inc=1, device_id=peer, device_id_type=MESH)

    def turn_in(src):
        for t in range(2):
            turn[t] = src[:, :, half(t)].astype(F32).reshape(CH * ROWS, LANES)

    def turned(r, t):
        return turn[t, pl.ds(r, CH, stride=ROWS), :]

    def edges(pack, t0, t1, r):
        pack = jnp.where(lane_wide == r, pltpu.roll(t0, r, 1), pack)
        return jnp.where(lane_wide == ROWS + r, pltpu.roll(t1, r + 17, 1), pack)

    def send_halo(field, pack, which, g_row, g_pack):
        pack_out[which] = jnp.concatenate([pack, jnp.zeros_like(pack)], axis=0).T[0:32]
        push(field.at[1, CH : 2 * CH], row_in.at[which, 1], g_row, (up, iw))
        push(field.at[ROWS, CH : 2 * CH], row_in.at[which, 0], g_row, (down, iw))
        for slot, where in enumerate(
            [(ia, right), (down, right), (up, right), (ia, left), (down, left), (up, left)]
        ):
            part = pack_out.at[which, pl.ds(16 if slot < 3 else 0, 16)]
            push(part, pack_in.at[which, pl.ds(16 * slot, 16)], g_pack, where)

    def take_halo(field, which, g_row, g_pack):
        arrived(row_in.at[which], g_row)
        arrived(pack_in.at[which], g_pack)
        field[0, CH : 2 * CH] = jnp.where(ia > 0, row_in[which, 0], jnp.zeros((CH, COLS), BF))
        field[ROWS + 1, CH : 2 * CH] = jnp.where(ia < NA - 1, row_in[which, 1], jnp.zeros((CH, COLS), BF))
        first = jnp.where(ia > 0, 0, 1)
        last = jnp.where(ia < NA - 1, ROWS + 2, ROWS + 1)
        got = jnp.concatenate([pack_in[which], jnp.zeros((32, LANES), BF)], axis=0).T[0:CH]

        def assemble(middle, above, below, has):
            joined = jnp.where(lane == 0, above, jnp.where(lane == ROWS + 1, below, middle))
            inside = (lane_wide >= first) & (lane_wide < jnp.where(has, last, 0))
            return jnp.where(inside, joined, jnp.zeros_like(joined))

        edge_l[...] = assemble(pltpu.roll(got, 1, 1), pltpu.roll(got, 97, 1), pltpu.roll(got, 113, 1), iw > 0)
        edge_r[...] = assemble(pltpu.roll(got, 81, 1), pltpu.roll(got, 49, 1), pltpu.roll(got, 65, 1), iw < NW - 1)

        def shifts(p, carry):
            t0 = field[p, CH : 2 * CH, half(0)]
            t1 = field[p, CH : 2 * CH, half(1)]
            a0, a1 = pltpu.roll(t0, 1, 1), pltpu.roll(t1, 1, 1)
            b0, b1 = pltpu.roll(t0, LANES - 1, 1), pltpu.roll(t1, LANES - 1, 1)
            lh = pltpu.roll(edge_l[...], lax.rem(LANES - p, LANES), 1)
            rh = pltpu.roll(edge_r[...], LANES - 1 - p, 1)
            field[p, 0:CH, half(0)] = jnp.where(lane == 0, lh, a0)
            field[p, 0:CH, half(1)] = jnp.where(lane == 0, a0, a1)
            field[p, 2 * CH :, half(0)] = jnp.where(lane == LANES - 1, b1, b0)
            field[p, 2 * CH :, half(1)] = jnp.where(lane == LANES - 1, rh, b1)
            return carry

        loop(ROWS + 2, shifts, unroll=9)

    def conv_start(w, field):
        y = dot(w, field[0])
        z = dot(w, field[1])
        return z[0:CH], y[0:CH] + z[CH : 2 * CH]

    def conv_step(w, field, r, carry):
        later, now = carry
        y = dot(w, field[r + 2])
        return now + y[2 * CH :], (y[0:CH], later + y[CH : 2 * CH])

    def step_a(n):
        over_near(lambda peer: a.at[n, peer], a_in.at[n, near], G_A + n)

    def step_b(n):
        arrived(a_in.at[n, pl.ds(0, NEAR - 1)], G_A + n)

        def widen(j, carry):
            for t in range(2):
                for r in range(2):
                    x32[n, pl.ds((r * 16 + j * 2 + t) * QC, QC), :] = a_in[n, j, t, r].astype(F32)
            return carry

        loop(NEAR, widen, unroll=8)

        for peer, place in zip([*far_peers, far], [*far_places, None]):
            base = peer // 8 * (16 * QC) + lax.rem(peer, 8) * 2
            slot = b_in if peer is far else b
            for k in range(2):
                slot[n, peer, :, half(k)] = x32[n, pl.ds(base + k, 16, stride=QC), :].astype(BF)
            if peer is not far:
                push(b.at[n, peer], b_in.at[n, far], G_B + n, place)

    def table(n):
        return b_in[n].reshape(256, 256)

    def step_c(n, mix):
        arrived(b_in.at[n, pl.ds(0, FAR - 1)], G_B + n)
        c[n] = dot(mix[...], table(n)).astype(BF).reshape(FAR, 16, 256)
        over_far(lambda peer: c.at[n, peer], c_in.at[n, far], G_C + n)
        c_in[n, far] = c[n, far]

    def step_d(n):
        arrived(c_in.at[n, pl.ds(0, FAR - 1)], G_C + n)

        def unpick(q, carry):
            for r in range(2):
                for k in range(2):
                    x32[n, pl.ds((r * QC + q * 2 + k) * 16, 16), :] = c_in[n, r * 8 + q, :, half(k)].astype(F32)
            return carry

        loop(8, unpick, unroll=8)

        for peer, place in zip([*near_peers, near], [*near_places, None]):
            slot = d_in if peer is near else d
            for t in range(2):
                for r in range(2):
                    slot[n, peer, t, r] = x32[n, pl.ds(r * QC * 16 + peer * 2 + t, QC, stride=16), :].astype(BF)
            if peer is not near:
                push(d.at[n, peer], d_in.at[n, near], G_D + n, place)

    def step_e(n):
        arrived(d_in.at[n, pl.ds(0, NEAR - 1)], G_D + n)

    def order(cell, row):
        found = (row & 0xC1) | ((row & 6) << 3) | ((row & 48) >> 2) | ((row & 8) >> 2)
        return jnp.where(cell == found, 1.0, 0.0).astype(BF)

    loads[0].wait()
    loads[1].wait()
    turn_in(frames)
    w_in[...] = w_in_t[...].astype(F32).T.astype(BF)

    def value_row(slot, peer, low):
        r = peer * 2 + low
        for t in range(2):
            x = turned(r, t)
            xb[r, :, half(t)] = x.astype(BF)
            off = x - jnp.mean(x, axis=0, keepdims=True)
            rstd = lax.rsqrt(jnp.mean(off * off, axis=0, keepdims=True) + EPS)
            u = off * rstd
            unit[r, :, half(t)] = u
            inv[r, :, half(t)] = jnp.broadcast_to(rstd, (8, LANES))
            nb[r, :, half(t)] = u.astype(BF)
        value, slope = gelu_parts(dot(w_in[HC:CH], nb[r]))
        dgelu[r, HC:CH] = slope
        value = value.astype(BF)
        for n in VALUES:
            for t in range(2):
                slot[n, peer, t, low] = value[n * QC : (n + 1) * QC, half(t)]

    for first in range(0, NEAR, 2):
        group = [*near_peers, near][first : first + 2]
        for peer in group:
            for low in range(2):
                value_row(a_in if peer is near else a, peer, low)
        if first == 0:
            pl.semaphore_wait(barrier, len(peers))
        for peer in group:
            if peer is not near:
                push(a.at[0, peer], a_in.at[0, near], G_A, near_device(peer))
    step_a(1)

    loads[2].wait()
    turn_in(cot)

    def cot_row(r, pack):
        t0, t1 = turned(r, 0).astype(BF), turned(r, 1).astype(BF)
        u3[r + 1, CH : 2 * CH, half(0)] = t0
        u3[r + 1, CH : 2 * CH, half(1)] = t1
        return edges(pack, t0, t1, r)

    pack = loop(ROWS, cot_row, jnp.zeros((CH, LANES), BF), unroll=8)
    send_halo(u3, pack, 0, G_ROW0, G_PACK0)

    def grid_gate_row(r, carry):
        value, slope = gelu_parts(dot(w_in[0:HC], nb[r]))
        gates[r, 0:HC] = value.astype(BF)
        dgelu[r, 0:HC] = slope
        return carry

    loop(ROWS, grid_gate_row, unroll=8)

    def block_gate_row(r, carry):
        value, slope = gelu_parts(dot(w_in[CH:], nb[r]))
        dgelu[r, CH:] = slope
        value = value.astype(BF)
        gates[r, HC:CH] = value[0:HC]
        bval[r] = value[HC:]
        return carry

    loop(ROWS, block_gate_row, unroll=8)
    for load in loads[3:]:
        load.wait()
    down_axis = lax.broadcasted_iota(jnp.int32, (COLS, COLS), 0)
    along_axis = lax.broadcasted_iota(jnp.int32, (COLS, COLS), 1)
    gather[...] = order(along_axis, down_axis)
    spread[...] = order(down_axis, along_axis)
    mixp[...] = dot(dot(gather[...], grid_mix[...]).astype(BF), spread[...]).astype(BF)
    mixp_t[...] = dot(dot_nt(gather[...], grid_mix[...]).astype(BF), spread[...]).astype(BF)

    back_w = jnp.concatenate(
        [jnp.concatenate([conv_w[2 - a, 2 - b] for a in range(3)], axis=1) for b in range(3)], axis=0
    ).astype(F32).T.astype(BF)
    w_out_t = w_out[...].astype(F32).T.astype(BF)
    take_halo(u3, 0, G_ROW0, G_PACK0)

    def back_row(r, carry):
        total, carry = conv_step(back_w, u3, r, carry)
        g = (total + u3[r + 1, CH : 2 * CH].astype(F32)).astype(BF)
        gj[r] = g
        up_gated = dot(w_out_t, g)
        gg[r] = up_gated
        mixed = (up_gated[0:HC] * gates[r, 0:HC].astype(F32)).astype(BF)
        for n in range(2):
            for t in range(2):
                a[2 + n, r // 2, t, r % 2] = mixed[n * QC : (n + 1) * QC, half(t)]
        return carry

    step_b(0)
    carry = conv_start(back_w, u3)
    for first in range(0, NEAR, 2):
        if first == NEAR // 2:
            step_b(1)
        for r in range(2 * first, 2 * first + 4):
            carry = back_row(r, carry)
        for peer in (first, first + 1):

            @pl.when(peer != near)
            def _():
                push(a.at[2, peer], a_in.at[2, near], G_A + 2, near_device(peer))

    step_a(3)
    for n in BACKS:
        a_in[n, near] = a[n, near]


    def put(ref):
        def store(k, t, value):
            ref[k, :, half(t)] = value

        return store

    swap_granules(lambda k, t: bval[k, :, half(t)], put(xt), HC)
    values = xt[...].reshape(ROWS * HC, COLS)
    mixed = dot_nt(values, block_mix[...]).astype(BF)
    swap_granules(lambda k, t: mixed[k * HC : (k + 1) * HC, half(t)], put(bm), HC)

    step_c(0, mixp)
    step_b(2)
    step_c(1, mixp)
    step_b(3)

    def block_back(k, t):
        return (gg[k, HC:, half(t)] * gates[k, HC:, half(t)].astype(F32)).astype(BF)

    swap_granules(block_back, put(bt), HC)
    backs = bt[...].reshape(ROWS * HC, COLS)
    unmixed = dot(backs, block_mix[...]).astype(BF)
    swap_granules(lambda k, t: unmixed[k * HC : (k + 1) * HC, half(t)], put(gbv), HC)
    part_block = dot_tn(backs, values).astype(BF)
    se[2 * COLS : 3 * COLS] = part_block[:, half(0)]
    se[3 * COLS :] = part_block[:, half(1)]

    def block_before_row(r, carry):
        d = dgelu[r, CH:]
        gbef[r, CH : CH + HC] = (d[0:HC] * (gg[r, HC:] * (bm[r].astype(F32) + 1.0))).astype(BF)
        gbef[r, CH + HC :] = (d[HC:] * gbv[r].astype(F32)).astype(BF)
        gbef[r, HC:CH] = jnp.zeros((HC, COLS), BF)
        return carry

    loop(ROWS, block_before_row, unroll=4)
    for k in (0, 1, ROWS + 2, ROWS + 3):
        jp[k] = jnp.zeros((CH, COLS), BF)

    step_d(0)
    step_d(1)
    step_c(2, mixp_t)
    step_c(3, mixp_t)

    part_grid = (dot_nt(table(2), table(0)) + dot_nt(table(3), table(1))).astype(BF)
    part_grid = dot(dot(spread[...], part_grid).astype(BF), gather[...]).astype(BF)
    se[0:COLS] = part_grid[:, half(0)]
    se[COLS : 2 * COLS] = part_grid[:, half(1)]
    push(se.at[pl.ds(pl.multiple_of(512 - mine, 512), 512)], re0, G_E0, near_device(twin))

    step_e(0)
    step_e(1)

    arrived(re0, G_E0)
    e0[...] = (se[pl.ds(pl.multiple_of(mine, 512), 512)].astype(F32) + re0[...].astype(F32)).astype(BF)
    over_y(lambda peer: e0.at[pl.ds(pl.multiple_of(peer * 128, 128), 128)], re1.at[level], G_E1)
    re1[level] = e0[pl.ds(pl.multiple_of(level * 128, 128), 128)]

    def returned(chains, r):
        return [
            jnp.concatenate([d_in[n, r // 2, t, lax.rem(r, 2)] for n in chains], axis=0).astype(F32) for t in range(2)
        ]

    def joined_row(r, pack):
        grid_mixed = returned(VALUES, r)
        for t in range(2):
            gates_t = gates[r, :, half(t)].astype(F32)
            more = grid_mixed[t] + 1.0
            gated[r, 0:HC, half(t)] = (gates_t[0:HC] * more).astype(BF)
            gated[r, HC:, half(t)] = (gates_t[HC:] * (bm[r, :, half(t)].astype(F32) + 1.0)).astype(BF)
            gbef[r, 0:HC, half(t)] = (dgelu[r, 0:HC, half(t)] * (gg[r, 0:HC, half(t)] * more)).astype(BF)
        j = (xb[r].astype(F32) + dot(w_out[...], gated[r])).astype(BF)
        jp[r + 2] = j
        v3[r + 1, CH : 2 * CH] = j
        return edges(pack, j[:, half(0)], j[:, half(1)], r)

    pack = loop(ROWS, joined_row, jnp.zeros((CH, LANES), BF), unroll=8)

    def pixels(ref, rows=slice(None)):
        return jnp.concatenate([ref[r, rows] for r in range(ROWS)], axis=1)

    p_conv = dot_nt(
        jnp.concatenate([u3[p] for p in range(ROWS + 2)], axis=1),
        jnp.concatenate([jp[p : p + 3].reshape(3 * CH, COLS) for p in range(ROWS + 2)], axis=1),
    )
    p_in = dot_nt(pixels(nb), pixels(gbef))
    p_out = dot_nt(pixels(gj), pixels(gated))
    st[0 : 3 * CH] = p_conv[:, half(0)].astype(BF)
    st[3 * CH : 4 * CH] = p_in.astype(BF)
    third = p_conv[:, 2 * CH :]
    st[4 * CH :] = jnp.concatenate(
        [third[: 2 * CH], jnp.concatenate([third[2 * CH :], p_out], axis=0)], axis=1
    ).astype(BF)
    over_near(lambda peer: st.at[pl.ds(pl.multiple_of(peer * 48, 16), 48)], rt1.at[near], G_T1)
    rt1[near] = st[pl.ds(pl.multiple_of(near * 48, 16), 48)]
    send_halo(v3, pack, 1, G_ROW1, G_PACK1)

    arrived(re1.at[pl.ds(0, 3)], G_E1)
    total = re1[0].astype(F32)
    for k in range(1, 4):
        total = total + re1[k].astype(F32)
    e1[...] = total
    over_x(lambda peer: e1.at[pl.ds(pl.multiple_of(peer * 32, 32), 32)], re2.at[across], G_E2)
    re2[across] = e1[pl.ds(pl.multiple_of(across * 32, 32), 32)]

    step_d(2)
    step_d(3)

    take_halo(v3, 1, G_ROW1, G_PACK1)

    for n in VALUES + BACKS:
        for ref, count, g in ((a_in, NEAR, G_A), (b_in, FAR, G_B), (c_in, FAR, G_C)):
            gone(ref.at[n, pl.ds(0, count - 1)], g + n)
    for n in VALUES:
        gone(d_in.at[n, pl.ds(0, NEAR - 1)], G_D + n)

    from_near(rt1, G_T1)
    total = rt1[0].astype(F32)
    for k in range(1, NEAR):
        total = total + rt1[k].astype(F32)
    t1[...] = total.astype(BF)
    over_x(lambda peer: t1, rt2.at[across], G_T2)
    rt2[across] = t1[...]

    arrived(re2.at[pl.ds(0, 3)], G_E2)
    e2[...] = re2[0] + re2[1] + re2[2] + re2[3]
    over_z(lambda peer: e2, re3.at[deep], G_E3)
    re3[deep] = e2[...]

    conv_k = jnp.concatenate(
        [jnp.concatenate([conv_w[a, b] for b in range(3)], axis=1) for a in range(3)], axis=0
    )

    def out_row(r, carry):
        total, carry = conv_step(conv_k, v3, r, carry)
        total = total + v3[r + 1, CH : 2 * CH].astype(F32)
        for t in range(2):
            rest_out[t, pl.ds(r * CH, CH), :] = total[:, half(t)]
        return carry

    carry = loop(ROWS // 2, out_row, conv_start(conv_k, v3), unroll=8)

    step_e(2)
    step_e(3)

    def value_before_row(r, carry):
        grid_back = returned(BACKS, r)
        for t in range(2):
            gbef[r, HC:CH, half(t)] = (dgelu[r, HC:CH, half(t)] * grid_back[t]).astype(BF)
        return carry

    loop(ROWS, value_before_row, unroll=4)
    p_value = dot_nt(pixels(gbef, slice(HC, CH)), pixels(nb))
    sq[...] = jnp.concatenate([p_value[0:16], p_value[16:]], axis=1).astype(BF)
    over_near(lambda peer: sq, rq1.at[near], G_Q1)
    rq1[near] = sq[...]

    arrived(re3.at[pl.ds(0, 3)], G_E3)
    e3[...] = (re3[0] + re3[1] + re3[2] + re3[3]).astype(BF)
    over_x(lambda peer: e3, re4.at[across], G_E4)
    re4[across] = e3[...]

    arrived(rt2.at[pl.ds(0, 3)], G_T2)
    total = rt2[0].astype(F32)
    for k in range(1, 4):
        total = total + rt2[k].astype(F32)
    t2[...] = total.astype(BF)
    over_z(lambda peer: t2, rt3.at[deep], G_T3)
    rt3[deep] = t2[...]

    def frame_row(r, carry):
        normed = dot(w_in_t[...], gbef[r])
        u = unit[r]
        mean_grad = jnp.mean(normed, axis=0, keepdims=True)
        mean_proj = jnp.mean(normed * u, axis=0, keepdims=True)
        source = gj[r].astype(F32) + inv[r, 0:1] * (normed - mean_grad - u * mean_proj)
        for t in range(2):
            gframe_out[t, pl.ds(r * CH, CH), :] = source[:, half(t)]
        return carry

    loop(ROWS, frame_row, unroll=8)

    from_near(rq1, G_Q1)
    total = rq1[0].astype(F32)
    for k in range(1, NEAR):
        total = total + rq1[k].astype(F32)
    q1[...] = total.astype(BF)
    over_far(lambda peer: q1, rq2.at[far], G_Q2)
    rq2[far] = q1[...]

    arrived(re4.at[pl.ds(0, 3)], G_E4)
    over_y(lambda peer: re4, re5.at[level], G_E5)
    re5[level] = re4[...]

    arrived(rt3.at[pl.ds(0, 3)], G_T3)
    total = rt3[0].astype(F32)
    for k in range(1, 4):
        total = total + rt3[k].astype(F32)
    t3[...] = total.astype(BF)
    over_near(lambda peer: t3, rt4.at[near], G_T4)
    rt4[near] = t3[...]


    loop(ROWS // 2, lambda r, carry: out_row(r + ROWS // 2, carry), carry, unroll=8)

    arrived(re5.at[pl.ds(0, 3)], G_E5)
    push(re5, re6, G_E6, near_device(twin))
    early_out[pl.ds(pl.multiple_of(mine, 512), 512)] = re5[...].reshape(512, LANES)

    from_far(rq2, G_Q2)
    total = rq2[0].astype(F32)
    for k in range(1, FAR):
        total = total + rq2[k].astype(F32)
    value_out[...] = total
    from_near(rt4, G_T4)
    tail_out[...] = rt4[...]
    arrived(re6, G_E6)
    early_out[pl.ds(pl.multiple_of(512 - mine, 512), 512)] = re6[...].reshape(512, LANES)

    for which, g_row, g_pack in ((0, G_ROW0, G_PACK0), (1, G_ROW1, G_PACK1)):
        gone(row_in.at[which], g_row)
        gone(pack_in.at[which], g_pack)
    for n in BACKS:
        gone(d_in.at[n, pl.ds(0, NEAR - 1)], G_D + n)
    for ref, g in ((rt1, G_T1), (rt4, G_T4), (rq1, G_Q1)):
        gone(ref.at[pl.ds(0, NEAR - 1)], g)
    gone(rq2.at[pl.ds(0, FAR - 1)], G_Q2)
    gone(re0, G_E0)
    for ref, g in ((re1, G_E1), (re2, G_E2), (re3, G_E3), (re4, G_E4), (re5, G_E5), (rt2, G_T2), (rt3, G_T3)):
        gone(ref.at[pl.ds(0, 3)], g)
    gone(re6, G_E6)


def finish(rest, gframe, early, tail, value, *refs):
    outs, sem = (refs[:7], refs[7:14]), refs[14]
    restored, grad_frames, grad_w_in_t, grad_grid, grad_block, grad_w_out, grad_conv = outs[1]
    copies = []

    def leave(k, part=None):
        src, dst = outs[1][k], outs[0][k]
        if part is not None:
            src, dst = src.at[part], dst.at[part]
        copies.append(pltpu.make_async_copy(src, dst, sem.at[len(copies)]))
        copies[-1].start()

    def turn_out(src, dst, k):
        for first in range(0, CH, CH // 2):

            def channel(c, carry):
                for t in range(2):
                    dst[first + c, :, half(t)] = src[t, pl.ds(first + c, ROWS, stride=CH), :].astype(BF)
                return carry

            loop(CH // 2, channel, unroll=16)
            leave(k, pl.ds(first, CH // 2))

    scale = float(ROWS * NA * COLS * NW) ** (-0.5)
    for k in range(2):
        grad_grid[:, half(k)] = early[k * COLS : (k + 1) * COLS].astype(F32) * scale
        grad_block[:, half(k)] = early[(2 + k) * COLS : (3 + k) * COLS].astype(F32) * scale
    leave(3)
    leave(4)
    turn_out(gframe, grad_frames, 1)
    turn_out(rest, restored, 0)
    quarter = value[...] * scale
    zeros = jnp.zeros((HC, CH), F32)
    quarter = jnp.concatenate([zeros, quarter[:, :CH], quarter[:, CH:], zeros, zeros], axis=0)
    grad_w_in_t[...] = tail[3 * CH : 4 * CH].astype(F32) * scale + quarter.T
    leave(2)
    last = tail[4 * CH :].astype(F32) * scale
    grad_w_out[...] = last[CH:, CH:]
    leave(5)
    for b in range(3):
        rows = slice((2 - b) * CH, (3 - b) * CH)
        pair = tail[rows].astype(F32) * scale
        grad_conv[0, b] = pair[:, :CH]
        grad_conv[1, b] = pair[:, CH:]
    grad_conv[2, 2] = last[:CH, :CH]
    grad_conv[2, 1] = last[CH:, :CH]
    grad_conv[2, 0] = last[:CH, CH:]
    leave(6)
    for copy in copies:
        copy.wait()


def vm(*shape, dtype=BF):
    return pltpu.VMEM(shape, dtype)


def exchange():
    message_w = vm(4, NEAR, 2, 2, QC, LANES)
    message_a = vm(4, FAR, 16, 256)
    return [message_w, message_w, vm(4, 2 * 16 * QC, LANES, dtype=F32)] + [message_a] * 4 + [message_w] * 2


SCRATCH = [
    vm(CH, ROWS, COLS),
    vm(CH, 2 * CH),
    vm(COLS, COLS),
    vm(COLS, COLS),
    vm(CH, CH),
    vm(3, 3, CH, CH),
    vm(CH, ROWS, COLS),
    vm(2 * CH, CH),
    vm(2, CH * ROWS, LANES, dtype=F32),
    vm(ROWS, CH, COLS),
    vm(ROWS, CH, COLS),
    vm(ROWS, CH, COLS, dtype=F32),
    vm(ROWS, 8, COLS, dtype=F32),
    vm(ROWS, 2 * CH, COLS, dtype=F32),
    vm(ROWS, CH, COLS),
    vm(ROWS, HC, COLS),
    vm(ROWS + 2, 3 * CH, COLS),
    vm(ROWS + 2, 3 * CH, COLS),
    vm(ROWS, CH, COLS),
    vm(ROWS, CH, COLS, dtype=F32),
    vm(ROWS, HC, COLS),
    vm(ROWS, HC, COLS),
    vm(ROWS, HC, COLS),
    vm(ROWS, HC, COLS),
    *exchange(),
    vm(ROWS, CH, COLS),
    vm(ROWS, 2 * CH, COLS),
    vm(ROWS + 4, CH, COLS),
    vm(2, 2, CH, COLS),
    vm(2, 32, LANES),
    vm(2, 96, LANES),
    vm(CH, LANES),
    vm(CH, LANES),
    vm(COLS, COLS),
    vm(COLS, COLS),
    vm(COLS, COLS),
    vm(COLS, COLS),
    vm(4 * COLS, LANES),
    vm(512, LANES),
    vm(512, LANES),
    vm(4, 128, LANES),
    vm(128, LANES, dtype=F32),
    vm(4, 32, LANES, dtype=F32),
    vm(32, LANES, dtype=F32),
    vm(4, 32, LANES, dtype=F32),
    vm(32, LANES),
    vm(4, 32, LANES),
    vm(4, 4, 32, LANES),
    vm(4, 4, 32, LANES),
    vm(6 * CH, LANES),
    vm(NW, 48, LANES),
    vm(48, LANES),
    vm(4, 48, LANES),
    vm(48, LANES),
    vm(4, 48, LANES),
    vm(48, LANES),
    vm(NEAR, 48, LANES),
    vm(16, LANES),
    vm(NEAR, 16, LANES),
    vm(16, LANES),
    vm(FAR, 16, LANES),
    pltpu.SemaphoreType.DMA((GROUPS,)),
    pltpu.SemaphoreType.DMA((GROUPS,)),
    pltpu.SemaphoreType.DMA((7,)),
]


def body(frames, w_in, grid_mix, block_mix, w_out, conv_w, cotangent):
    operands = (frames, w_in.T, grid_mix, block_mix, w_out, conv_w, cotangent)
    vmem = pl.BlockSpec(memory_space=pltpu.VMEM)
    shape = jax.ShapeDtypeStruct
    rest, gframe, early, tail, value = pl.pallas_call(
        kernel,
        out_shape=(
            shape((2, ROWS * CH, LANES), F32),
            shape((2, ROWS * CH, LANES), F32),
            shape((4 * COLS, LANES), BF),
            shape((NEAR, 48, LANES), BF),
            shape((16, LANES), F32),
        ),
        in_specs=[pl.BlockSpec(memory_space=pltpu.HBM)] * 7,
        out_specs=(vmem,) * 5,
        scratch_shapes=SCRATCH,
        compiler_params=pltpu.CompilerParams(
            collective_id=0, has_side_effects=True, vmem_limit_bytes=32 * 1024 * 1024
        ),
    )(*[pltpu.with_memory_space_constraint(x, pltpu.HBM) for x in operands])
    restored, grad_frames, grad_w_in_t, grad_grid, grad_block, grad_w_out, grad_conv = pl.pallas_call(
        finish,
        out_shape=(
            shape((CH, ROWS, COLS), BF),
            shape((CH, ROWS, COLS), BF),
            shape((CH, 2 * CH), F32),
            shape((COLS, COLS), F32),
            shape((COLS, COLS), F32),
            shape((CH, CH), F32),
            shape((3, 3, CH, CH), F32),
        ),
        in_specs=[vmem] * 5,
        out_specs=(pl.BlockSpec(memory_space=pl.ANY),) * 7,
        scratch_shapes=[
            vm(CH, ROWS, COLS),
            vm(CH, ROWS, COLS),
            vm(CH, 2 * CH, dtype=F32),
            vm(COLS, COLS, dtype=F32),
            vm(COLS, COLS, dtype=F32),
            vm(CH, CH, dtype=F32),
            vm(3, 3, CH, CH, dtype=F32),
            pltpu.SemaphoreType.DMA((9,)),
        ],
        compiler_params=pltpu.CompilerParams(vmem_limit_bytes=16 * 1024 * 1024),
    )(rest, gframe, early, tail.reshape(6 * CH, LANES), value)
    return restored, grad_frames, grad_w_in_t.T, grad_grid, grad_block, grad_w_out, grad_conv


def solution(mesh):
    placed = (P(None, "ha", "wa"), P(), P(), P(), P(), P(), P(None, "ha", "wa"))
    return jax.shard_map(
        body,
        mesh=mesh,
        in_specs=placed,
        out_specs=(P(None, "ha", "wa"), P(None, "ha", "wa"), P(), P(), P(), P(), P()),
        check_vma=False,
    )
```

```python
import jax
import jax.numpy as jnp
from jax import lax
from jax.experimental import pallas as pl
from jax.experimental.pallas import tpu as pltpu
from jax.sharding import PartitionSpec as P

BF = jnp.bfloat16
F32 = jnp.float32
EPS = 1e-06
MESH = pl.DeviceIdType.MESH

CH = 64
HC = 32
ROWS = 16
COLS = 256
LANES = 128
NA = 16
NW = 8
NEAR = 8
FAR = 16

(G_ROW0, G_PACK0, G_ROW1, G_PACK1) = range(4)
(G_E0, G_E1, G_E2, G_E3, G_E4, G_E5, G_E6, G_T1, G_T2, G_T3, G_Q1, G_Q2) = range(4, 16)
VALUES, BACKS = (0, 1), (2, 3)
G_A, G_B, G_C, G_D = 16, 20, 24, 28
GROUPS = 32
QC = 16


def dot(a, b):
    return lax.dot_general(a, b, (((1,), (0,)), ((), ())), preferred_element_type=F32)


def dot_nt(a, b):
    return lax.dot_general(a, b, (((1,), (1,)), ((), ())), preferred_element_type=F32)


def dot_tn(a, b):
    return lax.dot_general(a, b, (((0,), (0,)), ((), ())), preferred_element_type=F32)


def swap_granules(load, store, depth):
    lane = lax.broadcasted_iota(jnp.int16, (depth, LANES), 1)
    for row_half in range(2):
        for col_half in range(2):
            held = [load(row_half * 8 + k, col_half) for k in range(8)]
            for s in range(3):
                width = 16 << s
                low = (lane & width) == 0
                for k in range(8):
                    if not k & (1 << s):
                        a, b = held[k], held[k | (1 << s)]
                        held[k] = jnp.where(low, a, pltpu.roll(b, width, 1))
                        held[k | (1 << s)] = jnp.where(low, pltpu.roll(a, LANES - width, 1), b)
            for k in range(8):
                store(col_half * 8 + k, row_half, held[k])


def half(t):
    return slice(t * LANES, (t + 1) * LANES)


def loop(count, step, carry=0, unroll=1):
    return lax.fori_loop(0, count, step, carry, unroll=unroll)


def gelu_parts(x):
    root = 0.7978845608028654
    cube = root * 0.044715
    square = x * x
    h = 0.5 * jnp.tanh(x * (cube * square + root)) + 0.5
    value = x * h
    return value, h + value * (1.0 - h) * ((6.0 * cube) * square + 2.0 * root)


def kernel(
    frames_hbm, w_in_t_hbm, grid_mix_hbm, block_mix_hbm, w_out_hbm, conv_w_hbm, cot_hbm,
    rest_out, gframe_out, early_out, tail_out, value_out,
    frames, w_in_t, grid_mix, block_mix, w_out, conv_w, cot, w_in,
    turn, xb, nb, unit, inv, dgelu, gates, bval, u3, v3, gj, gg, xt, bt, bm, gbv,
    a, a_in, x32, b, b_in, c, c_in, d, d_in,
    gated, gbef, jp, row_in, pack_out, pack_in, edge_l, edge_r,
    mixp, mixp_t, gather, spread, se, re0, e0, re1, e1, re2, e2, re3, e3, re4, re5, re6,
    st, rt1, t1, rt2, t2, rt3, sq, rq1, q1, rq2,
    ssem, rsem, isem,
):
    ia = lax.axis_index("ha")
    iw = lax.axis_index("wa")
    up, down = lax.rem(ia + NA - 1, NA), lax.rem(ia + 1, NA)
    left, right = lax.rem(iw + NW - 1, NW), lax.rem(iw + 1, NW)
    lane = lax.broadcasted_iota(jnp.int16, (CH, LANES), 1)
    lane_wide = lax.broadcasted_iota(jnp.int32, (CH, LANES), 1)

    loads = [
        pltpu.make_async_copy(src, dst, isem.at[k])
        for k, (src, dst) in enumerate(
            [
                (frames_hbm, frames),
                (w_in_t_hbm, w_in_t),
                (cot_hbm, cot),
                (conv_w_hbm, conv_w),
                (w_out_hbm, w_out),
                (block_mix_hbm, block_mix),
                (grid_mix_hbm, grid_mix),
            ]
        )
    ]
    for load in loads:
        load.start()

    def push(src, dst, g, where):
        pltpu.make_async_remote_copy(
            src_ref=src, dst_ref=dst, send_sem=ssem.at[g], recv_sem=rsem.at[g], device_id=where, device_id_type=MESH
        ).start()

    near = lax.rem(iw, 2) * 4 + lax.rem(ia, 4)
    far = ia // 4 * 4 + iw // 2

    def near_device(peer):
        return ia // 4 * 4 + lax.rem(peer, 4), iw // 2 * 2 + peer // 4

    def far_device(peer):
        return peer // 4 * 4 + lax.rem(ia, 4), lax.rem(peer, 4) * 2 + lax.rem(iw, 2)

    near_peers = [lax.rem(near + k, NEAR) for k in range(1, NEAR)]
    far_peers = [lax.rem(far + k, FAR) for k in range(1, FAR)]
    twin = near + 1 - 2 * lax.rem(near, 2)

    near_places = [near_device(peer) for peer in near_peers]
    far_places = [far_device(peer) for peer in far_peers]

    def over_near(src_of, dst, g):
        for peer, place in zip(near_peers, near_places):
            push(src_of(peer), dst, g, place)

    def over_far(src_of, dst, g):
        for peer, place in zip(far_peers, far_places):
            push(src_of(peer), dst, g, place)

    def over_x(src_of, dst, g):
        for k in range(1, 4):
            peer = lax.rem(iw // 2 + k, 4)
            push(src_of(peer), dst, g, (ia, peer * 2 + lax.rem(iw, 2)))

    def over_z(src_of, dst, g):
        for k in range(1, 4):
            peer = lax.rem(ia // 4 + k, 4)
            push(src_of(peer), dst, g, (peer * 4 + lax.rem(ia, 4), iw))

    def over_y(src_of, dst, g):
        for k in range(1, 4):
            peer = lax.rem(near + 2 * k, NEAR)
            push(src_of(peer // 2), dst, g, near_device(peer))

    def arrived(ref, g):
        pltpu.make_async_copy(ref, ref, rsem.at[g]).wait()

    def gone(ref, g):
        pltpu.make_async_copy(ref, ref, ssem.at[g]).wait()

    def from_near(ref, g):
        arrived(ref.at[pl.ds(0, NEAR - 1)], g)

    def from_far(ref, g):
        arrived(ref.at[pl.ds(0, FAR - 1)], g)

    mine = lax.rem(near, 2) * 512
    level, across, deep = near // 2, iw // 2, ia // 4

    barrier = pltpu.get_barrier_semaphore()
    peers = [near_device(peer) for peer in near_peers]
    peers += [far_device(peer) for peer in far_peers]
    peers += [(a, b) for a in (up, ia, down) for b in (left, right)] + [(up, iw), (down, iw)]
    for peer in peers:
        pl.semaphore_signal(barrier, inc=1, device_id=peer, device_id_type=MESH)

    def turn_in(src):
        for t in range(2):
            turn[t] = src[:, :, half(t)].astype(F32).reshape(CH * ROWS, LANES)

    def turned(r, t):
        return turn[t, pl.ds(r, CH, stride=ROWS), :]

    def edges(pack, t0, t1, r):
        pack = jnp.where(lane_wide == r, pltpu.roll(t0, r, 1), pack)
        return jnp.where(lane_wide == ROWS + r, pltpu.roll(t1, r + 17, 1), pack)

    def send_halo(field, pack, which, g_row, g_pack):
        pack_out[which] = jnp.concatenate([pack, jnp.zeros_like(pack)], axis=0).T[0:32]
        push(field.at[1, CH : 2 * CH], row_in.at[which, 1], g_row, (up, iw))
        push(field.at[ROWS, CH : 2 * CH], row_in.at[which, 0], g_row, (down, iw))
        for slot, where in enumerate(
            [(ia, right), (down, right), (up, right), (ia, left), (down, left), (up, left)]
        ):
            part = pack_out.at[which, pl.ds(16 if slot < 3 else 0, 16)]
            push(part, pack_in.at[which, pl.ds(16 * slot, 16)], g_pack, where)

    def take_halo(field, which, g_row, g_pack):
        arrived(row_in.at[which], g_row)
        arrived(pack_in.at[which], g_pack)
        field[0, CH : 2 * CH] = jnp.where(ia > 0, row_in[which, 0], jnp.zeros((CH, COLS), BF))
        field[ROWS + 1, CH : 2 * CH] = jnp.where(ia < NA - 1, row_in[which, 1], jnp.zeros((CH, COLS), BF))
        first = jnp.where(ia > 0, 0, 1)
        last = jnp.where(ia < NA - 1, ROWS + 2, ROWS + 1)
        got = jnp.concatenate([pack_in[which], jnp.zeros((32, LANES), BF)], axis=0).T[0:CH]

        def assemble(middle, above, below, has):
            joined = jnp.where(lane == 0, above, jnp.where(lane == ROWS + 1, below, middle))
            inside = (lane_wide >= first) & (lane_wide < jnp.where(has, last, 0))
            return jnp.where(inside, joined, jnp.zeros_like(joined))

        edge_l[...] = assemble(pltpu.roll(got, 1, 1), pltpu.roll(got, 97, 1), pltpu.roll(got, 113, 1), iw > 0)
        edge_r[...] = assemble(pltpu.roll(got, 81, 1), pltpu.roll(got, 49, 1), pltpu.roll(got, 65, 1), iw < NW - 1)

        def shifts(p, carry):
            t0 = field[p, CH : 2 * CH, half(0)]
            t1 = field[p, CH : 2 * CH, half(1)]
            a0, a1 = pltpu.roll(t0, 1, 1), pltpu.roll(t1, 1, 1)
            b0, b1 = pltpu.roll(t0, LANES - 1, 1), pltpu.roll(t1, LANES - 1, 1)
            lh = pltpu.roll(edge_l[...], lax.rem(LANES - p, LANES), 1)
            rh = pltpu.roll(edge_r[...], LANES - 1 - p, 1)
            field[p, 0:CH, half(0)] = jnp.where(lane == 0, lh, a0)
            field[p, 0:CH, half(1)] = jnp.where(lane == 0, a0, a1)
            field[p, 2 * CH :, half(0)] = jnp.where(lane == LANES - 1, b1, b0)
            field[p, 2 * CH :, half(1)] = jnp.where(lane == LANES - 1, rh, b1)
            return carry

        loop(ROWS + 2, shifts, unroll=9)

    def conv_start(w, field):
        y = dot(w, field[0])
        z = dot(w, field[1])
        return z[0:CH], y[0:CH] + z[CH : 2 * CH]

    def conv_step(w, field, r, carry):
        later, now = carry
        y = dot(w, field[r + 2])
        return now + y[2 * CH :], (y[0:CH], later + y[CH : 2 * CH])

    def step_a(n):
        over_near(lambda peer: a.at[n, peer], a_in.at[n, near], G_A + n)

    def step_b(n):
        arrived(a_in.at[n, pl.ds(0, NEAR - 1)], G_A + n)

        def widen(j, carry):
            for t in range(2):
                for r in range(2):
                    x32[n, pl.ds((r * 16 + j * 2 + t) * QC, QC), :] = a_in[n, j, t, r].astype(F32)
            return carry

        loop(NEAR, widen, unroll=8)

        for peer, place in zip([*far_peers, far], [*far_places, None]):
            base = peer // 8 * (16 * QC) + lax.rem(peer, 8) * 2
            slot = b_in if peer is far else b
            for k in range(2):
                slot[n, peer, :, half(k)] = x32[n, pl.ds(base + k, 16, stride=QC), :].astype(BF)
            if peer is not far:
                push(b.at[n, peer], b_in.at[n, far], G_B + n, place)

    def table(n):
        return b_in[n].reshape(256, 256)

    def step_c(n, mix):
        arrived(b_in.at[n, pl.ds(0, FAR - 1)], G_B + n)
        c[n] = dot(mix[...], table(n)).astype(BF).reshape(FAR, 16, 256)
        over_far(lambda peer: c.at[n, peer], c_in.at[n, far], G_C + n)
        c_in[n, far] = c[n, far]

    def step_d(n):
        arrived(c_in.at[n, pl.ds(0, FAR - 1)], G_C + n)

        def unpick(q, carry):
            for r in range(2):
                for k in range(2):
                    x32[n, pl.ds((r * QC + q * 2 + k) * 16, 16), :] = c_in[n, r * 8 + q, :, half(k)].astype(F32)
            return carry

        loop(8, unpick, unroll=8)

        for peer, place in zip([*near_peers, near], [*near_places, None]):
            slot = d_in if peer is near else d
            for t in range(2):
                for r in range(2):
                    slot[n, peer, t, r] = x32[n, pl.ds(r * QC * 16 + peer * 2 + t, QC, stride=16), :].astype(BF)
            if peer is not near:
                push(d.at[n, peer], d_in.at[n, near], G_D + n, place)

    def step_e(n):
        arrived(d_in.at[n, pl.ds(0, NEAR - 1)], G_D + n)

    def order(cell, row):
        found = (row & 0xC1) | ((row & 6) << 3) | ((row & 48) >> 2) | ((row & 8) >> 2)
        return jnp.where(cell == found, 1.0, 0.0).astype(BF)

    loads[0].wait()
    loads[1].wait()
    turn_in(frames)
    w_in[...] = w_in_t[...].astype(F32).T.astype(BF)

    def value_row(slot, peer, low):
        r = peer * 2 + low
        for t in range(2):
            x = turned(r, t)
            xb[r, :, half(t)] = x.astype(BF)
            off = x - jnp.mean(x, axis=0, keepdims=True)
            rstd = lax.rsqrt(jnp.mean(off * off, axis=0, keepdims=True) + EPS)
            u = off * rstd
            unit[r, :, half(t)] = u
            inv[r, :, half(t)] = jnp.broadcast_to(rstd, (8, LANES))
            nb[r, :, half(t)] = u.astype(BF)
        value, slope = gelu_parts(dot(w_in[HC:CH], nb[r]))
        dgelu[r, HC:CH] = slope
        value = value.astype(BF)
        for n in VALUES:
            for t in range(2):
                slot[n, peer, t, low] = value[n * QC : (n + 1) * QC, half(t)]

    for first in range(0, NEAR, 2):
        group = [*near_peers, near][first : first + 2]
        for peer in group:
            for low in range(2):
                value_row(a_in if peer is near else a, peer, low)
        if first == 0:
            pl.semaphore_wait(barrier, len(peers))
        for peer in group:
            if peer is not near:
                push(a.at[0, peer], a_in.at[0, near], G_A, near_device(peer))
    step_a(1)

    loads[2].wait()
    turn_in(cot)

    def cot_row(r, pack):
        t0, t1 = turned(r, 0).astype(BF), turned(r, 1).astype(BF)
        u3[r + 1, CH : 2 * CH, half(0)] = t0
        u3[r + 1, CH : 2 * CH, half(1)] = t1
        return edges(pack, t0, t1, r)

    pack = loop(ROWS, cot_row, jnp.zeros((CH, LANES), BF), unroll=8)
    send_halo(u3, pack, 0, G_ROW0, G_PACK0)

    def grid_gate_row(r, carry):
        value, slope = gelu_parts(dot(w_in[0:HC], nb[r]))
        gates[r, 0:HC] = value.astype(BF)
        dgelu[r, 0:HC] = slope
        return carry

    loop(ROWS, grid_gate_row, unroll=8)

    def block_gate_row(r, carry):
        value, slope = gelu_parts(dot(w_in[CH:], nb[r]))
        dgelu[r, CH:] = slope
        value = value.astype(BF)
        gates[r, HC:CH] = value[0:HC]
        bval[r] = value[HC:]
        return carry

    loop(ROWS, block_gate_row, unroll=8)
    for load in loads[3:]:
        load.wait()
    down_axis = lax.broadcasted_iota(jnp.int32, (COLS, COLS), 0)
    along_axis = lax.broadcasted_iota(jnp.int32, (COLS, COLS), 1)
    gather[...] = order(along_axis, down_axis)
    spread[...] = order(down_axis, along_axis)
    mixp[...] = dot(dot(gather[...], grid_mix[...]).astype(BF), spread[...]).astype(BF)
    mixp_t[...] = dot(dot_nt(gather[...], grid_mix[...]).astype(BF), spread[...]).astype(BF)

    back_w = jnp.concatenate(
        [jnp.concatenate([conv_w[2 - a, 2 - b] for a in range(3)], axis=1) for b in range(3)], axis=0
    ).astype(F32).T.astype(BF)
    w_out_t = w_out[...].astype(F32).T.astype(BF)
    take_halo(u3, 0, G_ROW0, G_PACK0)

    def back_row(r, carry):
        total, carry = conv_step(back_w, u3, r, carry)
        g = (total + u3[r + 1, CH : 2 * CH].astype(F32)).astype(BF)
        gj[r] = g
        up_gated = dot(w_out_t, g)
        gg[r] = up_gated
        mixed = (up_gated[0:HC] * gates[r, 0:HC].astype(F32)).astype(BF)
        for n in range(2):
            for t in range(2):
                a[2 + n, r // 2, t, r % 2] = mixed[n * QC : (n + 1) * QC, half(t)]
        return carry

    step_b(0)
    carry = conv_start(back_w, u3)
    for first in range(0, NEAR, 2):
        if first == NEAR // 2:
            step_b(1)
        for r in range(2 * first, 2 * first + 4):
            carry = back_row(r, carry)
        for peer in (first, first + 1):

            @pl.when(peer != near)
            def _():
                push(a.at[2, peer], a_in.at[2, near], G_A + 2, near_device(peer))

    step_a(3)
    for n in BACKS:
        a_in[n, near] = a[n, near]


    def put(ref):
        def store(k, t, value):
            ref[k, :, half(t)] = value

        return store

    swap_granules(lambda k, t: bval[k, :, half(t)], put(xt), HC)
    values = xt[...].reshape(ROWS * HC, COLS)
    mixed = dot_nt(values, block_mix[...]).astype(BF)
    swap_granules(lambda k, t: mixed[k * HC : (k + 1) * HC, half(t)], put(bm), HC)

    step_c(0, mixp)
    step_b(2)
    step_c(1, mixp)
    step_b(3)

    def block_back(k, t):
        return (gg[k, HC:, half(t)] * gates[k, HC:, half(t)].astype(F32)).astype(BF)

    swap_granules(block_back, put(bt), HC)
    backs = bt[...].reshape(ROWS * HC, COLS)
    unmixed = dot(backs, block_mix[...]).astype(BF)
    swap_granules(lambda k, t: unmixed[k * HC : (k + 1) * HC, half(t)], put(gbv), HC)
    part_block = dot_tn(backs, values).astype(BF)
    se[2 * COLS : 3 * COLS] = part_block[:, half(0)]
    se[3 * COLS :] = part_block[:, half(1)]

    def block_before_row(r, carry):
        d = dgelu[r, CH:]
        gbef[r, CH : CH + HC] = (d[0:HC] * (gg[r, HC:] * (bm[r].astype(F32) + 1.0))).astype(BF)
        gbef[r, CH + HC :] = (d[HC:] * gbv[r].astype(F32)).astype(BF)
        gbef[r, HC:CH] = jnp.zeros((HC, COLS), BF)
        return carry

    loop(ROWS, block_before_row, unroll=4)
    for k in (0, 1, ROWS + 2, ROWS + 3):
        jp[k] = jnp.zeros((CH, COLS), BF)

    step_d(0)
    step_d(1)
    step_c(2, mixp_t)
    step_c(3, mixp_t)

    part_grid = (dot_nt(table(2), table(0)) + dot_nt(table(3), table(1))).astype(BF)
    part_grid = dot(dot(spread[...], part_grid).astype(BF), gather[...]).astype(BF)
    se[0:COLS] = part_grid[:, half(0)]
    se[COLS : 2 * COLS] = part_grid[:, half(1)]
    push(se.at[pl.ds(pl.multiple_of(512 - mine, 512), 512)], re0, G_E0, near_device(twin))

    step_e(0)
    step_e(1)

    arrived(re0, G_E0)
    e0[...] = (se[pl.ds(pl.multiple_of(mine, 512), 512)].astype(F32) + re0[...].astype(F32)).astype(BF)
    over_y(lambda peer: e0.at[pl.ds(pl.multiple_of(peer * 128, 128), 128)], re1.at[level], G_E1)
    re1[level] = e0[pl.ds(pl.multiple_of(level * 128, 128), 128)]

    def returned(chains, r):
        return [
            jnp.concatenate([d_in[n, r // 2, t, lax.rem(r, 2)] for n in chains], axis=0).astype(F32) for t in range(2)
        ]

    def joined_row(r, pack):
        grid_mixed = returned(VALUES, r)
        for t in range(2):
            gates_t = gates[r, :, half(t)].astype(F32)
            more = grid_mixed[t] + 1.0
            gated[r, 0:HC, half(t)] = (gates_t[0:HC] * more).astype(BF)
            gated[r, HC:, half(t)] = (gates_t[HC:] * (bm[r, :, half(t)].astype(F32) + 1.0)).astype(BF)
            gbef[r, 0:HC, half(t)] = (dgelu[r, 0:HC, half(t)] * (gg[r, 0:HC, half(t)] * more)).astype(BF)
        j = (xb[r].astype(F32) + dot(w_out[...], gated[r])).astype(BF)
        jp[r + 2] = j
        v3[r + 1, CH : 2 * CH] = j
        return edges(pack, j[:, half(0)], j[:, half(1)], r)

    pack = loop(ROWS, joined_row, jnp.zeros((CH, LANES), BF), unroll=8)
    send_halo(v3, pack, 1, G_ROW1, G_PACK1)

    def pixels(ref, rows=slice(None)):
        return jnp.concatenate([ref[r, rows] for r in range(ROWS)], axis=1)

    p_conv = dot_nt(
        jnp.concatenate([u3[p] for p in range(ROWS + 2)], axis=1),
        jnp.concatenate([jp[p : p + 3].reshape(3 * CH, COLS) for p in range(ROWS + 2)], axis=1),
    )
    p_in = dot_nt(pixels(nb), pixels(gbef))
    p_out = dot_nt(pixels(gj), pixels(gated))
    st[0 : 3 * CH] = p_conv[:, half(0)].astype(BF)
    st[3 * CH : 4 * CH] = p_in.astype(BF)
    third = p_conv[:, 2 * CH :]
    st[4 * CH :] = jnp.concatenate(
        [third[: 2 * CH], jnp.concatenate([third[2 * CH :], p_out], axis=0)], axis=1
    ).astype(BF)
    summing = far < 12
    for peer, place in zip(far_peers, far_places):

        @pl.when(peer < 12)
        def _():
            push(st.at[pl.ds(pl.multiple_of(peer * 32, 32), 32)], rt1.at[far], G_T1, place)

    @pl.when(summing)
    def _():
        rt1[far] = st[pl.ds(pl.multiple_of(far * 32, 32), 32)]

    step_d(2)
    step_d(3)

    arrived(re1.at[pl.ds(0, 3)], G_E1)
    total = re1[0].astype(F32)
    for k in range(1, 4):
        total = total + re1[k].astype(F32)
    e1[...] = total
    over_x(lambda peer: e1.at[pl.ds(pl.multiple_of(peer * 32, 32), 32)], re2.at[across], G_E2)
    re2[across] = e1[pl.ds(pl.multiple_of(across * 32, 32), 32)]

    take_halo(v3, 1, G_ROW1, G_PACK1)

    conv_k = jnp.concatenate(
        [jnp.concatenate([conv_w[a, b] for b in range(3)], axis=1) for a in range(3)], axis=0
    )

    def out_row(r, carry):
        total, carry = conv_step(conv_k, v3, r, carry)
        total = total + v3[r + 1, CH : 2 * CH].astype(F32)
        for t in range(2):
            rest_out[t, pl.ds(r * CH, CH), :] = total[:, half(t)]
        return carry

    carry = loop(ROWS // 2, out_row, conv_start(conv_k, v3), unroll=8)

    for n in VALUES + BACKS:
        for ref, count, g in ((a_in, NEAR, G_A), (b_in, FAR, G_B), (c_in, FAR, G_C)):
            gone(ref.at[n, pl.ds(0, count - 1)], g + n)
    for n in VALUES:
        gone(d_in.at[n, pl.ds(0, NEAR - 1)], G_D + n)

    @pl.when(summing)
    def _():
        from_far(rt1, G_T1)
        total = rt1[0].astype(F32)
        for k in range(1, FAR):
            total = total + rt1[k].astype(F32)
        t1[...] = total.astype(BF)
        over_near(lambda peer: t1, rt2.at[near], G_T2)
        rt2[near] = t1[...]

    arrived(re2.at[pl.ds(0, 3)], G_E2)
    e2[...] = re2[0] + re2[1] + re2[2] + re2[3]
    over_z(lambda peer: e2, re3.at[deep], G_E3)
    re3[deep] = e2[...]

    step_e(2)
    step_e(3)

    def value_before_row(r, carry):
        grid_back = returned(BACKS, r)
        for t in range(2):
            gbef[r, HC:CH, half(t)] = (dgelu[r, HC:CH, half(t)] * grid_back[t]).astype(BF)
        return carry

    loop(ROWS, value_before_row, unroll=4)
    p_value = dot_nt(pixels(gbef, slice(HC, CH)), pixels(nb))
    sq[...] = jnp.concatenate([p_value[0:16], p_value[16:]], axis=1).astype(BF)
    over_near(lambda peer: sq, rq1.at[near], G_Q1)
    rq1[near] = sq[...]

    @pl.when(summing)
    def _():
        from_near(rt2, G_T2)
        total = rt2[0].astype(F32)
        for k in range(1, NEAR):
            total = total + rt2[k].astype(F32)
        t2[...] = total.astype(BF)
        over_far(lambda peer: t2, rt3.at[far], G_T3)
        rt3[far] = t2[...]

    arrived(re3.at[pl.ds(0, 3)], G_E3)
    e3[...] = (re3[0] + re3[1] + re3[2] + re3[3]).astype(BF)
    over_x(lambda peer: e3, re4.at[across], G_E4)
    re4[across] = e3[...]

    def frame_row(r, carry):
        normed = dot(w_in_t[...], gbef[r])
        u = unit[r]
        mean_grad = jnp.mean(normed, axis=0, keepdims=True)
        mean_proj = jnp.mean(normed * u, axis=0, keepdims=True)
        source = gj[r].astype(F32) + inv[r, 0:1] * (normed - mean_grad - u * mean_proj)
        for t in range(2):
            gframe_out[t, pl.ds(r * CH, CH), :] = source[:, half(t)]
        return carry

    loop(ROWS, frame_row, unroll=8)

    from_near(rq1, G_Q1)
    total = rq1[0].astype(F32)
    for k in range(1, NEAR):
        total = total + rq1[k].astype(F32)
    q1[...] = total.astype(BF)
    over_far(lambda peer: q1, rq2.at[far], G_Q2)
    rq2[far] = q1[...]

    arrived(re4.at[pl.ds(0, 3)], G_E4)
    over_y(lambda peer: re4, re5.at[level], G_E5)
    re5[level] = re4[...]

    loop(ROWS // 2, lambda r, carry: out_row(r + ROWS // 2, carry), carry, unroll=8)

    arrived(re5.at[pl.ds(0, 3)], G_E5)
    push(re5, re6, G_E6, near_device(twin))
    early_out[pl.ds(pl.multiple_of(mine, 512), 512)] = re5[...].reshape(512, LANES)

    from_far(rq2, G_Q2)
    total = rq2[0].astype(F32)
    for k in range(1, FAR):
        total = total + rq2[k].astype(F32)
    value_out[...] = total

    @pl.when(summing)
    def _():
        arrived(rt3.at[pl.ds(0, 11)], G_T3)
        gone(rt1.at[pl.ds(0, 11)], G_T1)
        gone(rt2.at[pl.ds(0, NEAR - 1)], G_T2)
        gone(rt1.at[pl.ds(0, FAR - 1)], G_T3)

    @pl.when(far >= 12)
    def _():
        arrived(rt3, G_T3)
        gone(rt1.at[pl.ds(0, 12)], G_T1)

    tail_out[...] = rt3[...]
    arrived(re6, G_E6)
    early_out[pl.ds(pl.multiple_of(512 - mine, 512), 512)] = re6[...].reshape(512, LANES)

    for which, g_row, g_pack in ((0, G_ROW0, G_PACK0), (1, G_ROW1, G_PACK1)):
        gone(row_in.at[which], g_row)
        gone(pack_in.at[which], g_pack)
    for n in BACKS:
        gone(d_in.at[n, pl.ds(0, NEAR - 1)], G_D + n)
    gone(rq1.at[pl.ds(0, NEAR - 1)], G_Q1)
    gone(rq2.at[pl.ds(0, FAR - 1)], G_Q2)
    gone(re0, G_E0)
    for ref, g in ((re1, G_E1), (re2, G_E2), (re3, G_E3), (re4, G_E4), (re5, G_E5)):
        gone(ref.at[pl.ds(0, 3)], g)
    gone(re6, G_E6)


def finish(rest, gframe, early, tail, value, *refs):
    outs, sem = (refs[:7], refs[7:14]), refs[14]
    restored, grad_frames, grad_w_in_t, grad_grid, grad_block, grad_w_out, grad_conv = outs[1]
    copies = []

    def leave(k, part=None):
        src, dst = outs[1][k], outs[0][k]
        if part is not None:
            src, dst = src.at[part], dst.at[part]
        copies.append(pltpu.make_async_copy(src, dst, sem.at[len(copies)]))
        copies[-1].start()

    def turn_out(src, dst, k):
        for first in range(0, CH, CH // 2):

            def channel(c, carry):
                for t in range(2):
                    dst[first + c, :, half(t)] = src[t, pl.ds(first + c, ROWS, stride=CH), :].astype(BF)
                return carry

            loop(CH // 2, channel, unroll=16)
            leave(k, pl.ds(first, CH // 2))

    scale = float(ROWS * NA * COLS * NW) ** (-0.5)
    for k in range(2):
        grad_grid[:, half(k)] = early[k * COLS : (k + 1) * COLS].astype(F32) * scale
        grad_block[:, half(k)] = early[(2 + k) * COLS : (3 + k) * COLS].astype(F32) * scale
    leave(3)
    leave(4)
    turn_out(gframe, grad_frames, 1)
    turn_out(rest, restored, 0)
    quarter = value[...] * scale
    zeros = jnp.zeros((HC, CH), F32)
    quarter = jnp.concatenate([zeros, quarter[:, :CH], quarter[:, CH:], zeros, zeros], axis=0)
    grad_w_in_t[...] = tail[3 * CH : 4 * CH].astype(F32) * scale + quarter.T
    leave(2)
    last = tail[4 * CH :].astype(F32) * scale
    grad_w_out[...] = last[CH:, CH:]
    leave(5)
    for b in range(3):
        rows = slice((2 - b) * CH, (3 - b) * CH)
        pair = tail[rows].astype(F32) * scale
        grad_conv[0, b] = pair[:, :CH]
        grad_conv[1, b] = pair[:, CH:]
    grad_conv[2, 2] = last[:CH, :CH]
    grad_conv[2, 1] = last[CH:, :CH]
    grad_conv[2, 0] = last[:CH, CH:]
    leave(6)
    for copy in copies:
        copy.wait()


def vm(*shape, dtype=BF):
    return pltpu.VMEM(shape, dtype)


def exchange():
    message_w = vm(4, NEAR, 2, 2, QC, LANES)
    message_a = vm(4, FAR, 16, 256)
    return [message_w, message_w, vm(4, 2 * 16 * QC, LANES, dtype=F32)] + [message_a] * 4 + [message_w] * 2


SCRATCH = [
    vm(CH, ROWS, COLS),
    vm(CH, 2 * CH),
    vm(COLS, COLS),
    vm(COLS, COLS),
    vm(CH, CH),
    vm(3, 3, CH, CH),
    vm(CH, ROWS, COLS),
    vm(2 * CH, CH),
    vm(2, CH * ROWS, LANES, dtype=F32),
    vm(ROWS, CH, COLS),
    vm(ROWS, CH, COLS),
    vm(ROWS, CH, COLS, dtype=F32),
    vm(ROWS, 8, COLS, dtype=F32),
    vm(ROWS, 2 * CH, COLS, dtype=F32),
    vm(ROWS, CH, COLS),
    vm(ROWS, HC, COLS),
    vm(ROWS + 2, 3 * CH, COLS),
    vm(ROWS + 2, 3 * CH, COLS),
    vm(ROWS, CH, COLS),
    vm(ROWS, CH, COLS, dtype=F32),
    vm(ROWS, HC, COLS),
    vm(ROWS, HC, COLS),
    vm(ROWS, HC, COLS),
    vm(ROWS, HC, COLS),
    *exchange(),
    vm(ROWS, CH, COLS),
    vm(ROWS, 2 * CH, COLS),
    vm(ROWS + 4, CH, COLS),
    vm(2, 2, CH, COLS),
    vm(2, 32, LANES),
    vm(2, 96, LANES),
    vm(CH, LANES),
    vm(CH, LANES),
    vm(COLS, COLS),
    vm(COLS, COLS),
    vm(COLS, COLS),
    vm(COLS, COLS),
    vm(4 * COLS, LANES),
    vm(512, LANES),
    vm(512, LANES),
    vm(4, 128, LANES),
    vm(128, LANES, dtype=F32),
    vm(4, 32, LANES, dtype=F32),
    vm(32, LANES, dtype=F32),
    vm(4, 32, LANES, dtype=F32),
    vm(32, LANES),
    vm(4, 32, LANES),
    vm(4, 4, 32, LANES),
    vm(4, 4, 32, LANES),
    vm(6 * CH, LANES),
    vm(FAR, 32, LANES),
    vm(32, LANES),
    vm(NEAR, 32, LANES),
    vm(32, LANES),
    vm(12, 32, LANES),
    vm(16, LANES),
    vm(NEAR, 16, LANES),
    vm(16, LANES),
    vm(FAR, 16, LANES),
    pltpu.SemaphoreType.DMA((GROUPS,)),
    pltpu.SemaphoreType.DMA((GROUPS,)),
    pltpu.SemaphoreType.DMA((7,)),
]


def body(frames, w_in, grid_mix, block_mix, w_out, conv_w, cotangent):
    operands = (frames, w_in.T, grid_mix, block_mix, w_out, conv_w, cotangent)
    vmem = pl.BlockSpec(memory_space=pltpu.VMEM)
    shape = jax.ShapeDtypeStruct
    rest, gframe, early, tail, value = pl.pallas_call(
        kernel,
        out_shape=(
            shape((2, ROWS * CH, LANES), F32),
            shape((2, ROWS * CH, LANES), F32),
            shape((4 * COLS, LANES), BF),
            shape((12, 32, LANES), BF),
            shape((16, LANES), F32),
        ),
        in_specs=[pl.BlockSpec(memory_space=pltpu.HBM)] * 7,
        out_specs=(vmem,) * 5,
        scratch_shapes=SCRATCH,
        compiler_params=pltpu.CompilerParams(
            collective_id=0, has_side_effects=True, vmem_limit_bytes=32 * 1024 * 1024
        ),
    )(*[pltpu.with_memory_space_constraint(x, pltpu.HBM) for x in operands])
    restored, grad_frames, grad_w_in_t, grad_grid, grad_block, grad_w_out, grad_conv = pl.pallas_call(
        finish,
        out_shape=(
            shape((CH, ROWS, COLS), BF),
            shape((CH, ROWS, COLS), BF),
            shape((CH, 2 * CH), F32),
            shape((COLS, COLS), F32),
            shape((COLS, COLS), F32),
            shape((CH, CH), F32),
            shape((3, 3, CH, CH), F32),
        ),
        in_specs=[vmem] * 5,
        out_specs=(pl.BlockSpec(memory_space=pl.ANY),) * 7,
        scratch_shapes=[
            vm(CH, ROWS, COLS),
            vm(CH, ROWS, COLS),
            vm(CH, 2 * CH, dtype=F32),
            vm(COLS, COLS, dtype=F32),
            vm(COLS, COLS, dtype=F32),
            vm(CH, CH, dtype=F32),
            vm(3, 3, CH, CH, dtype=F32),
            pltpu.SemaphoreType.DMA((9,)),
        ],
        compiler_params=pltpu.CompilerParams(vmem_limit_bytes=16 * 1024 * 1024),
    )(rest, gframe, early, tail.reshape(6 * CH, LANES), value)
    return restored, grad_frames, grad_w_in_t.T, grad_grid, grad_block, grad_w_out, grad_conv


def solution(mesh):
    placed = (P(None, "ha", "wa"), P(), P(), P(), P(), P(), P(None, "ha", "wa"))
    return jax.shard_map(
        body,
        mesh=mesh,
        in_specs=placed,
        out_specs=(P(None, "ha", "wa"), P(None, "ha", "wa"), P(), P(), P(), P(), P()),
        check_vma=False,
    )
```

```python
import jax
import jax.numpy as jnp
from jax import lax
from jax.experimental import pallas as pl
from jax.experimental.pallas import tpu as pltpu
from jax.sharding import PartitionSpec as P

BF = jnp.bfloat16
F32 = jnp.float32
EPS = 1e-06
MESH = pl.DeviceIdType.MESH

CH = 64
HC = 32
ROWS = 16
COLS = 256
LANES = 128
NA = 16
NW = 8
NEAR = 8
FAR = 16

(G_ROW0, G_PACK0, G_ROW1, G_PACK1) = range(4)
(G_E0, G_E1, G_E2, G_E3, G_E4, G_E5, G_E6, G_T1, G_T2, G_T3, G_Q1, G_Q2) = range(4, 16)
VALUES, BACKS = (0, 1), (2, 3)
G_A, G_B, G_C, G_D = 16, 20, 24, 28
GROUPS = 32
QC = 16


def dot(a, b):
    return lax.dot_general(a, b, (((1,), (0,)), ((), ())), preferred_element_type=F32)


def dot_nt(a, b):
    return lax.dot_general(a, b, (((1,), (1,)), ((), ())), preferred_element_type=F32)


def dot_tn(a, b):
    return lax.dot_general(a, b, (((0,), (0,)), ((), ())), preferred_element_type=F32)


def swap_granules(load, store, depth):
    lane = lax.broadcasted_iota(jnp.int16, (depth, LANES), 1)
    for row_half in range(2):
        for col_half in range(2):
            held = [load(row_half * 8 + k, col_half) for k in range(8)]
            for s in range(3):
                width = 16 << s
                low = (lane & width) == 0
                for k in range(8):
                    if not k & (1 << s):
                        a, b = held[k], held[k | (1 << s)]
                        held[k] = jnp.where(low, a, pltpu.roll(b, width, 1))
                        held[k | (1 << s)] = jnp.where(low, pltpu.roll(a, LANES - width, 1), b)
            for k in range(8):
                store(col_half * 8 + k, row_half, held[k])


def half(t):
    return slice(t * LANES, (t + 1) * LANES)


def loop(count, step, carry=0, unroll=1):
    return lax.fori_loop(0, count, step, carry, unroll=unroll)


def gelu_parts(x):
    root = 0.7978845608028654
    cube = root * 0.044715
    square = x * x
    h = 0.5 * jnp.tanh(x * (cube * square + root)) + 0.5
    value = x * h
    return value, h + value * (1.0 - h) * ((6.0 * cube) * square + 2.0 * root)


def kernel(
    frames_hbm, w_in_t_hbm, grid_mix_hbm, block_mix_hbm, w_out_hbm, conv_w_hbm, cot_hbm,
    rest_out, gframe_out, early_out, tail_out, value_out,
    frames, w_in_t, grid_mix, block_mix, w_out, conv_w, cot, w_in,
    turn, xb, nb, unit, inv, dgelu, gates, bval, u3, v3, gj, gg, xt, bt, bm, gbv,
    a, a_in, x32, b, b_in, c, c_in, d, d_in,
    gated, gbef, jp, row_in, pack_out, pack_in, edge_l, edge_r,
    mixp, mixp_t, gather, spread, se, re0, e0, re1, e1, re2, e2, re3, e3, re4, re5, re6,
    st, rt1, t1, rt2, t2, rt3, sq, rq1, q1, rq2,
    ssem, rsem, isem,
):
    ia = lax.axis_index("ha")
    iw = lax.axis_index("wa")
    up, down = lax.rem(ia + NA - 1, NA), lax.rem(ia + 1, NA)
    left, right = lax.rem(iw + NW - 1, NW), lax.rem(iw + 1, NW)
    lane = lax.broadcasted_iota(jnp.int16, (CH, LANES), 1)
    lane_wide = lax.broadcasted_iota(jnp.int32, (CH, LANES), 1)

    loads = [
        pltpu.make_async_copy(src, dst, isem.at[k])
        for k, (src, dst) in enumerate(
            [
                (frames_hbm, frames),
                (w_in_t_hbm, w_in_t),
                (cot_hbm, cot),
                (conv_w_hbm, conv_w),
                (w_out_hbm, w_out),
                (block_mix_hbm, block_mix),
                (grid_mix_hbm, grid_mix),
            ]
        )
    ]
    for load in loads:
        load.start()

    def push(src, dst, g, where):
        pltpu.make_async_remote_copy(
            src_ref=src, dst_ref=dst, send_sem=ssem.at[g], recv_sem=rsem.at[g], device_id=where, device_id_type=MESH
        ).start()

    near = lax.rem(iw, 2) * 4 + lax.rem(ia, 4)
    far = ia // 4 * 4 + iw // 2

    def near_device(peer):
        return ia // 4 * 4 + lax.rem(peer, 4), iw // 2 * 2 + peer // 4

    def far_device(peer):
        return peer // 4 * 4 + lax.rem(ia, 4), lax.rem(peer, 4) * 2 + lax.rem(iw, 2)

    near_peers = [lax.rem(near + k, NEAR) for k in range(1, NEAR)]
    far_peers = [lax.rem(far + k, FAR) for k in range(1, FAR)]
    twin = near + 1 - 2 * lax.rem(near, 2)

    near_places = [near_device(peer) for peer in near_peers]
    far_places = [far_device(peer) for peer in far_peers]

    def over_near(src_of, dst, g):
        for peer, place in zip(near_peers, near_places):
            push(src_of(peer), dst, g, place)

    def over_far(src_of, dst, g):
        for peer, place in zip(far_peers, far_places):
            push(src_of(peer), dst, g, place)

    def over_x(src_of, dst, g):
        for k in range(1, 4):
            peer = lax.rem(iw // 2 + k, 4)
            push(src_of(peer), dst, g, (ia, peer * 2 + lax.rem(iw, 2)))

    def over_z(src_of, dst, g):
        for k in range(1, 4):
            peer = lax.rem(ia // 4 + k, 4)
            push(src_of(peer), dst, g, (peer * 4 + lax.rem(ia, 4), iw))

    def over_y(src_of, dst, g):
        for k in range(1, 4):
            peer = lax.rem(near + 2 * k, NEAR)
            push(src_of(peer // 2), dst, g, near_device(peer))

    def arrived(ref, g):
        pltpu.make_async_copy(ref, ref, rsem.at[g]).wait()

    def gone(ref, g):
        pltpu.make_async_copy(ref, ref, ssem.at[g]).wait()

    def from_near(ref, g):
        arrived(ref.at[pl.ds(0, NEAR - 1)], g)

    def from_far(ref, g):
        arrived(ref.at[pl.ds(0, FAR - 1)], g)

    mine = lax.rem(near, 2) * 512
    level, across, deep = near // 2, iw // 2, ia // 4

    barrier = pltpu.get_barrier_semaphore()
    peers = [near_device(peer) for peer in near_peers]
    peers += [far_device(peer) for peer in far_peers]
    peers += [(a, b) for a in (up, ia, down) for b in (left, right)] + [(up, iw), (down, iw)]
    for peer in peers:
        pl.semaphore_signal(barrier, inc=1, device_id=peer, device_id_type=MESH)

    def turn_in(src):
        for t in range(2):
            turn[t] = src[:, :, half(t)].astype(F32).reshape(CH * ROWS, LANES)

    def turned(r, t):
        return turn[t, pl.ds(r, CH, stride=ROWS), :]

    def edges(pack, t0, t1, r):
        pack = jnp.where(lane_wide == r, pltpu.roll(t0, r, 1), pack)
        return jnp.where(lane_wide == ROWS + r, pltpu.roll(t1, r + 17, 1), pack)

    def send_halo(field, pack, which, g_row, g_pack):
        pack_out[which] = jnp.concatenate([pack, jnp.zeros_like(pack)], axis=0).T[0:32]
        push(field.at[1, CH : 2 * CH], row_in.at[which, 1], g_row, (up, iw))
        push(field.at[ROWS, CH : 2 * CH], row_in.at[which, 0], g_row, (down, iw))
        for slot, where in enumerate(
            [(ia, right), (down, right), (up, right), (ia, left), (down, left), (up, left)]
        ):
            part = pack_out.at[which, pl.ds(16 if slot < 3 else 0, 16)]
            push(part, pack_in.at[which, pl.ds(16 * slot, 16)], g_pack, where)

    def take_halo(field, which, g_row, g_pack):
        arrived(row_in.at[which], g_row)
        arrived(pack_in.at[which], g_pack)
        field[0, CH : 2 * CH] = jnp.where(ia > 0, row_in[which, 0], jnp.zeros((CH, COLS), BF))
        field[ROWS + 1, CH : 2 * CH] = jnp.where(ia < NA - 1, row_in[which, 1], jnp.zeros((CH, COLS), BF))
        first = jnp.where(ia > 0, 0, 1)
        last = jnp.where(ia < NA - 1, ROWS + 2, ROWS + 1)
        got = jnp.concatenate([pack_in[which], jnp.zeros((32, LANES), BF)], axis=0).T[0:CH]

        def assemble(middle, above, below, has):
            joined = jnp.where(lane == 0, above, jnp.where(lane == ROWS + 1, below, middle))
            inside = (lane_wide >= first) & (lane_wide < jnp.where(has, last, 0))
            return jnp.where(inside, joined, jnp.zeros_like(joined))

        edge_l[...] = assemble(pltpu.roll(got, 1, 1), pltpu.roll(got, 97, 1), pltpu.roll(got, 113, 1), iw > 0)
        edge_r[...] = assemble(pltpu.roll(got, 81, 1), pltpu.roll(got, 49, 1), pltpu.roll(got, 65, 1), iw < NW - 1)

        def shifts(p, carry):
            t0 = field[p, CH : 2 * CH, half(0)]
            t1 = field[p, CH : 2 * CH, half(1)]
            a0, a1 = pltpu.roll(t0, 1, 1), pltpu.roll(t1, 1, 1)
            b0, b1 = pltpu.roll(t0, LANES - 1, 1), pltpu.roll(t1, LANES - 1, 1)
            lh = pltpu.roll(edge_l[...], lax.rem(LANES - p, LANES), 1)
            rh = pltpu.roll(edge_r[...], LANES - 1 - p, 1)
            field[p, 0:CH, half(0)] = jnp.where(lane == 0, lh, a0)
            field[p, 0:CH, half(1)] = jnp.where(lane == 0, a0, a1)
            field[p, 2 * CH :, half(0)] = jnp.where(lane == LANES - 1, b1, b0)
            field[p, 2 * CH :, half(1)] = jnp.where(lane == LANES - 1, rh, b1)
            return carry

        loop(ROWS + 2, shifts, unroll=9)

    def conv_start(w, field):
        y = dot(w, field[0])
        z = dot(w, field[1])
        return z[0:CH], y[0:CH] + z[CH : 2 * CH]

    def conv_step(w, field, r, carry):
        later, now = carry
        y = dot(w, field[r + 2])
        return now + y[2 * CH :], (y[0:CH], later + y[CH : 2 * CH])

    def step_a(n):
        over_near(lambda peer: a.at[n, peer], a_in.at[n, near], G_A + n)

    def step_b(n):
        arrived(a_in.at[n, pl.ds(0, NEAR - 1)], G_A + n)

        def widen(j, carry):
            for t in range(2):
                for r in range(2):
                    x32[n, pl.ds((r * 16 + j * 2 + t) * QC, QC), :] = a_in[n, j, t, r].astype(F32)
            return carry

        loop(NEAR, widen, unroll=8)

        for peer, place in zip([*far_peers, far], [*far_places, None]):
            base = peer // 8 * (16 * QC) + lax.rem(peer, 8) * 2
            slot = b_in if peer is far else b
            for k in range(2):
                slot[n, peer, :, half(k)] = x32[n, pl.ds(base + k, 16, stride=QC), :].astype(BF)
            if peer is not far:
                push(b.at[n, peer], b_in.at[n, far], G_B + n, place)

    def table(n):
        return b_in[n].reshape(256, 256)

    def step_c(n, mix):
        arrived(b_in.at[n, pl.ds(0, FAR - 1)], G_B + n)
        c[n] = dot(mix[...], table(n)).astype(BF).reshape(FAR, 16, 256)
        over_far(lambda peer: c.at[n, peer], c_in.at[n, far], G_C + n)
        c_in[n, far] = c[n, far]

    def step_d(n):
        arrived(c_in.at[n, pl.ds(0, FAR - 1)], G_C + n)

        def unpick(q, carry):
            for r in range(2):
                for k in range(2):
                    x32[n, pl.ds((r * QC + q * 2 + k) * 16, 16), :] = c_in[n, r * 8 + q, :, half(k)].astype(F32)
            return carry

        loop(8, unpick, unroll=8)

        for peer, place in zip([*near_peers, near], [*near_places, None]):
            slot = d_in if peer is near else d
            for t in range(2):
                for r in range(2):
                    slot[n, peer, t, r] = x32[n, pl.ds(r * QC * 16 + peer * 2 + t, QC, stride=16), :].astype(BF)
            if peer is not near:
                push(d.at[n, peer], d_in.at[n, near], G_D + n, place)

    def step_e(n):
        arrived(d_in.at[n, pl.ds(0, NEAR - 1)], G_D + n)

    def order(cell, row):
        found = (row & 0xC1) | ((row & 6) << 3) | ((row & 48) >> 2) | ((row & 8) >> 2)
        return jnp.where(cell == found, 1.0, 0.0).astype(BF)

    loads[0].wait()
    loads[1].wait()
    turn_in(frames)
    w_in[...] = w_in_t[...].astype(F32).T.astype(BF)

    def value_row(slot, peer, low):
        r = peer * 2 + low
        for t in range(2):
            x = turned(r, t)
            xb[r, :, half(t)] = x.astype(BF)
            off = x - jnp.mean(x, axis=0, keepdims=True)
            rstd = lax.rsqrt(jnp.mean(off * off, axis=0, keepdims=True) + EPS)
            u = off * rstd
            unit[r, :, half(t)] = u
            inv[r, :, half(t)] = jnp.broadcast_to(rstd, (8, LANES))
            nb[r, :, half(t)] = u.astype(BF)
        value, slope = gelu_parts(dot(w_in[HC:CH], nb[r]))
        dgelu[r, HC:CH] = slope
        value = value.astype(BF)
        for n in VALUES:
            for t in range(2):
                slot[n, peer, t, low] = value[n * QC : (n + 1) * QC, half(t)]

    for first in range(0, NEAR, 2):
        group = [*near_peers, near][first : first + 2]
        for peer in group:
            for low in range(2):
                value_row(a_in if peer is near else a, peer, low)
        if first == 0:
            pl.semaphore_wait(barrier, len(peers))
        for peer in group:
            if peer is not near:
                push(a.at[0, peer], a_in.at[0, near], G_A, near_device(peer))
    step_a(1)

    loads[2].wait()
    turn_in(cot)

    def cot_row(r, pack):
        t0, t1 = turned(r, 0).astype(BF), turned(r, 1).astype(BF)
        u3[r + 1, CH : 2 * CH, half(0)] = t0
        u3[r + 1, CH : 2 * CH, half(1)] = t1
        return edges(pack, t0, t1, r)

    pack = loop(ROWS, cot_row, jnp.zeros((CH, LANES), BF), unroll=8)
    send_halo(u3, pack, 0, G_ROW0, G_PACK0)

    def grid_gate_row(r, carry):
        value, slope = gelu_parts(dot(w_in[0:HC], nb[r]))
        gates[r, 0:HC] = value.astype(BF)
        dgelu[r, 0:HC] = slope
        return carry

    loop(ROWS, grid_gate_row, unroll=8)

    def block_gate_row(r, carry):
        value, slope = gelu_parts(dot(w_in[CH:], nb[r]))
        dgelu[r, CH:] = slope
        value = value.astype(BF)
        gates[r, HC:CH] = value[0:HC]
        bval[r] = value[HC:]
        return carry

    loop(ROWS, block_gate_row, unroll=8)
    for load in loads[3:]:
        load.wait()
    down_axis = lax.broadcasted_iota(jnp.int32, (COLS, COLS), 0)
    along_axis = lax.broadcasted_iota(jnp.int32, (COLS, COLS), 1)
    gather[...] = order(along_axis, down_axis)
    spread[...] = order(down_axis, along_axis)
    mixp[...] = dot(dot(gather[...], grid_mix[...]).astype(BF), spread[...]).astype(BF)
    mixp_t[...] = dot(dot_nt(gather[...], grid_mix[...]).astype(BF), spread[...]).astype(BF)

    back_w = jnp.concatenate(
        [jnp.concatenate([conv_w[2 - a, 2 - b] for a in range(3)], axis=1) for b in range(3)], axis=0
    ).astype(F32).T.astype(BF)
    w_out_t = w_out[...].astype(F32).T.astype(BF)
    take_halo(u3, 0, G_ROW0, G_PACK0)

    def back_row(r, carry):
        total, carry = conv_step(back_w, u3, r, carry)
        g = (total + u3[r + 1, CH : 2 * CH].astype(F32)).astype(BF)
        gj[r] = g
        up_gated = dot(w_out_t, g)
        gg[r] = up_gated
        mixed = (up_gated[0:HC] * gates[r, 0:HC].astype(F32)).astype(BF)
        for n in range(2):
            for t in range(2):
                a[2 + n, r // 2, t, r % 2] = mixed[n * QC : (n + 1) * QC, half(t)]
        return carry

    step_b(0)
    carry = conv_start(back_w, u3)
    for first in range(0, NEAR, 2):
        if first == NEAR // 2:
            step_b(1)
        for r in range(2 * first, 2 * first + 4):
            carry = back_row(r, carry)
        for peer in (first, first + 1):

            @pl.when(peer != near)
            def _():
                push(a.at[2, peer], a_in.at[2, near], G_A + 2, near_device(peer))

    step_a(3)
    for n in BACKS:
        a_in[n, near] = a[n, near]


    def put(ref):
        def store(k, t, value):
            ref[k, :, half(t)] = value

        return store

    swap_granules(lambda k, t: bval[k, :, half(t)], put(xt), HC)
    values = xt[...].reshape(ROWS * HC, COLS)
    mixed = dot_nt(values, block_mix[...]).astype(BF)
    swap_granules(lambda k, t: mixed[k * HC : (k + 1) * HC, half(t)], put(bm), HC)

    step_c(0, mixp)
    step_b(2)
    step_c(1, mixp)
    step_b(3)

    def block_back(k, t):
        return (gg[k, HC:, half(t)] * gates[k, HC:, half(t)].astype(F32)).astype(BF)

    swap_granules(block_back, put(bt), HC)
    backs = bt[...].reshape(ROWS * HC, COLS)
    unmixed = dot(backs, block_mix[...]).astype(BF)
    swap_granules(lambda k, t: unmixed[k * HC : (k + 1) * HC, half(t)], put(gbv), HC)
    part_block = dot_tn(backs, values).astype(BF)
    se[2 * COLS : 3 * COLS] = part_block[:, half(0)]
    se[3 * COLS :] = part_block[:, half(1)]

    def block_before_row(r, carry):
        d = dgelu[r, CH:]
        gbef[r, CH : CH + HC] = (d[0:HC] * (gg[r, HC:] * (bm[r].astype(F32) + 1.0))).astype(BF)
        gbef[r, CH + HC :] = (d[HC:] * gbv[r].astype(F32)).astype(BF)
        gbef[r, HC:CH] = jnp.zeros((HC, COLS), BF)
        return carry

    loop(ROWS, block_before_row, unroll=4)
    for k in (0, 1, ROWS + 2, ROWS + 3):
        jp[k] = jnp.zeros((CH, COLS), BF)

    step_d(0)
    step_d(1)
    step_c(2, mixp_t)
    step_c(3, mixp_t)

    part_grid = (dot_nt(table(2), table(0)) + dot_nt(table(3), table(1))).astype(BF)
    part_grid = dot(dot(spread[...], part_grid).astype(BF), gather[...]).astype(BF)
    se[0:COLS] = part_grid[:, half(0)]
    se[COLS : 2 * COLS] = part_grid[:, half(1)]
    push(se.at[pl.ds(pl.multiple_of(512 - mine, 512), 512)], re0, G_E0, near_device(twin))

    arrived(re0, G_E0)
    e0[...] = (se[pl.ds(pl.multiple_of(mine, 512), 512)].astype(F32) + re0[...].astype(F32)).astype(BF)
    over_y(lambda peer: e0.at[pl.ds(pl.multiple_of(peer * 128, 128), 128)], re1.at[level], G_E1)
    re1[level] = e0[pl.ds(pl.multiple_of(level * 128, 128), 128)]

    step_e(0)
    step_e(1)

    def returned(chains, r):
        return [
            jnp.concatenate([d_in[n, r // 2, t, lax.rem(r, 2)] for n in chains], axis=0).astype(F32) for t in range(2)
        ]

    def joined_row(r, pack):
        grid_mixed = returned(VALUES, r)
        for t in range(2):
            gates_t = gates[r, :, half(t)].astype(F32)
            more = grid_mixed[t] + 1.0
            gated[r, 0:HC, half(t)] = (gates_t[0:HC] * more).astype(BF)
            gated[r, HC:, half(t)] = (gates_t[HC:] * (bm[r, :, half(t)].astype(F32) + 1.0)).astype(BF)
            gbef[r, 0:HC, half(t)] = (dgelu[r, 0:HC, half(t)] * (gg[r, 0:HC, half(t)] * more)).astype(BF)
        j = (xb[r].astype(F32) + dot(w_out[...], gated[r])).astype(BF)
        jp[r + 2] = j
        v3[r + 1, CH : 2 * CH] = j
        return edges(pack, j[:, half(0)], j[:, half(1)], r)

    pack = loop(ROWS, joined_row, jnp.zeros((CH, LANES), BF), unroll=8)
    send_halo(v3, pack, 1, G_ROW1, G_PACK1)

    step_d(2)
    step_d(3)

    def pixels(ref, rows=slice(None)):
        return jnp.concatenate([ref[r, rows] for r in range(ROWS)], axis=1)

    p_conv = dot_nt(
        jnp.concatenate([u3[p] for p in range(ROWS + 2)], axis=1),
        jnp.concatenate([jp[p : p + 3].reshape(3 * CH, COLS) for p in range(ROWS + 2)], axis=1),
    )
    arrived(re1.at[pl.ds(0, 3)], G_E1)
    total = re1[0].astype(F32)
    for k in range(1, 4):
        total = total + re1[k].astype(F32)
    e1[...] = total
    over_x(lambda peer: e1.at[pl.ds(pl.multiple_of(peer * 32, 32), 32)], re2.at[across], G_E2)
    re2[across] = e1[pl.ds(pl.multiple_of(across * 32, 32), 32)]

    p_in = dot_nt(pixels(nb), pixels(gbef))
    p_out = dot_nt(pixels(gj), pixels(gated))
    st[0 : 3 * CH] = p_conv[:, half(0)].astype(BF)
    st[3 * CH : 4 * CH] = p_in.astype(BF)
    third = p_conv[:, 2 * CH :]
    st[4 * CH :] = jnp.concatenate(
        [third[: 2 * CH], jnp.concatenate([third[2 * CH :], p_out], axis=0)], axis=1
    ).astype(BF)
    summing = far < 12
    for peer, place in zip(far_peers, far_places):

        @pl.when(peer < 12)
        def _():
            push(st.at[pl.ds(pl.multiple_of(peer * 32, 32), 32)], rt1.at[far], G_T1, place)

    @pl.when(summing)
    def _():
        rt1[far] = st[pl.ds(pl.multiple_of(far * 32, 32), 32)]

    take_halo(v3, 1, G_ROW1, G_PACK1)

    arrived(re2.at[pl.ds(0, 3)], G_E2)
    e2[...] = re2[0] + re2[1] + re2[2] + re2[3]
    over_z(lambda peer: e2, re3.at[deep], G_E3)
    re3[deep] = e2[...]

    conv_k = jnp.concatenate(
        [jnp.concatenate([conv_w[a, b] for b in range(3)], axis=1) for a in range(3)], axis=0
    )

    def out_row(r, carry):
        total, carry = conv_step(conv_k, v3, r, carry)
        total = total + v3[r + 1, CH : 2 * CH].astype(F32)
        for t in range(2):
            rest_out[t, pl.ds(r * CH, CH), :] = total[:, half(t)]
        return carry

    carry = loop(ROWS // 2, out_row, conv_start(conv_k, v3), unroll=8)

    step_e(2)
    step_e(3)

    def value_before_row(r, carry):
        grid_back = returned(BACKS, r)
        for t in range(2):
            gbef[r, HC:CH, half(t)] = (dgelu[r, HC:CH, half(t)] * grid_back[t]).astype(BF)
        return carry

    loop(ROWS, value_before_row, unroll=4)
    p_value = dot_nt(pixels(gbef, slice(HC, CH)), pixels(nb))
    sq[...] = jnp.concatenate([p_value[0:16], p_value[16:]], axis=1).astype(BF)
    over_near(lambda peer: sq, rq1.at[near], G_Q1)
    rq1[near] = sq[...]

    for n in VALUES + BACKS:
        for ref, count, g in ((a_in, NEAR, G_A), (b_in, FAR, G_B), (c_in, FAR, G_C)):
            gone(ref.at[n, pl.ds(0, count - 1)], g + n)
    for n in VALUES:
        gone(d_in.at[n, pl.ds(0, NEAR - 1)], G_D + n)

    @pl.when(summing)
    def _():
        from_far(rt1, G_T1)
        total = rt1[0].astype(F32)
        for k in range(1, FAR):
            total = total + rt1[k].astype(F32)
        t1[...] = total.astype(BF)
        over_near(lambda peer: t1, rt2.at[near], G_T2)
        rt2[near] = t1[...]

    arrived(re3.at[pl.ds(0, 3)], G_E3)
    e3[...] = (re3[0] + re3[1] + re3[2] + re3[3]).astype(BF)
    over_x(lambda peer: e3, re4.at[across], G_E4)
    re4[across] = e3[...]

    def frame_row(r, carry):
        normed = dot(w_in_t[...], gbef[r])
        u = unit[r]
        mean_grad = jnp.mean(normed, axis=0, keepdims=True)
        mean_proj = jnp.mean(normed * u, axis=0, keepdims=True)
        source = gj[r].astype(F32) + inv[r, 0:1] * (normed - mean_grad - u * mean_proj)
        for t in range(2):
            gframe_out[t, pl.ds(r * CH, CH), :] = source[:, half(t)]
        return carry

    loop(ROWS, frame_row, unroll=8)

    from_near(rq1, G_Q1)
    total = rq1[0].astype(F32)
    for k in range(1, NEAR):
        total = total + rq1[k].astype(F32)
    q1[...] = total.astype(BF)
    over_far(lambda peer: q1, rq2.at[far], G_Q2)
    rq2[far] = q1[...]

    arrived(re4.at[pl.ds(0, 3)], G_E4)
    over_y(lambda peer: re4, re5.at[level], G_E5)
    re5[level] = re4[...]

    @pl.when(summing)
    def _():
        from_near(rt2, G_T2)
        total = rt2[0].astype(F32)
        for k in range(1, NEAR):
            total = total + rt2[k].astype(F32)
        t2[...] = total.astype(BF)
        over_far(lambda peer: t2, rt3.at[far], G_T3)
        rt3[far] = t2[...]

    loop(ROWS // 2, lambda r, carry: out_row(r + ROWS // 2, carry), carry, unroll=8)

    from_far(rq2, G_Q2)
    total = rq2[0].astype(F32)
    for k in range(1, FAR):
        total = total + rq2[k].astype(F32)
    value_out[...] = total

    arrived(re5.at[pl.ds(0, 3)], G_E5)
    push(re5, re6, G_E6, near_device(twin))
    early_out[pl.ds(pl.multiple_of(mine, 512), 512)] = re5[...].reshape(512, LANES)

    @pl.when(summing)
    def _():
        arrived(rt3.at[pl.ds(0, 11)], G_T3)
        gone(rt1.at[pl.ds(0, 11)], G_T1)
        gone(rt2.at[pl.ds(0, NEAR - 1)], G_T2)
        gone(rt1.at[pl.ds(0, FAR - 1)], G_T3)

    @pl.when(far >= 12)
    def _():
        arrived(rt3, G_T3)
        gone(rt1.at[pl.ds(0, 12)], G_T1)

    tail_out[...] = rt3[...]
    arrived(re6, G_E6)
    early_out[pl.ds(pl.multiple_of(512 - mine, 512), 512)] = re6[...].reshape(512, LANES)

    for which, g_row, g_pack in ((0, G_ROW0, G_PACK0), (1, G_ROW1, G_PACK1)):
        gone(row_in.at[which], g_row)
        gone(pack_in.at[which], g_pack)
    for n in BACKS:
        gone(d_in.at[n, pl.ds(0, NEAR - 1)], G_D + n)
    gone(rq1.at[pl.ds(0, NEAR - 1)], G_Q1)
    gone(rq2.at[pl.ds(0, FAR - 1)], G_Q2)
    gone(re0, G_E0)
    for ref, g in ((re1, G_E1), (re2, G_E2), (re3, G_E3), (re4, G_E4), (re5, G_E5)):
        gone(ref.at[pl.ds(0, 3)], g)
    gone(re6, G_E6)


def finish(rest, gframe, early, tail, value, *refs):
    outs, sem = (refs[:7], refs[7:14]), refs[14]
    restored, grad_frames, grad_w_in_t, grad_grid, grad_block, grad_w_out, grad_conv = outs[1]
    copies = []

    def leave(k, part=None):
        src, dst = outs[1][k], outs[0][k]
        if part is not None:
            src, dst = src.at[part], dst.at[part]
        copies.append(pltpu.make_async_copy(src, dst, sem.at[len(copies)]))
        copies[-1].start()

    def turn_out(src, dst, k):
        for first in range(0, CH, CH // 2):

            def channel(c, carry):
                for t in range(2):
                    dst[first + c, :, half(t)] = src[t, pl.ds(first + c, ROWS, stride=CH), :].astype(BF)
                return carry

            loop(CH // 2, channel, unroll=16)
            leave(k, pl.ds(first, CH // 2))

    scale = float(ROWS * NA * COLS * NW) ** (-0.5)
    for k in range(2):
        grad_grid[:, half(k)] = early[k * COLS : (k + 1) * COLS].astype(F32) * scale
        grad_block[:, half(k)] = early[(2 + k) * COLS : (3 + k) * COLS].astype(F32) * scale
    leave(3)
    leave(4)
    turn_out(gframe, grad_frames, 1)
    turn_out(rest, restored, 0)
    quarter = value[...] * scale
    zeros = jnp.zeros((HC, CH), F32)
    quarter = jnp.concatenate([zeros, quarter[:, :CH], quarter[:, CH:], zeros, zeros], axis=0)
    grad_w_in_t[...] = tail[3 * CH : 4 * CH].astype(F32) * scale + quarter.T
    leave(2)
    last = tail[4 * CH :].astype(F32) * scale
    grad_w_out[...] = last[CH:, CH:]
    leave(5)
    for b in range(3):
        rows = slice((2 - b) * CH, (3 - b) * CH)
        pair = tail[rows].astype(F32) * scale
        grad_conv[0, b] = pair[:, :CH]
        grad_conv[1, b] = pair[:, CH:]
    grad_conv[2, 2] = last[:CH, :CH]
    grad_conv[2, 1] = last[CH:, :CH]
    grad_conv[2, 0] = last[:CH, CH:]
    leave(6)
    for copy in copies:
        copy.wait()


def vm(*shape, dtype=BF):
    return pltpu.VMEM(shape, dtype)


def exchange():
    message_w = vm(4, NEAR, 2, 2, QC, LANES)
    message_a = vm(4, FAR, 16, 256)
    return [message_w, message_w, vm(4, 2 * 16 * QC, LANES, dtype=F32)] + [message_a] * 4 + [message_w] * 2


SCRATCH = [
    vm(CH, ROWS, COLS),
    vm(CH, 2 * CH),
    vm(COLS, COLS),
    vm(COLS, COLS),
    vm(CH, CH),
    vm(3, 3, CH, CH),
    vm(CH, ROWS, COLS),
    vm(2 * CH, CH),
    vm(2, CH * ROWS, LANES, dtype=F32),
    vm(ROWS, CH, COLS),
    vm(ROWS, CH, COLS),
    vm(ROWS, CH, COLS, dtype=F32),
    vm(ROWS, 8, COLS, dtype=F32),
    vm(ROWS, 2 * CH, COLS, dtype=F32),
    vm(ROWS, CH, COLS),
    vm(ROWS, HC, COLS),
    vm(ROWS + 2, 3 * CH, COLS),
    vm(ROWS + 2, 3 * CH, COLS),
    vm(ROWS, CH, COLS),
    vm(ROWS, CH, COLS, dtype=F32),
    vm(ROWS, HC, COLS),
    vm(ROWS, HC, COLS),
    vm(ROWS, HC, COLS),
    vm(ROWS, HC, COLS),
    *exchange(),
    vm(ROWS, CH, COLS),
    vm(ROWS, 2 * CH, COLS),
    vm(ROWS + 4, CH, COLS),
    vm(2, 2, CH, COLS),
    vm(2, 32, LANES),
    vm(2, 96, LANES),
    vm(CH, LANES),
    vm(CH, LANES),
    vm(COLS, COLS),
    vm(COLS, COLS),
    vm(COLS, COLS),
    vm(COLS, COLS),
    vm(4 * COLS, LANES),
    vm(512, LANES),
    vm(512, LANES),
    vm(4, 128, LANES),
    vm(128, LANES, dtype=F32),
    vm(4, 32, LANES, dtype=F32),
    vm(32, LANES, dtype=F32),
    vm(4, 32, LANES, dtype=F32),
    vm(32, LANES),
    vm(4, 32, LANES),
    vm(4, 4, 32, LANES),
    vm(4, 4, 32, LANES),
    vm(6 * CH, LANES),
    vm(FAR, 32, LANES),
    vm(32, LANES),
    vm(NEAR, 32, LANES),
    vm(32, LANES),
    vm(12, 32, LANES),
    vm(16, LANES),
    vm(NEAR, 16, LANES),
    vm(16, LANES),
    vm(FAR, 16, LANES),
    pltpu.SemaphoreType.DMA((GROUPS,)),
    pltpu.SemaphoreType.DMA((GROUPS,)),
    pltpu.SemaphoreType.DMA((7,)),
]


def body(frames, w_in, grid_mix, block_mix, w_out, conv_w, cotangent):
    operands = (frames, w_in.T, grid_mix, block_mix, w_out, conv_w, cotangent)
    vmem = pl.BlockSpec(memory_space=pltpu.VMEM)
    shape = jax.ShapeDtypeStruct
    rest, gframe, early, tail, value = pl.pallas_call(
        kernel,
        out_shape=(
            shape((2, ROWS * CH, LANES), F32),
            shape((2, ROWS * CH, LANES), F32),
            shape((4 * COLS, LANES), BF),
            shape((12, 32, LANES), BF),
            shape((16, LANES), F32),
        ),
        in_specs=[pl.BlockSpec(memory_space=pltpu.HBM)] * 7,
        out_specs=(vmem,) * 5,
        scratch_shapes=SCRATCH,
        compiler_params=pltpu.CompilerParams(
            collective_id=0, has_side_effects=True, vmem_limit_bytes=32 * 1024 * 1024
        ),
    )(*[pltpu.with_memory_space_constraint(x, pltpu.HBM) for x in operands])
    restored, grad_frames, grad_w_in_t, grad_grid, grad_block, grad_w_out, grad_conv = pl.pallas_call(
        finish,
        out_shape=(
            shape((CH, ROWS, COLS), BF),
            shape((CH, ROWS, COLS), BF),
            shape((CH, 2 * CH), F32),
            shape((COLS, COLS), F32),
            shape((COLS, COLS), F32),
            shape((CH, CH), F32),
            shape((3, 3, CH, CH), F32),
        ),
        in_specs=[vmem] * 5,
        out_specs=(pl.BlockSpec(memory_space=pl.ANY),) * 7,
        scratch_shapes=[
            vm(CH, ROWS, COLS),
            vm(CH, ROWS, COLS),
            vm(CH, 2 * CH, dtype=F32),
            vm(COLS, COLS, dtype=F32),
            vm(COLS, COLS, dtype=F32),
            vm(CH, CH, dtype=F32),
            vm(3, 3, CH, CH, dtype=F32),
            pltpu.SemaphoreType.DMA((9,)),
        ],
        compiler_params=pltpu.CompilerParams(vmem_limit_bytes=16 * 1024 * 1024),
    )(rest, gframe, early, tail.reshape(6 * CH, LANES), value)
    return restored, grad_frames, grad_w_in_t.T, grad_grid, grad_block, grad_w_out, grad_conv


def solution(mesh):
    placed = (P(None, "ha", "wa"), P(), P(), P(), P(), P(), P(None, "ha", "wa"))
    return jax.shard_map(
        body,
        mesh=mesh,
        in_specs=placed,
        out_specs=(P(None, "ha", "wa"), P(None, "ha", "wa"), P(), P(), P(), P(), P()),
        check_vma=False,
    )
```

```python
import jax
import jax.numpy as jnp
from jax import lax
from jax.experimental import pallas as pl
from jax.experimental.pallas import tpu as pltpu
from jax.sharding import PartitionSpec as P

BF = jnp.bfloat16
F32 = jnp.float32
EPS = 1e-06
MESH = pl.DeviceIdType.MESH

CH = 64
HC = 32
ROWS = 16
COLS = 256
LANES = 128
NA = 16
NW = 8
NEAR = 8
FAR = 16

(G_ROW0, G_PACK0, G_ROW1, G_PACK1) = range(4)
(G_E0, G_E1, G_E2, G_E3, G_E4, G_E5, G_E6, G_T1, G_T2, G_T3, G_Q1, G_Q2) = range(4, 16)
VALUES, BACKS = (0, 1), (2, 3)
G_A, G_B, G_C, G_D = 16, 20, 24, 28
GROUPS = 32
QC = 16


def dot(a, b):
    return lax.dot_general(a, b, (((1,), (0,)), ((), ())), preferred_element_type=F32)


def dot_nt(a, b):
    return lax.dot_general(a, b, (((1,), (1,)), ((), ())), preferred_element_type=F32)


def dot_tn(a, b):
    return lax.dot_general(a, b, (((0,), (0,)), ((), ())), preferred_element_type=F32)


def swap_granules(load, store, depth):
    lane = lax.broadcasted_iota(jnp.int16, (depth, LANES), 1)
    for row_half in range(2):
        for col_half in range(2):
            held = [load(row_half * 8 + k, col_half) for k in range(8)]
            for s in range(3):
                width = 16 << s
                low = (lane & width) == 0
                for k in range(8):
                    if not k & (1 << s):
                        a, b = held[k], held[k | (1 << s)]
                        held[k] = jnp.where(low, a, pltpu.roll(b, width, 1))
                        held[k | (1 << s)] = jnp.where(low, pltpu.roll(a, LANES - width, 1), b)
            for k in range(8):
                store(col_half * 8 + k, row_half, held[k])


def half(t):
    return slice(t * LANES, (t + 1) * LANES)


def loop(count, step, carry=0, unroll=1):
    return lax.fori_loop(0, count, step, carry, unroll=unroll)


def gelu_parts(x):
    root = 0.7978845608028654
    cube = root * 0.044715
    square = x * x
    h = 0.5 * jnp.tanh(x * (cube * square + root)) + 0.5
    value = x * h
    return value, h + value * (1.0 - h) * ((6.0 * cube) * square + 2.0 * root)


def kernel(
    frames_hbm, w_in_t_hbm, grid_mix_hbm, block_mix_hbm, w_out_hbm, conv_w_hbm, cot_hbm,
    rest_out, gframe_out, early_out, tail_out, value_out,
    frames, w_in_t, grid_mix, block_mix, w_out, conv_w, cot, w_in,
    turn, xb, nb, unit, inv, dgelu, gates, bval, u3, v3, gj, gg, xt, bt, bm, gbv,
    a, a_in, x32, b, b_in, c, c_in, d, d_in,
    gated, gbef, jp, row_in, pack_out, pack_in, edge_l, edge_r,
    mixp, mixp_t, gather, spread, se, re0, e0, re1, e1, re2, e2, re3, e3, re4, re5, re6,
    st, rt1, t1, rt2, t2, rt3, sq, rq1, q1, rq2,
    ssem, rsem, isem,
):
    ia = lax.axis_index("ha")
    iw = lax.axis_index("wa")
    up, down = lax.rem(ia + NA - 1, NA), lax.rem(ia + 1, NA)
    left, right = lax.rem(iw + NW - 1, NW), lax.rem(iw + 1, NW)
    lane = lax.broadcasted_iota(jnp.int16, (CH, LANES), 1)
    lane_wide = lax.broadcasted_iota(jnp.int32, (CH, LANES), 1)

    loads = [
        pltpu.make_async_copy(src, dst, isem.at[k])
        for k, (src, dst) in enumerate(
            [
                (frames_hbm, frames),
                (w_in_t_hbm, w_in_t),
                (cot_hbm, cot),
                (conv_w_hbm, conv_w),
                (w_out_hbm, w_out),
                (block_mix_hbm, block_mix),
                (grid_mix_hbm, grid_mix),
            ]
        )
    ]
    for load in loads:
        load.start()

    def push(src, dst, g, where):
        pltpu.make_async_remote_copy(
            src_ref=src, dst_ref=dst, send_sem=ssem.at[g], recv_sem=rsem.at[g], device_id=where, device_id_type=MESH
        ).start()

    near = lax.rem(iw, 2) * 4 + lax.rem(ia, 4)
    far = ia // 4 * 4 + iw // 2

    def near_device(peer):
        return ia // 4 * 4 + lax.rem(peer, 4), iw // 2 * 2 + peer // 4

    def far_device(peer):
        return peer // 4 * 4 + lax.rem(ia, 4), lax.rem(peer, 4) * 2 + lax.rem(iw, 2)

    near_peers = [lax.rem(near + k, NEAR) for k in range(1, NEAR)]
    far_peers = [lax.rem(far + k, FAR) for k in range(1, FAR)]
    twin = near + 1 - 2 * lax.rem(near, 2)

    near_places = [near_device(peer) for peer in near_peers]
    far_places = [far_device(peer) for peer in far_peers]

    def over_near(src_of, dst, g):
        for peer, place in zip(near_peers, near_places):
            push(src_of(peer), dst, g, place)

    def over_far(src_of, dst, g):
        for peer, place in zip(far_peers, far_places):
            push(src_of(peer), dst, g, place)

    def over_x(src_of, dst, g):
        for k in range(1, 4):
            peer = lax.rem(iw // 2 + k, 4)
            push(src_of(peer), dst, g, (ia, peer * 2 + lax.rem(iw, 2)))

    def over_z(src_of, dst, g):
        for k in range(1, 4):
            peer = lax.rem(ia // 4 + k, 4)
            push(src_of(peer), dst, g, (peer * 4 + lax.rem(ia, 4), iw))

    def over_y(src_of, dst, g):
        for k in range(1, 4):
            peer = lax.rem(near + 2 * k, NEAR)
            push(src_of(peer // 2), dst, g, near_device(peer))

    def arrived(ref, g):
        pltpu.make_async_copy(ref, ref, rsem.at[g]).wait()

    def gone(ref, g):
        pltpu.make_async_copy(ref, ref, ssem.at[g]).wait()

    def from_near(ref, g):
        arrived(ref.at[pl.ds(0, NEAR - 1)], g)

    def from_far(ref, g):
        arrived(ref.at[pl.ds(0, FAR - 1)], g)

    mine = lax.rem(near, 2) * 512
    level, across, deep = near // 2, iw // 2, ia // 4

    barrier = pltpu.get_barrier_semaphore()
    peers = [near_device(peer) for peer in near_peers]
    peers += [far_device(peer) for peer in far_peers]
    peers += [(a, b) for a in (up, ia, down) for b in (left, right)] + [(up, iw), (down, iw)]
    for peer in peers:
        pl.semaphore_signal(barrier, inc=1, device_id=peer, device_id_type=MESH)

    def turn_in(src):
        for t in range(2):
            turn[t] = src[:, :, half(t)].astype(F32).reshape(CH * ROWS, LANES)

    def turned(r, t):
        return turn[t, pl.ds(r, CH, stride=ROWS), :]

    def edges(pack, t0, t1, r):
        pack = jnp.where(lane_wide == r, pltpu.roll(t0, r, 1), pack)
        return jnp.where(lane_wide == ROWS + r, pltpu.roll(t1, r + 17, 1), pack)

    def send_halo(field, pack, which, g_row, g_pack):
        pack_out[which] = jnp.concatenate([pack, jnp.zeros_like(pack)], axis=0).T[0:32]
        push(field.at[1, CH : 2 * CH], row_in.at[which, 1], g_row, (up, iw))
        push(field.at[ROWS, CH : 2 * CH], row_in.at[which, 0], g_row, (down, iw))
        for slot, where in enumerate(
            [(ia, right), (down, right), (up, right), (ia, left), (down, left), (up, left)]
        ):
            part = pack_out.at[which, pl.ds(16 if slot < 3 else 0, 16)]
            push(part, pack_in.at[which, pl.ds(16 * slot, 16)], g_pack, where)

    def take_halo(field, which, g_row, g_pack):
        arrived(row_in.at[which], g_row)
        arrived(pack_in.at[which], g_pack)
        field[0, CH : 2 * CH] = jnp.where(ia > 0, row_in[which, 0], jnp.zeros((CH, COLS), BF))
        field[ROWS + 1, CH : 2 * CH] = jnp.where(ia < NA - 1, row_in[which, 1], jnp.zeros((CH, COLS), BF))
        first = jnp.where(ia > 0, 0, 1)
        last = jnp.where(ia < NA - 1, ROWS + 2, ROWS + 1)
        got = jnp.concatenate([pack_in[which], jnp.zeros((32, LANES), BF)], axis=0).T[0:CH]

        def assemble(middle, above, below, has):
            joined = jnp.where(lane == 0, above, jnp.where(lane == ROWS + 1, below, middle))
            inside = (lane_wide >= first) & (lane_wide < jnp.where(has, last, 0))
            return jnp.where(inside, joined, jnp.zeros_like(joined))

        edge_l[...] = assemble(pltpu.roll(got, 1, 1), pltpu.roll(got, 97, 1), pltpu.roll(got, 113, 1), iw > 0)
        edge_r[...] = assemble(pltpu.roll(got, 81, 1), pltpu.roll(got, 49, 1), pltpu.roll(got, 65, 1), iw < NW - 1)

        def shifts(p, carry):
            t0 = field[p, CH : 2 * CH, half(0)]
            t1 = field[p, CH : 2 * CH, half(1)]
            a0, a1 = pltpu.roll(t0, 1, 1), pltpu.roll(t1, 1, 1)
            b0, b1 = pltpu.roll(t0, LANES - 1, 1), pltpu.roll(t1, LANES - 1, 1)
            lh = pltpu.roll(edge_l[...], lax.rem(LANES - p, LANES), 1)
            rh = pltpu.roll(edge_r[...], LANES - 1 - p, 1)
            field[p, 0:CH, half(0)] = jnp.where(lane == 0, lh, a0)
            field[p, 0:CH, half(1)] = jnp.where(lane == 0, a0, a1)
            field[p, 2 * CH :, half(0)] = jnp.where(lane == LANES - 1, b1, b0)
            field[p, 2 * CH :, half(1)] = jnp.where(lane == LANES - 1, rh, b1)
            return carry

        loop(ROWS + 2, shifts, unroll=9)

    def conv_step(w, field, r):
        return dot(w, field[pl.ds(r, 3)].reshape(9 * CH, COLS))

    def step_a(n):
        over_near(lambda peer: a.at[n, peer], a_in.at[n, near], G_A + n)

    def step_b(n):
        arrived(a_in.at[n, pl.ds(0, NEAR - 1)], G_A + n)

        def widen(j, carry):
            for t in range(2):
                for r in range(2):
                    x32[n, pl.ds((r * 16 + j * 2 + t) * QC, QC), :] = a_in[n, j, t, r].astype(F32)
            return carry

        loop(NEAR, widen, unroll=8)

        for peer, place in zip([*far_peers, far], [*far_places, None]):
            base = peer // 8 * (16 * QC) + lax.rem(peer, 8) * 2
            slot = b_in if peer is far else b
            for k in range(2):
                slot[n, peer, :, half(k)] = x32[n, pl.ds(base + k, 16, stride=QC), :].astype(BF)
            if peer is not far:
                push(b.at[n, peer], b_in.at[n, far], G_B + n, place)

    def table(n):
        return b_in[n].reshape(256, 256)

    def step_c(n, mix):
        arrived(b_in.at[n, pl.ds(0, FAR - 1)], G_B + n)
        c[n] = dot(mix[...], table(n)).astype(BF).reshape(FAR, 16, 256)
        over_far(lambda peer: c.at[n, peer], c_in.at[n, far], G_C + n)
        c_in[n, far] = c[n, far]

    def step_d(n):
        arrived(c_in.at[n, pl.ds(0, FAR - 1)], G_C + n)

        def unpick(q, carry):
            for r in range(2):
                for k in range(2):
                    x32[n, pl.ds((r * QC + q * 2 + k) * 16, 16), :] = c_in[n, r * 8 + q, :, half(k)].astype(F32)
            return carry

        loop(8, unpick, unroll=8)

        for peer, place in zip([*near_peers, near], [*near_places, None]):
            slot = d_in if peer is near else d
            for t in range(2):
                for r in range(2):
                    slot[n, peer, t, r] = x32[n, pl.ds(r * QC * 16 + peer * 2 + t, QC, stride=16), :].astype(BF)
            if peer is not near:
                push(d.at[n, peer], d_in.at[n, near], G_D + n, place)

    def step_e(n):
        arrived(d_in.at[n, pl.ds(0, NEAR - 1)], G_D + n)

    def order(cell, row):
        found = (row & 0xC1) | ((row & 6) << 3) | ((row & 48) >> 2) | ((row & 8) >> 2)
        return jnp.where(cell == found, 1.0, 0.0).astype(BF)

    loads[0].wait()
    loads[1].wait()
    turn_in(frames)
    w_in[...] = w_in_t[...].astype(F32).T.astype(BF)

    def value_row(slot, peer, low):
        r = peer * 2 + low
        for t in range(2):
            x = turned(r, t)
            xb[r, :, half(t)] = x.astype(BF)
            off = x - jnp.mean(x, axis=0, keepdims=True)
            rstd = lax.rsqrt(jnp.mean(off * off, axis=0, keepdims=True) + EPS)
            u = off * rstd
            unit[r, :, half(t)] = u
            inv[r, :, half(t)] = jnp.broadcast_to(rstd, (8, LANES))
            nb[r, :, half(t)] = u.astype(BF)
        value, slope = gelu_parts(dot(w_in[HC:CH], nb[r]))
        dgelu[r, HC:CH] = slope
        value = value.astype(BF)
        for n in VALUES:
            for t in range(2):
                slot[n, peer, t, low] = value[n * QC : (n + 1) * QC, half(t)]

    for first in range(0, NEAR, 2):
        group = [*near_peers, near][first : first + 2]
        for peer in group:
            for low in range(2):
                value_row(a_in if peer is near else a, peer, low)
        if first == 0:
            pl.semaphore_wait(barrier, len(peers))
        for peer in group:
            if peer is not near:
                push(a.at[0, peer], a_in.at[0, near], G_A, near_device(peer))
    step_a(1)

    loads[2].wait()
    turn_in(cot)

    def cot_row(r, pack):
        t0, t1 = turned(r, 0).astype(BF), turned(r, 1).astype(BF)
        u3[r + 1, CH : 2 * CH, half(0)] = t0
        u3[r + 1, CH : 2 * CH, half(1)] = t1
        return edges(pack, t0, t1, r)

    pack = loop(ROWS, cot_row, jnp.zeros((CH, LANES), BF), unroll=8)
    send_halo(u3, pack, 0, G_ROW0, G_PACK0)

    def grid_gate_row(r, carry):
        value, slope = gelu_parts(dot(w_in[0:HC], nb[r]))
        gates[r, 0:HC] = value.astype(BF)
        dgelu[r, 0:HC] = slope
        return carry

    loop(ROWS, grid_gate_row, unroll=8)

    def block_gate_row(r, carry):
        value, slope = gelu_parts(dot(w_in[CH:], nb[r]))
        dgelu[r, CH:] = slope
        value = value.astype(BF)
        gates[r, HC:CH] = value[0:HC]
        bval[r] = value[HC:]
        return carry

    loop(ROWS, block_gate_row, unroll=8)
    for load in loads[3:]:
        load.wait()
    down_axis = lax.broadcasted_iota(jnp.int32, (COLS, COLS), 0)
    along_axis = lax.broadcasted_iota(jnp.int32, (COLS, COLS), 1)
    gather[...] = order(along_axis, down_axis)
    spread[...] = order(down_axis, along_axis)
    mixp[...] = dot(dot(gather[...], grid_mix[...]).astype(BF), spread[...]).astype(BF)
    mixp_t[...] = dot(dot_nt(gather[...], grid_mix[...]).astype(BF), spread[...]).astype(BF)

    back_w = jnp.concatenate(
        [conv_w[2 - a, 2 - b] for a in range(3) for b in range(3)], axis=0
    ).astype(F32).T.astype(BF)
    w_out_t = w_out[...].astype(F32).T.astype(BF)
    take_halo(u3, 0, G_ROW0, G_PACK0)

    def back_row(r):
        total = conv_step(back_w, u3, r)
        g = (total + u3[r + 1, CH : 2 * CH].astype(F32)).astype(BF)
        gj[r] = g
        up_gated = dot(w_out_t, g)
        gg[r] = up_gated
        mixed = (up_gated[0:HC] * gates[r, 0:HC].astype(F32)).astype(BF)
        for n in range(2):
            for t in range(2):
                a[2 + n, r // 2, t, r % 2] = mixed[n * QC : (n + 1) * QC, half(t)]

    step_b(0)
    for first in range(0, NEAR, 2):
        if first == NEAR // 2:
            step_b(1)
        for r in range(2 * first, 2 * first + 4):
            back_row(r)
        for peer in (first, first + 1):

            @pl.when(peer != near)
            def _():
                push(a.at[2, peer], a_in.at[2, near], G_A + 2, near_device(peer))

    step_a(3)
    for n in BACKS:
        a_in[n, near] = a[n, near]


    def put(ref):
        def store(k, t, value):
            ref[k, :, half(t)] = value

        return store

    swap_granules(lambda k, t: bval[k, :, half(t)], put(xt), HC)
    values = xt[...].reshape(ROWS * HC, COLS)
    mixed = dot_nt(values, block_mix[...]).astype(BF)
    swap_granules(lambda k, t: mixed[k * HC : (k + 1) * HC, half(t)], put(bm), HC)

    step_c(0, mixp)
    step_b(2)
    step_c(1, mixp)
    step_b(3)

    def block_back(k, t):
        return (gg[k, HC:, half(t)] * gates[k, HC:, half(t)].astype(F32)).astype(BF)

    swap_granules(block_back, put(bt), HC)
    backs = bt[...].reshape(ROWS * HC, COLS)
    unmixed = dot(backs, block_mix[...]).astype(BF)
    swap_granules(lambda k, t: unmixed[k * HC : (k + 1) * HC, half(t)], put(gbv), HC)
    part_block = dot_tn(backs, values).astype(BF)
    se[2 * COLS : 3 * COLS] = part_block[:, half(0)]
    se[3 * COLS :] = part_block[:, half(1)]

    def block_before_row(r, carry):
        d = dgelu[r, CH:]
        gbef[r, CH : CH + HC] = (d[0:HC] * (gg[r, HC:] * (bm[r].astype(F32) + 1.0))).astype(BF)
        gbef[r, CH + HC :] = (d[HC:] * gbv[r].astype(F32)).astype(BF)
        gbef[r, HC:CH] = jnp.zeros((HC, COLS), BF)
        return carry

    loop(ROWS, block_before_row, unroll=4)
    for k in (0, 1, ROWS + 2, ROWS + 3):
        jp[k] = jnp.zeros((CH, COLS), BF)

    step_d(0)
    step_d(1)
    step_c(2, mixp_t)
    step_c(3, mixp_t)

    part_grid = (dot_nt(table(2), table(0)) + dot_nt(table(3), table(1))).astype(BF)
    part_grid = dot(dot(spread[...], part_grid).astype(BF), gather[...]).astype(BF)
    se[0:COLS] = part_grid[:, half(0)]
    se[COLS : 2 * COLS] = part_grid[:, half(1)]
    push(se.at[pl.ds(pl.multiple_of(512 - mine, 512), 512)], re0, G_E0, near_device(twin))

    arrived(re0, G_E0)
    e0[...] = (se[pl.ds(pl.multiple_of(mine, 512), 512)].astype(F32) + re0[...].astype(F32)).astype(BF)
    over_y(lambda peer: e0.at[pl.ds(pl.multiple_of(peer * 128, 128), 128)], re1.at[level], G_E1)
    re1[level] = e0[pl.ds(pl.multiple_of(level * 128, 128), 128)]

    step_e(0)
    step_e(1)

    def returned(chains, r):
        return [
            jnp.concatenate([d_in[n, r // 2, t, lax.rem(r, 2)] for n in chains], axis=0).astype(F32) for t in range(2)
        ]

    def joined_row(r, pack):
        grid_mixed = returned(VALUES, r)
        for t in range(2):
            gates_t = gates[r, :, half(t)].astype(F32)
            more = grid_mixed[t] + 1.0
            gated[r, 0:HC, half(t)] = (gates_t[0:HC] * more).astype(BF)
            gated[r, HC:, half(t)] = (gates_t[HC:] * (bm[r, :, half(t)].astype(F32) + 1.0)).astype(BF)
            gbef[r, 0:HC, half(t)] = (dgelu[r, 0:HC, half(t)] * (gg[r, 0:HC, half(t)] * more)).astype(BF)
        j = (xb[r].astype(F32) + dot(w_out[...], gated[r])).astype(BF)
        jp[r + 2] = j
        v3[r + 1, CH : 2 * CH] = j
        return edges(pack, j[:, half(0)], j[:, half(1)], r)

    pack = loop(ROWS, joined_row, jnp.zeros((CH, LANES), BF), unroll=8)
    send_halo(v3, pack, 1, G_ROW1, G_PACK1)

    step_d(2)
    step_d(3)

    def pixels(ref, rows=slice(None)):
        return jnp.concatenate([ref[r, rows] for r in range(ROWS)], axis=1)

    p_conv = dot_nt(
        jnp.concatenate([u3[p] for p in range(ROWS + 2)], axis=1),
        jnp.concatenate([jp[p : p + 3].reshape(3 * CH, COLS) for p in range(ROWS + 2)], axis=1),
    )
    arrived(re1.at[pl.ds(0, 3)], G_E1)
    total = re1[0].astype(F32)
    for k in range(1, 4):
        total = total + re1[k].astype(F32)
    e1[...] = total
    over_x(lambda peer: e1.at[pl.ds(pl.multiple_of(peer * 32, 32), 32)], re2.at[across], G_E2)
    re2[across] = e1[pl.ds(pl.multiple_of(across * 32, 32), 32)]

    p_in = dot_nt(pixels(nb), pixels(gbef))
    p_out = dot_nt(pixels(gj), pixels(gated))
    st[0 : 3 * CH] = p_conv[:, half(0)].astype(BF)
    st[3 * CH : 4 * CH] = p_in.astype(BF)
    third = p_conv[:, 2 * CH :]
    st[4 * CH :] = jnp.concatenate(
        [third[: 2 * CH], jnp.concatenate([third[2 * CH :], p_out], axis=0)], axis=1
    ).astype(BF)
    summing = far < 12
    for peer, place in zip(far_peers, far_places):

        @pl.when(peer < 12)
        def _():
            push(st.at[pl.ds(pl.multiple_of(peer * 32, 32), 32)], rt1.at[far], G_T1, place)

    @pl.when(summing)
    def _():
        rt1[far] = st[pl.ds(pl.multiple_of(far * 32, 32), 32)]

    take_halo(v3, 1, G_ROW1, G_PACK1)

    arrived(re2.at[pl.ds(0, 3)], G_E2)
    e2[...] = re2[0] + re2[1] + re2[2] + re2[3]
    over_z(lambda peer: e2, re3.at[deep], G_E3)
    re3[deep] = e2[...]

    conv_k = jnp.concatenate(
        [conv_w[a, b].astype(F32).T for a in range(3) for b in range(3)], axis=0
    ).T.astype(BF)

    def out_row(r, carry):
        total = conv_step(conv_k, v3, r) + v3[r + 1, CH : 2 * CH].astype(F32)
        for t in range(2):
            rest_out[t, pl.ds(r * CH, CH), :] = total[:, half(t)]
        return carry

    loop(ROWS // 2, out_row, unroll=8)

    step_e(2)
    step_e(3)

    def value_before_row(r, carry):
        grid_back = returned(BACKS, r)
        for t in range(2):
            gbef[r, HC:CH, half(t)] = (dgelu[r, HC:CH, half(t)] * grid_back[t]).astype(BF)
        return carry

    loop(ROWS, value_before_row, unroll=4)
    p_value = dot_nt(pixels(gbef, slice(HC, CH)), pixels(nb))
    sq[...] = jnp.concatenate([p_value[0:16], p_value[16:]], axis=1).astype(BF)
    over_near(lambda peer: sq, rq1.at[near], G_Q1)
    rq1[near] = sq[...]

    for n in VALUES + BACKS:
        for ref, count, g in ((a_in, NEAR, G_A), (b_in, FAR, G_B), (c_in, FAR, G_C)):
            gone(ref.at[n, pl.ds(0, count - 1)], g + n)
    for n in VALUES:
        gone(d_in.at[n, pl.ds(0, NEAR - 1)], G_D + n)

    @pl.when(summing)
    def _():
        from_far(rt1, G_T1)
        total = rt1[0].astype(F32)
        for k in range(1, FAR):
            total = total + rt1[k].astype(F32)
        t1[...] = total.astype(BF)
        over_near(lambda peer: t1, rt2.at[near], G_T2)
        rt2[near] = t1[...]

    arrived(re3.at[pl.ds(0, 3)], G_E3)
    e3[...] = (re3[0] + re3[1] + re3[2] + re3[3]).astype(BF)
    over_x(lambda peer: e3, re4.at[across], G_E4)
    re4[across] = e3[...]

    def frame_row(r, carry):
        normed = dot(w_in_t[...], gbef[r])
        u = unit[r]
        mean_grad = jnp.mean(normed, axis=0, keepdims=True)
        mean_proj = jnp.mean(normed * u, axis=0, keepdims=True)
        source = gj[r].astype(F32) + inv[r, 0:1] * (normed - mean_grad - u * mean_proj)
        for t in range(2):
            gframe_out[t, pl.ds(r * CH, CH), :] = source[:, half(t)]
        return carry

    loop(ROWS, frame_row, unroll=8)

    from_near(rq1, G_Q1)
    total = rq1[0].astype(F32)
    for k in range(1, NEAR):
        total = total + rq1[k].astype(F32)
    q1[...] = total.astype(BF)
    over_far(lambda peer: q1, rq2.at[far], G_Q2)
    rq2[far] = q1[...]

    arrived(re4.at[pl.ds(0, 3)], G_E4)
    over_y(lambda peer: re4, re5.at[level], G_E5)
    re5[level] = re4[...]

    @pl.when(summing)
    def _():
        from_near(rt2, G_T2)
        total = rt2[0].astype(F32)
        for k in range(1, NEAR):
            total = total + rt2[k].astype(F32)
        t2[...] = total.astype(BF)
        over_far(lambda peer: t2, rt3.at[far], G_T3)
        rt3[far] = t2[...]

    loop(ROWS // 2, lambda r, carry: out_row(r + ROWS // 2, carry), unroll=8)

    from_far(rq2, G_Q2)
    total = rq2[0].astype(F32)
    for k in range(1, FAR):
        total = total + rq2[k].astype(F32)
    value_out[...] = total

    arrived(re5.at[pl.ds(0, 3)], G_E5)
    push(re5, re6, G_E6, near_device(twin))
    early_out[pl.ds(pl.multiple_of(mine, 512), 512)] = re5[...].reshape(512, LANES)

    @pl.when(summing)
    def _():
        arrived(rt3.at[pl.ds(0, 11)], G_T3)
        gone(rt1.at[pl.ds(0, 11)], G_T1)
        gone(rt2.at[pl.ds(0, NEAR - 1)], G_T2)
        gone(rt1.at[pl.ds(0, FAR - 1)], G_T3)

    @pl.when(far >= 12)
    def _():
        arrived(rt3, G_T3)
        gone(rt1.at[pl.ds(0, 12)], G_T1)

    tail_out[...] = rt3[...]
    arrived(re6, G_E6)
    early_out[pl.ds(pl.multiple_of(512 - mine, 512), 512)] = re6[...].reshape(512, LANES)

    for which, g_row, g_pack in ((0, G_ROW0, G_PACK0), (1, G_ROW1, G_PACK1)):
        gone(row_in.at[which], g_row)
        gone(pack_in.at[which], g_pack)
    for n in BACKS:
        gone(d_in.at[n, pl.ds(0, NEAR - 1)], G_D + n)
    gone(rq1.at[pl.ds(0, NEAR - 1)], G_Q1)
    gone(rq2.at[pl.ds(0, FAR - 1)], G_Q2)
    gone(re0, G_E0)
    for ref, g in ((re1, G_E1), (re2, G_E2), (re3, G_E3), (re4, G_E4), (re5, G_E5)):
        gone(ref.at[pl.ds(0, 3)], g)
    gone(re6, G_E6)


def finish(rest, gframe, early, tail, value, *refs):
    outs, sem = (refs[:7], refs[7:14]), refs[14]
    restored, grad_frames, grad_w_in_t, grad_grid, grad_block, grad_w_out, grad_conv = outs[1]
    copies = []

    def leave(k, part=None):
        src, dst = outs[1][k], outs[0][k]
        if part is not None:
            src, dst = src.at[part], dst.at[part]
        copies.append(pltpu.make_async_copy(src, dst, sem.at[len(copies)]))
        copies[-1].start()

    def turn_out(src, dst, k):
        for first in range(0, CH, CH // 2):

            def channel(c, carry):
                for t in range(2):
                    dst[first + c, :, half(t)] = src[t, pl.ds(first + c, ROWS, stride=CH), :].astype(BF)
                return carry

            loop(CH // 2, channel, unroll=16)
            leave(k, pl.ds(first, CH // 2))

    scale = float(ROWS * NA * COLS * NW) ** (-0.5)
    for k in range(2):
        grad_grid[:, half(k)] = early[k * COLS : (k + 1) * COLS].astype(F32) * scale
        grad_block[:, half(k)] = early[(2 + k) * COLS : (3 + k) * COLS].astype(F32) * scale
    leave(3)
    leave(4)
    turn_out(gframe, grad_frames, 1)
    turn_out(rest, restored, 0)
    quarter = value[...] * scale
    zeros = jnp.zeros((HC, CH), F32)
    quarter = jnp.concatenate([zeros, quarter[:, :CH], quarter[:, CH:], zeros, zeros], axis=0)
    grad_w_in_t[...] = tail[3 * CH : 4 * CH].astype(F32) * scale + quarter.T
    leave(2)
    last = tail[4 * CH :].astype(F32) * scale
    grad_w_out[...] = last[CH:, CH:]
    leave(5)
    for b in range(3):
        rows = slice((2 - b) * CH, (3 - b) * CH)
        pair = tail[rows].astype(F32) * scale
        grad_conv[0, b] = pair[:, :CH]
        grad_conv[1, b] = pair[:, CH:]
    grad_conv[2, 2] = last[:CH, :CH]
    grad_conv[2, 1] = last[CH:, :CH]
    grad_conv[2, 0] = last[:CH, CH:]
    leave(6)
    for copy in copies:
        copy.wait()


def vm(*shape, dtype=BF):
    return pltpu.VMEM(shape, dtype)


def exchange():
    message_w = vm(4, NEAR, 2, 2, QC, LANES)
    message_a = vm(4, FAR, 16, 256)
    return [message_w, message_w, vm(4, 2 * 16 * QC, LANES, dtype=F32)] + [message_a] * 4 + [message_w] * 2


SCRATCH = [
    vm(CH, ROWS, COLS),
    vm(CH, 2 * CH),
    vm(COLS, COLS),
    vm(COLS, COLS),
    vm(CH, CH),
    vm(3, 3, CH, CH),
    vm(CH, ROWS, COLS),
    vm(2 * CH, CH),
    vm(2, CH * ROWS, LANES, dtype=F32),
    vm(ROWS, CH, COLS),
    vm(ROWS, CH, COLS),
    vm(ROWS, CH, COLS, dtype=F32),
    vm(ROWS, 8, COLS, dtype=F32),
    vm(ROWS, 2 * CH, COLS, dtype=F32),
    vm(ROWS, CH, COLS),
    vm(ROWS, HC, COLS),
    vm(ROWS + 2, 3 * CH, COLS),
    vm(ROWS + 2, 3 * CH, COLS),
    vm(ROWS, CH, COLS),
    vm(ROWS, CH, COLS, dtype=F32),
    vm(ROWS, HC, COLS),
    vm(ROWS, HC, COLS),
    vm(ROWS, HC, COLS),
    vm(ROWS, HC, COLS),
    *exchange(),
    vm(ROWS, CH, COLS),
    vm(ROWS, 2 * CH, COLS),
    vm(ROWS + 4, CH, COLS),
    vm(2, 2, CH, COLS),
    vm(2, 32, LANES),
    vm(2, 96, LANES),
    vm(CH, LANES),
    vm(CH, LANES),
    vm(COLS, COLS),
    vm(COLS, COLS),
    vm(COLS, COLS),
    vm(COLS, COLS),
    vm(4 * COLS, LANES),
    vm(512, LANES),
    vm(512, LANES),
    vm(4, 128, LANES),
    vm(128, LANES, dtype=F32),
    vm(4, 32, LANES, dtype=F32),
    vm(32, LANES, dtype=F32),
    vm(4, 32, LANES, dtype=F32),
    vm(32, LANES),
    vm(4, 32, LANES),
    vm(4, 4, 32, LANES),
    vm(4, 4, 32, LANES),
    vm(6 * CH, LANES),
    vm(FAR, 32, LANES),
    vm(32, LANES),
    vm(NEAR, 32, LANES),
    vm(32, LANES),
    vm(12, 32, LANES),
    vm(16, LANES),
    vm(NEAR, 16, LANES),
    vm(16, LANES),
    vm(FAR, 16, LANES),
    pltpu.SemaphoreType.DMA((GROUPS,)),
    pltpu.SemaphoreType.DMA((GROUPS,)),
    pltpu.SemaphoreType.DMA((7,)),
]


def body(frames, w_in, grid_mix, block_mix, w_out, conv_w, cotangent):
    operands = (frames, w_in.T, grid_mix, block_mix, w_out, conv_w, cotangent)
    vmem = pl.BlockSpec(memory_space=pltpu.VMEM)
    shape = jax.ShapeDtypeStruct
    rest, gframe, early, tail, value = pl.pallas_call(
        kernel,
        out_shape=(
            shape((2, ROWS * CH, LANES), F32),
            shape((2, ROWS * CH, LANES), F32),
            shape((4 * COLS, LANES), BF),
            shape((12, 32, LANES), BF),
            shape((16, LANES), F32),
        ),
        in_specs=[pl.BlockSpec(memory_space=pltpu.HBM)] * 7,
        out_specs=(vmem,) * 5,
        scratch_shapes=SCRATCH,
        compiler_params=pltpu.CompilerParams(
            collective_id=0, has_side_effects=True, vmem_limit_bytes=32 * 1024 * 1024
        ),
    )(*[pltpu.with_memory_space_constraint(x, pltpu.HBM) for x in operands])
    restored, grad_frames, grad_w_in_t, grad_grid, grad_block, grad_w_out, grad_conv = pl.pallas_call(
        finish,
        out_shape=(
            shape((CH, ROWS, COLS), BF),
            shape((CH, ROWS, COLS), BF),
            shape((CH, 2 * CH), F32),
            shape((COLS, COLS), F32),
            shape((COLS, COLS), F32),
            shape((CH, CH), F32),
            shape((3, 3, CH, CH), F32),
        ),
        in_specs=[vmem] * 5,
        out_specs=(pl.BlockSpec(memory_space=pl.ANY),) * 7,
        scratch_shapes=[
            vm(CH, ROWS, COLS),
            vm(CH, ROWS, COLS),
            vm(CH, 2 * CH, dtype=F32),
            vm(COLS, COLS, dtype=F32),
            vm(COLS, COLS, dtype=F32),
            vm(CH, CH, dtype=F32),
            vm(3, 3, CH, CH, dtype=F32),
            pltpu.SemaphoreType.DMA((9,)),
        ],
        compiler_params=pltpu.CompilerParams(vmem_limit_bytes=16 * 1024 * 1024),
    )(rest, gframe, early, tail.reshape(6 * CH, LANES), value)
    return restored, grad_frames, grad_w_in_t.T, grad_grid, grad_block, grad_w_out, grad_conv


def solution(mesh):
    placed = (P(None, "ha", "wa"), P(), P(), P(), P(), P(), P(None, "ha", "wa"))
    return jax.shard_map(
        body,
        mesh=mesh,
        in_specs=placed,
        out_specs=(P(None, "ha", "wa"), P(None, "ha", "wa"), P(), P(), P(), P(), P()),
        check_vma=False,
    )
```

```python
import jax
import jax.numpy as jnp
from jax import lax
from jax.experimental import pallas as pl
from jax.experimental.pallas import tpu as pltpu
from jax.sharding import PartitionSpec as P

BF = jnp.bfloat16
F32 = jnp.float32
EPS = 1e-06
MESH = pl.DeviceIdType.MESH

CH = 64
HC = 32
ROWS = 16
COLS = 256
LANES = 128
NA = 16
NW = 8
NEAR = 8
FAR = 16

(G_ROW0, G_PACK0, G_ROW1, G_PACK1) = range(4)
(G_E0, G_E1, G_E2, G_E3, G_E4, G_E5, G_E6, G_T1, G_T2, G_T3, G_Q1, G_Q2) = range(4, 16)
VALUES, BACKS = (0, 1), (2, 3)
G_A, G_B, G_C, G_D = 16, 20, 24, 28
GROUPS = 32
QC = 16


def dot(a, b):
    return lax.dot_general(a, b, (((1,), (0,)), ((), ())), preferred_element_type=F32)


def dot_nt(a, b):
    return lax.dot_general(a, b, (((1,), (1,)), ((), ())), preferred_element_type=F32)


def dot_tn(a, b):
    return lax.dot_general(a, b, (((0,), (0,)), ((), ())), preferred_element_type=F32)


def swap_granules(load, store, depth):
    lane = lax.broadcasted_iota(jnp.int16, (depth, LANES), 1)
    for row_half in range(2):
        for col_half in range(2):
            held = [load(row_half * 8 + k, col_half) for k in range(8)]
            for s in range(3):
                width = 16 << s
                low = (lane & width) == 0
                for k in range(8):
                    if not k & (1 << s):
                        a, b = held[k], held[k | (1 << s)]
                        held[k] = jnp.where(low, a, pltpu.roll(b, width, 1))
                        held[k | (1 << s)] = jnp.where(low, pltpu.roll(a, LANES - width, 1), b)
            for k in range(8):
                store(col_half * 8 + k, row_half, held[k])


def half(t):
    return slice(t * LANES, (t + 1) * LANES)


def loop(count, step, carry=0, unroll=1):
    return lax.fori_loop(0, count, step, carry, unroll=unroll)


def gelu_parts(x):
    root = 0.7978845608028654
    cube = root * 0.044715
    square = x * x
    h = 0.5 * jnp.tanh(x * (cube * square + root)) + 0.5
    value = x * h
    return value, h + value * (1.0 - h) * ((6.0 * cube) * square + 2.0 * root)


def kernel(
    frames_hbm, w_in_t_hbm, grid_mix_hbm, block_mix_hbm, w_out_hbm, conv_w_hbm, cot_hbm,
    rest_out, gframe_out, early_out, tail_out, value_out,
    frames, w_in_t, grid_mix, block_mix, w_out, conv_w, cot, w_in,
    turn, xb, nb, unit, inv, dgelu, gates, bval, u3, v3, gj, gg, xt, bt, bm, gbv,
    a, a_in, x32, b, b_in, c, c_in, d, d_in,
    gated, gbef, jp, row_in, pack_out, pack_in, edge_l, edge_r,
    mixp, mixp_t, gather, spread, se, re0, e0, re1, e1, re2, e2, re3, e3, re4, re5, re6,
    st, rt1, t1, rt2, t2, rt3, sq, rq1, q1, rq2,
    ssem, rsem, isem,
):
    ia = lax.axis_index("ha")
    iw = lax.axis_index("wa")
    up, down = lax.rem(ia + NA - 1, NA), lax.rem(ia + 1, NA)
    left, right = lax.rem(iw + NW - 1, NW), lax.rem(iw + 1, NW)
    lane = lax.broadcasted_iota(jnp.int16, (CH, LANES), 1)
    lane_wide = lax.broadcasted_iota(jnp.int32, (CH, LANES), 1)

    loads = [
        pltpu.make_async_copy(src, dst, isem.at[k])
        for k, (src, dst) in enumerate(
            [
                (frames_hbm, frames),
                (w_in_t_hbm, w_in_t),
                (cot_hbm, cot),
                (conv_w_hbm, conv_w),
                (w_out_hbm, w_out),
                (block_mix_hbm, block_mix),
                (grid_mix_hbm, grid_mix),
            ]
        )
    ]
    for load in loads:
        load.start()

    def push(src, dst, g, where):
        pltpu.make_async_remote_copy(
            src_ref=src, dst_ref=dst, send_sem=ssem.at[g], recv_sem=rsem.at[g], device_id=where, device_id_type=MESH
        ).start()

    near = lax.rem(iw, 2) * 4 + lax.rem(ia, 4)
    far = ia // 4 * 4 + iw // 2

    def near_device(peer):
        return ia // 4 * 4 + lax.rem(peer, 4), iw // 2 * 2 + peer // 4

    def far_device(peer):
        return peer // 4 * 4 + lax.rem(ia, 4), lax.rem(peer, 4) * 2 + lax.rem(iw, 2)

    near_peers = [lax.rem(near + k, NEAR) for k in range(1, NEAR)]
    far_peers = [lax.rem(far + k, FAR) for k in range(1, FAR)]
    twin = near + 1 - 2 * lax.rem(near, 2)

    near_places = [near_device(peer) for peer in near_peers]
    far_places = [far_device(peer) for peer in far_peers]

    def over_near(src_of, dst, g):
        for peer, place in zip(near_peers, near_places):
            push(src_of(peer), dst, g, place)

    def over_far(src_of, dst, g):
        for peer, place in zip(far_peers, far_places):
            push(src_of(peer), dst, g, place)

    def over_x(src_of, dst, g):
        for k in range(1, 4):
            peer = lax.rem(iw // 2 + k, 4)
            push(src_of(peer), dst, g, (ia, peer * 2 + lax.rem(iw, 2)))

    def over_z(src_of, dst, g):
        for k in range(1, 4):
            peer = lax.rem(ia // 4 + k, 4)
            push(src_of(peer), dst, g, (peer * 4 + lax.rem(ia, 4), iw))

    def over_y(src_of, dst, g):
        for k in range(1, 4):
            peer = lax.rem(near + 2 * k, NEAR)
            push(src_of(peer // 2), dst, g, near_device(peer))

    def arrived(ref, g):
        pltpu.make_async_copy(ref, ref, rsem.at[g]).wait()

    def gone(ref, g):
        pltpu.make_async_copy(ref, ref, ssem.at[g]).wait()

    def from_near(ref, g):
        arrived(ref.at[pl.ds(0, NEAR - 1)], g)

    def from_far(ref, g):
        arrived(ref.at[pl.ds(0, FAR - 1)], g)

    mine = lax.rem(near, 2) * 512
    level, across, deep = near // 2, iw // 2, ia // 4

    barrier = pltpu.get_barrier_semaphore()
    peers = [near_device(peer) for peer in near_peers]
    peers += [far_device(peer) for peer in far_peers]
    peers += [(a, b) for a in (up, ia, down) for b in (left, right)] + [(up, iw), (down, iw)]
    for peer in peers:
        pl.semaphore_signal(barrier, inc=1, device_id=peer, device_id_type=MESH)

    def turn_in(src):
        for t in range(2):
            turn[t] = src[:, :, half(t)].astype(F32).reshape(CH * ROWS, LANES)

    def turned(r, t):
        return turn[t, pl.ds(r, CH, stride=ROWS), :]

    def edges(pack, t0, t1, r):
        pack = jnp.where(lane_wide == r, pltpu.roll(t0, r, 1), pack)
        return jnp.where(lane_wide == ROWS + r, pltpu.roll(t1, r + 17, 1), pack)

    def send_halo(field, pack, which, g_row, g_pack):
        pack_out[which] = jnp.concatenate([pack, jnp.zeros_like(pack)], axis=0).T[0:32]
        push(field.at[1, CH : 2 * CH], row_in.at[which, 1], g_row, (up, iw))
        push(field.at[ROWS, CH : 2 * CH], row_in.at[which, 0], g_row, (down, iw))
        for slot, where in enumerate(
            [(ia, right), (down, right), (up, right), (ia, left), (down, left), (up, left)]
        ):
            part = pack_out.at[which, pl.ds(16 if slot < 3 else 0, 16)]
            push(part, pack_in.at[which, pl.ds(16 * slot, 16)], g_pack, where)

    def take_halo(field, which, g_row, g_pack):
        arrived(row_in.at[which], g_row)
        arrived(pack_in.at[which], g_pack)
        field[0, CH : 2 * CH] = jnp.where(ia > 0, row_in[which, 0], jnp.zeros((CH, COLS), BF))
        field[ROWS + 1, CH : 2 * CH] = jnp.where(ia < NA - 1, row_in[which, 1], jnp.zeros((CH, COLS), BF))
        first = jnp.where(ia > 0, 0, 1)
        last = jnp.where(ia < NA - 1, ROWS + 2, ROWS + 1)
        got = jnp.concatenate([pack_in[which], jnp.zeros((32, LANES), BF)], axis=0).T[0:CH]

        def assemble(middle, above, below, has):
            joined = jnp.where(lane == 0, above, jnp.where(lane == ROWS + 1, below, middle))
            inside = (lane_wide >= first) & (lane_wide < jnp.where(has, last, 0))
            return jnp.where(inside, joined, jnp.zeros_like(joined))

        edge_l[...] = assemble(pltpu.roll(got, 1, 1), pltpu.roll(got, 97, 1), pltpu.roll(got, 113, 1), iw > 0)
        edge_r[...] = assemble(pltpu.roll(got, 81, 1), pltpu.roll(got, 49, 1), pltpu.roll(got, 65, 1), iw < NW - 1)

        def shifts(p, carry):
            t0 = field[p, CH : 2 * CH, half(0)]
            t1 = field[p, CH : 2 * CH, half(1)]
            a0, a1 = pltpu.roll(t0, 1, 1), pltpu.roll(t1, 1, 1)
            b0, b1 = pltpu.roll(t0, LANES - 1, 1), pltpu.roll(t1, LANES - 1, 1)
            lh = pltpu.roll(edge_l[...], lax.rem(LANES - p, LANES), 1)
            rh = pltpu.roll(edge_r[...], LANES - 1 - p, 1)
            field[p, 0:CH, half(0)] = jnp.where(lane == 0, lh, a0)
            field[p, 0:CH, half(1)] = jnp.where(lane == 0, a0, a1)
            field[p, 2 * CH :, half(0)] = jnp.where(lane == LANES - 1, b1, b0)
            field[p, 2 * CH :, half(1)] = jnp.where(lane == LANES - 1, rh, b1)
            return carry

        loop(ROWS + 2, shifts, unroll=9)

    def conv_start(w, field):
        y = dot(w, field[0])
        z = dot(w, field[1])
        return z[0:CH], y[0:CH] + z[CH : 2 * CH]

    def conv_step(w, field, r, carry):
        later, now = carry
        y = dot(w, field[r + 2])
        return now + y[2 * CH :], (y[0:CH], later + y[CH : 2 * CH])

    def step_a(n):
        over_near(lambda peer: a.at[n, peer], a_in.at[n, near], G_A + n)

    def step_b(n):
        arrived(a_in.at[n, pl.ds(0, NEAR - 1)], G_A + n)

        def widen(j, carry):
            for t in range(2):
                for r in range(2):
                    x32[n, pl.ds((r * 16 + j * 2 + t) * QC, QC), :] = a_in[n, j, t, r].astype(F32)
            return carry

        loop(NEAR, widen, unroll=8)

        for peer, place in zip([*far_peers, far], [*far_places, None]):
            base = peer // 8 * (16 * QC) + lax.rem(peer, 8) * 2
            slot = b_in if peer is far else b
            for k in range(2):
                slot[n, peer, :, half(k)] = x32[n, pl.ds(base + k, 16, stride=QC), :].astype(BF)
            if peer is not far:
                push(b.at[n, peer], b_in.at[n, far], G_B + n, place)

    def table(n):
        return b_in[n].reshape(256, 256)

    def step_c(n, mix):
        arrived(b_in.at[n, pl.ds(0, FAR - 1)], G_B + n)
        c[n] = dot(mix[...], table(n)).astype(BF).reshape(FAR, 16, 256)
        over_far(lambda peer: c.at[n, peer], c_in.at[n, far], G_C + n)
        c_in[n, far] = c[n, far]

    def step_d(n):
        arrived(c_in.at[n, pl.ds(0, FAR - 1)], G_C + n)

        def unpick(q, carry):
            for r in range(2):
                for k in range(2):
                    x32[n, pl.ds((r * QC + q * 2 + k) * 16, 16), :] = c_in[n, r * 8 + q, :, half(k)].astype(F32)
            return carry

        loop(8, unpick, unroll=8)

        for peer, place in zip([*near_peers, near], [*near_places, None]):
            slot = d_in if peer is near else d
            for t in range(2):
                for r in range(2):
                    slot[n, peer, t, r] = x32[n, pl.ds(r * QC * 16 + peer * 2 + t, QC, stride=16), :].astype(BF)
            if peer is not near:
                push(d.at[n, peer], d_in.at[n, near], G_D + n, place)

    def step_e(n):
        arrived(d_in.at[n, pl.ds(0, NEAR - 1)], G_D + n)

    def order(cell, row):
        found = (row & 0xC1) | ((row & 6) << 3) | ((row & 48) >> 2) | ((row & 8) >> 2)
        return jnp.where(cell == found, 1.0, 0.0).astype(BF)

    loads[0].wait()
    loads[1].wait()
    turn_in(frames)
    w_in[...] = w_in_t[...].astype(F32).T.astype(BF)

    def value_row(slot, peer, low):
        r = peer * 2 + low
        for t in range(2):
            x = turned(r, t)
            xb[r, :, half(t)] = x.astype(BF)
            off = x - jnp.mean(x, axis=0, keepdims=True)
            rstd = lax.rsqrt(jnp.mean(off * off, axis=0, keepdims=True) + EPS)
            u = off * rstd
            unit[r, :, half(t)] = u
            inv[r, :, half(t)] = jnp.broadcast_to(rstd, (8, LANES))
            nb[r, :, half(t)] = u.astype(BF)
        value, slope = gelu_parts(dot(w_in[HC:CH], nb[r]))
        dgelu[r, HC:CH] = slope
        value = value.astype(BF)
        for n in VALUES:
            for t in range(2):
                slot[n, peer, t, low] = value[n * QC : (n + 1) * QC, half(t)]

    for first in range(0, NEAR, 4):
        group = [*near_peers, near][first : first + 4]
        for peer in group:
            for low in range(2):
                value_row(a_in if peer is near else a, peer, low)
        if first == 0:
            pl.semaphore_wait(barrier, len(peers))
        for peer in group:
            if peer is not near:
                push(a.at[0, peer], a_in.at[0, near], G_A, near_device(peer))
    step_a(1)

    loads[2].wait()
    turn_in(cot)

    def cot_row(r, pack):
        t0, t1 = turned(r, 0).astype(BF), turned(r, 1).astype(BF)
        u3[r + 1, CH : 2 * CH, half(0)] = t0
        u3[r + 1, CH : 2 * CH, half(1)] = t1
        return edges(pack, t0, t1, r)

    pack = loop(ROWS, cot_row, jnp.zeros((CH, LANES), BF), unroll=16)
    send_halo(u3, pack, 0, G_ROW0, G_PACK0)

    def grid_gate_row(r, carry):
        value, slope = gelu_parts(dot(w_in[0:HC], nb[r]))
        gates[r, 0:HC] = value.astype(BF)
        dgelu[r, 0:HC] = slope
        return carry

    loop(ROWS, grid_gate_row, unroll=16)

    def block_gate_row(r, carry):
        value, slope = gelu_parts(dot(w_in[CH:], nb[r]))
        dgelu[r, CH:] = slope
        value = value.astype(BF)
        gates[r, HC:CH] = value[0:HC]
        bval[r] = value[HC:]
        return carry

    loop(ROWS, block_gate_row, unroll=16)
    for load in loads[3:]:
        load.wait()
    down_axis = lax.broadcasted_iota(jnp.int32, (COLS, COLS), 0)
    along_axis = lax.broadcasted_iota(jnp.int32, (COLS, COLS), 1)
    gather[...] = order(along_axis, down_axis)
    spread[...] = order(down_axis, along_axis)
    mixp[...] = dot(dot(gather[...], grid_mix[...]).astype(BF), spread[...]).astype(BF)
    mixp_t[...] = mixp[...].T

    back_w = jnp.concatenate(
        [jnp.concatenate([conv_w[2 - a, 2 - b] for a in range(3)], axis=1) for b in range(3)], axis=0
    ).astype(F32).T.astype(BF)
    w_out_t = w_out[...].astype(F32).T.astype(BF)
    take_halo(u3, 0, G_ROW0, G_PACK0)

    def back_row(r, carry):
        total, carry = conv_step(back_w, u3, r, carry)
        g = (total + u3[r + 1, CH : 2 * CH].astype(F32)).astype(BF)
        gj[r] = g
        up_gated = dot(w_out_t, g)
        gg[r] = up_gated
        mixed = (up_gated[0:HC] * gates[r, 0:HC].astype(F32)).astype(BF)
        for n in range(2):
            for t in range(2):
                a[2 + n, r // 2, t, r % 2] = mixed[n * QC : (n + 1) * QC, half(t)]
        return carry

    step_b(0)
    carry = conv_start(back_w, u3)
    for first in range(0, NEAR, 4):
        if first:
            step_b(1)
        for r in range(2 * first, 2 * first + 8):
            carry = back_row(r, carry)
        for peer in range(first, first + 4):

            @pl.when(peer != near)
            def _():
                push(a.at[2, peer], a_in.at[2, near], G_A + 2, near_device(peer))

    step_a(3)
    for n in BACKS:
        a_in[n, near] = a[n, near]


    def put(ref):
        def store(k, t, value):
            ref[k, :, half(t)] = value

        return store

    swap_granules(lambda k, t: bval[k, :, half(t)], put(xt), HC)
    values = xt[...].reshape(ROWS * HC, COLS)
    mixed = dot_nt(values, block_mix[...]).astype(BF)
    swap_granules(lambda k, t: mixed[k * HC : (k + 1) * HC, half(t)], put(bm), HC)

    step_c(0, mixp)
    step_b(2)
    step_c(1, mixp)
    step_b(3)

    def block_back(k, t):
        return (gg[k, HC:, half(t)] * gates[k, HC:, half(t)].astype(F32)).astype(BF)

    swap_granules(block_back, put(bt), HC)
    backs = bt[...].reshape(ROWS * HC, COLS)
    unmixed = dot(backs, block_mix[...]).astype(BF)
    swap_granules(lambda k, t: unmixed[k * HC : (k + 1) * HC, half(t)], put(gbv), HC)
    part_block = dot_tn(backs, values).astype(BF)
    se[2 * COLS : 3 * COLS] = part_block[:, half(0)]
    se[3 * COLS :] = part_block[:, half(1)]

    def block_before_row(r, carry):
        d = dgelu[r, CH:]
        gbef[r, CH : CH + HC] = (d[0:HC] * (gg[r, HC:] * (bm[r].astype(F32) + 1.0))).astype(BF)
        gbef[r, CH + HC :] = (d[HC:] * gbv[r].astype(F32)).astype(BF)
        gbef[r, HC:CH] = jnp.zeros((HC, COLS), BF)
        return carry

    loop(ROWS, block_before_row, unroll=8)
    for k in (0, 1, ROWS + 2, ROWS + 3):
        jp[k] = jnp.zeros((CH, COLS), BF)

    step_d(0)
    step_d(1)
    step_c(2, mixp_t)
    step_c(3, mixp_t)

    part_grid = (dot_nt(table(2), table(0)) + dot_nt(table(3), table(1))).astype(BF)
    part_grid = dot(dot(spread[...], part_grid).astype(BF), gather[...]).astype(BF)
    se[0:COLS] = part_grid[:, half(0)]
    se[COLS : 2 * COLS] = part_grid[:, half(1)]
    push(se.at[pl.ds(pl.multiple_of(512 - mine, 512), 512)], re0, G_E0, near_device(twin))

    arrived(re0, G_E0)
    e0[...] = (se[pl.ds(pl.multiple_of(mine, 512), 512)].astype(F32) + re0[...].astype(F32)).astype(BF)
    over_y(lambda peer: e0.at[pl.ds(pl.multiple_of(peer * 128, 128), 128)], re1.at[level], G_E1)
    re1[level] = e0[pl.ds(pl.multiple_of(level * 128, 128), 128)]

    step_e(0)
    step_e(1)

    def returned(chains, r):
        return [
            jnp.concatenate([d_in[n, r // 2, t, lax.rem(r, 2)] for n in chains], axis=0).astype(F32) for t in range(2)
        ]

    def joined_row(r, pack):
        grid_mixed = returned(VALUES, r)
        for t in range(2):
            gates_t = gates[r, :, half(t)].astype(F32)
            more = grid_mixed[t] + 1.0
            gated[r, 0:HC, half(t)] = (gates_t[0:HC] * more).astype(BF)
            gated[r, HC:, half(t)] = (gates_t[HC:] * (bm[r, :, half(t)].astype(F32) + 1.0)).astype(BF)
            gbef[r, 0:HC, half(t)] = (dgelu[r, 0:HC, half(t)] * (gg[r, 0:HC, half(t)] * more)).astype(BF)
        j = (xb[r].astype(F32) + dot(w_out[...], gated[r])).astype(BF)
        jp[r + 2] = j
        v3[r + 1, CH : 2 * CH] = j
        return edges(pack, j[:, half(0)], j[:, half(1)], r)

    pack = loop(ROWS, joined_row, jnp.zeros((CH, LANES), BF), unroll=16)
    send_halo(v3, pack, 1, G_ROW1, G_PACK1)

    step_d(2)
    step_d(3)

    def pixels(ref, rows=slice(None)):
        return jnp.concatenate([ref[r, rows] for r in range(ROWS)], axis=1)

    p_conv = dot_nt(
        jnp.concatenate([u3[p] for p in range(ROWS + 2)], axis=1),
        jnp.concatenate([jp[p : p + 3].reshape(3 * CH, COLS) for p in range(ROWS + 2)], axis=1),
    )
    arrived(re1.at[pl.ds(0, 3)], G_E1)
    total = re1[0].astype(F32)
    for k in range(1, 4):
        total = total + re1[k].astype(F32)
    e1[...] = total
    over_x(lambda peer: e1.at[pl.ds(pl.multiple_of(peer * 32, 32), 32)], re2.at[across], G_E2)
    re2[across] = e1[pl.ds(pl.multiple_of(across * 32, 32), 32)]

    p_in = dot_nt(pixels(nb), pixels(gbef))
    p_out = dot_nt(pixels(gj), pixels(gated))
    st[0 : 3 * CH] = p_conv[:, half(0)].astype(BF)
    st[3 * CH : 4 * CH] = p_in.astype(BF)
    third = p_conv[:, 2 * CH :]
    st[4 * CH :] = jnp.concatenate(
        [third[: 2 * CH], jnp.concatenate([third[2 * CH :], p_out], axis=0)], axis=1
    ).astype(BF)
    summing = far < 12
    for peer, place in zip(far_peers, far_places):

        @pl.when(peer < 12)
        def _():
            push(st.at[pl.ds(pl.multiple_of(peer * 32, 32), 32)], rt1.at[far], G_T1, place)

    @pl.when(summing)
    def _():
        rt1[far] = st[pl.ds(pl.multiple_of(far * 32, 32), 32)]

    take_halo(v3, 1, G_ROW1, G_PACK1)

    arrived(re2.at[pl.ds(0, 3)], G_E2)
    e2[...] = re2[0] + re2[1] + re2[2] + re2[3]
    over_z(lambda peer: e2, re3.at[deep], G_E3)
    re3[deep] = e2[...]

    conv_k = jnp.concatenate(
        [jnp.concatenate([conv_w[a, b] for b in range(3)], axis=1) for a in range(3)], axis=0
    )

    def out_row(r, carry):
        total, carry = conv_step(conv_k, v3, r, carry)
        total = total + v3[r + 1, CH : 2 * CH].astype(F32)
        for t in range(2):
            rest_out[t, pl.ds(r * CH, CH), :] = total[:, half(t)]
        return carry

    carry = loop(ROWS // 2, out_row, conv_start(conv_k, v3), unroll=8)

    step_e(2)
    step_e(3)

    def value_before_row(r, carry):
        grid_back = returned(BACKS, r)
        for t in range(2):
            gbef[r, HC:CH, half(t)] = (dgelu[r, HC:CH, half(t)] * grid_back[t]).astype(BF)
        return carry

    loop(ROWS, value_before_row, unroll=8)
    p_value = dot_nt(pixels(gbef, slice(HC, CH)), pixels(nb))
    sq[...] = jnp.concatenate([p_value[0:16], p_value[16:]], axis=1).astype(BF)
    over_near(lambda peer: sq, rq1.at[near], G_Q1)
    rq1[near] = sq[...]

    for n in VALUES + BACKS:
        for ref, count, g in ((a_in, NEAR, G_A), (b_in, FAR, G_B), (c_in, FAR, G_C)):
            gone(ref.at[n, pl.ds(0, count - 1)], g + n)
    for n in VALUES:
        gone(d_in.at[n, pl.ds(0, NEAR - 1)], G_D + n)

    @pl.when(summing)
    def _():
        from_far(rt1, G_T1)
        total = rt1[0].astype(F32)
        for k in range(1, FAR):
            total = total + rt1[k].astype(F32)
        t1[...] = total.astype(BF)
        over_near(lambda peer: t1, rt2.at[near], G_T2)
        rt2[near] = t1[...]

    arrived(re3.at[pl.ds(0, 3)], G_E3)
    e3[...] = (re3[0] + re3[1] + re3[2] + re3[3]).astype(BF)
    over_x(lambda peer: e3, re4.at[across], G_E4)
    re4[across] = e3[...]

    def frame_row(r, carry):
        normed = dot(w_in_t[...], gbef[r])
        u = unit[r]
        mean_grad = jnp.mean(normed, axis=0, keepdims=True)
        mean_proj = jnp.mean(normed * u, axis=0, keepdims=True)
        source = gj[r].astype(F32) + inv[r, 0:1] * (normed - mean_grad - u * mean_proj)
        for t in range(2):
            gframe_out[t, pl.ds(r * CH, CH), :] = source[:, half(t)]
        return carry

    loop(ROWS, frame_row, unroll=16)

    from_near(rq1, G_Q1)
    total = rq1[0].astype(F32)
    for k in range(1, NEAR):
        total = total + rq1[k].astype(F32)
    q1[...] = total.astype(BF)
    over_far(lambda peer: q1, rq2.at[far], G_Q2)
    rq2[far] = q1[...]

    arrived(re4.at[pl.ds(0, 3)], G_E4)
    over_y(lambda peer: re4, re5.at[level], G_E5)
    re5[level] = re4[...]

    @pl.when(summing)
    def _():
        from_near(rt2, G_T2)
        total = rt2[0].astype(F32)
        for k in range(1, NEAR):
            total = total + rt2[k].astype(F32)
        t2[...] = total.astype(BF)
        over_far(lambda peer: t2, rt3.at[far], G_T3)
        rt3[far] = t2[...]

    loop(ROWS // 2, lambda r, carry: out_row(r + ROWS // 2, carry), carry, unroll=8)

    from_far(rq2, G_Q2)
    total = rq2[0].astype(F32)
    for k in range(1, FAR):
        total = total + rq2[k].astype(F32)
    value_out[...] = total

    arrived(re5.at[pl.ds(0, 3)], G_E5)
    push(re5, re6, G_E6, near_device(twin))
    early_out[pl.ds(pl.multiple_of(mine, 512), 512)] = re5[...].reshape(512, LANES)

    @pl.when(summing)
    def _():
        arrived(rt3.at[pl.ds(0, 11)], G_T3)
        gone(rt1.at[pl.ds(0, 11)], G_T1)
        gone(rt2.at[pl.ds(0, NEAR - 1)], G_T2)
        gone(rt1.at[pl.ds(0, FAR - 1)], G_T3)

    @pl.when(far >= 12)
    def _():
        arrived(rt3, G_T3)
        gone(rt1.at[pl.ds(0, 12)], G_T1)

    tail_out[...] = rt3[...]
    arrived(re6, G_E6)
    early_out[pl.ds(pl.multiple_of(512 - mine, 512), 512)] = re6[...].reshape(512, LANES)

    for which, g_row, g_pack in ((0, G_ROW0, G_PACK0), (1, G_ROW1, G_PACK1)):
        gone(row_in.at[which], g_row)
        gone(pack_in.at[which], g_pack)
    for n in BACKS:
        gone(d_in.at[n, pl.ds(0, NEAR - 1)], G_D + n)
    gone(rq1.at[pl.ds(0, NEAR - 1)], G_Q1)
    gone(rq2.at[pl.ds(0, FAR - 1)], G_Q2)
    gone(re0, G_E0)
    for ref, g in ((re1, G_E1), (re2, G_E2), (re3, G_E3), (re4, G_E4), (re5, G_E5)):
        gone(ref.at[pl.ds(0, 3)], g)
    gone(re6, G_E6)


def finish(rest, gframe, early, tail, value, *refs):
    outs, sem = (refs[:7], refs[7:14]), refs[14]
    restored, grad_frames, grad_w_in_t, grad_grid, grad_block, grad_w_out, grad_conv = outs[1]
    copies = []

    def leave(k, part=None):
        src, dst = outs[1][k], outs[0][k]
        if part is not None:
            src, dst = src.at[part], dst.at[part]
        copies.append(pltpu.make_async_copy(src, dst, sem.at[len(copies)]))
        copies[-1].start()

    def turn_out(src, dst, k):
        for first in range(0, CH, CH // 2):

            def channel(c, carry):
                for t in range(2):
                    dst[first + c, :, half(t)] = src[t, pl.ds(first + c, ROWS, stride=CH), :].astype(BF)
                return carry

            loop(CH // 2, channel, unroll=16)
            leave(k, pl.ds(first, CH // 2))

    scale = float(ROWS * NA * COLS * NW) ** (-0.5)
    for k in range(2):
        grad_grid[:, half(k)] = early[k * COLS : (k + 1) * COLS].astype(F32) * scale
        grad_block[:, half(k)] = early[(2 + k) * COLS : (3 + k) * COLS].astype(F32) * scale
    leave(3)
    leave(4)
    turn_out(gframe, grad_frames, 1)
    turn_out(rest, restored, 0)
    quarter = value[...] * scale
    zeros = jnp.zeros((HC, CH), F32)
    quarter = jnp.concatenate([zeros, quarter[:, :CH], quarter[:, CH:], zeros, zeros], axis=0)
    grad_w_in_t[...] = tail[3 * CH : 4 * CH].astype(F32) * scale + quarter.T
    leave(2)
    last = tail[4 * CH :].astype(F32) * scale
    grad_w_out[...] = last[CH:, CH:]
    leave(5)
    for b in range(3):
        rows = slice((2 - b) * CH, (3 - b) * CH)
        pair = tail[rows].astype(F32) * scale
        grad_conv[0, b] = pair[:, :CH]
        grad_conv[1, b] = pair[:, CH:]
    grad_conv[2, 2] = last[:CH, :CH]
    grad_conv[2, 1] = last[CH:, :CH]
    grad_conv[2, 0] = last[:CH, CH:]
    leave(6)
    for copy in copies:
        copy.wait()


def vm(*shape, dtype=BF):
    return pltpu.VMEM(shape, dtype)


def exchange():
    message_w = vm(4, NEAR, 2, 2, QC, LANES)
    message_a = vm(4, FAR, 16, 256)
    return [message_w, message_w, vm(4, 2 * 16 * QC, LANES, dtype=F32)] + [message_a] * 4 + [message_w] * 2


SCRATCH = [
    vm(CH, ROWS, COLS),
    vm(CH, 2 * CH),
    vm(COLS, COLS),
    vm(COLS, COLS),
    vm(CH, CH),
    vm(3, 3, CH, CH),
    vm(CH, ROWS, COLS),
    vm(2 * CH, CH),
    vm(2, CH * ROWS, LANES, dtype=F32),
    vm(ROWS, CH, COLS),
    vm(ROWS, CH, COLS),
    vm(ROWS, CH, COLS, dtype=F32),
    vm(ROWS, 8, COLS, dtype=F32),
    vm(ROWS, 2 * CH, COLS, dtype=F32),
    vm(ROWS, CH, COLS),
    vm(ROWS, HC, COLS),
    vm(ROWS + 2, 3 * CH, COLS),
    vm(ROWS + 2, 3 * CH, COLS),
    vm(ROWS, CH, COLS),
    vm(ROWS, CH, COLS, dtype=F32),
    vm(ROWS, HC, COLS),
    vm(ROWS, HC, COLS),
    vm(ROWS, HC, COLS),
    vm(ROWS, HC, COLS),
    *exchange(),
    vm(ROWS, CH, COLS),
    vm(ROWS, 2 * CH, COLS),
    vm(ROWS + 4, CH, COLS),
    vm(2, 2, CH, COLS),
    vm(2, 32, LANES),
    vm(2, 96, LANES),
    vm(CH, LANES),
    vm(CH, LANES),
    vm(COLS, COLS),
    vm(COLS, COLS),
    vm(COLS, COLS),
    vm(COLS, COLS),
    vm(4 * COLS, LANES),
    vm(512, LANES),
    vm(512, LANES),
    vm(4, 128, LANES),
    vm(128, LANES, dtype=F32),
    vm(4, 32, LANES, dtype=F32),
    vm(32, LANES, dtype=F32),
    vm(4, 32, LANES, dtype=F32),
    vm(32, LANES),
    vm(4, 32, LANES),
    vm(4, 4, 32, LANES),
    vm(4, 4, 32, LANES),
    vm(6 * CH, LANES),
    vm(FAR, 32, LANES),
    vm(32, LANES),
    vm(NEAR, 32, LANES),
    vm(32, LANES),
    vm(12, 32, LANES),
    vm(16, LANES),
    vm(NEAR, 16, LANES),
    vm(16, LANES),
    vm(FAR, 16, LANES),
    pltpu.SemaphoreType.DMA((GROUPS,)),
    pltpu.SemaphoreType.DMA((GROUPS,)),
    pltpu.SemaphoreType.DMA((7,)),
]


def body(frames, w_in, grid_mix, block_mix, w_out, conv_w, cotangent):
    operands = (frames, w_in.T, grid_mix, block_mix, w_out, conv_w, cotangent)
    vmem = pl.BlockSpec(memory_space=pltpu.VMEM)
    shape = jax.ShapeDtypeStruct
    rest, gframe, early, tail, value = pl.pallas_call(
        kernel,
        out_shape=(
            shape((2, ROWS * CH, LANES), F32),
            shape((2, ROWS * CH, LANES), F32),
            shape((4 * COLS, LANES), BF),
            shape((12, 32, LANES), BF),
            shape((16, LANES), F32),
        ),
        in_specs=[pl.BlockSpec(memory_space=pltpu.HBM)] * 7,
        out_specs=(vmem,) * 5,
        scratch_shapes=SCRATCH,
        compiler_params=pltpu.CompilerParams(
            collective_id=0, has_side_effects=True, vmem_limit_bytes=32 * 1024 * 1024
        ),
    )(*[pltpu.with_memory_space_constraint(x, pltpu.HBM) for x in operands])
    restored, grad_frames, grad_w_in_t, grad_grid, grad_block, grad_w_out, grad_conv = pl.pallas_call(
        finish,
        out_shape=(
            shape((CH, ROWS, COLS), BF),
            shape((CH, ROWS, COLS), BF),
            shape((CH, 2 * CH), F32),
            shape((COLS, COLS), F32),
            shape((COLS, COLS), F32),
            shape((CH, CH), F32),
            shape((3, 3, CH, CH), F32),
        ),
        in_specs=[vmem] * 5,
        out_specs=(pl.BlockSpec(memory_space=pl.ANY),) * 7,
        scratch_shapes=[
            vm(CH, ROWS, COLS),
            vm(CH, ROWS, COLS),
            vm(CH, 2 * CH, dtype=F32),
            vm(COLS, COLS, dtype=F32),
            vm(COLS, COLS, dtype=F32),
            vm(CH, CH, dtype=F32),
            vm(3, 3, CH, CH, dtype=F32),
            pltpu.SemaphoreType.DMA((9,)),
        ],
        compiler_params=pltpu.CompilerParams(vmem_limit_bytes=16 * 1024 * 1024),
    )(rest, gframe, early, tail.reshape(6 * CH, LANES), value)
    return restored, grad_frames, grad_w_in_t.T, grad_grid, grad_block, grad_w_out, grad_conv


def solution(mesh):
    placed = (P(None, "ha", "wa"), P(), P(), P(), P(), P(), P(None, "ha", "wa"))
    return jax.shard_map(
        body,
        mesh=mesh,
        in_specs=placed,
        out_specs=(P(None, "ha", "wa"), P(None, "ha", "wa"), P(), P(), P(), P(), P()),
        check_vma=False,
    )
```

```python
import jax
import jax.numpy as jnp
from jax import lax
from jax.experimental import pallas as pl
from jax.experimental.pallas import tpu as pltpu
from jax.sharding import PartitionSpec as P

BF = jnp.bfloat16
F32 = jnp.float32
EPS = 1e-06
MESH = pl.DeviceIdType.MESH

CH = 64
HC = 32
ROWS = 16
COLS = 256
LANES = 128
NA = 16
NW = 8
NEAR = 8
FAR = 16

(G_ROW0, G_PACK0, G_ROW1, G_PACK1) = range(4)
(G_E0, G_E1, G_E2, G_E3, G_E4, G_E5, G_E6, G_T1, G_T2, G_T3, G_Q1, G_Q2) = range(4, 16)
VALUES, BACKS = (0, 1), 2
G_A, G_B, G_C, G_D = 16, 19, 22, 25
GROUPS = 28
QC = 16


def dot(a, b):
    return lax.dot_general(a, b, (((1,), (0,)), ((), ())), preferred_element_type=F32)


def dot_nt(a, b):
    return lax.dot_general(a, b, (((1,), (1,)), ((), ())), preferred_element_type=F32)


def dot_tn(a, b):
    return lax.dot_general(a, b, (((0,), (0,)), ((), ())), preferred_element_type=F32)


def swap_granules(load, store, depth):
    lane = lax.broadcasted_iota(jnp.int16, (depth, LANES), 1)
    for row_half in range(2):
        for col_half in range(2):
            held = [load(row_half * 8 + k, col_half) for k in range(8)]
            for s in range(3):
                width = 16 << s
                low = (lane & width) == 0
                for k in range(8):
                    if not k & (1 << s):
                        a, b = held[k], held[k | (1 << s)]
                        held[k] = jnp.where(low, a, pltpu.roll(b, width, 1))
                        held[k | (1 << s)] = jnp.where(low, pltpu.roll(a, LANES - width, 1), b)
            for k in range(8):
                store(col_half * 8 + k, row_half, held[k])


def half(t):
    return slice(t * LANES, (t + 1) * LANES)


def loop(count, step, carry=0, unroll=1):
    return lax.fori_loop(0, count, step, carry, unroll=unroll)


def gelu_parts(x):
    root = 0.7978845608028654
    cube = root * 0.044715
    square = x * x
    h = 0.5 * jnp.tanh(x * (cube * square + root)) + 0.5
    value = x * h
    return value, h + value * (1.0 - h) * ((6.0 * cube) * square + 2.0 * root)


def kernel(
    frames_hbm, w_in_t_hbm, grid_mix_hbm, block_mix_hbm, w_out_hbm, conv_w_hbm, cot_hbm,
    rest_out, gframe_out, early_out, tail_out, value_out,
    frames, w_in_t, grid_mix, block_mix, w_out, conv_w, cot, w_in,
    turn, xb, nb, unit, inv, dgelu, gates, bval, u3, v3, gj, gg, xt, bt, bm, gbv,
    a, a_in, x32, b, b_in, c, c_in, d, d_in,
    ga, ga_in, gx32, gb, gb_in, gc, gc_in, gd, gd_in,
    gated, gbef, jp, row_in, pack_out, pack_in, edge_l, edge_r,
    mixp, mixp_t, gather, spread, se, re0, e0, re1, e1, re2, e2, re3, e3, re4, re5, re6,
    st, rt1, t1, rt2, t2, rt3, sq, rq1, q1, rq2,
    ssem, rsem, isem,
):
    ia = lax.axis_index("ha")
    iw = lax.axis_index("wa")
    up, down = lax.rem(ia + NA - 1, NA), lax.rem(ia + 1, NA)
    left, right = lax.rem(iw + NW - 1, NW), lax.rem(iw + 1, NW)
    lane = lax.broadcasted_iota(jnp.int16, (CH, LANES), 1)
    lane_wide = lax.broadcasted_iota(jnp.int32, (CH, LANES), 1)

    loads = [
        pltpu.make_async_copy(src, dst, isem.at[k])
        for k, (src, dst) in enumerate(
            [
                (frames_hbm, frames),
                (w_in_t_hbm, w_in_t),
                (cot_hbm, cot),
                (conv_w_hbm, conv_w),
                (w_out_hbm, w_out),
                (block_mix_hbm, block_mix),
                (grid_mix_hbm, grid_mix),
            ]
        )
    ]
    for load in loads:
        load.start()

    def push(src, dst, g, where):
        pltpu.make_async_remote_copy(
            src_ref=src, dst_ref=dst, send_sem=ssem.at[g], recv_sem=rsem.at[g], device_id=where, device_id_type=MESH
        ).start()

    near = lax.rem(iw, 2) * 4 + lax.rem(ia, 4)
    far = ia // 4 * 4 + iw // 2

    def near_device(peer):
        return ia // 4 * 4 + lax.rem(peer, 4), iw // 2 * 2 + peer // 4

    def far_device(peer):
        return peer // 4 * 4 + lax.rem(ia, 4), lax.rem(peer, 4) * 2 + lax.rem(iw, 2)

    near_peers = [lax.rem(near + k, NEAR) for k in range(1, NEAR)]
    far_peers = [lax.rem(far + k, FAR) for k in range(1, FAR)]
    twin = near + 1 - 2 * lax.rem(near, 2)

    near_places = [near_device(peer) for peer in near_peers]
    far_places = [far_device(peer) for peer in far_peers]

    def over_near(src_of, dst, g):
        for peer, place in zip(near_peers, near_places):
            push(src_of(peer), dst, g, place)

    def over_far(src_of, dst, g):
        for peer, place in zip(far_peers, far_places):
            push(src_of(peer), dst, g, place)

    def over_x(src_of, dst, g):
        for k in range(1, 4):
            peer = lax.rem(iw // 2 + k, 4)
            push(src_of(peer), dst, g, (ia, peer * 2 + lax.rem(iw, 2)))

    def over_z(src_of, dst, g):
        for k in range(1, 4):
            peer = lax.rem(ia // 4 + k, 4)
            push(src_of(peer), dst, g, (peer * 4 + lax.rem(ia, 4), iw))

    def over_y(src_of, dst, g):
        for k in range(1, 4):
            peer = lax.rem(near + 2 * k, NEAR)
            push(src_of(peer // 2), dst, g, near_device(peer))

    def arrived(ref, g):
        pltpu.make_async_copy(ref, ref, rsem.at[g]).wait()

    def gone(ref, g):
        pltpu.make_async_copy(ref, ref, ssem.at[g]).wait()

    def from_near(ref, g):
        arrived(ref.at[pl.ds(0, NEAR - 1)], g)

    def from_far(ref, g):
        arrived(ref.at[pl.ds(0, FAR - 1)], g)

    mine = lax.rem(near, 2) * 512
    level, across, deep = near // 2, iw // 2, ia // 4

    barrier = pltpu.get_barrier_semaphore()
    peers = [near_device(peer) for peer in near_peers]
    peers += [far_device(peer) for peer in far_peers]
    peers += [(a, b) for a in (up, ia, down) for b in (left, right)] + [(up, iw), (down, iw)]
    for peer in peers:
        pl.semaphore_signal(barrier, inc=1, device_id=peer, device_id_type=MESH)

    def turn_in(src):
        for t in range(2):
            turn[t] = src[:, :, half(t)].astype(F32).reshape(CH * ROWS, LANES)

    def turned(r, t):
        return turn[t, pl.ds(r, CH, stride=ROWS), :]

    def edges(pack, t0, t1, r):
        pack = jnp.where(lane_wide == r, pltpu.roll(t0, r, 1), pack)
        return jnp.where(lane_wide == ROWS + r, pltpu.roll(t1, r + 17, 1), pack)

    def send_halo(field, pack, which, g_row, g_pack):
        pack_out[which] = jnp.concatenate([pack, jnp.zeros_like(pack)], axis=0).T[0:32]
        push(field.at[1, CH : 2 * CH], row_in.at[which, 1], g_row, (up, iw))
        push(field.at[ROWS, CH : 2 * CH], row_in.at[which, 0], g_row, (down, iw))
        for slot, where in enumerate(
            [(ia, right), (down, right), (up, right), (ia, left), (down, left), (up, left)]
        ):
            part = pack_out.at[which, pl.ds(16 if slot < 3 else 0, 16)]
            push(part, pack_in.at[which, pl.ds(16 * slot, 16)], g_pack, where)

    def take_halo(field, which, g_row, g_pack):
        arrived(row_in.at[which], g_row)
        arrived(pack_in.at[which], g_pack)
        field[0, CH : 2 * CH] = jnp.where(ia > 0, row_in[which, 0], jnp.zeros((CH, COLS), BF))
        field[ROWS + 1, CH : 2 * CH] = jnp.where(ia < NA - 1, row_in[which, 1], jnp.zeros((CH, COLS), BF))
        first = jnp.where(ia > 0, 0, 1)
        last = jnp.where(ia < NA - 1, ROWS + 2, ROWS + 1)
        got = jnp.concatenate([pack_in[which], jnp.zeros((32, LANES), BF)], axis=0).T[0:CH]

        def assemble(middle, above, below, has):
            joined = jnp.where(lane == 0, above, jnp.where(lane == ROWS + 1, below, middle))
            inside = (lane_wide >= first) & (lane_wide < jnp.where(has, last, 0))
            return jnp.where(inside, joined, jnp.zeros_like(joined))

        edge_l[...] = assemble(pltpu.roll(got, 1, 1), pltpu.roll(got, 97, 1), pltpu.roll(got, 113, 1), iw > 0)
        edge_r[...] = assemble(pltpu.roll(got, 81, 1), pltpu.roll(got, 49, 1), pltpu.roll(got, 65, 1), iw < NW - 1)

        def shifts(p, carry):
            t0 = field[p, CH : 2 * CH, half(0)]
            t1 = field[p, CH : 2 * CH, half(1)]
            a0, a1 = pltpu.roll(t0, 1, 1), pltpu.roll(t1, 1, 1)
            b0, b1 = pltpu.roll(t0, LANES - 1, 1), pltpu.roll(t1, LANES - 1, 1)
            lh = pltpu.roll(edge_l[...], lax.rem(LANES - p, LANES), 1)
            rh = pltpu.roll(edge_r[...], LANES - 1 - p, 1)
            field[p, 0:CH, half(0)] = jnp.where(lane == 0, lh, a0)
            field[p, 0:CH, half(1)] = jnp.where(lane == 0, a0, a1)
            field[p, 2 * CH :, half(0)] = jnp.where(lane == LANES - 1, b1, b0)
            field[p, 2 * CH :, half(1)] = jnp.where(lane == LANES - 1, rh, b1)
            return carry

        loop(ROWS + 2, shifts, unroll=9)

    def conv_start(w, field):
        y = dot(w, field[0])
        z = dot(w, field[1])
        return z[0:CH], y[0:CH] + z[CH : 2 * CH]

    def conv_step(w, field, r, carry):
        later, now = carry
        y = dot(w, field[r + 2])
        return now + y[2 * CH :], (y[0:CH], later + y[CH : 2 * CH])

    chains = [[ref.at[n] for ref in (a, a_in, x32, b, b_in, c, c_in, d, d_in)] + [QC, n] for n in VALUES]
    chains.append([ga, ga_in, gx32, gb, gb_in, gc, gc_in, gd, gd_in, HC, BACKS])

    def channels(count):
        return [k // 2 * QC + k % 2 for k in range(count // 8)]

    def step_a(n):
        src, dst = chains[n][:2]
        over_near(lambda peer: src.at[peer], dst.at[near], G_A + n)

    def step_b(n):
        _, a_in, x, b, b_in, *_, count, _ = chains[n]
        arrived(a_in.at[pl.ds(0, NEAR - 1)], G_A + n)

        def widen(j, carry):
            for t in range(2):
                for r in range(2):
                    x[pl.ds((r * 16 + j * 2 + t) * count, count), :] = a_in[j, t, r].astype(F32)
            return carry

        loop(NEAR, widen, unroll=8)

        for peer, place in zip([*far_peers, far], [*far_places, None]):
            base = peer // 8 * (16 * count) + lax.rem(peer, 8) * 2
            slot = b_in if peer is far else b
            for k, channel in enumerate(channels(count)):
                slot[peer, :, half(k)] = x[pl.ds(base + channel, 16, stride=count), :].astype(BF)
            if peer is not far:
                push(b.at[peer], b_in.at[far], G_B + n, place)

    def table(n):
        return chains[n][4][...].reshape(256, -1)

    def step_c(n, mix):
        b_in, c, c_in = chains[n][4:7]
        arrived(b_in.at[pl.ds(0, FAR - 1)], G_B + n)
        c[...] = dot(mix[...], table(n)).astype(BF).reshape(c.shape)
        over_far(lambda peer: c.at[peer], c_in.at[far], G_C + n)
        c_in[far] = c[far]

    def step_d(n):
        _, _, x, _, _, _, c_in, d, d_in, count, _ = chains[n]
        arrived(c_in.at[pl.ds(0, FAR - 1)], G_C + n)

        def unpick(q, carry):
            for r in range(2):
                for k, channel in enumerate(channels(count)):
                    x[pl.ds((r * count + q * 2 + channel) * 16, 16), :] = c_in[r * 8 + q, :, half(k)].astype(F32)
            return carry

        loop(8, unpick, unroll=8)

        for peer, place in zip([*near_peers, near], [*near_places, None]):
            slot = d_in if peer is near else d
            for t in range(2):
                for r in range(2):
                    slot[peer, t, r] = x[pl.ds(r * count * 16 + peer * 2 + t, count, stride=16), :].astype(BF)
            if peer is not near:
                push(d.at[peer], d_in.at[near], G_D + n, place)

    def step_e(n):
        arrived(chains[n][8].at[pl.ds(0, NEAR - 1)], G_D + n)

    def order(cell, row):
        found = (row & 0xC1) | ((row & 6) << 3) | ((row & 48) >> 2) | ((row & 8) >> 2)
        return jnp.where(cell == found, 1.0, 0.0).astype(BF)

    loads[0].wait()
    loads[1].wait()
    turn_in(frames)
    w_in[...] = w_in_t[...].astype(F32).T.astype(BF)

    def value_row(slot, peer, low):
        r = peer * 2 + low
        normed = []
        for t in range(2):
            x = turned(r, t)
            xb[r, :, half(t)] = x.astype(BF)
            off = x - jnp.mean(x, axis=0, keepdims=True)
            rstd = lax.rsqrt(jnp.mean(off * off, axis=0, keepdims=True) + EPS)
            u = off * rstd
            unit[r, :, half(t)] = u
            inv[r, :, half(t)] = jnp.broadcast_to(rstd, (8, LANES))
            normed.append(u.astype(BF))
        normed = jnp.concatenate(normed, axis=1)
        nb[r] = normed
        value, slope = gelu_parts(dot(w_in[HC:CH], normed))
        dgelu[r, HC:CH] = slope
        value = value.astype(BF)
        for n in VALUES:
            for t in range(2):
                slot[n, peer, t, low] = value[n * QC : (n + 1) * QC, half(t)]

    for first in range(0, NEAR, 4):
        group = [*near_peers, near][first : first + 4]
        for peer in group:
            for low in range(2):
                value_row(a_in if peer is near else a, peer, low)
        if first == 0:
            pl.semaphore_wait(barrier, len(peers))
        for peer in group:
            if peer is not near:
                push(a.at[0, peer], a_in.at[0, near], G_A, near_device(peer))
    step_a(1)

    loads[2].wait()
    turn_in(cot)

    def cot_row(r, pack):
        t0, t1 = turned(r, 0).astype(BF), turned(r, 1).astype(BF)
        u3[r + 1, CH : 2 * CH, half(0)] = t0
        u3[r + 1, CH : 2 * CH, half(1)] = t1
        return edges(pack, t0, t1, r)

    pack = loop(ROWS, cot_row, jnp.zeros((CH, LANES), BF), unroll=16)
    send_halo(u3, pack, 0, G_ROW0, G_PACK0)

    w_rest = jnp.concatenate([w_in[0:HC], w_in[CH:]], axis=0)

    def gate_row(r, carry):
        before = dot(w_rest, nb[r])
        value, slope = gelu_parts(before[0:HC])
        gates[r, 0:HC] = value.astype(BF)
        dgelu[r, 0:HC] = slope
        value, slope = gelu_parts(before[HC:])
        dgelu[r, CH:] = slope
        value = value.astype(BF)
        gates[r, HC:CH] = value[0:HC]
        bval[r] = value[HC:]
        return carry

    loop(ROWS, gate_row, unroll=8)
    for load in loads[3:]:
        load.wait()
    down_axis = lax.broadcasted_iota(jnp.int32, (COLS, COLS), 0)
    along_axis = lax.broadcasted_iota(jnp.int32, (COLS, COLS), 1)
    gather[...] = order(along_axis, down_axis)
    spread[...] = order(down_axis, along_axis)
    mixp[...] = dot(dot(gather[...], grid_mix[...]).astype(BF), spread[...]).astype(BF)
    mixp_t[...] = mixp[...].T

    back_w = jnp.concatenate(
        [jnp.concatenate([conv_w[2 - a, 2 - b] for a in range(3)], axis=1) for b in range(3)], axis=0
    ).astype(F32).T.astype(BF)
    w_out_t = w_out[...].astype(F32).T.astype(BF)
    take_halo(u3, 0, G_ROW0, G_PACK0)

    def back_row(r, carry):
        total, carry = conv_step(back_w, u3, r, carry)
        g = (total + u3[r + 1, CH : 2 * CH].astype(F32)).astype(BF)
        gj[r] = g
        up_gated = dot(w_out_t, g)
        gg[r] = up_gated
        mixed = (up_gated[0:HC] * gates[r, 0:HC].astype(F32)).astype(BF)
        for t in range(2):
            ga[r // 2, t, r % 2] = mixed[:, half(t)]
        return carry

    step_b(0)
    carry = conv_start(back_w, u3)
    for first in range(0, NEAR, 4):
        if first:
            step_b(1)
        for r in range(2 * first, 2 * first + 8):
            carry = back_row(r, carry)
        for peer in range(first, first + 4):

            @pl.when(peer != near)
            def _():
                push(ga.at[peer], ga_in.at[near], G_A + BACKS, near_device(peer))

    ga_in[near] = ga[near]


    def put(ref):
        def store(k, t, value):
            ref[k, :, half(t)] = value

        return store

    swap_granules(lambda k, t: bval[k, :, half(t)], put(xt), HC)
    values = xt[...].reshape(ROWS * HC, COLS)
    mixed = dot_nt(values, block_mix[...]).astype(BF)
    swap_granules(lambda k, t: mixed[k * HC : (k + 1) * HC, half(t)], put(bm), HC)

    step_c(0, mixp)
    step_c(1, mixp)
    step_b(BACKS)

    def block_back(k, t):
        return (gg[k, HC:, half(t)] * gates[k, HC:, half(t)].astype(F32)).astype(BF)

    swap_granules(block_back, put(bt), HC)
    backs = bt[...].reshape(ROWS * HC, COLS)
    unmixed = dot(backs, block_mix[...]).astype(BF)
    swap_granules(lambda k, t: unmixed[k * HC : (k + 1) * HC, half(t)], put(gbv), HC)
    part_block = dot_tn(backs, values).astype(BF)
    se[2 * COLS : 3 * COLS] = part_block[:, half(0)]
    se[3 * COLS :] = part_block[:, half(1)]

    def block_before_row(r, carry):
        d = dgelu[r, CH:]
        gbef[r, CH : CH + HC] = (d[0:HC] * (gg[r, HC:] * (bm[r].astype(F32) + 1.0))).astype(BF)
        gbef[r, CH + HC :] = (d[HC:] * gbv[r].astype(F32)).astype(BF)
        gbef[r, HC:CH] = jnp.zeros((HC, COLS), BF)
        return carry

    loop(ROWS, block_before_row, unroll=8)
    for k in (0, 1, ROWS + 2, ROWS + 3):
        jp[k] = jnp.zeros((CH, COLS), BF)

    step_d(0)
    step_d(1)
    step_c(BACKS, mixp_t)

    part_grid = dot_nt(table(BACKS), jnp.concatenate([table(0), table(1)], axis=1)).astype(BF)
    part_grid = dot(dot(spread[...], part_grid).astype(BF), gather[...]).astype(BF)
    se[0:COLS] = part_grid[:, half(0)]
    se[COLS : 2 * COLS] = part_grid[:, half(1)]
    push(se.at[pl.ds(pl.multiple_of(512 - mine, 512), 512)], re0, G_E0, near_device(twin))

    arrived(re0, G_E0)
    e0[...] = (se[pl.ds(pl.multiple_of(mine, 512), 512)].astype(F32) + re0[...].astype(F32)).astype(BF)
    over_y(lambda peer: e0.at[pl.ds(pl.multiple_of(peer * 128, 128), 128)], re1.at[level], G_E1)
    re1[level] = e0[pl.ds(pl.multiple_of(level * 128, 128), 128)]

    step_e(0)
    step_e(1)

    def returned_values(r):
        return [
            jnp.concatenate([d_in[n, r // 2, t, lax.rem(r, 2)] for n in VALUES], axis=0).astype(F32) for t in range(2)
        ]

    def joined_row(r, pack):
        grid_mixed = returned_values(r)
        for t in range(2):
            gates_t = gates[r, :, half(t)].astype(F32)
            more = grid_mixed[t] + 1.0
            gated[r, 0:HC, half(t)] = (gates_t[0:HC] * more).astype(BF)
            gated[r, HC:, half(t)] = (gates_t[HC:] * (bm[r, :, half(t)].astype(F32) + 1.0)).astype(BF)
            gbef[r, 0:HC, half(t)] = (dgelu[r, 0:HC, half(t)] * (gg[r, 0:HC, half(t)] * more)).astype(BF)
        j = (xb[r].astype(F32) + dot(w_out[...], gated[r])).astype(BF)
        jp[r + 2] = j
        v3[r + 1, CH : 2 * CH] = j
        return edges(pack, j[:, half(0)], j[:, half(1)], r)

    pack = loop(ROWS, joined_row, jnp.zeros((CH, LANES), BF), unroll=16)
    send_halo(v3, pack, 1, G_ROW1, G_PACK1)

    step_d(BACKS)

    def pixels(ref, rows=slice(None)):
        return jnp.concatenate([ref[r, rows] for r in range(ROWS)], axis=1)

    p_conv = dot_nt(
        jnp.concatenate([u3[p] for p in range(ROWS + 2)], axis=1),
        jnp.concatenate([jp[p : p + 3].reshape(3 * CH, COLS) for p in range(ROWS + 2)], axis=1),
    )
    arrived(re1.at[pl.ds(0, 3)], G_E1)
    total = re1[0].astype(F32)
    for k in range(1, 4):
        total = total + re1[k].astype(F32)
    e1[...] = total
    over_x(lambda peer: e1.at[pl.ds(pl.multiple_of(peer * 32, 32), 32)], re2.at[across], G_E2)
    re2[across] = e1[pl.ds(pl.multiple_of(across * 32, 32), 32)]

    p_in = dot_nt(pixels(nb), pixels(gbef))
    p_out = dot_nt(pixels(gj), pixels(gated))
    st[0 : 3 * CH] = p_conv[:, half(0)].astype(BF)
    st[3 * CH : 4 * CH] = p_in.astype(BF)
    third = p_conv[:, 2 * CH :]
    st[4 * CH :] = jnp.concatenate(
        [third[: 2 * CH], jnp.concatenate([third[2 * CH :], p_out], axis=0)], axis=1
    ).astype(BF)
    summing = far < 12
    for peer, place in zip(far_peers, far_places):

        @pl.when(peer < 12)
        def _():
            push(st.at[pl.ds(pl.multiple_of(peer * 32, 32), 32)], rt1.at[far], G_T1, place)

    @pl.when(summing)
    def _():
        rt1[far] = st[pl.ds(pl.multiple_of(far * 32, 32), 32)]

    take_halo(v3, 1, G_ROW1, G_PACK1)

    arrived(re2.at[pl.ds(0, 3)], G_E2)
    e2[...] = re2[0] + re2[1] + re2[2] + re2[3]
    over_z(lambda peer: e2, re3.at[deep], G_E3)
    re3[deep] = e2[...]

    conv_k = jnp.concatenate(
        [jnp.concatenate([conv_w[a, b] for b in range(3)], axis=1) for a in range(3)], axis=0
    )

    def out_row(r, carry):
        total, carry = conv_step(conv_k, v3, r, carry)
        total = total + v3[r + 1, CH : 2 * CH].astype(F32)
        for t in range(2):
            rest_out[t, pl.ds(r * CH, CH), :] = total[:, half(t)]
        return carry

    carry = loop(ROWS // 2, out_row, conv_start(conv_k, v3), unroll=8)

    step_e(BACKS)

    def value_before_row(r, carry):
        for t in range(2):
            grid_back = gd_in[r // 2, t, lax.rem(r, 2)].astype(F32)
            gbef[r, HC:CH, half(t)] = (dgelu[r, HC:CH, half(t)] * grid_back).astype(BF)
        return carry

    loop(ROWS, value_before_row, unroll=8)
    p_value = dot_nt(pixels(gbef, slice(HC, CH)), pixels(nb))
    sq[...] = jnp.concatenate([p_value[0:16], p_value[16:]], axis=1).astype(BF)
    over_near(lambda peer: sq, rq1.at[near], G_Q1)
    rq1[near] = sq[...]

    for n in (*VALUES, BACKS):
        _, a_in, _, _, b_in, _, c_in, *_ = chains[n]
        gone(a_in.at[pl.ds(0, NEAR - 1)], G_A + n)
        gone(b_in.at[pl.ds(0, FAR - 1)], G_B + n)
        gone(c_in.at[pl.ds(0, FAR - 1)], G_C + n)
    for n in VALUES:
        gone(d_in.at[n, pl.ds(0, NEAR - 1)], G_D + n)

    @pl.when(summing)
    def _():
        from_far(rt1, G_T1)
        total = rt1[0].astype(F32)
        for k in range(1, FAR):
            total = total + rt1[k].astype(F32)
        t1[...] = total.astype(BF)
        over_near(lambda peer: t1, rt2.at[near], G_T2)
        rt2[near] = t1[...]

    arrived(re3.at[pl.ds(0, 3)], G_E3)
    e3[...] = (re3[0] + re3[1] + re3[2] + re3[3]).astype(BF)
    over_x(lambda peer: e3, re4.at[across], G_E4)
    re4[across] = e3[...]

    def frame_row(r, carry):
        normed = dot(w_in_t[...], gbef[r])
        u = unit[r]
        mean_grad = jnp.mean(normed, axis=0, keepdims=True)
        mean_proj = jnp.mean(normed * u, axis=0, keepdims=True)
        source = gj[r].astype(F32) + inv[r, 0:1] * (normed - mean_grad - u * mean_proj)
        for t in range(2):
            gframe_out[t, pl.ds(r * CH, CH), :] = source[:, half(t)]
        return carry

    loop(ROWS, frame_row, unroll=16)

    from_near(rq1, G_Q1)
    total = rq1[0].astype(F32)
    for k in range(1, NEAR):
        total = total + rq1[k].astype(F32)
    q1[...] = total.astype(BF)
    over_far(lambda peer: q1, rq2.at[far], G_Q2)
    rq2[far] = q1[...]

    arrived(re4.at[pl.ds(0, 3)], G_E4)
    over_y(lambda peer: re4, re5.at[level], G_E5)
    re5[level] = re4[...]

    @pl.when(summing)
    def _():
        from_near(rt2, G_T2)
        total = rt2[0].astype(F32)
        for k in range(1, NEAR):
            total = total + rt2[k].astype(F32)
        t2[...] = total.astype(BF)
        over_far(lambda peer: t2, rt3.at[far], G_T3)
        rt3[far] = t2[...]

    loop(ROWS // 2, lambda r, carry: out_row(r + ROWS // 2, carry), carry, unroll=8)

    from_far(rq2, G_Q2)
    total = rq2[0].astype(F32)
    for k in range(1, FAR):
        total = total + rq2[k].astype(F32)
    value_out[...] = total

    arrived(re5.at[pl.ds(0, 3)], G_E5)
    push(re5, re6, G_E6, near_device(twin))
    early_out[pl.ds(pl.multiple_of(mine, 512), 512)] = re5[...].reshape(512, LANES)

    @pl.when(summing)
    def _():
        arrived(rt3.at[pl.ds(0, 11)], G_T3)
        gone(rt1.at[pl.ds(0, 11)], G_T1)
        gone(rt2.at[pl.ds(0, NEAR - 1)], G_T2)
        gone(rt1.at[pl.ds(0, FAR - 1)], G_T3)

    @pl.when(far >= 12)
    def _():
        arrived(rt3, G_T3)
        gone(rt1.at[pl.ds(0, 12)], G_T1)

    tail_out[...] = rt3[...]
    arrived(re6, G_E6)
    early_out[pl.ds(pl.multiple_of(512 - mine, 512), 512)] = re6[...].reshape(512, LANES)

    for which, g_row, g_pack in ((0, G_ROW0, G_PACK0), (1, G_ROW1, G_PACK1)):
        gone(row_in.at[which], g_row)
        gone(pack_in.at[which], g_pack)
    gone(gd_in.at[pl.ds(0, NEAR - 1)], G_D + BACKS)
    gone(rq1.at[pl.ds(0, NEAR - 1)], G_Q1)
    gone(rq2.at[pl.ds(0, FAR - 1)], G_Q2)
    gone(re0, G_E0)
    for ref, g in ((re1, G_E1), (re2, G_E2), (re3, G_E3), (re4, G_E4), (re5, G_E5)):
        gone(ref.at[pl.ds(0, 3)], g)
    gone(re6, G_E6)


def finish(rest, gframe, early, tail, value, *refs):
    outs, sem = (refs[:7], refs[7:14]), refs[14]
    restored, grad_frames, grad_w_in_t, grad_grid, grad_block, grad_w_out, grad_conv = outs[1]
    copies = []

    def leave(k, part=None):
        src, dst = outs[1][k], outs[0][k]
        if part is not None:
            src, dst = src.at[part], dst.at[part]
        copies.append(pltpu.make_async_copy(src, dst, sem.at[len(copies)]))
        copies[-1].start()

    def turn_out(src, dst, k):
        for first in range(0, CH, CH // 2):

            def channel(c, carry):
                for t in range(2):
                    dst[first + c, :, half(t)] = src[t, pl.ds(first + c, ROWS, stride=CH), :].astype(BF)
                return carry

            loop(CH // 2, channel, unroll=16)
            leave(k, pl.ds(first, CH // 2))

    scale = float(ROWS * NA * COLS * NW) ** (-0.5)
    for k in range(2):
        grad_grid[:, half(k)] = early[k * COLS : (k + 1) * COLS].astype(F32) * scale
        grad_block[:, half(k)] = early[(2 + k) * COLS : (3 + k) * COLS].astype(F32) * scale
    leave(3)
    leave(4)
    turn_out(gframe, grad_frames, 1)
    turn_out(rest, restored, 0)
    quarter = value[...] * scale
    zeros = jnp.zeros((HC, CH), F32)
    quarter = jnp.concatenate([zeros, quarter[:, :CH], quarter[:, CH:], zeros, zeros], axis=0)
    grad_w_in_t[...] = tail[3 * CH : 4 * CH].astype(F32) * scale + quarter.T
    leave(2)
    last = tail[4 * CH :].astype(F32) * scale
    grad_w_out[...] = last[CH:, CH:]
    leave(5)
    for b in range(3):
        rows = slice((2 - b) * CH, (3 - b) * CH)
        pair = tail[rows].astype(F32) * scale
        grad_conv[0, b] = pair[:, :CH]
        grad_conv[1, b] = pair[:, CH:]
    grad_conv[2, 2] = last[:CH, :CH]
    grad_conv[2, 1] = last[CH:, :CH]
    grad_conv[2, 0] = last[:CH, CH:]
    leave(6)
    for copy in copies:
        copy.wait()


def vm(*shape, dtype=BF):
    return pltpu.VMEM(shape, dtype)


def exchange(count, *several):
    message_w = vm(*several, NEAR, 2, 2, count, LANES)
    message_a = vm(*several, FAR, 16, 16 * count)
    wide = vm(*several, 2 * 16 * count, LANES, dtype=F32)
    return [message_w, message_w, wide] + [message_a] * 4 + [message_w] * 2


SCRATCH = [
    vm(CH, ROWS, COLS),
    vm(CH, 2 * CH),
    vm(COLS, COLS),
    vm(COLS, COLS),
    vm(CH, CH),
    vm(3, 3, CH, CH),
    vm(CH, ROWS, COLS),
    vm(2 * CH, CH),
    vm(2, CH * ROWS, LANES, dtype=F32),
    vm(ROWS, CH, COLS),
    vm(ROWS, CH, COLS),
    vm(ROWS, CH, COLS, dtype=F32),
    vm(ROWS, 8, COLS, dtype=F32),
    vm(ROWS, 2 * CH, COLS, dtype=F32),
    vm(ROWS, CH, COLS),
    vm(ROWS, HC, COLS),
    vm(ROWS + 2, 3 * CH, COLS),
    vm(ROWS + 2, 3 * CH, COLS),
    vm(ROWS, CH, COLS),
    vm(ROWS, CH, COLS, dtype=F32),
    vm(ROWS, HC, COLS),
    vm(ROWS, HC, COLS),
    vm(ROWS, HC, COLS),
    vm(ROWS, HC, COLS),
    *exchange(QC, 2),
    *exchange(HC),
    vm(ROWS, CH, COLS),
    vm(ROWS, 2 * CH, COLS),
    vm(ROWS + 4, CH, COLS),
    vm(2, 2, CH, COLS),
    vm(2, 32, LANES),
    vm(2, 96, LANES),
    vm(CH, LANES),
    vm(CH, LANES),
    vm(COLS, COLS),
    vm(COLS, COLS),
    vm(COLS, COLS),
    vm(COLS, COLS),
    vm(4 * COLS, LANES),
    vm(512, LANES),
    vm(512, LANES),
    vm(4, 128, LANES),
    vm(128, LANES, dtype=F32),
    vm(4, 32, LANES, dtype=F32),
    vm(32, LANES, dtype=F32),
    vm(4, 32, LANES, dtype=F32),
    vm(32, LANES),
    vm(4, 32, LANES),
    vm(4, 4, 32, LANES),
    vm(4, 4, 32, LANES),
    vm(6 * CH, LANES),
    vm(FAR, 32, LANES),
    vm(32, LANES),
    vm(NEAR, 32, LANES),
    vm(32, LANES),
    vm(12, 32, LANES),
    vm(16, LANES),
    vm(NEAR, 16, LANES),
    vm(16, LANES),
    vm(FAR, 16, LANES),
    pltpu.SemaphoreType.DMA((GROUPS,)),
    pltpu.SemaphoreType.DMA((GROUPS,)),
    pltpu.SemaphoreType.DMA((7,)),
]


def body(frames, w_in, grid_mix, block_mix, w_out, conv_w, cotangent):
    operands = (frames, w_in.T, grid_mix, block_mix, w_out, conv_w, cotangent)
    vmem = pl.BlockSpec(memory_space=pltpu.VMEM)
    shape = jax.ShapeDtypeStruct
    rest, gframe, early, tail, value = pl.pallas_call(
        kernel,
        out_shape=(
            shape((2, ROWS * CH, LANES), F32),
            shape((2, ROWS * CH, LANES), F32),
            shape((4 * COLS, LANES), BF),
            shape((12, 32, LANES), BF),
            shape((16, LANES), F32),
        ),
        in_specs=[pl.BlockSpec(memory_space=pltpu.HBM)] * 7,
        out_specs=(vmem,) * 5,
        scratch_shapes=SCRATCH,
        compiler_params=pltpu.CompilerParams(
            collective_id=0, has_side_effects=True, vmem_limit_bytes=32 * 1024 * 1024
        ),
    )(*[pltpu.with_memory_space_constraint(x, pltpu.HBM) for x in operands])
    restored, grad_frames, grad_w_in_t, grad_grid, grad_block, grad_w_out, grad_conv = pl.pallas_call(
        finish,
        out_shape=(
            shape((CH, ROWS, COLS), BF),
            shape((CH, ROWS, COLS), BF),
            shape((CH, 2 * CH), F32),
            shape((COLS, COLS), F32),
            shape((COLS, COLS), F32),
            shape((CH, CH), F32),
            shape((3, 3, CH, CH), F32),
        ),
        in_specs=[vmem] * 5,
        out_specs=(pl.BlockSpec(memory_space=pl.ANY),) * 7,
        scratch_shapes=[
            vm(CH, ROWS, COLS),
            vm(CH, ROWS, COLS),
            vm(CH, 2 * CH, dtype=F32),
            vm(COLS, COLS, dtype=F32),
            vm(COLS, COLS, dtype=F32),
            vm(CH, CH, dtype=F32),
            vm(3, 3, CH, CH, dtype=F32),
            pltpu.SemaphoreType.DMA((9,)),
        ],
        compiler_params=pltpu.CompilerParams(vmem_limit_bytes=16 * 1024 * 1024),
    )(rest, gframe, early, tail.reshape(6 * CH, LANES), value)
    return restored, grad_frames, grad_w_in_t.T, grad_grid, grad_block, grad_w_out, grad_conv


def solution(mesh):
    placed = (P(None, "ha", "wa"), P(), P(), P(), P(), P(), P(None, "ha", "wa"))
    return jax.shard_map(
        body,
        mesh=mesh,
        in_specs=placed,
        out_specs=(P(None, "ha", "wa"), P(None, "ha", "wa"), P(), P(), P(), P(), P()),
        check_vma=False,
    )
```

```python
import jax
import jax.numpy as jnp
from jax import lax
from jax.experimental import pallas as pl
from jax.experimental.pallas import tpu as pltpu
from jax.sharding import PartitionSpec as P

BF = jnp.bfloat16
F32 = jnp.float32
EPS = 1e-06
MESH = pl.DeviceIdType.MESH

CH = 64
HC = 32
ROWS = 16
COLS = 256
LANES = 128
NA = 16
NW = 8
NEAR = 8
FAR = 16

(G_ROW0, G_PACK0, G_ROW1, G_PACK1) = range(4)
(G_E0, G_E1, G_E2, G_E3, G_E4, G_E5, G_E6, G_T1, G_T2, G_T3, G_Q1, G_Q2) = range(4, 16)
VALUES, BACKS = (0, 1), (2, 3)
G_A, G_B, G_C, G_D = 16, 20, 24, 28
GROUPS = 32
QC = 16


def dot(a, b):
    return lax.dot_general(a, b, (((1,), (0,)), ((), ())), preferred_element_type=F32)


def dot_nt(a, b):
    return lax.dot_general(a, b, (((1,), (1,)), ((), ())), preferred_element_type=F32)


def dot_tn(a, b):
    return lax.dot_general(a, b, (((0,), (0,)), ((), ())), preferred_element_type=F32)


def swap_granules(load, store, depth):
    lane = lax.broadcasted_iota(jnp.int16, (depth, LANES), 1)
    for row_half in range(2):
        for col_half in range(2):
            held = [load(row_half * 8 + k, col_half) for k in range(8)]
            for s in range(3):
                width = 16 << s
                low = (lane & width) == 0
                for k in range(8):
                    if not k & (1 << s):
                        a, b = held[k], held[k | (1 << s)]
                        held[k] = jnp.where(low, a, pltpu.roll(b, width, 1))
                        held[k | (1 << s)] = jnp.where(low, pltpu.roll(a, LANES - width, 1), b)
            for k in range(8):
                store(col_half * 8 + k, row_half, held[k])


def half(t):
    return slice(t * LANES, (t + 1) * LANES)


def loop(count, step, carry=0, unroll=1):
    return lax.fori_loop(0, count, step, carry, unroll=unroll)


def gelu_parts(x):
    root = 0.7978845608028654
    cube = root * 0.044715
    square = x * x
    h = 0.5 * jnp.tanh(x * (cube * square + root)) + 0.5
    value = x * h
    return value, h + value * (1.0 - h) * ((6.0 * cube) * square + 2.0 * root)


def kernel(
    frames_hbm, w_in_t_hbm, grid_mix_hbm, block_mix_hbm, w_out_hbm, conv_w_hbm, cot_hbm,
    rest_out, gframe_out, early_out, tail_out, value_out,
    frames, w_in_t, grid_mix, block_mix, w_out, conv_w, cot, w_in,
    turn, xb, nb, unit, inv, dgelu, gates, bval, u3, v3, gj, gg, xt, bt, bm, gbv,
    a, a_in, x32, b, b_in, c, c_in, d, d_in,
    gated, gbef, jp, row_in, pack_out, pack_in, edge_l, edge_r,
    mixp, mixp_t, gather, spread, se, re0, e0, re1, e1, re2, e2, re3, e3, re4, re5, re6,
    st, rt1, t1, rt2, t2, rt3, sq, rq1, q1, rq2,
    ssem, rsem, isem,
):
    ia = lax.axis_index("ha")
    iw = lax.axis_index("wa")
    up, down = lax.rem(ia + NA - 1, NA), lax.rem(ia + 1, NA)
    left, right = lax.rem(iw + NW - 1, NW), lax.rem(iw + 1, NW)
    lane = lax.broadcasted_iota(jnp.int16, (CH, LANES), 1)
    lane_wide = lax.broadcasted_iota(jnp.int32, (CH, LANES), 1)

    loads = [
        pltpu.make_async_copy(src, dst, isem.at[k])
        for k, (src, dst) in enumerate(
            [
                (frames_hbm, frames),
                (w_in_t_hbm, w_in_t),
                (cot_hbm, cot),
                (conv_w_hbm, conv_w),
                (w_out_hbm, w_out),
                (block_mix_hbm, block_mix),
                (grid_mix_hbm, grid_mix),
            ]
        )
    ]
    for load in loads:
        load.start()

    def push(src, dst, g, where):
        pltpu.make_async_remote_copy(
            src_ref=src, dst_ref=dst, send_sem=ssem.at[g], recv_sem=rsem.at[g], device_id=where, device_id_type=MESH
        ).start()

    near = lax.rem(iw, 2) * 4 + lax.rem(ia, 4)
    far = ia // 4 * 4 + iw // 2

    def near_device(peer):
        return ia // 4 * 4 + lax.rem(peer, 4), iw // 2 * 2 + peer // 4

    def far_device(peer):
        return peer // 4 * 4 + lax.rem(ia, 4), lax.rem(peer, 4) * 2 + lax.rem(iw, 2)

    near_peers = [lax.rem(near + k, NEAR) for k in range(1, NEAR)]
    far_peers = [lax.rem(far + k, FAR) for k in range(1, FAR)]
    twin = near + 1 - 2 * lax.rem(near, 2)

    near_places = [near_device(peer) for peer in near_peers]
    far_places = [far_device(peer) for peer in far_peers]

    def over_near(src_of, dst, g):
        for peer, place in zip(near_peers, near_places):
            push(src_of(peer), dst, g, place)

    def over_far(src_of, dst, g):
        for peer, place in zip(far_peers, far_places):
            push(src_of(peer), dst, g, place)

    def over_x(src_of, dst, g):
        for k in range(1, 4):
            peer = lax.rem(iw // 2 + k, 4)
            push(src_of(peer), dst, g, (ia, peer * 2 + lax.rem(iw, 2)))

    def over_z(src_of, dst, g):
        for k in range(1, 4):
            peer = lax.rem(ia // 4 + k, 4)
            push(src_of(peer), dst, g, (peer * 4 + lax.rem(ia, 4), iw))

    def over_y(src_of, dst, g):
        for k in range(1, 4):
            peer = lax.rem(near + 2 * k, NEAR)
            push(src_of(peer // 2), dst, g, near_device(peer))

    def arrived(ref, g):
        pltpu.make_async_copy(ref, ref, rsem.at[g]).wait()

    def gone(ref, g):
        pltpu.make_async_copy(ref, ref, ssem.at[g]).wait()

    def from_near(ref, g):
        arrived(ref.at[pl.ds(0, NEAR - 1)], g)

    def from_far(ref, g):
        arrived(ref.at[pl.ds(0, FAR - 1)], g)

    mine = lax.rem(near, 2) * 512
    level, across, deep = near // 2, iw // 2, ia // 4

    barrier = pltpu.get_barrier_semaphore()
    peers = [near_device(peer) for peer in near_peers]
    peers += [far_device(peer) for peer in far_peers]
    peers += [(a, b) for a in (up, ia, down) for b in (left, right)] + [(up, iw), (down, iw)]
    for peer in peers:
        pl.semaphore_signal(barrier, inc=1, device_id=peer, device_id_type=MESH)

    def turn_in(src):
        for t in range(2):
            turn[t] = src[:, :, half(t)].astype(F32).reshape(CH * ROWS, LANES)

    def turned(r, t):
        return turn[t, pl.ds(r, CH, stride=ROWS), :]

    def edges(pack, t0, t1, r):
        pack = jnp.where(lane_wide == r, pltpu.roll(t0, r, 1), pack)
        return jnp.where(lane_wide == ROWS + r, pltpu.roll(t1, r + 17, 1), pack)

    def send_halo(field, pack, which, g_row, g_pack):
        pack_out[which] = jnp.concatenate([pack, jnp.zeros_like(pack)], axis=0).T[0:32]
        push(field.at[1, CH : 2 * CH], row_in.at[which, 1], g_row, (up, iw))
        push(field.at[ROWS, CH : 2 * CH], row_in.at[which, 0], g_row, (down, iw))
        for slot, where in enumerate(
            [(ia, right), (down, right), (up, right), (ia, left), (down, left), (up, left)]
        ):
            part = pack_out.at[which, pl.ds(16 if slot < 3 else 0, 16)]
            push(part, pack_in.at[which, pl.ds(16 * slot, 16)], g_pack, where)

    def take_halo(field, which, g_row, g_pack):
        arrived(row_in.at[which], g_row)
        arrived(pack_in.at[which], g_pack)
        field[0, CH : 2 * CH] = jnp.where(ia > 0, row_in[which, 0], jnp.zeros((CH, COLS), BF))
        field[ROWS + 1, CH : 2 * CH] = jnp.where(ia < NA - 1, row_in[which, 1], jnp.zeros((CH, COLS), BF))
        first = jnp.where(ia > 0, 0, 1)
        last = jnp.where(ia < NA - 1, ROWS + 2, ROWS + 1)
        got = jnp.concatenate([pack_in[which], jnp.zeros((32, LANES), BF)], axis=0).T[0:CH]

        def assemble(middle, above, below, has):
            joined = jnp.where(lane == 0, above, jnp.where(lane == ROWS + 1, below, middle))
            inside = (lane_wide >= first) & (lane_wide < jnp.where(has, last, 0))
            return jnp.where(inside, joined, jnp.zeros_like(joined))

        edge_l[...] = assemble(pltpu.roll(got, 1, 1), pltpu.roll(got, 97, 1), pltpu.roll(got, 113, 1), iw > 0)
        edge_r[...] = assemble(pltpu.roll(got, 81, 1), pltpu.roll(got, 49, 1), pltpu.roll(got, 65, 1), iw < NW - 1)

        def shifts(p, carry):
            t0 = field[p, CH : 2 * CH, half(0)]
            t1 = field[p, CH : 2 * CH, half(1)]
            a0, a1 = pltpu.roll(t0, 1, 1), pltpu.roll(t1, 1, 1)
            b0, b1 = pltpu.roll(t0, LANES - 1, 1), pltpu.roll(t1, LANES - 1, 1)
            lh = pltpu.roll(edge_l[...], lax.rem(LANES - p, LANES), 1)
            rh = pltpu.roll(edge_r[...], LANES - 1 - p, 1)
            field[p, 0:CH, half(0)] = jnp.where(lane == 0, lh, a0)
            field[p, 0:CH, half(1)] = jnp.where(lane == 0, a0, a1)
            field[p, 2 * CH :, half(0)] = jnp.where(lane == LANES - 1, b1, b0)
            field[p, 2 * CH :, half(1)] = jnp.where(lane == LANES - 1, rh, b1)
            return carry

        loop(ROWS + 2, shifts, unroll=9)

    def conv_start(w, field):
        y = dot(w, field[0])
        z = dot(w, field[1])
        return z[0:CH], y[0:CH] + z[CH : 2 * CH]

    def conv_step(w, field, r, carry):
        later, now = carry
        y = dot(w, field[r + 2])
        return now + y[2 * CH :], (y[0:CH], later + y[CH : 2 * CH])

    def step_a(n):
        over_near(lambda peer: a.at[n, peer], a_in.at[n, near], G_A + n)

    def step_b(n):
        arrived(a_in.at[n, pl.ds(0, NEAR - 1)], G_A + n)

        def widen(j, carry):
            for t in range(2):
                for r in range(2):
                    x32[n, pl.ds((r * 16 + j * 2 + t) * QC, QC), :] = a_in[n, j, t, r].astype(F32)
            return carry

        loop(NEAR, widen, unroll=8)

        for peer, place in zip([*far_peers, far], [*far_places, None]):
            base = peer // 8 * (16 * QC) + lax.rem(peer, 8) * 2
            slot = b_in if peer is far else b
            for k in range(2):
                slot[n, peer, :, half(k)] = x32[n, pl.ds(base + k, 16, stride=QC), :].astype(BF)
            if peer is not far:
                push(b.at[n, peer], b_in.at[n, far], G_B + n, place)

    def table(n):
        return b_in[n].reshape(256, 256)

    def step_c(n, mix):
        arrived(b_in.at[n, pl.ds(0, FAR - 1)], G_B + n)
        c[n] = dot(mix[...], table(n)).astype(BF).reshape(FAR, 16, 256)
        over_far(lambda peer: c.at[n, peer], c_in.at[n, far], G_C + n)
        c_in[n, far] = c[n, far]

    def step_d(n):
        arrived(c_in.at[n, pl.ds(0, FAR - 1)], G_C + n)

        def unpick(q, carry):
            for r in range(2):
                for k in range(2):
                    x32[n, pl.ds((r * QC + q * 2 + k) * 16, 16), :] = c_in[n, r * 8 + q, :, half(k)].astype(F32)
            return carry

        loop(8, unpick, unroll=8)

        for peer, place in zip([*near_peers, near], [*near_places, None]):
            slot = d_in if peer is near else d
            for t in range(2):
                for r in range(2):
                    slot[n, peer, t, r] = x32[n, pl.ds(r * QC * 16 + peer * 2 + t, QC, stride=16), :].astype(BF)
            if peer is not near:
                push(d.at[n, peer], d_in.at[n, near], G_D + n, place)

    def step_e(n):
        arrived(d_in.at[n, pl.ds(0, NEAR - 1)], G_D + n)

    def order(cell, row):
        found = (row & 0xC1) | ((row & 6) << 3) | ((row & 48) >> 2) | ((row & 8) >> 2)
        return jnp.where(cell == found, 1.0, 0.0).astype(BF)

    loads[0].wait()
    loads[1].wait()
    turn_in(frames)
    w_in[...] = w_in_t[...].astype(F32).T.astype(BF)

    def value_row(slot, peer, low):
        r = peer * 2 + low
        normed = []
        for t in range(2):
            x = turned(r, t)
            xb[r, :, half(t)] = x.astype(BF)
            off = x - jnp.mean(x, axis=0, keepdims=True)
            rstd = lax.rsqrt(jnp.mean(off * off, axis=0, keepdims=True) + EPS)
            u = off * rstd
            unit[r, :, half(t)] = u
            inv[r, :, half(t)] = jnp.broadcast_to(rstd, (8, LANES))
            normed.append(u.astype(BF))
        normed = jnp.concatenate(normed, axis=1)
        nb[r] = normed
        value, slope = gelu_parts(dot(w_in[HC:CH], normed))
        dgelu[r, HC:CH] = slope
        value = value.astype(BF)
        for n in VALUES:
            for t in range(2):
                slot[n, peer, t, low] = value[n * QC : (n + 1) * QC, half(t)]

    for first in range(0, NEAR, 4):
        group = [*near_peers, near][first : first + 4]
        for peer in group:
            for low in range(2):
                value_row(a_in if peer is near else a, peer, low)
        if first == 0:
            pl.semaphore_wait(barrier, len(peers))
        for peer in group:
            if peer is not near:
                push(a.at[0, peer], a_in.at[0, near], G_A, near_device(peer))
    step_a(1)

    loads[2].wait()
    turn_in(cot)

    def cot_row(r, pack):
        t0, t1 = turned(r, 0).astype(BF), turned(r, 1).astype(BF)
        u3[r + 1, CH : 2 * CH, half(0)] = t0
        u3[r + 1, CH : 2 * CH, half(1)] = t1
        return edges(pack, t0, t1, r)

    pack = loop(ROWS, cot_row, jnp.zeros((CH, LANES), BF), unroll=16)
    send_halo(u3, pack, 0, G_ROW0, G_PACK0)

    w_rest = jnp.concatenate([w_in[0:HC], w_in[CH:]], axis=0)

    def gate_row(r, carry):
        before = dot(w_rest, nb[r])
        value, slope = gelu_parts(before[0:HC])
        gates[r, 0:HC] = value.astype(BF)
        dgelu[r, 0:HC] = slope
        value, slope = gelu_parts(before[HC:])
        dgelu[r, CH:] = slope
        value = value.astype(BF)
        gates[r, HC:CH] = value[0:HC]
        bval[r] = value[HC:]
        return carry

    loop(ROWS, gate_row, unroll=8)
    for load in loads[3:]:
        load.wait()
    down_axis = lax.broadcasted_iota(jnp.int32, (COLS, COLS), 0)
    along_axis = lax.broadcasted_iota(jnp.int32, (COLS, COLS), 1)
    gather[...] = order(along_axis, down_axis)
    spread[...] = order(down_axis, along_axis)
    mixp[...] = dot(dot(gather[...], grid_mix[...]).astype(BF), spread[...]).astype(BF)
    mixp_t[...] = mixp[...].T

    back_w = jnp.concatenate(
        [jnp.concatenate([conv_w[2 - a, 2 - b] for a in range(3)], axis=1) for b in range(3)], axis=0
    ).astype(F32).T.astype(BF)
    w_out_t = w_out[...].astype(F32).T.astype(BF)
    take_halo(u3, 0, G_ROW0, G_PACK0)

    def back_row(r, carry):
        total, carry = conv_step(back_w, u3, r, carry)
        g = (total + u3[r + 1, CH : 2 * CH].astype(F32)).astype(BF)
        gj[r] = g
        up_gated = dot(w_out_t, g)
        gg[r] = up_gated
        mixed = (up_gated[0:HC] * gates[r, 0:HC].astype(F32)).astype(BF)
        for n in range(2):
            for t in range(2):
                a[2 + n, r // 2, t, r % 2] = mixed[n * QC : (n + 1) * QC, half(t)]
        return carry

    step_b(0)
    carry = conv_start(back_w, u3)
    for first in range(0, NEAR, 4):
        if first:
            step_b(1)
        for r in range(2 * first, 2 * first + 8):
            carry = back_row(r, carry)
        for peer in range(first, first + 4):

            @pl.when(peer != near)
            def _():
                push(a.at[2, peer], a_in.at[2, near], G_A + 2, near_device(peer))

    step_a(3)
    for n in BACKS:
        a_in[n, near] = a[n, near]


    def put(ref):
        def store(k, t, value):
            ref[k, :, half(t)] = value

        return store

    swap_granules(lambda k, t: bval[k, :, half(t)], put(xt), HC)
    values = xt[...].reshape(ROWS * HC, COLS)
    mixed = dot_nt(values, block_mix[...]).astype(BF)
    swap_granules(lambda k, t: mixed[k * HC : (k + 1) * HC, half(t)], put(bm), HC)

    step_c(0, mixp)

    def block_back(k, t):
        return (gg[k, HC:, half(t)] * gates[k, HC:, half(t)].astype(F32)).astype(BF)

    swap_granules(block_back, put(bt), HC)
    backs = bt[...].reshape(ROWS * HC, COLS)
    unmixed = dot(backs, block_mix[...]).astype(BF)
    swap_granules(lambda k, t: unmixed[k * HC : (k + 1) * HC, half(t)], put(gbv), HC)

    step_c(1, mixp)
    step_b(2)

    part_block = dot_tn(backs, values).astype(BF)
    se[2 * COLS : 3 * COLS] = part_block[:, half(0)]
    se[3 * COLS :] = part_block[:, half(1)]

    step_b(3)

    def block_before_row(r, carry):
        d = dgelu[r, CH:]
        gbef[r, CH : CH + HC] = (d[0:HC] * (gg[r, HC:] * (bm[r].astype(F32) + 1.0))).astype(BF)
        gbef[r, CH + HC :] = (d[HC:] * gbv[r].astype(F32)).astype(BF)
        gbef[r, HC:CH] = jnp.zeros((HC, COLS), BF)
        return carry

    loop(ROWS, block_before_row, unroll=8)
    for k in (0, 1, ROWS + 2, ROWS + 3):
        jp[k] = jnp.zeros((CH, COLS), BF)

    step_d(0)
    step_d(1)
    step_c(2, mixp_t)
    step_c(3, mixp_t)

    part_grid = (dot_nt(table(2), table(0)) + dot_nt(table(3), table(1))).astype(BF)
    part_grid = dot(dot(spread[...], part_grid).astype(BF), gather[...]).astype(BF)
    se[0:COLS] = part_grid[:, half(0)]
    se[COLS : 2 * COLS] = part_grid[:, half(1)]
    push(se.at[pl.ds(pl.multiple_of(512 - mine, 512), 512)], re0, G_E0, near_device(twin))

    arrived(re0, G_E0)
    e0[...] = (se[pl.ds(pl.multiple_of(mine, 512), 512)].astype(F32) + re0[...].astype(F32)).astype(BF)
    over_y(lambda peer: e0.at[pl.ds(pl.multiple_of(peer * 128, 128), 128)], re1.at[level], G_E1)
    re1[level] = e0[pl.ds(pl.multiple_of(level * 128, 128), 128)]

    step_e(0)
    step_e(1)

    def returned(chains, r):
        return [
            jnp.concatenate([d_in[n, r // 2, t, lax.rem(r, 2)] for n in chains], axis=0).astype(F32) for t in range(2)
        ]

    def joined_row(r, pack):
        grid_mixed = returned(VALUES, r)
        for t in range(2):
            gates_t = gates[r, :, half(t)].astype(F32)
            more = grid_mixed[t] + 1.0
            gated[r, 0:HC, half(t)] = (gates_t[0:HC] * more).astype(BF)
            gated[r, HC:, half(t)] = (gates_t[HC:] * (bm[r, :, half(t)].astype(F32) + 1.0)).astype(BF)
            gbef[r, 0:HC, half(t)] = (dgelu[r, 0:HC, half(t)] * (gg[r, 0:HC, half(t)] * more)).astype(BF)
        j = (xb[r].astype(F32) + dot(w_out[...], gated[r])).astype(BF)
        jp[r + 2] = j
        v3[r + 1, CH : 2 * CH] = j
        return edges(pack, j[:, half(0)], j[:, half(1)], r)

    pack = loop(ROWS, joined_row, jnp.zeros((CH, LANES), BF), unroll=16)
    send_halo(v3, pack, 1, G_ROW1, G_PACK1)

    step_d(2)
    step_d(3)

    def pixels(ref, rows=slice(None)):
        return jnp.concatenate([ref[r, rows] for r in range(ROWS)], axis=1)

    p_conv = dot_nt(
        jnp.concatenate([u3[p] for p in range(ROWS + 2)], axis=1),
        jnp.concatenate([jp[p : p + 3].reshape(3 * CH, COLS) for p in range(ROWS + 2)], axis=1),
    )
    arrived(re1.at[pl.ds(0, 3)], G_E1)
    total = re1[0].astype(F32)
    for k in range(1, 4):
        total = total + re1[k].astype(F32)
    e1[...] = total
    over_x(lambda peer: e1.at[pl.ds(pl.multiple_of(peer * 32, 32), 32)], re2.at[across], G_E2)
    re2[across] = e1[pl.ds(pl.multiple_of(across * 32, 32), 32)]

    p_in = dot_nt(pixels(nb), pixels(gbef))
    p_out = dot_nt(pixels(gj), pixels(gated))
    st[0 : 3 * CH] = p_conv[:, half(0)].astype(BF)
    st[3 * CH : 4 * CH] = p_in.astype(BF)
    third = p_conv[:, 2 * CH :]
    st[4 * CH :] = jnp.concatenate(
        [third[: 2 * CH], jnp.concatenate([third[2 * CH :], p_out], axis=0)], axis=1
    ).astype(BF)
    summing = far < 12
    for peer, place in zip(far_peers, far_places):

        @pl.when(peer < 12)
        def _():
            push(st.at[pl.ds(pl.multiple_of(peer * 32, 32), 32)], rt1.at[far], G_T1, place)

    @pl.when(summing)
    def _():
        rt1[far] = st[pl.ds(pl.multiple_of(far * 32, 32), 32)]

    take_halo(v3, 1, G_ROW1, G_PACK1)

    arrived(re2.at[pl.ds(0, 3)], G_E2)
    e2[...] = re2[0] + re2[1] + re2[2] + re2[3]
    over_z(lambda peer: e2, re3.at[deep], G_E3)
    re3[deep] = e2[...]

    conv_k = jnp.concatenate(
        [jnp.concatenate([conv_w[a, b] for b in range(3)], axis=1) for a in range(3)], axis=0
    )

    def out_row(r, carry):
        total, carry = conv_step(conv_k, v3, r, carry)
        total = total + v3[r + 1, CH : 2 * CH].astype(F32)
        for t in range(2):
            rest_out[t, pl.ds(r * CH, CH), :] = total[:, half(t)]
        return carry

    carry = loop(ROWS // 2, out_row, conv_start(conv_k, v3), unroll=8)

    step_e(2)
    step_e(3)

    def value_before_row(r, carry):
        grid_back = returned(BACKS, r)
        for t in range(2):
            gbef[r, HC:CH, half(t)] = (dgelu[r, HC:CH, half(t)] * grid_back[t]).astype(BF)
        return carry

    loop(ROWS, value_before_row, unroll=8)
    p_value = dot_nt(pixels(gbef, slice(HC, CH)), pixels(nb))
    sq[...] = jnp.concatenate([p_value[0:16], p_value[16:]], axis=1).astype(BF)
    over_near(lambda peer: sq, rq1.at[near], G_Q1)
    rq1[near] = sq[...]

    for n in VALUES + BACKS:
        for ref, count, g in ((a_in, NEAR, G_A), (b_in, FAR, G_B), (c_in, FAR, G_C)):
            gone(ref.at[n, pl.ds(0, count - 1)], g + n)
    for n in VALUES:
        gone(d_in.at[n, pl.ds(0, NEAR - 1)], G_D + n)

    @pl.when(summing)
    def _():
        from_far(rt1, G_T1)
        total = rt1[0].astype(F32)
        for k in range(1, FAR):
            total = total + rt1[k].astype(F32)
        t1[...] = total.astype(BF)
        over_near(lambda peer: t1, rt2.at[near], G_T2)
        rt2[near] = t1[...]

    arrived(re3.at[pl.ds(0, 3)], G_E3)
    e3[...] = (re3[0] + re3[1] + re3[2] + re3[3]).astype(BF)
    over_x(lambda peer: e3, re4.at[across], G_E4)
    re4[across] = e3[...]

    def frame_row(r, carry):
        normed = dot(w_in_t[...], gbef[r])
        u = unit[r]
        mean_grad = jnp.mean(normed, axis=0, keepdims=True)
        mean_proj = jnp.mean(normed * u, axis=0, keepdims=True)
        source = gj[r].astype(F32) + inv[r, 0:1] * (normed - mean_grad - u * mean_proj)
        for t in range(2):
            gframe_out[t, pl.ds(r * CH, CH), :] = source[:, half(t)]
        return carry

    loop(ROWS, frame_row, unroll=16)

    from_near(rq1, G_Q1)
    total = rq1[0].astype(F32)
    for k in range(1, NEAR):
        total = total + rq1[k].astype(F32)
    q1[...] = total.astype(BF)
    over_far(lambda peer: q1, rq2.at[far], G_Q2)
    rq2[far] = q1[...]

    arrived(re4.at[pl.ds(0, 3)], G_E4)
    over_y(lambda peer: re4, re5.at[level], G_E5)
    re5[level] = re4[...]

    @pl.when(summing)
    def _():
        from_near(rt2, G_T2)
        total = rt2[0].astype(F32)
        for k in range(1, NEAR):
            total = total + rt2[k].astype(F32)
        t2[...] = total.astype(BF)
        over_far(lambda peer: t2, rt3.at[far], G_T3)
        rt3[far] = t2[...]

    loop(ROWS // 2, lambda r, carry: out_row(r + ROWS // 2, carry), carry, unroll=8)

    from_far(rq2, G_Q2)
    total = rq2[0].astype(F32)
    for k in range(1, FAR):
        total = total + rq2[k].astype(F32)
    value_out[...] = total

    arrived(re5.at[pl.ds(0, 3)], G_E5)
    push(re5, re6, G_E6, near_device(twin))
    early_out[pl.ds(pl.multiple_of(mine, 512), 512)] = re5[...].reshape(512, LANES)

    @pl.when(summing)
    def _():
        arrived(rt3.at[pl.ds(0, 11)], G_T3)
        gone(rt1.at[pl.ds(0, 11)], G_T1)
        gone(rt2.at[pl.ds(0, NEAR - 1)], G_T2)
        gone(rt1.at[pl.ds(0, FAR - 1)], G_T3)

    @pl.when(far >= 12)
    def _():
        arrived(rt3, G_T3)
        gone(rt1.at[pl.ds(0, 12)], G_T1)

    tail_out[...] = rt3[...]
    arrived(re6, G_E6)
    early_out[pl.ds(pl.multiple_of(512 - mine, 512), 512)] = re6[...].reshape(512, LANES)

    for which, g_row, g_pack in ((0, G_ROW0, G_PACK0), (1, G_ROW1, G_PACK1)):
        gone(row_in.at[which], g_row)
        gone(pack_in.at[which], g_pack)
    for n in BACKS:
        gone(d_in.at[n, pl.ds(0, NEAR - 1)], G_D + n)
    gone(rq1.at[pl.ds(0, NEAR - 1)], G_Q1)
    gone(rq2.at[pl.ds(0, FAR - 1)], G_Q2)
    gone(re0, G_E0)
    for ref, g in ((re1, G_E1), (re2, G_E2), (re3, G_E3), (re4, G_E4), (re5, G_E5)):
        gone(ref.at[pl.ds(0, 3)], g)
    gone(re6, G_E6)


def finish(rest, gframe, early, tail, value, *refs):
    outs, sem = (refs[:7], refs[7:14]), refs[14]
    restored, grad_frames, grad_w_in_t, grad_grid, grad_block, grad_w_out, grad_conv = outs[1]
    copies = []

    def leave(k, part=None):
        src, dst = outs[1][k], outs[0][k]
        if part is not None:
            src, dst = src.at[part], dst.at[part]
        copies.append(pltpu.make_async_copy(src, dst, sem.at[len(copies)]))
        copies[-1].start()

    def turn_out(src, dst, k):
        for first in range(0, CH, CH // 2):

            def channel(c, carry):
                for t in range(2):
                    dst[first + c, :, half(t)] = src[t, pl.ds(first + c, ROWS, stride=CH), :].astype(BF)
                return carry

            loop(CH // 2, channel, unroll=16)
            leave(k, pl.ds(first, CH // 2))

    scale = float(ROWS * NA * COLS * NW) ** (-0.5)
    for k in range(2):
        grad_grid[:, half(k)] = early[k * COLS : (k + 1) * COLS].astype(F32) * scale
        grad_block[:, half(k)] = early[(2 + k) * COLS : (3 + k) * COLS].astype(F32) * scale
    leave(3)
    leave(4)
    turn_out(gframe, grad_frames, 1)
    turn_out(rest, restored, 0)
    quarter = value[...] * scale
    zeros = jnp.zeros((HC, CH), F32)
    quarter = jnp.concatenate([zeros, quarter[:, :CH], quarter[:, CH:], zeros, zeros], axis=0)
    grad_w_in_t[...] = tail[3 * CH : 4 * CH].astype(F32) * scale + quarter.T
    leave(2)
    last = tail[4 * CH :].astype(F32) * scale
    grad_w_out[...] = last[CH:, CH:]
    leave(5)
    for b in range(3):
        rows = slice((2 - b) * CH, (3 - b) * CH)
        pair = tail[rows].astype(F32) * scale
        grad_conv[0, b] = pair[:, :CH]
        grad_conv[1, b] = pair[:, CH:]
    grad_conv[2, 2] = last[:CH, :CH]
    grad_conv[2, 1] = last[CH:, :CH]
    grad_conv[2, 0] = last[:CH, CH:]
    leave(6)
    for copy in copies:
        copy.wait()


def vm(*shape, dtype=BF):
    return pltpu.VMEM(shape, dtype)


def exchange():
    message_w = vm(4, NEAR, 2, 2, QC, LANES)
    message_a = vm(4, FAR, 16, 256)
    return [message_w, message_w, vm(4, 2 * 16 * QC, LANES, dtype=F32)] + [message_a] * 4 + [message_w] * 2


SCRATCH = [
    vm(CH, ROWS, COLS),
    vm(CH, 2 * CH),
    vm(COLS, COLS),
    vm(COLS, COLS),
    vm(CH, CH),
    vm(3, 3, CH, CH),
    vm(CH, ROWS, COLS),
    vm(2 * CH, CH),
    vm(2, CH * ROWS, LANES, dtype=F32),
    vm(ROWS, CH, COLS),
    vm(ROWS, CH, COLS),
    vm(ROWS, CH, COLS, dtype=F32),
    vm(ROWS, 8, COLS, dtype=F32),
    vm(ROWS, 2 * CH, COLS, dtype=F32),
    vm(ROWS, CH, COLS),
    vm(ROWS, HC, COLS),
    vm(ROWS + 2, 3 * CH, COLS),
    vm(ROWS + 2, 3 * CH, COLS),
    vm(ROWS, CH, COLS),
    vm(ROWS, CH, COLS, dtype=F32),
    vm(ROWS, HC, COLS),
    vm(ROWS, HC, COLS),
    vm(ROWS, HC, COLS),
    vm(ROWS, HC, COLS),
    *exchange(),
    vm(ROWS, CH, COLS),
    vm(ROWS, 2 * CH, COLS),
    vm(ROWS + 4, CH, COLS),
    vm(2, 2, CH, COLS),
    vm(2, 32, LANES),
    vm(2, 96, LANES),
    vm(CH, LANES),
    vm(CH, LANES),
    vm(COLS, COLS),
    vm(COLS, COLS),
    vm(COLS, COLS),
    vm(COLS, COLS),
    vm(4 * COLS, LANES),
    vm(512, LANES),
    vm(512, LANES),
    vm(4, 128, LANES),
    vm(128, LANES, dtype=F32),
    vm(4, 32, LANES, dtype=F32),
    vm(32, LANES, dtype=F32),
    vm(4, 32, LANES, dtype=F32),
    vm(32, LANES),
    vm(4, 32, LANES),
    vm(4, 4, 32, LANES),
    vm(4, 4, 32, LANES),
    vm(6 * CH, LANES),
    vm(FAR, 32, LANES),
    vm(32, LANES),
    vm(NEAR, 32, LANES),
    vm(32, LANES),
    vm(12, 32, LANES),
    vm(16, LANES),
    vm(NEAR, 16, LANES),
    vm(16, LANES),
    vm(FAR, 16, LANES),
    pltpu.SemaphoreType.DMA((GROUPS,)),
    pltpu.SemaphoreType.DMA((GROUPS,)),
    pltpu.SemaphoreType.DMA((7,)),
]


def body(frames, w_in, grid_mix, block_mix, w_out, conv_w, cotangent):
    operands = (frames, w_in.T, grid_mix, block_mix, w_out, conv_w, cotangent)
    vmem = pl.BlockSpec(memory_space=pltpu.VMEM)
    shape = jax.ShapeDtypeStruct
    rest, gframe, early, tail, value = pl.pallas_call(
        kernel,
        out_shape=(
            shape((2, ROWS * CH, LANES), F32),
            shape((2, ROWS * CH, LANES), F32),
            shape((4 * COLS, LANES), BF),
            shape((12, 32, LANES), BF),
            shape((16, LANES), F32),
        ),
        in_specs=[pl.BlockSpec(memory_space=pltpu.HBM)] * 7,
        out_specs=(vmem,) * 5,
        scratch_shapes=SCRATCH,
        compiler_params=pltpu.CompilerParams(
            collective_id=0, has_side_effects=True, vmem_limit_bytes=32 * 1024 * 1024
        ),
    )(*[pltpu.with_memory_space_constraint(x, pltpu.HBM) for x in operands])
    restored, grad_frames, grad_w_in_t, grad_grid, grad_block, grad_w_out, grad_conv = pl.pallas_call(
        finish,
        out_shape=(
            shape((CH, ROWS, COLS), BF),
            shape((CH, ROWS, COLS), BF),
            shape((CH, 2 * CH), F32),
            shape((COLS, COLS), F32),
            shape((COLS, COLS), F32),
            shape((CH, CH), F32),
            shape((3, 3, CH, CH), F32),
        ),
        in_specs=[vmem] * 5,
        out_specs=(pl.BlockSpec(memory_space=pl.ANY),) * 7,
        scratch_shapes=[
            vm(CH, ROWS, COLS),
            vm(CH, ROWS, COLS),
            vm(CH, 2 * CH, dtype=F32),
            vm(COLS, COLS, dtype=F32),
            vm(COLS, COLS, dtype=F32),
            vm(CH, CH, dtype=F32),
            vm(3, 3, CH, CH, dtype=F32),
            pltpu.SemaphoreType.DMA((9,)),
        ],
        compiler_params=pltpu.CompilerParams(vmem_limit_bytes=16 * 1024 * 1024),
    )(rest, gframe, early, tail.reshape(6 * CH, LANES), value)
    return restored, grad_frames, grad_w_in_t.T, grad_grid, grad_block, grad_w_out, grad_conv


def solution(mesh):
    placed = (P(None, "ha", "wa"), P(), P(), P(), P(), P(), P(None, "ha", "wa"))
    return jax.shard_map(
        body,
        mesh=mesh,
        in_specs=placed,
        out_specs=(P(None, "ha", "wa"), P(None, "ha", "wa"), P(), P(), P(), P(), P()),
        check_vma=False,
    )
```

```python
import jax
import jax.numpy as jnp
from jax import lax
from jax.experimental import pallas as pl
from jax.experimental.pallas import tpu as pltpu
from jax.sharding import PartitionSpec as P

BF = jnp.bfloat16
F32 = jnp.float32
EPS = 1e-06
MESH = pl.DeviceIdType.MESH

CH = 64
HC = 32
ROWS = 16
COLS = 256
LANES = 128
NA = 16
NW = 8
NEAR = 8
FAR = 16

(G_ROW0, G_PACK0, G_ROW1, G_PACK1) = range(4)
(G_E0, G_E1, G_E2, G_E3, G_E5, G_E6, G_T1, G_T2, G_T3, G_Q1, G_Q2) = range(4, 15)
VALUES, BACKS = (0, 1), (2, 3)
G_A, G_B, G_C, G_D = 16, 20, 24, 28
GROUPS = 32
QC = 16


def dot(a, b):
    return lax.dot_general(a, b, (((1,), (0,)), ((), ())), preferred_element_type=F32)


def dot_nt(a, b):
    return lax.dot_general(a, b, (((1,), (1,)), ((), ())), preferred_element_type=F32)


def dot_tn(a, b):
    return lax.dot_general(a, b, (((0,), (0,)), ((), ())), preferred_element_type=F32)


def swap_granules(load, store, depth):
    lane = lax.broadcasted_iota(jnp.int16, (depth, LANES), 1)
    for row_half in range(2):
        for col_half in range(2):
            held = [load(row_half * 8 + k, col_half) for k in range(8)]
            for s in range(3):
                width = 16 << s
                low = (lane & width) == 0
                for k in range(8):
                    if not k & (1 << s):
                        a, b = held[k], held[k | (1 << s)]
                        held[k] = jnp.where(low, a, pltpu.roll(b, width, 1))
                        held[k | (1 << s)] = jnp.where(low, pltpu.roll(a, LANES - width, 1), b)
            for k in range(8):
                store(col_half * 8 + k, row_half, held[k])


def half(t):
    return slice(t * LANES, (t + 1) * LANES)


def loop(count, step, carry=0, unroll=1):
    return lax.fori_loop(0, count, step, carry, unroll=unroll)


def gelu_parts(x):
    root = 0.7978845608028654
    cube = root * 0.044715
    square = x * x
    h = 0.5 * jnp.tanh(x * (cube * square + root)) + 0.5
    value = x * h
    return value, h + value * (1.0 - h) * ((6.0 * cube) * square + 2.0 * root)


def kernel(
    frames_hbm, w_in_t_hbm, grid_mix_hbm, block_mix_hbm, w_out_hbm, conv_w_hbm, cot_hbm,
    rest_out, gframe_out, early_out, tail_out, value_out,
    frames, w_in_t, grid_mix, block_mix, w_out, conv_w, cot, w_in,
    turn, xb, nb, unit, inv, dgelu, gates, bval, u3, v3, gj, gg, xt, bt, bm, gbv,
    a, a_in, x32, b, b_in, c, c_in, d, d_in,
    gated, gbef, jp, row_in, pack_out, pack_in, edge_l, edge_r,
    mixp, mixp_t, gather, spread, se, re0, e0, re1, e1, re2, e2, re3, e3, re5, re6,
    st, rt1, t1, rt2, t2, rt3, sq, rq1, q1, rq2,
    ssem, rsem, isem,
):
    ia = lax.axis_index("ha")
    iw = lax.axis_index("wa")
    up, down = lax.rem(ia + NA - 1, NA), lax.rem(ia + 1, NA)
    left, right = lax.rem(iw + NW - 1, NW), lax.rem(iw + 1, NW)
    lane = lax.broadcasted_iota(jnp.int16, (CH, LANES), 1)
    lane_wide = lax.broadcasted_iota(jnp.int32, (CH, LANES), 1)

    loads = [
        pltpu.make_async_copy(src, dst, isem.at[k])
        for k, (src, dst) in enumerate(
            [
                (frames_hbm, frames),
                (w_in_t_hbm, w_in_t),
                (cot_hbm, cot),
                (conv_w_hbm, conv_w),
                (w_out_hbm, w_out),
                (block_mix_hbm, block_mix),
                (grid_mix_hbm, grid_mix),
            ]
        )
    ]
    for load in loads:
        load.start()

    def push(src, dst, g, where):
        pltpu.make_async_remote_copy(
            src_ref=src, dst_ref=dst, send_sem=ssem.at[g], recv_sem=rsem.at[g], device_id=where, device_id_type=MESH
        ).start()

    near = lax.rem(iw, 2) * 4 + lax.rem(ia, 4)
    far = ia // 4 * 4 + iw // 2

    def near_device(peer):
        return ia // 4 * 4 + lax.rem(peer, 4), iw // 2 * 2 + peer // 4

    def far_device(peer):
        return peer // 4 * 4 + lax.rem(ia, 4), lax.rem(peer, 4) * 2 + lax.rem(iw, 2)

    near_peers = [lax.rem(near + k, NEAR) for k in range(1, NEAR)]
    far_peers = [lax.rem(far + k, FAR) for k in range(1, FAR)]
    twin = near + 1 - 2 * lax.rem(near, 2)

    near_places = [near_device(peer) for peer in near_peers]
    far_places = [far_device(peer) for peer in far_peers]

    def over_near(src_of, dst, g):
        for peer, place in zip(near_peers, near_places):
            push(src_of(peer), dst, g, place)

    def over_far(src_of, dst, g):
        for peer, place in zip(far_peers, far_places):
            push(src_of(peer), dst, g, place)

    def over_y(src_of, dst, g):
        for k in range(1, 4):
            peer = lax.rem(near + 2 * k, NEAR)
            push(src_of(peer // 2), dst, g, near_device(peer))

    def arrived(ref, g):
        pltpu.make_async_copy(ref, ref, rsem.at[g]).wait()

    def gone(ref, g):
        pltpu.make_async_copy(ref, ref, ssem.at[g]).wait()

    def from_near(ref, g):
        arrived(ref.at[pl.ds(0, NEAR - 1)], g)

    def from_far(ref, g):
        arrived(ref.at[pl.ds(0, FAR - 1)], g)

    mine = lax.rem(near, 2) * 512
    level = near // 2

    barrier = pltpu.get_barrier_semaphore()
    peers = [near_device(peer) for peer in near_peers]
    peers += [far_device(peer) for peer in far_peers]
    peers += [(a, b) for a in (up, ia, down) for b in (left, right)] + [(up, iw), (down, iw)]
    for peer in peers:
        pl.semaphore_signal(barrier, inc=1, device_id=peer, device_id_type=MESH)

    def turn_in(src):
        for t in range(2):
            turn[t] = src[:, :, half(t)].astype(F32).reshape(CH * ROWS, LANES)

    def turned(r, t):
        return turn[t, pl.ds(r, CH, stride=ROWS), :]

    def edges(pack, t0, t1, r):
        pack = jnp.where(lane_wide == r, pltpu.roll(t0, r, 1), pack)
        return jnp.where(lane_wide == ROWS + r, pltpu.roll(t1, r + 17, 1), pack)

    def send_halo(field, pack, which, g_row, g_pack):
        pack_out[which] = jnp.concatenate([pack, jnp.zeros_like(pack)], axis=0).T[0:32]
        push(field.at[1, CH : 2 * CH], row_in.at[which, 1], g_row, (up, iw))
        push(field.at[ROWS, CH : 2 * CH], row_in.at[which, 0], g_row, (down, iw))
        for slot, where in enumerate(
            [(ia, right), (down, right), (up, right), (ia, left), (down, left), (up, left)]
        ):
            part = pack_out.at[which, pl.ds(16 if slot < 3 else 0, 16)]
            push(part, pack_in.at[which, pl.ds(16 * slot, 16)], g_pack, where)

    def take_halo(field, which, g_row, g_pack):
        arrived(row_in.at[which], g_row)
        arrived(pack_in.at[which], g_pack)
        field[0, CH : 2 * CH] = jnp.where(ia > 0, row_in[which, 0], jnp.zeros((CH, COLS), BF))
        field[ROWS + 1, CH : 2 * CH] = jnp.where(ia < NA - 1, row_in[which, 1], jnp.zeros((CH, COLS), BF))
        first = jnp.where(ia > 0, 0, 1)
        last = jnp.where(ia < NA - 1, ROWS + 2, ROWS + 1)
        got = jnp.concatenate([pack_in[which], jnp.zeros((32, LANES), BF)], axis=0).T[0:CH]

        def assemble(middle, above, below, has):
            joined = jnp.where(lane == 0, above, jnp.where(lane == ROWS + 1, below, middle))
            inside = (lane_wide >= first) & (lane_wide < jnp.where(has, last, 0))
            return jnp.where(inside, joined, jnp.zeros_like(joined))

        edge_l[...] = assemble(pltpu.roll(got, 1, 1), pltpu.roll(got, 97, 1), pltpu.roll(got, 113, 1), iw > 0)
        edge_r[...] = assemble(pltpu.roll(got, 81, 1), pltpu.roll(got, 49, 1), pltpu.roll(got, 65, 1), iw < NW - 1)

        def shifts(p, carry):
            t0 = field[p, CH : 2 * CH, half(0)]
            t1 = field[p, CH : 2 * CH, half(1)]
            a0, a1 = pltpu.roll(t0, 1, 1), pltpu.roll(t1, 1, 1)
            b0, b1 = pltpu.roll(t0, LANES - 1, 1), pltpu.roll(t1, LANES - 1, 1)
            lh = pltpu.roll(edge_l[...], lax.rem(LANES - p, LANES), 1)
            rh = pltpu.roll(edge_r[...], LANES - 1 - p, 1)
            field[p, 0:CH, half(0)] = jnp.where(lane == 0, lh, a0)
            field[p, 0:CH, half(1)] = jnp.where(lane == 0, a0, a1)
            field[p, 2 * CH :, half(0)] = jnp.where(lane == LANES - 1, b1, b0)
            field[p, 2 * CH :, half(1)] = jnp.where(lane == LANES - 1, rh, b1)
            return carry

        loop(ROWS + 2, shifts, unroll=9)

    def conv_start(w, field):
        y = dot(w, field[0])
        z = dot(w, field[1])
        return z[0:CH], y[0:CH] + z[CH : 2 * CH]

    def conv_step(w, field, r, carry):
        later, now = carry
        y = dot(w, field[r + 2])
        return now + y[2 * CH :], (y[0:CH], later + y[CH : 2 * CH])

    def step_a(n):
        over_near(lambda peer: a.at[n, peer], a_in.at[n, near], G_A + n)

    def step_b(n):
        arrived(a_in.at[n, pl.ds(0, NEAR - 1)], G_A + n)

        def widen(j, carry):
            for t in range(2):
                for r in range(2):
                    x32[n, pl.ds((r * 16 + j * 2 + t) * QC, QC), :] = a_in[n, j, t, r].astype(F32)
            return carry

        loop(NEAR, widen, unroll=8)

        for peer, place in zip([*far_peers, far], [*far_places, None]):
            base = peer // 8 * (16 * QC) + lax.rem(peer, 8) * 2
            slot = b_in if peer is far else b
            for k in range(2):
                slot[n, peer, :, half(k)] = x32[n, pl.ds(base + k, 16, stride=QC), :].astype(BF)
            if peer is not far:
                push(b.at[n, peer], b_in.at[n, far], G_B + n, place)

    def table(n):
        return b_in[n].reshape(256, 256)

    def step_c(n, mix):
        arrived(b_in.at[n, pl.ds(0, FAR - 1)], G_B + n)
        c[n] = dot(mix[...], table(n)).astype(BF).reshape(FAR, 16, 256)
        over_far(lambda peer: c.at[n, peer], c_in.at[n, far], G_C + n)
        c_in[n, far] = c[n, far]

    def step_d(n):
        arrived(c_in.at[n, pl.ds(0, FAR - 1)], G_C + n)

        def unpick(q, carry):
            for r in range(2):
                for k in range(2):
                    x32[n, pl.ds((r * QC + q * 2 + k) * 16, 16), :] = c_in[n, r * 8 + q, :, half(k)].astype(F32)
            return carry

        loop(8, unpick, unroll=8)

        for peer, place in zip([*near_peers, near], [*near_places, None]):
            slot = d_in if peer is near else d
            for t in range(2):
                for r in range(2):
                    slot[n, peer, t, r] = x32[n, pl.ds(r * QC * 16 + peer * 2 + t, QC, stride=16), :].astype(BF)
            if peer is not near:
                push(d.at[n, peer], d_in.at[n, near], G_D + n, place)

    def step_e(n):
        arrived(d_in.at[n, pl.ds(0, NEAR - 1)], G_D + n)

    def order(cell, row):
        found = (row & 0xC1) | ((row & 6) << 3) | ((row & 48) >> 2) | ((row & 8) >> 2)
        return jnp.where(cell == found, 1.0, 0.0).astype(BF)

    loads[0].wait()
    loads[1].wait()
    turn_in(frames)
    w_in[...] = w_in_t[...].astype(F32).T.astype(BF)

    def value_row(slot, peer, low):
        r = peer * 2 + low
        normed = []
        for t in range(2):
            x = turned(r, t)
            xb[r, :, half(t)] = x.astype(BF)
            off = x - jnp.mean(x, axis=0, keepdims=True)
            rstd = lax.rsqrt(jnp.mean(off * off, axis=0, keepdims=True) + EPS)
            u = off * rstd
            unit[r, :, half(t)] = u
            inv[r, :, half(t)] = jnp.broadcast_to(rstd, (8, LANES))
            normed.append(u.astype(BF))
        normed = jnp.concatenate(normed, axis=1)
        nb[r] = normed
        value, slope = gelu_parts(dot(w_in[HC:CH], normed))
        dgelu[r, HC:CH] = slope
        value = value.astype(BF)
        for n in VALUES:
            for t in range(2):
                slot[n, peer, t, low] = value[n * QC : (n + 1) * QC, half(t)]

    for first in range(0, NEAR, 4):
        group = [*near_peers, near][first : first + 4]
        for peer in group:
            for low in range(2):
                value_row(a_in if peer is near else a, peer, low)
        if first == 0:
            pl.semaphore_wait(barrier, len(peers))
        for peer in group:
            if peer is not near:
                push(a.at[0, peer], a_in.at[0, near], G_A, near_device(peer))
    step_a(1)

    loads[2].wait()
    turn_in(cot)

    def cot_row(r, pack):
        t0, t1 = turned(r, 0).astype(BF), turned(r, 1).astype(BF)
        u3[r + 1, CH : 2 * CH, half(0)] = t0
        u3[r + 1, CH : 2 * CH, half(1)] = t1
        return edges(pack, t0, t1, r)

    pack = loop(ROWS, cot_row, jnp.zeros((CH, LANES), BF), unroll=16)
    send_halo(u3, pack, 0, G_ROW0, G_PACK0)

    w_rest = jnp.concatenate([w_in[0:HC], w_in[CH:]], axis=0)

    def gate_row(r, carry):
        before = dot(w_rest, nb[r])
        value, slope = gelu_parts(before[0:HC])
        gates[r, 0:HC] = value.astype(BF)
        dgelu[r, 0:HC] = slope
        value, slope = gelu_parts(before[HC:])
        dgelu[r, CH:] = slope
        value = value.astype(BF)
        gates[r, HC:CH] = value[0:HC]
        bval[r] = value[HC:]
        return carry

    loop(ROWS, gate_row, unroll=8)
    for load in loads[3:]:
        load.wait()
    down_axis = lax.broadcasted_iota(jnp.int32, (COLS, COLS), 0)
    along_axis = lax.broadcasted_iota(jnp.int32, (COLS, COLS), 1)
    gather[...] = order(along_axis, down_axis)
    spread[...] = order(down_axis, along_axis)
    mixp[...] = dot(dot(gather[...], grid_mix[...]).astype(BF), spread[...]).astype(BF)
    mixp_t[...] = mixp[...].T

    back_w = jnp.concatenate(
        [jnp.concatenate([conv_w[2 - a, 2 - b] for a in range(3)], axis=1) for b in range(3)], axis=0
    ).astype(F32).T.astype(BF)
    w_out_t = w_out[...].astype(F32).T.astype(BF)
    take_halo(u3, 0, G_ROW0, G_PACK0)

    def back_row(r, carry):
        total, carry = conv_step(back_w, u3, r, carry)
        g = (total + u3[r + 1, CH : 2 * CH].astype(F32)).astype(BF)
        gj[r] = g
        up_gated = dot(w_out_t, g)
        gg[r] = up_gated
        mixed = (up_gated[0:HC] * gates[r, 0:HC].astype(F32)).astype(BF)
        for n in range(2):
            for t in range(2):
                a[2 + n, r // 2, t, r % 2] = mixed[n * QC : (n + 1) * QC, half(t)]
        return carry

    step_b(0)
    carry = conv_start(back_w, u3)
    for first in range(0, NEAR, 4):
        if first:
            step_b(1)
        for r in range(2 * first, 2 * first + 8):
            carry = back_row(r, carry)
        for peer in range(first, first + 4):

            @pl.when(peer != near)
            def _():
                push(a.at[2, peer], a_in.at[2, near], G_A + 2, near_device(peer))

    step_a(3)
    for n in BACKS:
        a_in[n, near] = a[n, near]


    def put(ref):
        def store(k, t, value):
            ref[k, :, half(t)] = value

        return store

    swap_granules(lambda k, t: bval[k, :, half(t)], put(xt), HC)
    values = xt[...].reshape(ROWS * HC, COLS)
    mixed = dot_nt(values, block_mix[...]).astype(BF)
    swap_granules(lambda k, t: mixed[k * HC : (k + 1) * HC, half(t)], put(bm), HC)

    step_c(0, mixp)

    def block_back(k, t):
        return (gg[k, HC:, half(t)] * gates[k, HC:, half(t)].astype(F32)).astype(BF)

    swap_granules(block_back, put(bt), HC)
    backs = bt[...].reshape(ROWS * HC, COLS)
    unmixed = dot(backs, block_mix[...]).astype(BF)
    swap_granules(lambda k, t: unmixed[k * HC : (k + 1) * HC, half(t)], put(gbv), HC)

    step_c(1, mixp)
    step_b(2)

    part_block = dot_tn(backs, values).astype(BF)
    se[2 * COLS : 3 * COLS] = part_block[:, half(0)]
    se[3 * COLS :] = part_block[:, half(1)]

    step_b(3)

    def block_before_row(r, carry):
        d = dgelu[r, CH:]
        gbef[r, CH : CH + HC] = (d[0:HC] * (gg[r, HC:] * (bm[r].astype(F32) + 1.0))).astype(BF)
        gbef[r, CH + HC :] = (d[HC:] * gbv[r].astype(F32)).astype(BF)
        gbef[r, HC:CH] = jnp.zeros((HC, COLS), BF)
        return carry

    loop(ROWS, block_before_row, unroll=8)
    for k in (0, 1, ROWS + 2, ROWS + 3):
        jp[k] = jnp.zeros((CH, COLS), BF)

    step_d(0)
    step_d(1)
    step_c(2, mixp_t)
    step_c(3, mixp_t)

    part_grid = (dot_nt(table(2), table(0)) + dot_nt(table(3), table(1))).astype(BF)
    part_grid = dot(dot(spread[...], part_grid).astype(BF), gather[...]).astype(BF)
    se[0:COLS] = part_grid[:, half(0)]
    se[COLS : 2 * COLS] = part_grid[:, half(1)]
    push(se.at[pl.ds(pl.multiple_of(512 - mine, 512), 512)], re0, G_E0, near_device(twin))

    arrived(re0, G_E0)
    e0[...] = (se[pl.ds(pl.multiple_of(mine, 512), 512)].astype(F32) + re0[...].astype(F32)).astype(BF)
    over_y(lambda peer: e0.at[pl.ds(pl.multiple_of(peer * 128, 128), 128)], re1.at[level], G_E1)
    re1[level] = e0[pl.ds(pl.multiple_of(level * 128, 128), 128)]

    step_e(0)
    step_e(1)

    def returned(chains, r):
        return [
            jnp.concatenate([d_in[n, r // 2, t, lax.rem(r, 2)] for n in chains], axis=0).astype(F32) for t in range(2)
        ]

    def joined_row(r, pack):
        grid_mixed = returned(VALUES, r)
        for t in range(2):
            gates_t = gates[r, :, half(t)].astype(F32)
            more = grid_mixed[t] + 1.0
            gated[r, 0:HC, half(t)] = (gates_t[0:HC] * more).astype(BF)
            gated[r, HC:, half(t)] = (gates_t[HC:] * (bm[r, :, half(t)].astype(F32) + 1.0)).astype(BF)
            gbef[r, 0:HC, half(t)] = (dgelu[r, 0:HC, half(t)] * (gg[r, 0:HC, half(t)] * more)).astype(BF)
        j = (xb[r].astype(F32) + dot(w_out[...], gated[r])).astype(BF)
        jp[r + 2] = j
        v3[r + 1, CH : 2 * CH] = j
        return edges(pack, j[:, half(0)], j[:, half(1)], r)

    pack = loop(ROWS, joined_row, jnp.zeros((CH, LANES), BF), unroll=16)
    send_halo(v3, pack, 1, G_ROW1, G_PACK1)

    step_d(2)
    step_d(3)

    def pixels(ref, rows=slice(None)):
        return jnp.concatenate([ref[r, rows] for r in range(ROWS)], axis=1)

    p_conv = dot_nt(
        jnp.concatenate([u3[p] for p in range(ROWS + 2)], axis=1),
        jnp.concatenate([jp[p : p + 3].reshape(3 * CH, COLS) for p in range(ROWS + 2)], axis=1),
    )
    arrived(re1.at[pl.ds(0, 3)], G_E1)
    total = re1[0].astype(F32)
    for k in range(1, 4):
        total = total + re1[k].astype(F32)
    e1[...] = total
    over_far(lambda peer: e1.at[pl.ds(pl.multiple_of(peer * 8, 8), 8)], re2.at[far], G_E2)
    re2[far] = e1[pl.ds(pl.multiple_of(far * 8, 8), 8)]

    p_in = dot_nt(pixels(nb), pixels(gbef))
    p_out = dot_nt(pixels(gj), pixels(gated))
    st[0 : 3 * CH] = p_conv[:, half(0)].astype(BF)
    st[3 * CH : 4 * CH] = p_in.astype(BF)
    third = p_conv[:, 2 * CH :]
    st[4 * CH :] = jnp.concatenate(
        [third[: 2 * CH], jnp.concatenate([third[2 * CH :], p_out], axis=0)], axis=1
    ).astype(BF)
    summing = far < 12
    for peer, place in zip(far_peers, far_places):

        @pl.when(peer < 12)
        def _():
            push(st.at[pl.ds(pl.multiple_of(peer * 32, 32), 32)], rt1.at[far], G_T1, place)

    @pl.when(summing)
    def _():
        rt1[far] = st[pl.ds(pl.multiple_of(far * 32, 32), 32)]

    take_halo(v3, 1, G_ROW1, G_PACK1)

    conv_k = jnp.concatenate(
        [jnp.concatenate([conv_w[a, b] for b in range(3)], axis=1) for a in range(3)], axis=0
    )

    def out_row(r, carry):
        total, carry = conv_step(conv_k, v3, r, carry)
        total = total + v3[r + 1, CH : 2 * CH].astype(F32)
        for t in range(2):
            rest_out[t, pl.ds(r * CH, CH), :] = total[:, half(t)]
        return carry

    carry = loop(ROWS // 2, out_row, conv_start(conv_k, v3), unroll=8)

    from_far(re2, G_E2)
    total = re2[0]
    for k in range(1, FAR):
        total = total + re2[k]
    e2[...] = total
    over_far(lambda peer: e2, re3.at[far], G_E3)
    re3[far] = e2[...]

    step_e(2)
    step_e(3)

    def value_before_row(r, carry):
        grid_back = returned(BACKS, r)
        for t in range(2):
            gbef[r, HC:CH, half(t)] = (dgelu[r, HC:CH, half(t)] * grid_back[t]).astype(BF)
        return carry

    loop(ROWS, value_before_row, unroll=8)
    p_value = dot_nt(pixels(gbef, slice(HC, CH)), pixels(nb))
    sq[...] = jnp.concatenate([p_value[0:16], p_value[16:]], axis=1).astype(BF)
    over_near(lambda peer: sq, rq1.at[near], G_Q1)
    rq1[near] = sq[...]

    for n in VALUES + BACKS:
        for ref, count, g in ((a_in, NEAR, G_A), (b_in, FAR, G_B), (c_in, FAR, G_C)):
            gone(ref.at[n, pl.ds(0, count - 1)], g + n)
    for n in VALUES:
        gone(d_in.at[n, pl.ds(0, NEAR - 1)], G_D + n)

    @pl.when(summing)
    def _():
        from_far(rt1, G_T1)
        total = rt1[0].astype(F32)
        for k in range(1, FAR):
            total = total + rt1[k].astype(F32)
        t1[...] = total.astype(BF)
        over_near(lambda peer: t1, rt2.at[near], G_T2)
        rt2[near] = t1[...]

    from_far(re3, G_E3)
    e3[...] = re3[...].reshape(128, LANES).astype(BF)
    over_y(lambda peer: e3, re5.at[level], G_E5)
    re5[level] = e3[...]

    def frame_row(r, carry):
        normed = dot(w_in_t[...], gbef[r])
        u = unit[r]
        mean_grad = jnp.mean(normed, axis=0, keepdims=True)
        mean_proj = jnp.mean(normed * u, axis=0, keepdims=True)
        source = gj[r].astype(F32) + inv[r, 0:1] * (normed - mean_grad - u * mean_proj)
        for t in range(2):
            gframe_out[t, pl.ds(r * CH, CH), :] = source[:, half(t)]
        return carry

    loop(ROWS, frame_row, unroll=16)

    from_near(rq1, G_Q1)
    total = rq1[0].astype(F32)
    for k in range(1, NEAR):
        total = total + rq1[k].astype(F32)
    q1[...] = total.astype(BF)
    over_far(lambda peer: q1, rq2.at[far], G_Q2)
    rq2[far] = q1[...]

    @pl.when(summing)
    def _():
        from_near(rt2, G_T2)
        total = rt2[0].astype(F32)
        for k in range(1, NEAR):
            total = total + rt2[k].astype(F32)
        t2[...] = total.astype(BF)
        over_far(lambda peer: t2, rt3.at[far], G_T3)
        rt3[far] = t2[...]

    loop(ROWS // 2, lambda r, carry: out_row(r + ROWS // 2, carry), carry, unroll=8)

    from_far(rq2, G_Q2)
    total = rq2[0].astype(F32)
    for k in range(1, FAR):
        total = total + rq2[k].astype(F32)
    value_out[...] = total

    arrived(re5.at[pl.ds(0, 3)], G_E5)
    push(re5, re6, G_E6, near_device(twin))
    early_out[pl.ds(pl.multiple_of(mine, 512), 512)] = re5[...].reshape(512, LANES)

    @pl.when(summing)
    def _():
        arrived(rt3.at[pl.ds(0, 11)], G_T3)
        gone(rt1.at[pl.ds(0, 11)], G_T1)
        gone(rt2.at[pl.ds(0, NEAR - 1)], G_T2)
        gone(rt1.at[pl.ds(0, FAR - 1)], G_T3)

    @pl.when(far >= 12)
    def _():
        arrived(rt3, G_T3)
        gone(rt1.at[pl.ds(0, 12)], G_T1)

    tail_out[...] = rt3[...]
    arrived(re6, G_E6)
    early_out[pl.ds(pl.multiple_of(512 - mine, 512), 512)] = re6[...].reshape(512, LANES)

    for which, g_row, g_pack in ((0, G_ROW0, G_PACK0), (1, G_ROW1, G_PACK1)):
        gone(row_in.at[which], g_row)
        gone(pack_in.at[which], g_pack)
    for n in BACKS:
        gone(d_in.at[n, pl.ds(0, NEAR - 1)], G_D + n)
    gone(rq1.at[pl.ds(0, NEAR - 1)], G_Q1)
    gone(rq2.at[pl.ds(0, FAR - 1)], G_Q2)
    gone(re0, G_E0)
    for ref, g in ((re1, G_E1), (re5, G_E5)):
        gone(ref.at[pl.ds(0, 3)], g)
    for ref, g in ((re2, G_E2), (re3, G_E3)):
        gone(ref.at[pl.ds(0, FAR - 1)], g)
    gone(re6, G_E6)


def finish(rest, gframe, early, tail, value, *refs):
    outs, sem = (refs[:7], refs[7:14]), refs[14]
    restored, grad_frames, grad_w_in_t, grad_grid, grad_block, grad_w_out, grad_conv = outs[1]
    copies = []

    def leave(k, part=None):
        src, dst = outs[1][k], outs[0][k]
        if part is not None:
            src, dst = src.at[part], dst.at[part]
        copies.append(pltpu.make_async_copy(src, dst, sem.at[len(copies)]))
        copies[-1].start()

    def turn_out(src, dst, k):
        for first in range(0, CH, CH // 2):

            def channel(c, carry):
                for t in range(2):
                    dst[first + c, :, half(t)] = src[t, pl.ds(first + c, ROWS, stride=CH), :].astype(BF)
                return carry

            loop(CH // 2, channel, unroll=16)
            leave(k, pl.ds(first, CH // 2))

    scale = float(ROWS * NA * COLS * NW) ** (-0.5)
    for k in range(2):
        grad_grid[:, half(k)] = early[k * COLS : (k + 1) * COLS].astype(F32) * scale
        grad_block[:, half(k)] = early[(2 + k) * COLS : (3 + k) * COLS].astype(F32) * scale
    leave(3)
    leave(4)
    turn_out(gframe, grad_frames, 1)
    turn_out(rest, restored, 0)
    quarter = value[...] * scale
    zeros = jnp.zeros((HC, CH), F32)
    quarter = jnp.concatenate([zeros, quarter[:, :CH], quarter[:, CH:], zeros, zeros], axis=0)
    grad_w_in_t[...] = tail[3 * CH : 4 * CH].astype(F32) * scale + quarter.T
    leave(2)
    last = tail[4 * CH :].astype(F32) * scale
    grad_w_out[...] = last[CH:, CH:]
    leave(5)
    for b in range(3):
        rows = slice((2 - b) * CH, (3 - b) * CH)
        pair = tail[rows].astype(F32) * scale
        grad_conv[0, b] = pair[:, :CH]
        grad_conv[1, b] = pair[:, CH:]
    grad_conv[2, 2] = last[:CH, :CH]
    grad_conv[2, 1] = last[CH:, :CH]
    grad_conv[2, 0] = last[:CH, CH:]
    leave(6)
    for copy in copies:
        copy.wait()


def vm(*shape, dtype=BF):
    return pltpu.VMEM(shape, dtype)


def exchange():
    message_w = vm(4, NEAR, 2, 2, QC, LANES)
    message_a = vm(4, FAR, 16, 256)
    return [message_w, message_w, vm(4, 2 * 16 * QC, LANES, dtype=F32)] + [message_a] * 4 + [message_w] * 2


SCRATCH = [
    vm(CH, ROWS, COLS),
    vm(CH, 2 * CH),
    vm(COLS, COLS),
    vm(COLS, COLS),
    vm(CH, CH),
    vm(3, 3, CH, CH),
    vm(CH, ROWS, COLS),
    vm(2 * CH, CH),
    vm(2, CH * ROWS, LANES, dtype=F32),
    vm(ROWS, CH, COLS),
    vm(ROWS, CH, COLS),
    vm(ROWS, CH, COLS, dtype=F32),
    vm(ROWS, 8, COLS, dtype=F32),
    vm(ROWS, 2 * CH, COLS, dtype=F32),
    vm(ROWS, CH, COLS),
    vm(ROWS, HC, COLS),
    vm(ROWS + 2, 3 * CH, COLS),
    vm(ROWS + 2, 3 * CH, COLS),
    vm(ROWS, CH, COLS),
    vm(ROWS, CH, COLS, dtype=F32),
    vm(ROWS, HC, COLS),
    vm(ROWS, HC, COLS),
    vm(ROWS, HC, COLS),
    vm(ROWS, HC, COLS),
    *exchange(),
    vm(ROWS, CH, COLS),
    vm(ROWS, 2 * CH, COLS),
    vm(ROWS + 4, CH, COLS),
    vm(2, 2, CH, COLS),
    vm(2, 32, LANES),
    vm(2, 96, LANES),
    vm(CH, LANES),
    vm(CH, LANES),
    vm(COLS, COLS),
    vm(COLS, COLS),
    vm(COLS, COLS),
    vm(COLS, COLS),
    vm(4 * COLS, LANES),
    vm(512, LANES),
    vm(512, LANES),
    vm(4, 128, LANES),
    vm(128, LANES, dtype=F32),
    vm(FAR, 8, LANES, dtype=F32),
    vm(8, LANES, dtype=F32),
    vm(FAR, 8, LANES, dtype=F32),
    vm(128, LANES),
    vm(4, 128, LANES),
    vm(4, 128, LANES),
    vm(6 * CH, LANES),
    vm(FAR, 32, LANES),
    vm(32, LANES),
    vm(NEAR, 32, LANES),
    vm(32, LANES),
    vm(12, 32, LANES),
    vm(16, LANES),
    vm(NEAR, 16, LANES),
    vm(16, LANES),
    vm(FAR, 16, LANES),
    pltpu.SemaphoreType.DMA((GROUPS,)),
    pltpu.SemaphoreType.DMA((GROUPS,)),
    pltpu.SemaphoreType.DMA((7,)),
]


def body(frames, w_in, grid_mix, block_mix, w_out, conv_w, cotangent):
    operands = (frames, w_in.T, grid_mix, block_mix, w_out, conv_w, cotangent)
    vmem = pl.BlockSpec(memory_space=pltpu.VMEM)
    shape = jax.ShapeDtypeStruct
    rest, gframe, early, tail, value = pl.pallas_call(
        kernel,
        out_shape=(
            shape((2, ROWS * CH, LANES), F32),
            shape((2, ROWS * CH, LANES), F32),
            shape((4 * COLS, LANES), BF),
            shape((12, 32, LANES), BF),
            shape((16, LANES), F32),
        ),
        in_specs=[pl.BlockSpec(memory_space=pltpu.HBM)] * 7,
        out_specs=(vmem,) * 5,
        scratch_shapes=SCRATCH,
        compiler_params=pltpu.CompilerParams(
            collective_id=0, has_side_effects=True, vmem_limit_bytes=32 * 1024 * 1024
        ),
    )(*[pltpu.with_memory_space_constraint(x, pltpu.HBM) for x in operands])
    restored, grad_frames, grad_w_in_t, grad_grid, grad_block, grad_w_out, grad_conv = pl.pallas_call(
        finish,
        out_shape=(
            shape((CH, ROWS, COLS), BF),
            shape((CH, ROWS, COLS), BF),
            shape((CH, 2 * CH), F32),
            shape((COLS, COLS), F32),
            shape((COLS, COLS), F32),
            shape((CH, CH), F32),
            shape((3, 3, CH, CH), F32),
        ),
        in_specs=[vmem] * 5,
        out_specs=(pl.BlockSpec(memory_space=pl.ANY),) * 7,
        scratch_shapes=[
            vm(CH, ROWS, COLS),
            vm(CH, ROWS, COLS),
            vm(CH, 2 * CH, dtype=F32),
            vm(COLS, COLS, dtype=F32),
            vm(COLS, COLS, dtype=F32),
            vm(CH, CH, dtype=F32),
            vm(3, 3, CH, CH, dtype=F32),
            pltpu.SemaphoreType.DMA((9,)),
        ],
        compiler_params=pltpu.CompilerParams(vmem_limit_bytes=16 * 1024 * 1024),
    )(rest, gframe, early, tail.reshape(6 * CH, LANES), value)
    return restored, grad_frames, grad_w_in_t.T, grad_grid, grad_block, grad_w_out, grad_conv


def solution(mesh):
    placed = (P(None, "ha", "wa"), P(), P(), P(), P(), P(), P(None, "ha", "wa"))
    return jax.shard_map(
        body,
        mesh=mesh,
        in_specs=placed,
        out_specs=(P(None, "ha", "wa"), P(None, "ha", "wa"), P(), P(), P(), P(), P()),
        check_vma=False,
    )
```

```python
import jax
import jax.numpy as jnp
from jax import lax
from jax.experimental import pallas as pl
from jax.experimental.pallas import tpu as pltpu
from jax.sharding import PartitionSpec as P

BF = jnp.bfloat16
F32 = jnp.float32
EPS = 1e-06
MESH = pl.DeviceIdType.MESH

CH = 64
HC = 32
ROWS = 16
COLS = 256
LANES = 128
NA = 16
NW = 8
NEAR = 8
FAR = 16

(G_ROW0, G_PACK0, G_ROW1, G_PACK1) = range(4)
(G_E0, G_E1, G_E2, G_E3, G_E5, G_E6, G_T1, G_T2, G_T3, G_Q1, G_Q2) = range(4, 15)
VALUES, BACKS = (0, 1), (2, 3)
G_A, G_B, G_C, G_D = 16, 20, 24, 28
GROUPS = 32
QC = 16


def dot(a, b):
    return lax.dot_general(a, b, (((1,), (0,)), ((), ())), preferred_element_type=F32)


def dot_nt(a, b):
    return lax.dot_general(a, b, (((1,), (1,)), ((), ())), preferred_element_type=F32)


def dot_tn(a, b):
    return lax.dot_general(a, b, (((0,), (0,)), ((), ())), preferred_element_type=F32)


def swap_granules(load, store, depth):
    lane = lax.broadcasted_iota(jnp.int16, (depth, LANES), 1)
    for row_half in range(2):
        for col_half in range(2):
            held = [load(row_half * 8 + k, col_half) for k in range(8)]
            for s in range(3):
                width = 16 << s
                low = (lane & width) == 0
                for k in range(8):
                    if not k & (1 << s):
                        a, b = held[k], held[k | (1 << s)]
                        held[k] = jnp.where(low, a, pltpu.roll(b, width, 1))
                        held[k | (1 << s)] = jnp.where(low, pltpu.roll(a, LANES - width, 1), b)
            for k in range(8):
                store(col_half * 8 + k, row_half, held[k])


def half(t):
    return slice(t * LANES, (t + 1) * LANES)


def loop(count, step, carry=0, unroll=1):
    return lax.fori_loop(0, count, step, carry, unroll=unroll)


def gelu_parts(x):
    root = 0.7978845608028654
    cube = root * 0.044715
    square = x * x
    h = 0.5 * jnp.tanh(x * (cube * square + root)) + 0.5
    value = x * h
    return value, h + value * (1.0 - h) * ((6.0 * cube) * square + 2.0 * root)


def kernel(
    frames_hbm, w_in_t_hbm, grid_mix_hbm, block_mix_hbm, w_out_hbm, conv_w_hbm, cot_hbm,
    rest_out, gframe_out, early_out, tail_out, value_out,
    frames, w_in_t, grid_mix, block_mix, w_out, conv_w, cot, w_in,
    turn, xb, nb, unit, inv, dgelu, gates, bval, u3, v3, gj, gg, xt, bt, bm, gbv,
    a, a_in, x32, b, b_in, c, c_in, d, d_in,
    gated, gbef, jp, row_in, pack_out, pack_in, edge_l, edge_r,
    mixp, mixp_t, gather, spread, se, re0, e0, re1, e1, re2, e2, re3, e3, re5, re6,
    st, rt1, t1, rt2, t2, rt3, sq, rq1, q1, rq2,
    ssem, rsem, isem,
):
    ia = lax.axis_index("ha")
    iw = lax.axis_index("wa")
    up, down = lax.rem(ia + NA - 1, NA), lax.rem(ia + 1, NA)
    left, right = lax.rem(iw + NW - 1, NW), lax.rem(iw + 1, NW)
    lane = lax.broadcasted_iota(jnp.int16, (CH, LANES), 1)
    lane_wide = lax.broadcasted_iota(jnp.int32, (CH, LANES), 1)

    loads = [
        pltpu.make_async_copy(src, dst, isem.at[k])
        for k, (src, dst) in enumerate(
            [
                (frames_hbm, frames),
                (w_in_t_hbm, w_in_t),
                (cot_hbm, cot),
                (conv_w_hbm, conv_w),
                (w_out_hbm, w_out),
                (block_mix_hbm, block_mix),
                (grid_mix_hbm, grid_mix),
            ]
        )
    ]
    for load in loads:
        load.start()

    def push(src, dst, g, where):
        pltpu.make_async_remote_copy(
            src_ref=src, dst_ref=dst, send_sem=ssem.at[g], recv_sem=rsem.at[g], device_id=where, device_id_type=MESH
        ).start()

    near = lax.rem(iw, 2) * 4 + lax.rem(ia, 4)
    far = ia // 4 * 4 + iw // 2

    def near_device(peer):
        return ia // 4 * 4 + lax.rem(peer, 4), iw // 2 * 2 + peer // 4

    def far_device(peer):
        return peer // 4 * 4 + lax.rem(ia, 4), lax.rem(peer, 4) * 2 + lax.rem(iw, 2)

    near_peers = [lax.rem(near + k, NEAR) for k in range(1, NEAR)]
    far_peers = [lax.rem(far + k, FAR) for k in range(1, FAR)]
    twin = near + 1 - 2 * lax.rem(near, 2)

    near_places = [near_device(peer) for peer in near_peers]
    far_places = [far_device(peer) for peer in far_peers]

    def over_near(src_of, dst, g):
        for peer, place in zip(near_peers, near_places):
            push(src_of(peer), dst, g, place)

    def over_far(src_of, dst, g):
        for peer, place in zip(far_peers, far_places):
            push(src_of(peer), dst, g, place)

    def over_y(src_of, dst, g):
        for k in range(1, 4):
            peer = lax.rem(near + 2 * k, NEAR)
            push(src_of(peer // 2), dst, g, near_device(peer))

    def arrived(ref, g):
        pltpu.make_async_copy(ref, ref, rsem.at[g]).wait()

    def gone(ref, g):
        pltpu.make_async_copy(ref, ref, ssem.at[g]).wait()

    def from_near(ref, g):
        arrived(ref.at[pl.ds(0, NEAR - 1)], g)

    def from_far(ref, g):
        arrived(ref.at[pl.ds(0, FAR - 1)], g)

    mine = lax.rem(near, 2) * 512
    level = near // 2

    barrier = pltpu.get_barrier_semaphore()
    peers = [near_device(peer) for peer in near_peers]
    peers += [far_device(peer) for peer in far_peers]
    peers += [(a, b) for a in (up, ia, down) for b in (left, right)] + [(up, iw), (down, iw)]
    for peer in peers:
        pl.semaphore_signal(barrier, inc=1, device_id=peer, device_id_type=MESH)

    def turn_in(src):
        for t in range(2):
            turn[t] = src[:, :, half(t)].astype(F32).reshape(CH * ROWS, LANES)

    def turned(r, t):
        return turn[t, pl.ds(r, CH, stride=ROWS), :]

    def edges(pack, t0, t1, r):
        pack = jnp.where(lane_wide == r, pltpu.roll(t0, r, 1), pack)
        return jnp.where(lane_wide == ROWS + r, pltpu.roll(t1, r + 17, 1), pack)

    def send_halo(field, pack, which, g_row, g_pack):
        pack_out[which] = jnp.concatenate([pack, jnp.zeros_like(pack)], axis=0).T[0:32]
        push(field.at[1, CH : 2 * CH], row_in.at[which, 1], g_row, (up, iw))
        push(field.at[ROWS, CH : 2 * CH], row_in.at[which, 0], g_row, (down, iw))
        for slot, where in enumerate(
            [(ia, right), (down, right), (up, right), (ia, left), (down, left), (up, left)]
        ):
            part = pack_out.at[which, pl.ds(16 if slot < 3 else 0, 16)]
            push(part, pack_in.at[which, pl.ds(16 * slot, 16)], g_pack, where)

    def take_halo(field, which, g_row, g_pack):
        arrived(row_in.at[which], g_row)
        arrived(pack_in.at[which], g_pack)
        field[0, CH : 2 * CH] = jnp.where(ia > 0, row_in[which, 0], jnp.zeros((CH, COLS), BF))
        field[ROWS + 1, CH : 2 * CH] = jnp.where(ia < NA - 1, row_in[which, 1], jnp.zeros((CH, COLS), BF))
        first = jnp.where(ia > 0, 0, 1)
        last = jnp.where(ia < NA - 1, ROWS + 2, ROWS + 1)
        got = jnp.concatenate([pack_in[which], jnp.zeros((32, LANES), BF)], axis=0).T[0:CH]

        def assemble(middle, above, below, has):
            joined = jnp.where(lane == 0, above, jnp.where(lane == ROWS + 1, below, middle))
            inside = (lane_wide >= first) & (lane_wide < jnp.where(has, last, 0))
            return jnp.where(inside, joined, jnp.zeros_like(joined))

        edge_l[...] = assemble(pltpu.roll(got, 1, 1), pltpu.roll(got, 97, 1), pltpu.roll(got, 113, 1), iw > 0)
        edge_r[...] = assemble(pltpu.roll(got, 81, 1), pltpu.roll(got, 49, 1), pltpu.roll(got, 65, 1), iw < NW - 1)

        def shifts(p, carry):
            t0 = field[p, CH : 2 * CH, half(0)]
            t1 = field[p, CH : 2 * CH, half(1)]
            a0, a1 = pltpu.roll(t0, 1, 1), pltpu.roll(t1, 1, 1)
            b0, b1 = pltpu.roll(t0, LANES - 1, 1), pltpu.roll(t1, LANES - 1, 1)
            lh = pltpu.roll(edge_l[...], lax.rem(LANES - p, LANES), 1)
            rh = pltpu.roll(edge_r[...], LANES - 1 - p, 1)
            field[p, 0:CH, half(0)] = jnp.where(lane == 0, lh, a0)
            field[p, 0:CH, half(1)] = jnp.where(lane == 0, a0, a1)
            field[p, 2 * CH :, half(0)] = jnp.where(lane == LANES - 1, b1, b0)
            field[p, 2 * CH :, half(1)] = jnp.where(lane == LANES - 1, rh, b1)
            return carry

        loop(ROWS + 2, shifts, unroll=9)

    def conv_start(w, field):
        y = dot(w, field[0])
        z = dot(w, field[1])
        return z[0:CH], y[0:CH] + z[CH : 2 * CH]

    def conv_step(w, field, r, carry):
        later, now = carry
        y = dot(w, field[r + 2])
        return now + y[2 * CH :], (y[0:CH], later + y[CH : 2 * CH])

    def step_a(n):
        over_near(lambda peer: a.at[n, peer], a_in.at[n, near], G_A + n)

    def step_b(n):
        arrived(a_in.at[n, pl.ds(0, NEAR - 1)], G_A + n)

        def widen(j, carry):
            for t in range(2):
                for r in range(2):
                    x32[n, pl.ds((r * 16 + j * 2 + t) * QC, QC), :] = a_in[n, j, t, r].astype(F32)
            return carry

        loop(NEAR, widen, unroll=8)

        for peer, place in zip([*far_peers, far], [*far_places, None]):
            base = peer // 8 * (16 * QC) + lax.rem(peer, 8) * 2
            slot = b_in if peer is far else b
            for k in range(2):
                slot[n, peer, :, half(k)] = x32[n, pl.ds(base + k, 16, stride=QC), :].astype(BF)
            if peer is not far:
                push(b.at[n, peer], b_in.at[n, far], G_B + n, place)

    def table(n):
        return b_in[n].reshape(256, 256)

    def step_c(n, mix):
        arrived(b_in.at[n, pl.ds(0, FAR - 1)], G_B + n)
        c[n] = dot(mix[...], table(n)).astype(BF).reshape(FAR, 16, 256)
        over_far(lambda peer: c.at[n, peer], c_in.at[n, far], G_C + n)
        c_in[n, far] = c[n, far]

    def step_d(n):
        arrived(c_in.at[n, pl.ds(0, FAR - 1)], G_C + n)

        def unpick(q, carry):
            for r in range(2):
                for k in range(2):
                    x32[n, pl.ds((r * QC + q * 2 + k) * 16, 16), :] = c_in[n, r * 8 + q, :, half(k)].astype(F32)
            return carry

        loop(8, unpick, unroll=8)

        for peer, place in zip([*near_peers, near], [*near_places, None]):
            slot = d_in if peer is near else d
            for t in range(2):
                for r in range(2):
                    slot[n, peer, t, r] = x32[n, pl.ds(r * QC * 16 + peer * 2 + t, QC, stride=16), :].astype(BF)
            if peer is not near:
                push(d.at[n, peer], d_in.at[n, near], G_D + n, place)

    def step_e(n):
        arrived(d_in.at[n, pl.ds(0, NEAR - 1)], G_D + n)

    def order(cell, row):
        found = (row & 0xC1) | ((row & 6) << 3) | ((row & 48) >> 2) | ((row & 8) >> 2)
        return jnp.where(cell == found, 1.0, 0.0).astype(BF)

    loads[0].wait()
    loads[1].wait()
    turn_in(frames)
    w_in[...] = w_in_t[...].astype(F32).T.astype(BF)

    def value_row(slot, peer, low):
        r = peer * 2 + low
        normed = []
        for t in range(2):
            x = turned(r, t)
            xb[r, :, half(t)] = x.astype(BF)
            off = x - jnp.mean(x, axis=0, keepdims=True)
            rstd = lax.rsqrt(jnp.mean(off * off, axis=0, keepdims=True) + EPS)
            u = off * rstd
            unit[r, :, half(t)] = u
            inv[r, :, half(t)] = jnp.broadcast_to(rstd, (8, LANES))
            normed.append(u.astype(BF))
        normed = jnp.concatenate(normed, axis=1)
        nb[r] = normed
        value, slope = gelu_parts(dot(w_in[HC:CH], normed))
        dgelu[r, HC:CH] = slope
        value = value.astype(BF)
        for n in VALUES:
            for t in range(2):
                slot[n, peer, t, low] = value[n * QC : (n + 1) * QC, half(t)]

    for first in range(0, NEAR, 4):
        group = [*near_peers, near][first : first + 4]
        for peer in group:
            for low in range(2):
                value_row(a_in if peer is near else a, peer, low)
        if first == 0:
            pl.semaphore_wait(barrier, len(peers))
        for peer in group:
            if peer is not near:
                push(a.at[0, peer], a_in.at[0, near], G_A, near_device(peer))
    step_a(1)

    loads[2].wait()
    turn_in(cot)

    def cot_row(r, pack):
        t0, t1 = turned(r, 0).astype(BF), turned(r, 1).astype(BF)
        u3[r + 1, CH : 2 * CH, half(0)] = t0
        u3[r + 1, CH : 2 * CH, half(1)] = t1
        return edges(pack, t0, t1, r)

    pack = loop(ROWS, cot_row, jnp.zeros((CH, LANES), BF), unroll=16)
    send_halo(u3, pack, 0, G_ROW0, G_PACK0)

    w_rest = jnp.concatenate([w_in[0:HC], w_in[CH:]], axis=0)

    def gate_row(r, carry):
        before = dot(w_rest, nb[r])
        value, slope = gelu_parts(before[0:HC])
        gates[r, 0:HC] = value.astype(BF)
        dgelu[r, 0:HC] = slope
        value, slope = gelu_parts(before[HC:])
        dgelu[r, CH:] = slope
        value = value.astype(BF)
        gates[r, HC:CH] = value[0:HC]
        bval[r] = value[HC:]
        return carry

    loop(ROWS, gate_row, unroll=8)
    for load in loads[3:]:
        load.wait()
    down_axis = lax.broadcasted_iota(jnp.int32, (COLS, COLS), 0)
    along_axis = lax.broadcasted_iota(jnp.int32, (COLS, COLS), 1)
    gather[...] = order(along_axis, down_axis)
    spread[...] = order(down_axis, along_axis)
    mixp[...] = dot(dot(gather[...], grid_mix[...]).astype(BF), spread[...]).astype(BF)
    mixp_t[...] = mixp[...].T

    back_w = jnp.concatenate(
        [jnp.concatenate([conv_w[2 - a, 2 - b] for a in range(3)], axis=1) for b in range(3)], axis=0
    ).astype(F32).T.astype(BF)
    w_out_t = w_out[...].astype(F32).T.astype(BF)
    take_halo(u3, 0, G_ROW0, G_PACK0)

    def back_row(r, carry):
        total, carry = conv_step(back_w, u3, r, carry)
        g = (total + u3[r + 1, CH : 2 * CH].astype(F32)).astype(BF)
        gj[r] = g
        up_gated = dot(w_out_t, g)
        gg[r] = up_gated
        mixed = (up_gated[0:HC] * gates[r, 0:HC].astype(F32)).astype(BF)
        for n in range(2):
            for t in range(2):
                a[2 + n, r // 2, t, r % 2] = mixed[n * QC : (n + 1) * QC, half(t)]
        return carry

    step_b(0)
    carry = conv_start(back_w, u3)
    for first in range(0, NEAR, 4):
        if first:
            step_b(1)
        for r in range(2 * first, 2 * first + 8):
            carry = back_row(r, carry)
        for peer in range(first, first + 4):

            @pl.when(peer != near)
            def _():
                push(a.at[2, peer], a_in.at[2, near], G_A + 2, near_device(peer))

    step_a(3)
    for n in BACKS:
        a_in[n, near] = a[n, near]


    def put(ref):
        def store(k, t, value):
            ref[k, :, half(t)] = value

        return store

    swap_granules(lambda k, t: bval[k, :, half(t)], put(xt), HC)
    values = xt[...].reshape(ROWS * HC, COLS)
    mixed = dot_nt(values, block_mix[...]).astype(BF)
    swap_granules(lambda k, t: mixed[k * HC : (k + 1) * HC, half(t)], put(bm), HC)

    step_c(0, mixp)

    def block_back(k, t):
        return (gg[k, HC:, half(t)] * gates[k, HC:, half(t)].astype(F32)).astype(BF)

    swap_granules(block_back, put(bt), HC)
    backs = bt[...].reshape(ROWS * HC, COLS)
    unmixed = dot(backs, block_mix[...]).astype(BF)
    swap_granules(lambda k, t: unmixed[k * HC : (k + 1) * HC, half(t)], put(gbv), HC)

    step_c(1, mixp)
    step_b(2)

    part_block = dot_tn(backs, values).astype(BF)
    se[2 * COLS : 3 * COLS] = part_block[:, half(0)]
    se[3 * COLS :] = part_block[:, half(1)]

    step_b(3)

    def block_before_row(r, carry):
        d = dgelu[r, CH:]
        gbef[r, CH : CH + HC] = (d[0:HC] * (gg[r, HC:] * (bm[r].astype(F32) + 1.0))).astype(BF)
        gbef[r, CH + HC :] = (d[HC:] * gbv[r].astype(F32)).astype(BF)
        gbef[r, HC:CH] = jnp.zeros((HC, COLS), BF)
        return carry

    loop(ROWS, block_before_row, unroll=8)
    for k in (0, 1, ROWS + 2, ROWS + 3):
        jp[k] = jnp.zeros((CH, COLS), BF)

    step_d(0)
    step_d(1)
    step_c(2, mixp_t)
    step_c(3, mixp_t)

    part_grid = (dot_nt(table(2), table(0)) + dot_nt(table(3), table(1))).astype(BF)
    part_grid = dot(dot(spread[...], part_grid).astype(BF), gather[...]).astype(BF)
    se[0:COLS] = part_grid[:, half(0)]
    se[COLS : 2 * COLS] = part_grid[:, half(1)]
    push(se.at[pl.ds(pl.multiple_of(512 - mine, 512), 512)], re0, G_E0, near_device(twin))

    arrived(re0, G_E0)
    e0[...] = (se[pl.ds(pl.multiple_of(mine, 512), 512)].astype(F32) + re0[...].astype(F32)).astype(BF)
    over_y(lambda peer: e0.at[pl.ds(pl.multiple_of(peer * 128, 128), 128)], re1.at[level], G_E1)
    re1[level] = e0[pl.ds(pl.multiple_of(level * 128, 128), 128)]

    step_e(0)
    step_e(1)

    def returned(chains, r):
        return [
            jnp.concatenate([d_in[n, r // 2, t, lax.rem(r, 2)] for n in chains], axis=0).astype(F32) for t in range(2)
        ]

    def joined_row(r, pack):
        grid_mixed = returned(VALUES, r)
        for t in range(2):
            gates_t = gates[r, :, half(t)].astype(F32)
            more = grid_mixed[t] + 1.0
            gated[r, 0:HC, half(t)] = (gates_t[0:HC] * more).astype(BF)
            gated[r, HC:, half(t)] = (gates_t[HC:] * (bm[r, :, half(t)].astype(F32) + 1.0)).astype(BF)
            gbef[r, 0:HC, half(t)] = (dgelu[r, 0:HC, half(t)] * (gg[r, 0:HC, half(t)] * more)).astype(BF)
        j = (xb[r].astype(F32) + dot(w_out[...], gated[r])).astype(BF)
        jp[r + 2] = j
        v3[r + 1, CH : 2 * CH] = j
        return edges(pack, j[:, half(0)], j[:, half(1)], r)

    pack = loop(ROWS, joined_row, jnp.zeros((CH, LANES), BF), unroll=16)
    send_halo(v3, pack, 1, G_ROW1, G_PACK1)

    step_d(2)
    step_d(3)

    def pixels(ref, rows=slice(None)):
        return jnp.concatenate([ref[r, rows] for r in range(ROWS)], axis=1)

    p_conv = dot_nt(
        jnp.concatenate([u3[p] for p in range(ROWS + 2)], axis=1),
        jnp.concatenate([jp[p : p + 3].reshape(3 * CH, COLS) for p in range(ROWS + 2)], axis=1),
    )
    arrived(re1.at[pl.ds(0, 3)], G_E1)
    total = re1[0].astype(F32)
    for k in range(1, 4):
        total = total + re1[k].astype(F32)
    e1[...] = total
    over_far(lambda peer: e1.at[pl.ds(pl.multiple_of(peer * 8, 8), 8)], re2.at[far], G_E2)
    re2[far] = e1[pl.ds(pl.multiple_of(far * 8, 8), 8)]

    p_in = dot_nt(pixels(nb), pixels(gbef))
    p_out = dot_nt(pixels(gj), pixels(gated))
    st[0 : 3 * CH] = p_conv[:, half(0)].astype(BF)
    st[3 * CH : 4 * CH] = p_in.astype(BF)
    third = p_conv[:, 2 * CH :]
    st[4 * CH :] = jnp.concatenate(
        [third[: 2 * CH], jnp.concatenate([third[2 * CH :], p_out], axis=0)], axis=1
    ).astype(BF)
    summing = far < 12
    for peer, place in zip(far_peers, far_places):

        @pl.when(peer < 12)
        def _():
            push(st.at[pl.ds(pl.multiple_of(peer * 32, 32), 32)], rt1.at[far], G_T1, place)

    @pl.when(summing)
    def _():
        rt1[far] = st[pl.ds(pl.multiple_of(far * 32, 32), 32)]

    take_halo(v3, 1, G_ROW1, G_PACK1)

    conv_k = jnp.concatenate(
        [jnp.concatenate([conv_w[a, b] for b in range(3)], axis=1) for a in range(3)], axis=0
    )

    def out_row(r, carry):
        total, carry = conv_step(conv_k, v3, r, carry)
        total = total + v3[r + 1, CH : 2 * CH].astype(F32)
        for t in range(2):
            rest_out[t, pl.ds(r, CH, stride=ROWS), :] = total[:, half(t)]
        return carry

    carry = loop(ROWS // 2, out_row, conv_start(conv_k, v3), unroll=8)

    from_far(re2, G_E2)
    total = re2[0]
    for k in range(1, FAR):
        total = total + re2[k]
    e2[...] = total
    over_far(lambda peer: e2, re3.at[far], G_E3)
    re3[far] = e2[...]

    step_e(2)
    step_e(3)

    def value_before_row(r, carry):
        grid_back = returned(BACKS, r)
        for t in range(2):
            gbef[r, HC:CH, half(t)] = (dgelu[r, HC:CH, half(t)] * grid_back[t]).astype(BF)
        return carry

    loop(ROWS, value_before_row, unroll=8)
    p_value = dot_nt(pixels(gbef, slice(HC, CH)), pixels(nb))
    sq[...] = jnp.concatenate([p_value[0:16], p_value[16:]], axis=1).astype(BF)
    over_near(lambda peer: sq, rq1.at[near], G_Q1)
    rq1[near] = sq[...]

    for n in VALUES + BACKS:
        for ref, count, g in ((a_in, NEAR, G_A), (b_in, FAR, G_B), (c_in, FAR, G_C)):
            gone(ref.at[n, pl.ds(0, count - 1)], g + n)
    for n in VALUES:
        gone(d_in.at[n, pl.ds(0, NEAR - 1)], G_D + n)

    @pl.when(summing)
    def _():
        from_far(rt1, G_T1)
        total = rt1[0].astype(F32)
        for k in range(1, FAR):
            total = total + rt1[k].astype(F32)
        t1[...] = total.astype(BF)
        over_near(lambda peer: t1, rt2.at[near], G_T2)
        rt2[near] = t1[...]

    from_far(re3, G_E3)
    e3[...] = re3[...].reshape(128, LANES).astype(BF)
    over_y(lambda peer: e3, re5.at[level], G_E5)
    re5[level] = e3[...]

    def frame_row(r, carry):
        normed = dot(w_in_t[...], gbef[r])
        u = unit[r]
        mean_grad = jnp.mean(normed, axis=0, keepdims=True)
        mean_proj = jnp.mean(normed * u, axis=0, keepdims=True)
        source = gj[r].astype(F32) + inv[r, 0:1] * (normed - mean_grad - u * mean_proj)
        for t in range(2):
            gframe_out[t, pl.ds(r, CH, stride=ROWS), :] = source[:, half(t)]
        return carry

    loop(ROWS, frame_row, unroll=16)

    from_near(rq1, G_Q1)
    total = rq1[0].astype(F32)
    for k in range(1, NEAR):
        total = total + rq1[k].astype(F32)
    q1[...] = total.astype(BF)
    over_far(lambda peer: q1, rq2.at[far], G_Q2)
    rq2[far] = q1[...]

    @pl.when(summing)
    def _():
        from_near(rt2, G_T2)
        total = rt2[0].astype(F32)
        for k in range(1, NEAR):
            total = total + rt2[k].astype(F32)
        t2[...] = total.astype(BF)
        over_far(lambda peer: t2, rt3.at[far], G_T3)
        rt3[far] = t2[...]

    loop(ROWS // 2, lambda r, carry: out_row(r + ROWS // 2, carry), carry, unroll=8)

    from_far(rq2, G_Q2)
    total = rq2[0].astype(F32)
    for k in range(1, FAR):
        total = total + rq2[k].astype(F32)
    value_out[...] = total

    arrived(re5.at[pl.ds(0, 3)], G_E5)
    push(re5, re6, G_E6, near_device(twin))
    early_out[pl.ds(pl.multiple_of(mine, 512), 512)] = re5[...].reshape(512, LANES)

    @pl.when(summing)
    def _():
        arrived(rt3.at[pl.ds(0, 11)], G_T3)
        gone(rt1.at[pl.ds(0, 11)], G_T1)
        gone(rt2.at[pl.ds(0, NEAR - 1)], G_T2)
        gone(rt1.at[pl.ds(0, FAR - 1)], G_T3)

    @pl.when(far >= 12)
    def _():
        arrived(rt3, G_T3)
        gone(rt1.at[pl.ds(0, 12)], G_T1)

    tail_out[...] = rt3[...]
    arrived(re6, G_E6)
    early_out[pl.ds(pl.multiple_of(512 - mine, 512), 512)] = re6[...].reshape(512, LANES)

    for which, g_row, g_pack in ((0, G_ROW0, G_PACK0), (1, G_ROW1, G_PACK1)):
        gone(row_in.at[which], g_row)
        gone(pack_in.at[which], g_pack)
    for n in BACKS:
        gone(d_in.at[n, pl.ds(0, NEAR - 1)], G_D + n)
    gone(rq1.at[pl.ds(0, NEAR - 1)], G_Q1)
    gone(rq2.at[pl.ds(0, FAR - 1)], G_Q2)
    gone(re0, G_E0)
    for ref, g in ((re1, G_E1), (re5, G_E5)):
        gone(ref.at[pl.ds(0, 3)], g)
    for ref, g in ((re2, G_E2), (re3, G_E3)):
        gone(ref.at[pl.ds(0, FAR - 1)], g)
    gone(re6, G_E6)


def finish(rest, gframe, early, tail, value, *refs):
    outs, sem = (refs[:7], refs[7:14]), refs[14]
    restored, grad_frames, grad_w_in_t, grad_grid, grad_block, grad_w_out, grad_conv = outs[1]
    copies = []

    def leave(k, part=None):
        src, dst = outs[1][k], outs[0][k]
        if part is not None:
            src, dst = src.at[part], dst.at[part]
        copies.append(pltpu.make_async_copy(src, dst, sem.at[len(copies)]))
        copies[-1].start()

    def turn_out(src, dst, k):
        for first in range(0, CH, CH // 2):

            part = pl.ds(first * ROWS, CH // 2 * ROWS)
            for t in range(2):
                dst[first : first + CH // 2, :, half(t)] = src[t, part, :].astype(BF).reshape(CH // 2, ROWS, LANES)
            leave(k, pl.ds(first, CH // 2))

    scale = float(ROWS * NA * COLS * NW) ** (-0.5)
    for k in range(2):
        grad_grid[:, half(k)] = early[k * COLS : (k + 1) * COLS].astype(F32) * scale
        grad_block[:, half(k)] = early[(2 + k) * COLS : (3 + k) * COLS].astype(F32) * scale
    leave(3)
    leave(4)
    turn_out(gframe, grad_frames, 1)
    turn_out(rest, restored, 0)
    quarter = value[...] * scale
    zeros = jnp.zeros((HC, CH), F32)
    quarter = jnp.concatenate([zeros, quarter[:, :CH], quarter[:, CH:], zeros, zeros], axis=0)
    grad_w_in_t[...] = tail[3 * CH : 4 * CH].astype(F32) * scale + quarter.T
    leave(2)
    last = tail[4 * CH :].astype(F32) * scale
    grad_w_out[...] = last[CH:, CH:]
    leave(5)
    for b in range(3):
        rows = slice((2 - b) * CH, (3 - b) * CH)
        pair = tail[rows].astype(F32) * scale
        grad_conv[0, b] = pair[:, :CH]
        grad_conv[1, b] = pair[:, CH:]
    grad_conv[2, 2] = last[:CH, :CH]
    grad_conv[2, 1] = last[CH:, :CH]
    grad_conv[2, 0] = last[:CH, CH:]
    leave(6)
    for copy in copies:
        copy.wait()


def vm(*shape, dtype=BF):
    return pltpu.VMEM(shape, dtype)


def exchange():
    message_w = vm(4, NEAR, 2, 2, QC, LANES)
    message_a = vm(4, FAR, 16, 256)
    return [message_w, message_w, vm(4, 2 * 16 * QC, LANES, dtype=F32)] + [message_a] * 4 + [message_w] * 2


SCRATCH = [
    vm(CH, ROWS, COLS),
    vm(CH, 2 * CH),
    vm(COLS, COLS),
    vm(COLS, COLS),
    vm(CH, CH),
    vm(3, 3, CH, CH),
    vm(CH, ROWS, COLS),
    vm(2 * CH, CH),
    vm(2, CH * ROWS, LANES, dtype=F32),
    vm(ROWS, CH, COLS),
    vm(ROWS, CH, COLS),
    vm(ROWS, CH, COLS, dtype=F32),
    vm(ROWS, 8, COLS, dtype=F32),
    vm(ROWS, 2 * CH, COLS, dtype=F32),
    vm(ROWS, CH, COLS),
    vm(ROWS, HC, COLS),
    vm(ROWS + 2, 3 * CH, COLS),
    vm(ROWS + 2, 3 * CH, COLS),
    vm(ROWS, CH, COLS),
    vm(ROWS, CH, COLS, dtype=F32),
    vm(ROWS, HC, COLS),
    vm(ROWS, HC, COLS),
    vm(ROWS, HC, COLS),
    vm(ROWS, HC, COLS),
    *exchange(),
    vm(ROWS, CH, COLS),
    vm(ROWS, 2 * CH, COLS),
    vm(ROWS + 4, CH, COLS),
    vm(2, 2, CH, COLS),
    vm(2, 32, LANES),
    vm(2, 96, LANES),
    vm(CH, LANES),
    vm(CH, LANES),
    vm(COLS, COLS),
    vm(COLS, COLS),
    vm(COLS, COLS),
    vm(COLS, COLS),
    vm(4 * COLS, LANES),
    vm(512, LANES),
    vm(512, LANES),
    vm(4, 128, LANES),
    vm(128, LANES, dtype=F32),
    vm(FAR, 8, LANES, dtype=F32),
    vm(8, LANES, dtype=F32),
    vm(FAR, 8, LANES, dtype=F32),
    vm(128, LANES),
    vm(4, 128, LANES),
    vm(4, 128, LANES),
    vm(6 * CH, LANES),
    vm(FAR, 32, LANES),
    vm(32, LANES),
    vm(NEAR, 32, LANES),
    vm(32, LANES),
    vm(12, 32, LANES),
    vm(16, LANES),
    vm(NEAR, 16, LANES),
    vm(16, LANES),
    vm(FAR, 16, LANES),
    pltpu.SemaphoreType.DMA((GROUPS,)),
    pltpu.SemaphoreType.DMA((GROUPS,)),
    pltpu.SemaphoreType.DMA((7,)),
]


def body(frames, w_in, grid_mix, block_mix, w_out, conv_w, cotangent):
    operands = (frames, w_in.T, grid_mix, block_mix, w_out, conv_w, cotangent)
    vmem = pl.BlockSpec(memory_space=pltpu.VMEM)
    shape = jax.ShapeDtypeStruct
    rest, gframe, early, tail, value = pl.pallas_call(
        kernel,
        out_shape=(
            shape((2, ROWS * CH, LANES), F32),
            shape((2, ROWS * CH, LANES), F32),
            shape((4 * COLS, LANES), BF),
            shape((12, 32, LANES), BF),
            shape((16, LANES), F32),
        ),
        in_specs=[pl.BlockSpec(memory_space=pltpu.HBM)] * 7,
        out_specs=(vmem,) * 5,
        scratch_shapes=SCRATCH,
        compiler_params=pltpu.CompilerParams(
            collective_id=0, has_side_effects=True, vmem_limit_bytes=32 * 1024 * 1024
        ),
    )(*[pltpu.with_memory_space_constraint(x, pltpu.HBM) for x in operands])
    restored, grad_frames, grad_w_in_t, grad_grid, grad_block, grad_w_out, grad_conv = pl.pallas_call(
        finish,
        out_shape=(
            shape((CH, ROWS, COLS), BF),
            shape((CH, ROWS, COLS), BF),
            shape((CH, 2 * CH), F32),
            shape((COLS, COLS), F32),
            shape((COLS, COLS), F32),
            shape((CH, CH), F32),
            shape((3, 3, CH, CH), F32),
        ),
        in_specs=[vmem] * 5,
        out_specs=(pl.BlockSpec(memory_space=pl.ANY),) * 7,
        scratch_shapes=[
            vm(CH, ROWS, COLS),
            vm(CH, ROWS, COLS),
            vm(CH, 2 * CH, dtype=F32),
            vm(COLS, COLS, dtype=F32),
            vm(COLS, COLS, dtype=F32),
            vm(CH, CH, dtype=F32),
            vm(3, 3, CH, CH, dtype=F32),
            pltpu.SemaphoreType.DMA((9,)),
        ],
        compiler_params=pltpu.CompilerParams(vmem_limit_bytes=16 * 1024 * 1024),
    )(rest, gframe, early, tail.reshape(6 * CH, LANES), value)
    return restored, grad_frames, grad_w_in_t.T, grad_grid, grad_block, grad_w_out, grad_conv


def solution(mesh):
    placed = (P(None, "ha", "wa"), P(), P(), P(), P(), P(), P(None, "ha", "wa"))
    return jax.shard_map(
        body,
        mesh=mesh,
        in_specs=placed,
        out_specs=(P(None, "ha", "wa"), P(None, "ha", "wa"), P(), P(), P(), P(), P()),
        check_vma=False,
    )
```

```python
import jax
import jax.numpy as jnp
from jax import lax
from jax.experimental import pallas as pl
from jax.experimental.pallas import tpu as pltpu
from jax.sharding import PartitionSpec as P

BF = jnp.bfloat16
F32 = jnp.float32
EPS = 1e-06
MESH = pl.DeviceIdType.MESH

CH = 64
HC = 32
ROWS = 16
COLS = 256
LANES = 128
NA = 16
NW = 8
NEAR = 8
FAR = 16

(G_ROW0, G_PACK0, G_ROW1, G_PACK1) = range(4)
(G_E0, G_E1, G_E2, G_E3, G_E5, G_E6, G_T1, G_T2, G_T3, G_Q1, G_Q2) = range(4, 15)
VALUES, BACKS = (0, 1), (2, 3)
G_A, G_B, G_C, G_D = 16, 20, 24, 28
GROUPS = 32
QC = 16


def dot(a, b):
    return lax.dot_general(a, b, (((1,), (0,)), ((), ())), preferred_element_type=F32)


def dot_nt(a, b):
    return lax.dot_general(a, b, (((1,), (1,)), ((), ())), preferred_element_type=F32)


def dot_tn(a, b):
    return lax.dot_general(a, b, (((0,), (0,)), ((), ())), preferred_element_type=F32)


def swap_granules(load, store, depth):
    lane = lax.broadcasted_iota(jnp.int16, (depth, LANES), 1)
    for row_half in range(2):
        for col_half in range(2):
            held = [load(row_half * 8 + k, col_half) for k in range(8)]
            for s in range(3):
                width = 16 << s
                low = (lane & width) == 0
                for k in range(8):
                    if not k & (1 << s):
                        a, b = held[k], held[k | (1 << s)]
                        held[k] = jnp.where(low, a, pltpu.roll(b, width, 1))
                        held[k | (1 << s)] = jnp.where(low, pltpu.roll(a, LANES - width, 1), b)
            for k in range(8):
                store(col_half * 8 + k, row_half, held[k])


def half(t):
    return slice(t * LANES, (t + 1) * LANES)


def loop(count, step, carry=0, unroll=1):
    return lax.fori_loop(0, count, step, carry, unroll=unroll)


def gelu_parts(x):
    root = 0.7978845608028654
    cube = root * 0.044715
    square = x * x
    h = 0.5 * jnp.tanh(x * (cube * square + root)) + 0.5
    value = x * h
    return value, h + value * (1.0 - h) * ((6.0 * cube) * square + 2.0 * root)


def kernel(
    frames_hbm, w_in_t_hbm, grid_mix_hbm, block_mix_hbm, w_out_hbm, conv_w_hbm, cot_hbm,
    rest_out, gframe_out, early_out, tail_out, value_out,
    frames, w_in_t, grid_mix, block_mix, w_out, conv_w, cot, w_in,
    turn, xb, nb, unit, inv, dgelu, gates, bval, u3, v3, gj, gg, xt, bt, bm, gbv,
    a, a_in, x32, b, b_in, c, c_in, d, d_in,
    gated, gbef, jp, row_in, pack_out, pack_in, edge_l, edge_r,
    mixp, mixp_t, gather, spread, se, re0, e0, re1, e1, re2, e2, re3, e3, re5, re6,
    st, rt1, t1, rt2, t2, rt3, sq, rq1, q1, rq2,
    ssem, rsem, isem,
):
    ia = lax.axis_index("ha")
    iw = lax.axis_index("wa")
    up, down = lax.rem(ia + NA - 1, NA), lax.rem(ia + 1, NA)
    left, right = lax.rem(iw + NW - 1, NW), lax.rem(iw + 1, NW)
    lane = lax.broadcasted_iota(jnp.int16, (CH, LANES), 1)
    lane_wide = lax.broadcasted_iota(jnp.int32, (CH, LANES), 1)

    loads = [
        pltpu.make_async_copy(src, dst, isem.at[k])
        for k, (src, dst) in enumerate(
            [
                (frames_hbm, frames),
                (w_in_t_hbm, w_in_t),
                (cot_hbm, cot),
                (conv_w_hbm, conv_w),
                (w_out_hbm, w_out),
                (block_mix_hbm, block_mix),
                (grid_mix_hbm, grid_mix),
            ]
        )
    ]
    for load in loads:
        load.start()

    def push(src, dst, g, where):
        pltpu.make_async_remote_copy(
            src_ref=src, dst_ref=dst, send_sem=ssem.at[g], recv_sem=rsem.at[g], device_id=where, device_id_type=MESH
        ).start()

    near = lax.rem(iw, 2) * 4 + lax.rem(ia, 4)
    far = ia // 4 * 4 + iw // 2

    def near_device(peer):
        return ia // 4 * 4 + lax.rem(peer, 4), iw // 2 * 2 + peer // 4

    def far_device(peer):
        return peer // 4 * 4 + lax.rem(ia, 4), lax.rem(peer, 4) * 2 + lax.rem(iw, 2)

    near_peers = [lax.rem(near + k, NEAR) for k in range(1, NEAR)]
    far_peers = [lax.rem(far + k, FAR) for k in range(1, FAR)]
    twin = near + 1 - 2 * lax.rem(near, 2)

    near_places = [near_device(peer) for peer in near_peers]
    far_places = [far_device(peer) for peer in far_peers]

    def over_near(src_of, dst, g):
        for peer, place in zip(near_peers, near_places):
            push(src_of(peer), dst, g, place)

    def over_far(src_of, dst, g):
        for peer, place in zip(far_peers, far_places):
            push(src_of(peer), dst, g, place)

    def over_y(src_of, dst, g):
        for k in range(1, 4):
            peer = lax.rem(near + 2 * k, NEAR)
            push(src_of(peer // 2), dst, g, near_device(peer))

    def arrived(ref, g):
        pltpu.make_async_copy(ref, ref, rsem.at[g]).wait()

    def gone(ref, g):
        pltpu.make_async_copy(ref, ref, ssem.at[g]).wait()

    def from_near(ref, g):
        arrived(ref.at[pl.ds(0, NEAR - 1)], g)

    def from_far(ref, g):
        arrived(ref.at[pl.ds(0, FAR - 1)], g)

    mine = lax.rem(near, 2) * 512
    level = near // 2

    barrier = pltpu.get_barrier_semaphore()
    peers = [near_device(peer) for peer in near_peers]
    peers += [far_device(peer) for peer in far_peers]
    peers += [(a, b) for a in (up, ia, down) for b in (left, right)] + [(up, iw), (down, iw)]
    for peer in peers:
        pl.semaphore_signal(barrier, inc=1, device_id=peer, device_id_type=MESH)

    def turn_in(src):
        for t in range(2):
            turn[t] = src[:, :, half(t)].astype(F32).reshape(CH * ROWS, LANES)

    def turned(r, t):
        return turn[t, pl.ds(r, CH, stride=ROWS), :]

    def edges(pack, t0, t1, r):
        pack = jnp.where(lane_wide == r, pltpu.roll(t0, r, 1), pack)
        return jnp.where(lane_wide == ROWS + r, pltpu.roll(t1, r + 17, 1), pack)

    def send_halo(field, pack, which, g_row, g_pack):
        pack_out[which] = jnp.concatenate([pack, jnp.zeros_like(pack)], axis=0).T[0:32]
        push(field.at[1, CH : 2 * CH], row_in.at[which, 1], g_row, (up, iw))
        push(field.at[ROWS, CH : 2 * CH], row_in.at[which, 0], g_row, (down, iw))
        for slot, where in enumerate(
            [(ia, right), (down, right), (up, right), (ia, left), (down, left), (up, left)]
        ):
            part = pack_out.at[which, pl.ds(16 if slot < 3 else 0, 16)]
            push(part, pack_in.at[which, pl.ds(16 * slot, 16)], g_pack, where)

    def take_halo(field, which, g_row, g_pack):
        arrived(row_in.at[which], g_row)
        arrived(pack_in.at[which], g_pack)
        field[0, CH : 2 * CH] = jnp.where(ia > 0, row_in[which, 0], jnp.zeros((CH, COLS), BF))
        field[ROWS + 1, CH : 2 * CH] = jnp.where(ia < NA - 1, row_in[which, 1], jnp.zeros((CH, COLS), BF))
        first = jnp.where(ia > 0, 0, 1)
        last = jnp.where(ia < NA - 1, ROWS + 2, ROWS + 1)
        got = jnp.concatenate([pack_in[which], jnp.zeros((32, LANES), BF)], axis=0).T[0:CH]

        def assemble(middle, above, below, has):
            joined = jnp.where(lane == 0, above, jnp.where(lane == ROWS + 1, below, middle))
            inside = (lane_wide >= first) & (lane_wide < jnp.where(has, last, 0))
            return jnp.where(inside, joined, jnp.zeros_like(joined))

        edge_l[...] = assemble(pltpu.roll(got, 1, 1), pltpu.roll(got, 97, 1), pltpu.roll(got, 113, 1), iw > 0)
        edge_r[...] = assemble(pltpu.roll(got, 81, 1), pltpu.roll(got, 49, 1), pltpu.roll(got, 65, 1), iw < NW - 1)

        def shifts(p, carry):
            t0 = field[p, CH : 2 * CH, half(0)]
            t1 = field[p, CH : 2 * CH, half(1)]
            a0, a1 = pltpu.roll(t0, 1, 1), pltpu.roll(t1, 1, 1)
            b0, b1 = pltpu.roll(t0, LANES - 1, 1), pltpu.roll(t1, LANES - 1, 1)
            lh = pltpu.roll(edge_l[...], lax.rem(LANES - p, LANES), 1)
            rh = pltpu.roll(edge_r[...], LANES - 1 - p, 1)
            field[p, 0:CH, half(0)] = jnp.where(lane == 0, lh, a0)
            field[p, 0:CH, half(1)] = jnp.where(lane == 0, a0, a1)
            field[p, 2 * CH :, half(0)] = jnp.where(lane == LANES - 1, b1, b0)
            field[p, 2 * CH :, half(1)] = jnp.where(lane == LANES - 1, rh, b1)
            return carry

        loop(ROWS + 2, shifts, unroll=9)

    def conv_start(w, field):
        y = dot(w, field[0])
        z = dot(w, field[1])
        return z[0:CH], y[0:CH] + z[CH : 2 * CH]

    def conv_step(w, field, r, carry):
        later, now = carry
        y = dot(w, field[r + 2])
        return now + y[2 * CH :], (y[0:CH], later + y[CH : 2 * CH])

    def step_a(n):
        over_near(lambda peer: a.at[n, peer], a_in.at[n, near], G_A + n)

    def step_b(n):
        arrived(a_in.at[n, pl.ds(0, NEAR - 1)], G_A + n)

        def widen(j, carry):
            for t in range(2):
                for r in range(2):
                    x32[n, pl.ds((r * 16 + j * 2 + t) * QC, QC), :] = a_in[n, j, t, r].astype(F32)
            return carry

        loop(NEAR, widen, unroll=8)

        for peer, place in zip([*far_peers, far], [*far_places, None]):
            base = peer // 8 * (16 * QC) + lax.rem(peer, 8) * 2
            slot = b_in if peer is far else b
            for k in range(2):
                slot[n, peer, :, half(k)] = x32[n, pl.ds(base + k, 16, stride=QC), :].astype(BF)
            if peer is not far:
                push(b.at[n, peer], b_in.at[n, far], G_B + n, place)

    def table(n):
        return b_in[n].reshape(256, 256)

    def step_c(n, mix):
        arrived(b_in.at[n, pl.ds(0, FAR - 1)], G_B + n)
        c[n] = dot(mix[...], table(n)).astype(BF).reshape(FAR, 16, 256)
        over_far(lambda peer: c.at[n, peer], c_in.at[n, far], G_C + n)
        c_in[n, far] = c[n, far]

    def step_d(n):
        arrived(c_in.at[n, pl.ds(0, FAR - 1)], G_C + n)

        def unpick(q, carry):
            for r in range(2):
                for k in range(2):
                    x32[n, pl.ds((r * QC + q * 2 + k) * 16, 16), :] = c_in[n, r * 8 + q, :, half(k)].astype(F32)
            return carry

        loop(8, unpick, unroll=8)

        for peer, place in zip([*near_peers, near], [*near_places, None]):
            slot = d_in if peer is near else d
            for t in range(2):
                for r in range(2):
                    slot[n, peer, t, r] = x32[n, pl.ds(r * QC * 16 + peer * 2 + t, QC, stride=16), :].astype(BF)
            if peer is not near:
                push(d.at[n, peer], d_in.at[n, near], G_D + n, place)

    def step_e(n):
        arrived(d_in.at[n, pl.ds(0, NEAR - 1)], G_D + n)

    def order(cell, row):
        found = (row & 0xC1) | ((row & 6) << 3) | ((row & 48) >> 2) | ((row & 8) >> 2)
        return jnp.where(cell == found, 1.0, 0.0).astype(BF)

    loads[0].wait()
    loads[1].wait()
    turn_in(frames)
    w_in[...] = w_in_t[...].astype(F32).T.astype(BF)

    def value_row(slot, peer, low):
        r = peer * 2 + low
        normed = []
        for t in range(2):
            x = turned(r, t)
            xb[r, :, half(t)] = x.astype(BF)
            off = x - jnp.mean(x, axis=0, keepdims=True)
            rstd = lax.rsqrt(jnp.mean(off * off, axis=0, keepdims=True) + EPS)
            u = off * rstd
            unit[r, :, half(t)] = u
            inv[r, :, half(t)] = jnp.broadcast_to(rstd, (8, LANES))
            normed.append(u.astype(BF))
        normed = jnp.concatenate(normed, axis=1)
        nb[r] = normed
        value, slope = gelu_parts(dot(w_in[HC:CH], normed))
        dgelu[r, HC:CH] = slope
        value = value.astype(BF)
        for n in VALUES:
            for t in range(2):
                slot[n, peer, t, low] = value[n * QC : (n + 1) * QC, half(t)]

    for first in range(0, NEAR, 4):
        group = [*near_peers, near][first : first + 4]
        for peer in group:
            for low in range(2):
                value_row(a_in if peer is near else a, peer, low)
        if first == 0:
            pl.semaphore_wait(barrier, len(peers))
        for peer in group:
            if peer is not near:
                push(a.at[0, peer], a_in.at[0, near], G_A, near_device(peer))
    step_a(1)

    loads[2].wait()
    turn_in(cot)

    def cot_row(r, pack):
        t0, t1 = turned(r, 0).astype(BF), turned(r, 1).astype(BF)
        u3[r + 1, CH : 2 * CH, half(0)] = t0
        u3[r + 1, CH : 2 * CH, half(1)] = t1
        return edges(pack, t0, t1, r)

    pack = loop(ROWS, cot_row, jnp.zeros((CH, LANES), BF), unroll=16)
    send_halo(u3, pack, 0, G_ROW0, G_PACK0)

    w_rest = jnp.concatenate([w_in[0:HC], w_in[CH:]], axis=0)

    def gate_row(r, carry):
        before = dot(w_rest, nb[r])
        value, slope = gelu_parts(before[0:HC])
        gates[r, 0:HC] = value.astype(BF)
        dgelu[r, 0:HC] = slope
        value, slope = gelu_parts(before[HC:])
        dgelu[r, CH:] = slope
        value = value.astype(BF)
        gates[r, HC:CH] = value[0:HC]
        bval[r] = value[HC:]
        return carry

    loop(ROWS, gate_row, unroll=8)
    for load in loads[3:]:
        load.wait()
    down_axis = lax.broadcasted_iota(jnp.int32, (COLS, COLS), 0)
    along_axis = lax.broadcasted_iota(jnp.int32, (COLS, COLS), 1)
    gather[...] = order(along_axis, down_axis)
    spread[...] = order(down_axis, along_axis)
    mixp[...] = dot(dot(gather[...], grid_mix[...]).astype(BF), spread[...]).astype(BF)
    mixp_t[...] = mixp[...].T

    back_w = jnp.concatenate(
        [jnp.concatenate([conv_w[2 - a, 2 - b] for a in range(3)], axis=1) for b in range(3)], axis=0
    ).astype(F32).T.astype(BF)
    w_out_t = w_out[...].astype(F32).T.astype(BF)
    take_halo(u3, 0, G_ROW0, G_PACK0)

    def back_row(r, carry):
        total, carry = conv_step(back_w, u3, r, carry)
        g = (total + u3[r + 1, CH : 2 * CH].astype(F32)).astype(BF)
        gj[r] = g
        up_gated = dot(w_out_t, g)
        gg[r] = up_gated
        mixed = (up_gated[0:HC] * gates[r, 0:HC].astype(F32)).astype(BF)
        for n in range(2):
            for t in range(2):
                a[2 + n, r // 2, t, r % 2] = mixed[n * QC : (n + 1) * QC, half(t)]
        return carry

    step_b(0)
    carry = conv_start(back_w, u3)
    for first in range(0, NEAR, 4):
        if first:
            step_b(1)
        for r in range(2 * first, 2 * first + 8):
            carry = back_row(r, carry)
        for peer in range(first, first + 4):

            @pl.when(peer != near)
            def _():
                push(a.at[2, peer], a_in.at[2, near], G_A + 2, near_device(peer))

    step_a(3)
    for n in BACKS:
        a_in[n, near] = a[n, near]


    def put(ref):
        def store(k, t, value):
            ref[k, :, half(t)] = value

        return store

    swap_granules(lambda k, t: bval[k, :, half(t)], put(xt), HC)
    values = xt[...].reshape(ROWS * HC, COLS)
    mixed = dot_nt(values, block_mix[...]).astype(BF)
    swap_granules(lambda k, t: mixed[k * HC : (k + 1) * HC, half(t)], put(bm), HC)

    step_c(0, mixp)

    def block_back(k, t):
        return (gg[k, HC:, half(t)] * gates[k, HC:, half(t)].astype(F32)).astype(BF)

    swap_granules(block_back, put(bt), HC)
    backs = bt[...].reshape(ROWS * HC, COLS)
    unmixed = dot(backs, block_mix[...]).astype(BF)
    swap_granules(lambda k, t: unmixed[k * HC : (k + 1) * HC, half(t)], put(gbv), HC)

    step_c(1, mixp)
    step_b(2)

    part_block = dot_tn(backs, values).astype(BF)
    se[2 * COLS : 3 * COLS] = part_block[:, half(0)]
    se[3 * COLS :] = part_block[:, half(1)]

    step_b(3)

    def block_before_row(r, carry):
        d = dgelu[r, CH:]
        gbef[r, CH : CH + HC] = (d[0:HC] * (gg[r, HC:] * (bm[r].astype(F32) + 1.0))).astype(BF)
        gbef[r, CH + HC :] = (d[HC:] * gbv[r].astype(F32)).astype(BF)
        gbef[r, HC:CH] = jnp.zeros((HC, COLS), BF)
        return carry

    loop(ROWS, block_before_row, unroll=16)
    for k in (0, 1, ROWS + 2, ROWS + 3):
        jp[k] = jnp.zeros((CH, COLS), BF)

    step_d(0)
    step_d(1)
    step_c(2, mixp_t)
    step_c(3, mixp_t)

    part_grid = (dot_nt(table(2), table(0)) + dot_nt(table(3), table(1))).astype(BF)
    part_grid = dot(dot(spread[...], part_grid).astype(BF), gather[...]).astype(BF)
    se[0:COLS] = part_grid[:, half(0)]
    se[COLS : 2 * COLS] = part_grid[:, half(1)]
    push(se.at[pl.ds(pl.multiple_of(512 - mine, 512), 512)], re0, G_E0, near_device(twin))

    arrived(re0, G_E0)
    e0[...] = (se[pl.ds(pl.multiple_of(mine, 512), 512)].astype(F32) + re0[...].astype(F32)).astype(BF)
    over_y(lambda peer: e0.at[pl.ds(pl.multiple_of(peer * 128, 128), 128)], re1.at[level], G_E1)
    re1[level] = e0[pl.ds(pl.multiple_of(level * 128, 128), 128)]

    step_e(0)
    step_e(1)

    def returned(chains, r):
        return [
            jnp.concatenate([d_in[n, r // 2, t, lax.rem(r, 2)] for n in chains], axis=0).astype(F32) for t in range(2)
        ]

    def joined_row(r, pack):
        grid_mixed = returned(VALUES, r)
        for t in range(2):
            gates_t = gates[r, :, half(t)].astype(F32)
            more = grid_mixed[t] + 1.0
            gated[r, 0:HC, half(t)] = (gates_t[0:HC] * more).astype(BF)
            gated[r, HC:, half(t)] = (gates_t[HC:] * (bm[r, :, half(t)].astype(F32) + 1.0)).astype(BF)
            gbef[r, 0:HC, half(t)] = (dgelu[r, 0:HC, half(t)] * (gg[r, 0:HC, half(t)] * more)).astype(BF)
        j = (xb[r].astype(F32) + dot(w_out[...], gated[r])).astype(BF)
        jp[r + 2] = j
        v3[r + 1, CH : 2 * CH] = j
        return edges(pack, j[:, half(0)], j[:, half(1)], r)

    pack = loop(ROWS, joined_row, jnp.zeros((CH, LANES), BF), unroll=16)
    send_halo(v3, pack, 1, G_ROW1, G_PACK1)

    step_d(2)
    step_d(3)

    def pixels(ref, rows=slice(None)):
        return jnp.concatenate([ref[r, rows] for r in range(ROWS)], axis=1)

    p_conv = dot_nt(
        jnp.concatenate([u3[p] for p in range(ROWS + 2)], axis=1),
        jnp.concatenate([jp[p : p + 3].reshape(3 * CH, COLS) for p in range(ROWS + 2)], axis=1),
    )
    arrived(re1.at[pl.ds(0, 3)], G_E1)
    total = re1[0].astype(F32)
    for k in range(1, 4):
        total = total + re1[k].astype(F32)
    e1[...] = total
    over_far(lambda peer: e1.at[pl.ds(pl.multiple_of(peer * 8, 8), 8)], re2.at[far], G_E2)
    re2[far] = e1[pl.ds(pl.multiple_of(far * 8, 8), 8)]

    p_in = dot_nt(pixels(nb), pixels(gbef))
    p_out = dot_nt(pixels(gj), pixels(gated))
    st[0 : 3 * CH] = p_conv[:, half(0)].astype(BF)
    st[3 * CH : 4 * CH] = p_in.astype(BF)
    third = p_conv[:, 2 * CH :]
    st[4 * CH :] = jnp.concatenate(
        [third[: 2 * CH], jnp.concatenate([third[2 * CH :], p_out], axis=0)], axis=1
    ).astype(BF)
    summing = far < 12
    for peer, place in zip(far_peers, far_places):

        @pl.when(peer < 12)
        def _():
            push(st.at[pl.ds(pl.multiple_of(peer * 32, 32), 32)], rt1.at[far], G_T1, place)

    @pl.when(summing)
    def _():
        rt1[far] = st[pl.ds(pl.multiple_of(far * 32, 32), 32)]

    take_halo(v3, 1, G_ROW1, G_PACK1)

    conv_k = jnp.concatenate(
        [jnp.concatenate([conv_w[a, b] for b in range(3)], axis=1) for a in range(3)], axis=0
    )

    def out_row(r, carry):
        total, carry = conv_step(conv_k, v3, r, carry)
        total = total + v3[r + 1, CH : 2 * CH].astype(F32)
        for t in range(2):
            rest_out[t, pl.ds(r, CH, stride=ROWS), :] = total[:, half(t)]
        return carry

    carry = loop(ROWS // 2, out_row, conv_start(conv_k, v3), unroll=8)

    from_far(re2, G_E2)
    total = re2[0]
    for k in range(1, FAR):
        total = total + re2[k]
    e2[...] = total
    over_far(lambda peer: e2, re3.at[far], G_E3)
    re3[far] = e2[...]

    step_e(2)
    step_e(3)

    def value_before_row(r, carry):
        grid_back = returned(BACKS, r)
        for t in range(2):
            gbef[r, HC:CH, half(t)] = (dgelu[r, HC:CH, half(t)] * grid_back[t]).astype(BF)
        return carry

    loop(ROWS, value_before_row, unroll=16)
    p_value = dot_nt(pixels(gbef, slice(HC, CH)), pixels(nb))
    sq[...] = jnp.concatenate([p_value[0:16], p_value[16:]], axis=1).astype(BF)
    over_near(lambda peer: sq, rq1.at[near], G_Q1)
    rq1[near] = sq[...]

    for n in VALUES + BACKS:
        for ref, count, g in ((a_in, NEAR, G_A), (b_in, FAR, G_B), (c_in, FAR, G_C)):
            gone(ref.at[n, pl.ds(0, count - 1)], g + n)
    for n in VALUES:
        gone(d_in.at[n, pl.ds(0, NEAR - 1)], G_D + n)

    @pl.when(summing)
    def _():
        from_far(rt1, G_T1)
        total = rt1[0].astype(F32)
        for k in range(1, FAR):
            total = total + rt1[k].astype(F32)
        t1[...] = total.astype(BF)
        over_near(lambda peer: t1, rt2.at[near], G_T2)
        rt2[near] = t1[...]

    from_far(re3, G_E3)
    e3[...] = re3[...].reshape(128, LANES).astype(BF)
    over_y(lambda peer: e3, re5.at[level], G_E5)
    re5[level] = e3[...]

    def frame_row(r, carry):
        normed = dot(w_in_t[...], gbef[r])
        u = unit[r]
        mean_grad = jnp.mean(normed, axis=0, keepdims=True)
        mean_proj = jnp.mean(normed * u, axis=0, keepdims=True)
        source = gj[r].astype(F32) + inv[r, 0:1] * (normed - mean_grad - u * mean_proj)
        for t in range(2):
            gframe_out[t, pl.ds(r, CH, stride=ROWS), :] = source[:, half(t)]
        return carry

    loop(ROWS, frame_row, unroll=16)

    carry = loop(ROWS // 4, lambda r, carry: out_row(r + ROWS // 2, carry), carry, unroll=4)

    @pl.when(summing)
    def _():
        from_near(rt2, G_T2)
        total = rt2[0].astype(F32)
        for k in range(1, NEAR):
            total = total + rt2[k].astype(F32)
        t2[...] = total.astype(BF)
        over_far(lambda peer: t2, rt3.at[far], G_T3)
        rt3[far] = t2[...]

    from_near(rq1, G_Q1)
    total = rq1[0].astype(F32)
    for k in range(1, NEAR):
        total = total + rq1[k].astype(F32)
    q1[...] = total.astype(BF)
    over_far(lambda peer: q1, rq2.at[far], G_Q2)
    rq2[far] = q1[...]

    loop(ROWS // 4, lambda r, carry: out_row(r + 3 * ROWS // 4, carry), carry, unroll=4)

    from_far(rq2, G_Q2)
    total = rq2[0].astype(F32)
    for k in range(1, FAR):
        total = total + rq2[k].astype(F32)
    value_out[...] = total

    arrived(re5.at[pl.ds(0, 3)], G_E5)
    push(re5, re6, G_E6, near_device(twin))
    early_out[pl.ds(pl.multiple_of(mine, 512), 512)] = re5[...].reshape(512, LANES)

    @pl.when(summing)
    def _():
        arrived(rt3.at[pl.ds(0, 11)], G_T3)
        gone(rt1.at[pl.ds(0, 11)], G_T1)
        gone(rt2.at[pl.ds(0, NEAR - 1)], G_T2)
        gone(rt1.at[pl.ds(0, FAR - 1)], G_T3)

    @pl.when(far >= 12)
    def _():
        arrived(rt3, G_T3)
        gone(rt1.at[pl.ds(0, 12)], G_T1)

    tail_out[...] = rt3[...]
    arrived(re6, G_E6)
    early_out[pl.ds(pl.multiple_of(512 - mine, 512), 512)] = re6[...].reshape(512, LANES)

    for which, g_row, g_pack in ((0, G_ROW0, G_PACK0), (1, G_ROW1, G_PACK1)):
        gone(row_in.at[which], g_row)
        gone(pack_in.at[which], g_pack)
    for n in BACKS:
        gone(d_in.at[n, pl.ds(0, NEAR - 1)], G_D + n)
    gone(rq1.at[pl.ds(0, NEAR - 1)], G_Q1)
    gone(rq2.at[pl.ds(0, FAR - 1)], G_Q2)
    gone(re0, G_E0)
    for ref, g in ((re1, G_E1), (re5, G_E5)):
        gone(ref.at[pl.ds(0, 3)], g)
    for ref, g in ((re2, G_E2), (re3, G_E3)):
        gone(ref.at[pl.ds(0, FAR - 1)], g)
    gone(re6, G_E6)


def finish(rest, gframe, early, tail, value, *refs):
    outs, sem = (refs[:7], refs[7:14]), refs[14]
    restored, grad_frames, grad_w_in_t, grad_grid, grad_block, grad_w_out, grad_conv = outs[1]
    copies = []

    def leave(k, part=None):
        src, dst = outs[1][k], outs[0][k]
        if part is not None:
            src, dst = src.at[part], dst.at[part]
        copies.append(pltpu.make_async_copy(src, dst, sem.at[len(copies)]))
        copies[-1].start()

    def turn_out(src, dst, k):
        for first in range(0, CH, CH // 2):

            part = pl.ds(first * ROWS, CH // 2 * ROWS)
            for t in range(2):
                dst[first : first + CH // 2, :, half(t)] = src[t, part, :].astype(BF).reshape(CH // 2, ROWS, LANES)
            leave(k, pl.ds(first, CH // 2))

    scale = float(ROWS * NA * COLS * NW) ** (-0.5)
    for k in range(2):
        grad_grid[:, half(k)] = early[k * COLS : (k + 1) * COLS].astype(F32) * scale
        grad_block[:, half(k)] = early[(2 + k) * COLS : (3 + k) * COLS].astype(F32) * scale
    leave(3)
    leave(4)
    turn_out(gframe, grad_frames, 1)
    turn_out(rest, restored, 0)
    quarter = value[...] * scale
    zeros = jnp.zeros((HC, CH), F32)
    quarter = jnp.concatenate([zeros, quarter[:, :CH], quarter[:, CH:], zeros, zeros], axis=0)
    grad_w_in_t[...] = tail[3 * CH : 4 * CH].astype(F32) * scale + quarter.T
    leave(2)
    last = tail[4 * CH :].astype(F32) * scale
    grad_w_out[...] = last[CH:, CH:]
    leave(5)
    for b in range(3):
        rows = slice((2 - b) * CH, (3 - b) * CH)
        pair = tail[rows].astype(F32) * scale
        grad_conv[0, b] = pair[:, :CH]
        grad_conv[1, b] = pair[:, CH:]
    grad_conv[2, 2] = last[:CH, :CH]
    grad_conv[2, 1] = last[CH:, :CH]
    grad_conv[2, 0] = last[:CH, CH:]
    leave(6)
    for copy in copies:
        copy.wait()


def vm(*shape, dtype=BF):
    return pltpu.VMEM(shape, dtype)


def exchange():
    message_w = vm(4, NEAR, 2, 2, QC, LANES)
    message_a = vm(4, FAR, 16, 256)
    return [message_w, message_w, vm(4, 2 * 16 * QC, LANES, dtype=F32)] + [message_a] * 4 + [message_w] * 2


SCRATCH = [
    vm(CH, ROWS, COLS),
    vm(CH, 2 * CH),
    vm(COLS, COLS),
    vm(COLS, COLS),
    vm(CH, CH),
    vm(3, 3, CH, CH),
    vm(CH, ROWS, COLS),
    vm(2 * CH, CH),
    vm(2, CH * ROWS, LANES, dtype=F32),
    vm(ROWS, CH, COLS),
    vm(ROWS, CH, COLS),
    vm(ROWS, CH, COLS, dtype=F32),
    vm(ROWS, 8, COLS, dtype=F32),
    vm(ROWS, 2 * CH, COLS, dtype=F32),
    vm(ROWS, CH, COLS),
    vm(ROWS, HC, COLS),
    vm(ROWS + 2, 3 * CH, COLS),
    vm(ROWS + 2, 3 * CH, COLS),
    vm(ROWS, CH, COLS),
    vm(ROWS, CH, COLS, dtype=F32),
    vm(ROWS, HC, COLS),
    vm(ROWS, HC, COLS),
    vm(ROWS, HC, COLS),
    vm(ROWS, HC, COLS),
    *exchange(),
    vm(ROWS, CH, COLS),
    vm(ROWS, 2 * CH, COLS),
    vm(ROWS + 4, CH, COLS),
    vm(2, 2, CH, COLS),
    vm(2, 32, LANES),
    vm(2, 96, LANES),
    vm(CH, LANES),
    vm(CH, LANES),
    vm(COLS, COLS),
    vm(COLS, COLS),
    vm(COLS, COLS),
    vm(COLS, COLS),
    vm(4 * COLS, LANES),
    vm(512, LANES),
    vm(512, LANES),
    vm(4, 128, LANES),
    vm(128, LANES, dtype=F32),
    vm(FAR, 8, LANES, dtype=F32),
    vm(8, LANES, dtype=F32),
    vm(FAR, 8, LANES, dtype=F32),
    vm(128, LANES),
    vm(4, 128, LANES),
    vm(4, 128, LANES),
    vm(6 * CH, LANES),
    vm(FAR, 32, LANES),
    vm(32, LANES),
    vm(NEAR, 32, LANES),
    vm(32, LANES),
    vm(12, 32, LANES),
    vm(16, LANES),
    vm(NEAR, 16, LANES),
    vm(16, LANES),
    vm(FAR, 16, LANES),
    pltpu.SemaphoreType.DMA((GROUPS,)),
    pltpu.SemaphoreType.DMA((GROUPS,)),
    pltpu.SemaphoreType.DMA((7,)),
]


def body(frames, w_in, grid_mix, block_mix, w_out, conv_w, cotangent):
    operands = (frames, w_in.T, grid_mix, block_mix, w_out, conv_w, cotangent)
    vmem = pl.BlockSpec(memory_space=pltpu.VMEM)
    shape = jax.ShapeDtypeStruct
    rest, gframe, early, tail, value = pl.pallas_call(
        kernel,
        out_shape=(
            shape((2, ROWS * CH, LANES), F32),
            shape((2, ROWS * CH, LANES), F32),
            shape((4 * COLS, LANES), BF),
            shape((12, 32, LANES), BF),
            shape((16, LANES), F32),
        ),
        in_specs=[pl.BlockSpec(memory_space=pltpu.HBM)] * 7,
        out_specs=(vmem,) * 5,
        scratch_shapes=SCRATCH,
        compiler_params=pltpu.CompilerParams(
            collective_id=0, has_side_effects=True, vmem_limit_bytes=32 * 1024 * 1024
        ),
    )(*[pltpu.with_memory_space_constraint(x, pltpu.HBM) for x in operands])
    restored, grad_frames, grad_w_in_t, grad_grid, grad_block, grad_w_out, grad_conv = pl.pallas_call(
        finish,
        out_shape=(
            shape((CH, ROWS, COLS), BF),
            shape((CH, ROWS, COLS), BF),
            shape((CH, 2 * CH), F32),
            shape((COLS, COLS), F32),
            shape((COLS, COLS), F32),
            shape((CH, CH), F32),
            shape((3, 3, CH, CH), F32),
        ),
        in_specs=[vmem] * 5,
        out_specs=(pl.BlockSpec(memory_space=pl.ANY),) * 7,
        scratch_shapes=[
            vm(CH, ROWS, COLS),
            vm(CH, ROWS, COLS),
            vm(CH, 2 * CH, dtype=F32),
            vm(COLS, COLS, dtype=F32),
            vm(COLS, COLS, dtype=F32),
            vm(CH, CH, dtype=F32),
            vm(3, 3, CH, CH, dtype=F32),
            pltpu.SemaphoreType.DMA((9,)),
        ],
        compiler_params=pltpu.CompilerParams(vmem_limit_bytes=16 * 1024 * 1024),
    )(rest, gframe, early, tail.reshape(6 * CH, LANES), value)
    return restored, grad_frames, grad_w_in_t.T, grad_grid, grad_block, grad_w_out, grad_conv


def solution(mesh):
    placed = (P(None, "ha", "wa"), P(), P(), P(), P(), P(), P(None, "ha", "wa"))
    return jax.shard_map(
        body,
        mesh=mesh,
        in_specs=placed,
        out_specs=(P(None, "ha", "wa"), P(None, "ha", "wa"), P(), P(), P(), P(), P()),
        check_vma=False,
    )
```
